32 devices in a mesh: dp: 2 (over y), seq: 16 (over z, x, core).
Axes of the slice: x: 2, y: 2, z: 4, core: 2. Of those that a mesh axis runs over, the one named last changes fastest.
Arguments:
- enc_act: bfloat16 [2, 256, 18944], P('dp', None, 'seq'), may hold values from -6 to 6
- down_weight: bfloat16 [18944, 3584], P('seq'), may hold values from -0.046875 to 0.046875
- norm_gain: bfloat16 [3584], replicated, may hold values from 0.099609375 to 1.8984375
- text_in_weight: bfloat16 [3584, 3072], P(None, 'seq'), may hold values from -0.09375 to 0.09375
- modulation_weight: bfloat16 [256, 2, 3072], P(None, None, 'seq'), may hold values from -0.375 to 0.375
- key_value_weight: bfloat16 [3072, 4096], P('seq'), may hold values from -0.109375 to 0.109375
- timesteps: int32 [2], P('dp'), may hold values from 0 to 999
- lengths: int32 [2], P('dp'), may hold values from 32 to 256, as said below
- image_queries: bfloat16 [2, 2048, 2048], P('dp', 'seq'), may hold values from -8 to 8
- image_key_values: bfloat16 [2, 2048, 2, 2048], P('dp', 'seq'), may hold values from -8 to 8
Outputs:
- attended: bfloat16 [2, 2048, 2048], P('dp', 'seq')
- text_kv: bfloat16 [512, 4096], P(('dp', 'seq'))
The draws below stay inside these ranges and needn't reach their ends.
Inputs may be any that keep to these rules, and one draw needn't show every extreme that they name: `lengths`: some prompt has all 256 tokens valid.
All inputs are finite; a program needn't handle non-finite values.
Results may differ from the reference program's by a relative error of at most 0.022.
Values may be sent and summed in bfloat16 or wider, within the bound.
No kernel may reach another device: no remote copies, remote signals or barrier semaphores. Data moves between devices by JAX's collectives and lax.ppermute only.
A program may use at most 64 MiB of HBM per device.

```python
import math
import jax
import jax.numpy as jnp
from jax import lax

D_E = 3584
FF_E = 18944
D = 3072
HEAD_DIM = 128
HEADS = 16
TEMB = 256
TXT_LEN = 256
IMAGES = 2
IMG_LEN = 2048
N_SEQ = 16


def draw_image_queries(key, part):
    shape = (IMAGES, IMG_LEN, HEADS * HEAD_DIM)
    key = jax.random.fold_in(key, 11)
    base = jnp.clip(1.5 * jax.random.normal(key, shape, jnp.float32), -8.0, 8.0)
    return base.astype(jnp.bfloat16)


def draw_image_key_values(key, part):
    shape = (IMAGES, IMG_LEN, 2, HEADS * HEAD_DIM)
    key = jax.random.fold_in(key, 12)
    base = jnp.clip(1.5 * jax.random.normal(key, shape, jnp.float32), -8.0, 8.0)
    return base.astype(jnp.bfloat16)


def draw_lengths(key, part):
    key = jax.random.fold_in(key, 13)
    first, second = jax.random.split(key)
    drawn = jax.random.randint(first, (IMAGES,), TXT_LEN // 8, TXT_LEN + 1, jnp.int32)
    chosen = jax.random.randint(second, (), 0, IMAGES, jnp.int32)
    positions = jnp.arange(IMAGES, dtype=jnp.int32)
    return jnp.where(positions == chosen, TXT_LEN, drawn).astype(jnp.int32)


def block_scale(own_key, extent, cuts, least, high):
    loudness = 1.0
    for axis_at, blocks in cuts:
        steps = jax.random.uniform(jax.random.fold_in(jax.random.fold_in(own_key, 6), axis_at), (blocks,), jnp.float32, least / len(cuts), high / len(cuts))
        loudness = loudness * jnp.repeat(jnp.exp(steps), extent[axis_at] // blocks).reshape((-1,) + (1,) * (len(extent) - 1 - axis_at))
    return loudness


def bell_draw(key, extent, scale, limit, pieces=(), held_as=jnp.bfloat16):
    values = jax.random.normal(key, extent, jnp.float32) * scale
    if len(pieces) > 0:
        values = block_scale(key, extent, pieces, -0.22, 0.18) * values
    return jnp.clip(values, min=-limit, max=limit).astype(held_as)


def setup_inputs(seed: int = 0) -> dict:
    splits = jax.random.split(jax.random.key(seed), 11)
    return {
        "enc_act": bell_draw(splits[0], (IMAGES, TXT_LEN, FF_E), 1.0, 6.0, ((0, 2), (2, 16))),
        "down_weight": bell_draw(splits[1], (FF_E, D_E), FF_E ** -0.5, 0.046875, ((0, 16),)),
        "norm_gain": jnp.clip(1.0 + 0.18 * jax.random.normal(splits[2], (D_E,), jnp.float32), 0.099609375, 1.8984375).astype(jnp.bfloat16),
        "text_in_weight": bell_draw(splits[3], (D_E, D), D_E ** -0.5, 0.09375, ((1, 16),)),
        "modulation_weight": bell_draw(splits[4], (TEMB, 2, D), TEMB ** -0.5, 0.375, ((2, 16),)),
        "key_value_weight": bell_draw(splits[5], (D, 2 * HEADS * HEAD_DIM), D ** -0.5, 0.109375, ((0, 16),)),
        "timesteps": jax.random.randint(splits[6], (IMAGES,), 0, 1000).astype(jnp.int32),
        "lengths": draw_lengths(jax.random.fold_in(splits[10], 71), 0),
        "image_queries": draw_image_queries(jax.random.fold_in(splits[10], 71), 0),
        "image_key_values": draw_image_key_values(jax.random.fold_in(splits[10], 71), 0),
    }


epsilon = 1e-06

def rounded(value):
    return lax.optimization_barrier(value.astype(jnp.bfloat16)).astype(jnp.float32)

def normalize(summed, norm_gain):
    scale_rows = lax.rsqrt(lax.optimization_barrier(jnp.mean(summed * summed, 1, keepdims=True)) + epsilon)
    return (summed * scale_rows * norm_gain.astype(jnp.float32)).astype(jnp.bfloat16)

def time_embedding(timesteps, modulation_weight):
    half_width = TEMB // 2
    freqs = jnp.exp(-math.log(10000.0) * jnp.arange(half_width, dtype=jnp.float32) / half_width)
    angles = timesteps.astype(jnp.float32)[:, None] * freqs[None, :]
    embedding = jnp.concatenate([jnp.cos(angles), jnp.sin(angles)], 1)
    embedding = jax.nn.silu(embedding).astype(jnp.bfloat16)
    flat = modulation_weight.reshape(modulation_weight.shape[0], -1)
    product = jnp.dot(embedding, flat, preferred_element_type=jnp.float32)
    return product.reshape(timesteps.shape[0], 2, -1)

def attend(queries, key_rows, value_rows, text_keys, text_values, valid_len):
    factor = 1.0 / math.sqrt(queries.shape[1])
    contract = (((1,), (1,)), ((), ()))
    img_scores = lax.dot_general(queries, key_rows, contract, preferred_element_type=jnp.float32) * factor
    txt_scores = lax.dot_general(queries, text_keys, contract, preferred_element_type=jnp.float32) * factor
    positions = jnp.arange(text_keys.shape[0], dtype=jnp.int32)
    txt_scores = jnp.where(positions[None, :] < valid_len, txt_scores, -jnp.inf)
    row_max = jnp.maximum(lax.optimization_barrier(jnp.max(img_scores, 1)), lax.optimization_barrier(jnp.max(txt_scores, 1)))[:, None]
    img_weights = jnp.exp(img_scores - row_max)
    txt_weights = jnp.exp(txt_scores - row_max)
    denominator = lax.optimization_barrier(jnp.sum(img_weights, 1)) + lax.optimization_barrier(jnp.sum(txt_weights, 1))
    mixed = jnp.dot(img_weights.astype(jnp.bfloat16), value_rows, preferred_element_type=jnp.float32)
    mixed = mixed + jnp.dot(txt_weights.astype(jnp.bfloat16), text_values, preferred_element_type=jnp.float32)
    return (mixed / denominator[:, None]).astype(jnp.bfloat16)

def reference(enc_act, down_weight, norm_gain, text_in_weight, modulation_weight, key_value_weight, timesteps, lengths, image_queries, image_key_values):
    rows_all = IMAGES * TXT_LEN
    width = HEADS * HEAD_DIM
    hidden_act = enc_act.reshape(rows_all, FF_E)
    ff_share = FF_E // N_SEQ

    def encoder_term(index_s, summed):
        start = (index_s * ff_share).astype(jnp.int32)
        cols = lax.dynamic_slice_in_dim(hidden_act, start, ff_share, 1)
        weight_rows = lax.dynamic_slice_in_dim(down_weight, start, ff_share, 0)
        return summed + rounded(jnp.dot(cols, weight_rows, preferred_element_type=jnp.float32))
    summed = lax.fori_loop(0, N_SEQ, encoder_term, jnp.zeros((rows_all, D_E), jnp.float32))
    text_states = normalize(summed, norm_gain)
    text_proj = jnp.dot(text_states, text_in_weight, preferred_element_type=jnp.float32)
    mean_val = lax.optimization_barrier(jnp.sum(text_proj, 1)) / D
    variance = lax.optimization_barrier(jnp.sum(text_proj * text_proj, 1)) / D - mean_val * mean_val
    centred = (text_proj - mean_val[:, None]) * lax.rsqrt(variance + epsilon)[:, None]
    modulation = time_embedding(timesteps, modulation_weight)
    shaped = centred.reshape(IMAGES, TXT_LEN, D)
    modulated = (shaped * (1.0 + modulation[:, 1][:, None]) + modulation[:, 0][:, None]).astype(jnp.bfloat16)
    modulated = modulated.reshape(rows_all, D)
    d_share = D // N_SEQ

    def key_value_term(index_s, summed_kv):
        start = (index_s * d_share).astype(jnp.int32)
        cols = lax.dynamic_slice_in_dim(modulated, start, d_share, 1)
        weight_rows = lax.dynamic_slice_in_dim(key_value_weight, start, d_share, 0)
        return summed_kv + rounded(jnp.dot(cols, weight_rows, preferred_element_type=jnp.float32))
    text_sum = lax.fori_loop(0, N_SEQ, key_value_term, jnp.zeros((rows_all, 2 * width), jnp.float32))
    text_kv = text_sum.astype(jnp.bfloat16)
    queries = image_queries.reshape(IMAGES, IMG_LEN, HEADS, HEAD_DIM).transpose(0, 2, 1, 3)
    pairs = image_key_values.reshape(IMAGES, IMG_LEN, 2, HEADS, HEAD_DIM).transpose(0, 3, 2, 1, 4)
    text_pairs = text_kv.reshape(IMAGES, TXT_LEN, 2, HEADS, HEAD_DIM).transpose(0, 3, 2, 1, 4)

    def per_image(items):
        query_heads, pair_heads, text_heads, valid_len = items

        def per_head(inner):
            head_queries, head_pairs, head_text = inner
            return attend(head_queries, head_pairs[0], head_pairs[1], head_text[0], head_text[1], valid_len)
        return lax.map(per_head, (query_heads, pair_heads, text_heads))
    attended = lax.map(per_image, (queries, pairs, text_pairs, lengths))
    attended = attended.transpose(0, 2, 1, 3).reshape(IMAGES, IMG_LEN, width)
    return (attended, text_kv)
```

```python
import functools
import math

import jax
import jax.numpy as jnp
from jax import lax
from jax.experimental import pallas as pl
from jax.experimental.pallas import tpu as pltpu
from jax.sharding import PartitionSpec as P

HEAD_DIM = 128
HEADS = 16
TEMB = 256
VMEM_LIMIT = 56 * 1024 * 1024

epsilon = 1e-06

SMEM_SPEC = pl.BlockSpec(memory_space=pltpu.SMEM)
VMEM_SPEC = pl.BlockSpec(memory_space=pltpu.VMEM)


def params(**more):
    return pltpu.CompilerParams(vmem_limit_bytes=VMEM_LIMIT, **more)


def swap(value, mask):
    devices = lax.axis_size("seq")
    return lax.ppermute(value, "seq", [(i, i ^ mask) for i in range(devices)])


def reverse_bits(value, chips):
    count = chips.bit_length() - 1
    return sum(((value >> i) & 1) << (count - 1 - i) for i in range(count))


def normalize(summed, norm_gain):
    scale_rows = lax.rsqrt(jnp.mean(summed * summed, 1, keepdims=True) + epsilon)
    return (summed * scale_rows * norm_gain.astype(jnp.float32)).astype(jnp.bfloat16)


def time_embedding(timesteps, modulation_weight):
    half_width = TEMB // 2
    freqs = jnp.exp(-math.log(10000.0) * jnp.arange(half_width, dtype=jnp.float32) / half_width)
    angles = timesteps.astype(jnp.float32)[:, None] * freqs[None, :]
    embedding = jnp.concatenate([jnp.cos(angles), jnp.sin(angles)], 1)
    embedding = jax.nn.silu(embedding).astype(jnp.bfloat16)
    flat = modulation_weight.reshape(modulation_weight.shape[0], -1)
    product = jnp.dot(embedding, flat, preferred_element_type=jnp.float32)
    return product.reshape(timesteps.shape[0], 2, -1)


def encoder_kernel(chips, place_ref, act_ref, weight_ref, own_ref, other_ref, lhs_ref):
    chip_reversed, core = place_ref[0], place_ref[1]

    @pl.when(pl.program_id(0) == 0)
    def _():
        lhs_ref[...] = act_ref[...].T

    result = jnp.dot(lhs_ref[...], weight_ref[...], preferred_element_type=jnp.float32)
    half = result.shape[0] // 2
    share = half // chips
    first = core == 0
    own = jnp.where(first, result[:half], result[half:]).astype(own_ref.dtype)
    other = jnp.where(first, result[half:], result[:half]).astype(own_ref.dtype)
    own = own.reshape(chips, share, -1)
    other = other.reshape(chips, share, -1)
    for block in range(chips):
        at = chip_reversed ^ reverse_bits(block, chips)
        own_ref[at] = own[block]
        other_ref[at] = other[block]


def encoder(place, act, weight, chips):
    depth, rows = act.shape
    width = weight.shape[1]
    tile = 512
    share = rows // 2 // chips
    out = jax.ShapeDtypeStruct((chips, share, width), jnp.bfloat16)
    out_spec = pl.BlockSpec((chips, share, tile), lambda i: (0, 0, i))
    return pl.pallas_call(
        functools.partial(encoder_kernel, chips),
        grid=(width // tile,),
        out_shape=(out, out),
        in_specs=[
            SMEM_SPEC,
            pl.BlockSpec((depth, rows), lambda i: (0, 0)),
            pl.BlockSpec((depth, tile), lambda i: (0, i)),
        ],
        out_specs=(out_spec, out_spec),
        scratch_shapes=[pltpu.VMEM((rows, depth), jnp.bfloat16)],
        compiler_params=params(),
        cost_estimate=pl.CostEstimate(
            flops=2 * rows * depth * width,
            bytes_accessed=2 * (depth * rows + depth * width + rows * width),
            transcendentals=0,
        ),
        name="encoder",
    )(place, act, weight)


def project_kernel(chips, count, place_ref, *refs):
    pieces, refs = refs[:count], refs[count:]
    win0, win1, kv0, kv1, mod0, mod1, out_ref, sums_ref, states, lhs0, lhs1, sums = refs
    chip = place_ref[2]
    row = 0
    for piece in pieces:
        states[row : row + piece.shape[0], :] = piece[...]
        row += piece.shape[0]
    share = row // chips
    contract = (((1,), (1,)), ((), ()))
    proj0 = lax.dot_general(states[...], win0[...], contract, preferred_element_type=jnp.float32)
    proj1 = lax.dot_general(states[...], win1[...], contract, preferred_element_type=jnp.float32)
    first = jnp.sum(proj0, 1, keepdims=True) + jnp.sum(proj1, 1, keepdims=True)
    second = jnp.sum(proj0 * proj0, 1, keepdims=True) + jnp.sum(proj1 * proj1, 1, keepdims=True)
    lane = lax.broadcasted_iota(jnp.int32, sums.shape, 1)
    both = jnp.where(lane == 0, first, second)
    scaled0 = proj0 * (1.0 + mod0[1:2, :])
    scaled1 = proj1 * (1.0 + mod1[1:2, :])
    for at in range(chips):
        rows = pl.ds(pl.multiple_of((chip ^ reverse_bits(at, chips)) * share, share), share)
        lhs0[rows, :] = scaled0[at * share : (at + 1) * share]
        lhs1[rows, :] = scaled1[at * share : (at + 1) * share]
        sums[rows, :] = both[at * share : (at + 1) * share]
    sums_ref[...] = sums[...].T[: sums_ref.shape[0]]
    left0 = lhs0[...].astype(jnp.bfloat16)
    left1 = lhs1[...].astype(jnp.bfloat16)
    width = out_ref.shape[2] // 2
    half = kv0.shape[1] // 2
    for at in range(chips):
        for part in range(2):
            column = part * half + (chip ^ reverse_bits(at, chips)) * width
            columns = pl.ds(pl.multiple_of(column, width), width)
            value = jnp.dot(left0, kv0[:, columns], preferred_element_type=jnp.float32)
            value += jnp.dot(left1, kv1[:, columns], preferred_element_type=jnp.float32)
            out_ref[at, :, part * width : (part + 1) * width] = value.astype(out_ref.dtype)


def project(place, pieces, win0, win1, kv0, kv1, mod0, mod1, chips):
    rows = sum(piece.shape[0] for piece in pieces)
    features, depth = win0.shape
    width = kv0.shape[1]
    return pl.pallas_call(
        functools.partial(project_kernel, chips, len(pieces)),
        out_shape=(
            jax.ShapeDtypeStruct((chips, rows, width // chips), jnp.bfloat16),
            jax.ShapeDtypeStruct((8, rows), jnp.float32),
        ),
        in_specs=[SMEM_SPEC] + [VMEM_SPEC] * (len(pieces) + 6),
        out_specs=(VMEM_SPEC, VMEM_SPEC),
        scratch_shapes=[
            pltpu.VMEM((rows, depth), jnp.bfloat16),
            pltpu.VMEM((rows, features), jnp.float32),
            pltpu.VMEM((rows, features), jnp.float32),
            pltpu.VMEM((rows, 128), jnp.float32),
        ],
        compiler_params=params(),
        cost_estimate=pl.CostEstimate(
            flops=4 * rows * features * (depth + width),
            bytes_accessed=2 * (rows * depth + 2 * features * (depth + width) + rows * width),
            transcendentals=0,
        ),
        name="project",
    )(place, *pieces, win0, win1, kv0, kv1, mod0, mod1)


def image_kernel(factor, queries_ref, keys_ref, values_ref, sum_ref, norm_ref):
    contract = (((1,), (1,)), ((), ()))
    queries = queries_ref[...].reshape(-1, HEAD_DIM)
    keys = keys_ref[...].reshape(-1, HEAD_DIM)
    values = values_ref[...].reshape(-1, HEAD_DIM)
    scores = lax.dot_general(queries, keys, contract, preferred_element_type=jnp.float32) * factor
    top = jnp.max(scores, 1, keepdims=True)
    weights = jnp.exp2(scores - top)
    total = jnp.sum(weights, 1, keepdims=True)
    sum_ref[...] = jnp.dot(weights.astype(jnp.bfloat16), values, preferred_element_type=jnp.float32)
    lane = lax.broadcasted_iota(jnp.int32, norm_ref.shape, 1)
    norm_ref[...] = jnp.where(lane < 64, top, total)


def image_attention(packed, img_dev, part_rows, factor):
    devices = packed.shape[0]
    count = devices * part_rows
    group = max(1, 256 // part_rows)
    block = group * part_rows
    at = 2 * img_dev // part_rows
    out = jax.ShapeDtypeStruct((count, HEAD_DIM), jnp.float32)
    out_spec = pl.BlockSpec((block, HEAD_DIM), lambda i: (i, 0))
    keys = devices * img_dev
    return pl.pallas_call(
        functools.partial(image_kernel, factor),
        grid=(devices // group,),
        out_shape=(out, out),
        in_specs=[
            pl.BlockSpec((group, part_rows, HEAD_DIM), lambda i: (i, at, 0)),
            pl.BlockSpec((devices, img_dev, HEAD_DIM), lambda i: (0, 0, 0)),
            pl.BlockSpec((devices, img_dev, HEAD_DIM), lambda i: (0, 1, 0)),
        ],
        out_specs=(out_spec, out_spec),
        compiler_params=params(),
        cost_estimate=pl.CostEstimate(
            flops=4 * count * keys * HEAD_DIM,
            bytes_accessed=4 * keys * HEAD_DIM + 10 * count * HEAD_DIM,
            transcendentals=count * keys,
        ),
        name="image_attention",
    )(packed, packed, packed)


def finish_kernel(factor, place_ref, queries_ref, sum_ref, norm_ref, mine_ref, got_ref, out_ref):
    core, valid = place_ref[1], place_ref[3]
    devices, part_rows = queries_ref.shape[0], queries_ref.shape[1]
    half = mine_ref.shape[0]
    contract = (((1,), (1,)), ((), ()))
    mine, got = mine_ref[...], got_ref[...]
    keys = jnp.concatenate([mine[:, :HEAD_DIM], got[:, :HEAD_DIM]], 0)
    values = jnp.concatenate([mine[:, HEAD_DIM:], got[:, HEAD_DIM:]], 0)
    lane = lax.broadcasted_iota(jnp.int32, (1, 2 * half), 1)
    position = jnp.where((lane >= half) == (core == 0), half, 0) + lane % half
    group = max(1, 512 // part_rows)
    rows = group * part_rows
    for step in range(devices // group):
        span = slice(step * rows, (step + 1) * rows)
        queries = queries_ref[step * group : (step + 1) * group].reshape(rows, HEAD_DIM)
        scores = lax.dot_general(queries, keys, contract, preferred_element_type=jnp.float32) * factor
        scores = jnp.where(position < valid, scores, -jnp.inf)
        before = norm_ref[span, 0:1]
        top = jnp.maximum(before, jnp.max(scores, 1, keepdims=True))
        rescale = jnp.exp2(before - top)
        weights = jnp.exp2(scores - top)
        total = norm_ref[span, 64:65] * rescale + jnp.sum(weights, 1, keepdims=True)
        mixed = sum_ref[span, :] * rescale + jnp.dot(
            weights.astype(jnp.bfloat16), values, preferred_element_type=jnp.float32
        )
        mixed = (mixed / total).astype(out_ref.dtype)
        out_ref[step * group : (step + 1) * group, :part_rows, :] = mixed.reshape(group, part_rows, HEAD_DIM)
    low = jnp.where(core == 0, mine.astype(jnp.float32), got.astype(jnp.float32))
    high = jnp.where(core == 0, got.astype(jnp.float32), mine.astype(jnp.float32))
    share = 2 * half // devices
    for device in range(devices):
        source = low if device < devices // 2 else high
        start = device * share % half
        block = source[start : start + share]
        block = jnp.concatenate([block[:, :HEAD_DIM], block[:, HEAD_DIM:]], 0)
        out_ref[device, part_rows:, :] = block.astype(out_ref.dtype)


def finish(place, packed, summed, norms, mine, got, img_dev, part_rows, factor):
    devices = packed.shape[0]
    share = 2 * mine.shape[0] // devices
    count = devices * part_rows
    at = 2 * img_dev // part_rows
    return pl.pallas_call(
        functools.partial(finish_kernel, factor),
        grid=(1,),
        out_shape=jax.ShapeDtypeStruct((devices, part_rows + 2 * share, HEAD_DIM), jnp.bfloat16),
        in_specs=[
            SMEM_SPEC,
            pl.BlockSpec((devices, part_rows, HEAD_DIM), lambda i: (0, at, 0)),
            pl.BlockSpec((count, HEAD_DIM), lambda i: (0, 0)),
            pl.BlockSpec((count, HEAD_DIM), lambda i: (0, 0)),
            VMEM_SPEC,
            VMEM_SPEC,
        ],
        out_specs=pl.BlockSpec((devices, part_rows + 2 * share, HEAD_DIM), lambda i: (0, 0, 0)),
        compiler_params=params(),
        cost_estimate=pl.CostEstimate(
            flops=4 * count * 2 * mine.shape[0] * HEAD_DIM,
            bytes_accessed=12 * count * HEAD_DIM,
            transcendentals=count * 2 * mine.shape[0],
        ),
        name="finish",
    )(place, packed, summed, norms, mine, got)


def scatter_chips(blocks, chips):
    step = 2
    while blocks.shape[0] > 1:
        half = blocks.shape[0] // 2
        got = swap(blocks[half:].astype(jnp.bfloat16), step)
        blocks = blocks[:half] + got.astype(jnp.float32)
        step *= 2
    return blocks[0]


def gather_chips(piece, chips):
    pieces = piece
    step = chips
    while step > 1:
        pieces = jnp.concatenate([pieces, swap(pieces, step)], 0)
        step //= 2
    return pieces


def local(
    enc_act,
    down_weight,
    norm_gain,
    text_in_weight,
    modulation_weight,
    key_value_weight,
    timesteps,
    lengths,
    image_queries,
    image_key_values,
):
    devices = lax.axis_size("seq")
    chips = devices // 2
    copies = devices // HEADS
    text_len = enc_act.shape[1]
    share = text_len // devices
    img_dev = image_queries.shape[1]
    part_rows = img_dev // copies
    factor = math.log2(math.e) / math.sqrt(HEAD_DIM)
    index = lax.axis_index("seq")
    chip, core = index // 2, index % 2
    place = jnp.stack([reverse_bits(chip, chips), core, chip, lengths[0]]).astype(jnp.int32)

    pairs = image_key_values.reshape(img_dev, 2, HEADS, HEAD_DIM).transpose(2, 1, 0, 3)
    pairs = pairs.reshape(HEADS, 1, 2 * img_dev, HEAD_DIM)
    pairs = jnp.broadcast_to(pairs, (HEADS, copies, 2 * img_dev, HEAD_DIM))
    queries = image_queries.reshape(copies, part_rows, HEADS, HEAD_DIM).transpose(2, 0, 1, 3)
    packed = jnp.concatenate([pairs, queries], 2).reshape(devices, 2 * img_dev + part_rows, HEAD_DIM)
    packed = lax.all_to_all(packed, "seq", split_axis=0, concat_axis=0, tiled=True)

    win0, kv0 = text_in_weight.T, key_value_weight
    win1, kv1 = swap(win0, 1), swap(kv0, 1)
    mod0 = time_embedding(timesteps, modulation_weight)[0]
    mod1 = swap(mod0, 1)
    lines = jnp.stack([1.0 + mod0[1], mod0[0]])
    lines_high = lines.astype(jnp.bfloat16)
    lines_low = (lines - lines_high.astype(jnp.float32)).astype(jnp.bfloat16)
    lines = jnp.dot(
        jnp.concatenate([lines_high, lines_low]), kv0, preferred_element_type=jnp.float32
    )
    lines = lines[:2] + lines[2:]
    step = 1
    while step < devices:
        lines = lines + swap(lines, step)
        step *= 2
    width = HEADS * HEAD_DIM // chips
    lines = lax.dynamic_index_in_dim(lines.reshape(2, 2, chips, width), chip, 2, keepdims=False)
    lines = lines.reshape(2, 2 * width)

    own, other = encoder(place, enc_act[0].T, down_weight, chips)
    got = swap(other, 1)
    summed = scatter_chips(own.astype(jnp.float32) + got.astype(jnp.float32), chips)
    states = gather_chips(normalize(summed, norm_gain), chips)

    partial, sums = project(place, [states], win0, win1, kv0, kv1, mod0, mod1, chips)
    step = 2
    while step < devices:
        sums = sums + swap(sums, step)
        step *= 2
    total = scatter_chips(partial.astype(jnp.float32), chips)
    model_width = text_in_weight.shape[1] * devices
    mean_val = sums[0] / model_width
    variance = sums[1] / model_width - mean_val * mean_val
    text = (total - mean_val[:, None] * lines[0]) * lax.rsqrt(variance + epsilon)[:, None] + lines[1]
    text = text.astype(jnp.bfloat16).reshape(text_len // 2, 2, 2 // copies, HEAD_DIM)
    if copies == 1:
        mine = lax.dynamic_index_in_dim(text, core, 2, keepdims=False)
        sent = lax.dynamic_index_in_dim(text, 1 - core, 2, keepdims=False)
    else:
        mine = sent = text
    mine = mine.reshape(text_len // 2, 2 * HEAD_DIM)
    got = swap(sent.reshape(text_len // 2, 2 * HEAD_DIM), 1)

    image_sum, norms = image_attention(packed, img_dev, part_rows, factor)
    back = finish(place, packed, image_sum, norms, mine, got, img_dev, part_rows, factor)
    back = lax.all_to_all(back, "seq", split_axis=0, concat_axis=0, tiled=True)
    back = back.reshape(HEADS, copies, part_rows + 2 * share, HEAD_DIM)
    attended = back[:, :, :part_rows].transpose(1, 2, 0, 3).reshape(1, img_dev, HEADS * HEAD_DIM)
    text_kv = back[:, 0, part_rows:].reshape(HEADS, 2, share, HEAD_DIM).transpose(2, 1, 0, 3)
    return (attended, text_kv.reshape(share, 2 * HEADS * HEAD_DIM))


def solution(mesh):
    in_specs = (
        P("dp", None, "seq"),
        P("seq", None),
        P(),
        P(None, "seq"),
        P(None, None, "seq"),
        P("seq", None),
        P("dp"),
        P("dp"),
        P("dp", "seq", None),
        P("dp", "seq", None, None),
    )
    out_specs = (P("dp", "seq", None), P(("dp", "seq"), None))
    return jax.shard_map(local, mesh=mesh, in_specs=in_specs, out_specs=out_specs, check_vma=False)
```

```python
import functools
import math

import jax
import jax.numpy as jnp
from jax import lax
from jax.experimental import pallas as pl
from jax.experimental.pallas import tpu as pltpu
from jax.sharding import PartitionSpec as P

HEAD_DIM = 128
HEADS = 16
TEMB = 256
MIB = 1024 * 1024

epsilon = 1e-06

SMEM_SPEC = pl.BlockSpec(memory_space=pltpu.SMEM)
VMEM_SPEC = pl.BlockSpec(memory_space=pltpu.VMEM)


def params(mib):
    return pltpu.CompilerParams(vmem_limit_bytes=mib * MIB)


def swap(value, mask):
    devices = lax.axis_size("seq")
    return lax.ppermute(value, "seq", [(i, i ^ mask) for i in range(devices)])


def orders(chips):
    bits = [1 << i for i in range(chips.bit_length() - 1)]
    turn = len(bits) // 2
    return (bits, bits[turn:] + bits[:turn])


def position(chip, order):
    last = len(order) - 1
    return sum(((chip >> (bit.bit_length() - 1)) & 1) << (last - i) for i, bit in enumerate(order))


def member(at, order):
    last = len(order) - 1
    return sum(bit for i, bit in enumerate(order) if (at >> (last - i)) & 1)


def normalize(summed, norm_gain):
    scale_rows = lax.rsqrt(jnp.mean(summed * summed, 1, keepdims=True) + epsilon)
    return (summed * scale_rows * norm_gain.astype(jnp.float32)).astype(jnp.bfloat16)


def time_embedding(timesteps, modulation_weight):
    half_width = TEMB // 2
    freqs = jnp.exp(-math.log(10000.0) * jnp.arange(half_width, dtype=jnp.float32) / half_width)
    angles = timesteps.astype(jnp.float32)[:, None] * freqs[None, :]
    embedding = jnp.concatenate([jnp.cos(angles), jnp.sin(angles)], 1)
    embedding = jax.nn.silu(embedding).astype(jnp.bfloat16)
    flat = modulation_weight.reshape(modulation_weight.shape[0], -1)
    product = jnp.dot(embedding, flat, preferred_element_type=jnp.float32)
    return product.reshape(timesteps.shape[0], 2, -1)


def encoder_kernel(lane, order, place_ref, act_ref, weight_ref, own_ref, other_ref, lhs_ref):
    chips = own_ref.shape[0]
    at, core = place_ref[lane], place_ref[2]

    @pl.when(pl.program_id(0) == 0)
    def _():
        lhs_ref[...] = act_ref[...].T

    result = jnp.dot(lhs_ref[...], weight_ref[...], preferred_element_type=jnp.float32)
    half = result.shape[0] // 2
    share = half // chips
    first = core == 0
    own = jnp.where(first, result[:half], result[half:]).astype(own_ref.dtype)
    other = jnp.where(first, result[half:], result[:half]).astype(own_ref.dtype)
    own = own.reshape(chips, share, -1)
    other = other.reshape(chips, share, -1)
    for block in range(chips):
        own_ref[at ^ position(block, order)] = own[block]
        other_ref[at ^ position(block, order)] = other[block]


def encoder(lane, order, place, act, weight):
    chips = 1 << len(order)
    depth, rows = act.shape
    width = weight.shape[1] // 2
    steps = 2
    tile = width // steps
    share = rows // 2 // chips
    out = jax.ShapeDtypeStruct((chips, share, width), jnp.bfloat16)
    out_spec = pl.BlockSpec((chips, share, tile), lambda i: (0, 0, i))
    return pl.pallas_call(
        functools.partial(encoder_kernel, lane, order),
        grid=(steps,),
        out_shape=(out, out),
        in_specs=[
            SMEM_SPEC,
            pl.BlockSpec((depth, rows), lambda i: (0, 0)),
            pl.BlockSpec((depth, tile), lambda i: (0, lane * steps + i)),
        ],
        out_specs=(out_spec, out_spec),
        scratch_shapes=[pltpu.VMEM((rows, depth), jnp.bfloat16)],
        compiler_params=params(24),
        cost_estimate=pl.CostEstimate(
            flops=2 * rows * depth * width,
            bytes_accessed=2 * (depth * rows + depth * width + rows * width),
            transcendentals=0,
        ),
        name="encoder",
    )(place, act, weight)


def slot_rows(chips, width):
    per_slot = 2 * 128 // width
    return chips * per_slot, -(-(chips * per_slot + 2) // 16) * 16


def project_kernel(lanes, place_ref, *refs):
    pieces, refs = (refs[:2], refs[2:4]), refs[4:]
    win0, win1, kv0, kv1, mod0, mod1, keys_ref, values_ref, states, proj0, proj1, sums = refs
    chip = place_ref[3]
    chips = keys_ref.shape[0]
    rows = proj0.shape[0]
    share = rows // chips
    depth = states.shape[1]
    contract = (((1,), (1,)), ((), ()))
    for lane, order in enumerate(lanes):
        top, low = pieces[lane]
        states[: rows // 2, :] = top[...]
        states[rows // 2 :, :] = low[...]
        span = slice(lane * depth, (lane + 1) * depth)
        for win, proj in ((win0, proj0), (win1, proj1)):
            part = lax.dot_general(
                states[...], win[:, span], contract, preferred_element_type=jnp.float32
            )
            for at in range(chips):
                start = pl.multiple_of((chip ^ member(at, order)) * share, share)
                block = part[at * share : (at + 1) * share]
                if lane == 0:
                    proj[pl.ds(start, share), :] = block
                else:
                    proj[pl.ds(start, share), :] += block
    value0, value1 = proj0[...], proj1[...]
    first = jnp.sum(value0, 1, keepdims=True) + jnp.sum(value1, 1, keepdims=True)
    second = jnp.sum(value0 * value0, 1, keepdims=True) + jnp.sum(value1 * value1, 1, keepdims=True)
    lane = lax.broadcasted_iota(jnp.int32, sums.shape, 1)
    sums[...] = jnp.where(lane == 0, first, second).T
    left = []
    for value, mod in ((value0, mod0), (value1, mod1)):
        scale, shift = 1.0 + mod[1:2, :], mod[0:1, :]
        row = lax.broadcasted_iota(jnp.int32, (16, value.shape[1]), 0)
        lines = jnp.where(row < 2, scale, shift)
        high = lines.astype(jnp.bfloat16).astype(jnp.float32)
        lines = jnp.where(row % 2 == 0, high, lines - high)
        lines = jnp.where(row < 4, lines, 0.0)
        left.append(jnp.concatenate([value * scale, lines], 0).astype(jnp.bfloat16))
    width = keys_ref.shape[2]
    slots, extra = slot_rows(chips, width)
    per_slot = slots // chips
    row = lax.broadcasted_iota(jnp.int32, (extra, width), 0)
    column = lax.broadcasted_iota(jnp.int32, (extra, width), 1)
    half = kv0.shape[1] // 2
    for lane, (out_ref, order) in enumerate(zip((keys_ref, values_ref), lanes)):
        line = sums[lane : lane + 1, :]
        high = line.astype(jnp.bfloat16).astype(jnp.float32)
        low = line - high
        if per_slot == 1:
            line = jnp.concatenate([high, low], 1)
        else:
            line = jnp.where(row % 2 == 0, high, low)
        line = jnp.where(row // per_slot == chip, line, 0.0)
        for at in range(chips):
            start = lane * half + (chip ^ member(at, order)) * width
            columns = pl.ds(pl.multiple_of(start, width), width)
            value = jnp.dot(left[0], kv0[:, columns], preferred_element_type=jnp.float32)
            value += jnp.dot(left[1], kv1[:, columns], preferred_element_type=jnp.float32)
            out_ref[at, :rows, :] = value[:rows].astype(out_ref.dtype)
            below = jnp.where(row == slots, value[rows : rows + 1] + value[rows + 1 : rows + 2], line)
            below = jnp.where(
                row == slots + 1, value[rows + 2 : rows + 3] + value[rows + 3 : rows + 4], below
            )
            out_ref[at, rows:, :] = below.astype(out_ref.dtype)


def project(lanes, place, pieces, win0, win1, kv0, kv1, mod0, mod1):
    chips = 1 << len(lanes[0])
    rows = 2 * pieces[0].shape[0]
    features, depth = win0.shape
    total = kv0.shape[1]
    width = total // 2 // chips
    extra = slot_rows(chips, width)[1]
    out = jax.ShapeDtypeStruct((chips, rows + extra, width), jnp.bfloat16)
    return pl.pallas_call(
        functools.partial(project_kernel, lanes),
        out_shape=(out, out),
        in_specs=[SMEM_SPEC] + [VMEM_SPEC] * 10,
        out_specs=(VMEM_SPEC, VMEM_SPEC),
        scratch_shapes=[
            pltpu.VMEM((rows, depth // 2), jnp.bfloat16),
            pltpu.VMEM((rows, features), jnp.float32),
            pltpu.VMEM((rows, features), jnp.float32),
            pltpu.VMEM((rows, 128), jnp.float32),
        ],
        compiler_params=params(20),
        cost_estimate=pl.CostEstimate(
            flops=4 * rows * features * (depth + total),
            bytes_accessed=2 * (rows * depth + 2 * features * (depth + total) + rows * total),
            transcendentals=0,
        ),
        name="project",
    )(place, *pieces, win0, win1, kv0, kv1, mod0, mod1)


def combine_kernel(chips, model_width, place_ref, *refs):
    refs, mine_ref, sent_ref = refs[:4], refs[4], refs[5]
    core = place_ref[2]
    rows = mine_ref.shape[0]
    width = refs[0].shape[1]
    slots = slot_rows(chips, width)[0]
    totals = [
        refs[2 * lane][...].astype(jnp.float32) + refs[2 * lane + 1][...].astype(jnp.float32)
        for lane in range(2)
    ]
    sums = []
    for total in totals:
        line = jnp.sum(total[rows : rows + slots], 0, keepdims=True)
        if width > 128:
            line = line[:, :128] + line[:, 128:]
        sums.append(line)
    mean_val = sums[0] / model_width
    scale = lax.rsqrt(sums[1] / model_width - mean_val * mean_val + epsilon)
    mean_val = jnp.broadcast_to(mean_val, (rows, rows)).T[:, 0:1]
    scale = jnp.broadcast_to(scale, (rows, rows)).T[:, 0:1]
    texts = []
    for total in totals:
        text = (total[:rows] - mean_val * total[rows + slots : rows + slots + 1]) * scale
        texts.append(text + total[rows + slots + 1 : rows + slots + 2])
    for part, text in enumerate(texts):
        span = slice(part * HEAD_DIM, (part + 1) * HEAD_DIM)
        if width > HEAD_DIM:
            low, high = text[:, :HEAD_DIM], text[:, HEAD_DIM:]
            mine_ref[:, span] = jnp.where(core == 0, low, high).astype(mine_ref.dtype)
            sent_ref[:, span] = jnp.where(core == 0, high, low).astype(mine_ref.dtype)
        else:
            mine_ref[:, span] = text.astype(mine_ref.dtype)
            sent_ref[:, span] = text.astype(mine_ref.dtype)


def combine(place, parts, chips, rows, model_width):
    out = jax.ShapeDtypeStruct((rows, 2 * HEAD_DIM), jnp.bfloat16)
    return pl.pallas_call(
        functools.partial(combine_kernel, chips, model_width),
        out_shape=(out, out),
        in_specs=[SMEM_SPEC] + [VMEM_SPEC] * 4,
        out_specs=(VMEM_SPEC, VMEM_SPEC),
        compiler_params=params(8),
        cost_estimate=pl.CostEstimate(
            flops=8 * rows * 512, bytes_accessed=12 * rows * 512, transcendentals=0
        ),
        name="combine",
    )(place, *parts)


def pack_kernel(copies, queries_ref, keys_ref, values_ref, out_ref):
    img_dev = keys_ref.shape[0]
    part_rows = img_dev // copies
    for device in range(out_ref.shape[0]):
        head, copy = device // copies, device % copies
        span = slice(head * HEAD_DIM, (head + 1) * HEAD_DIM)
        out_ref[device, :img_dev, :] = keys_ref[:, span]
        out_ref[device, img_dev : 2 * img_dev, :] = values_ref[:, span]
        out_ref[device, 2 * img_dev :, :] = queries_ref[copy * part_rows : (copy + 1) * part_rows, span]


def pack(copies, queries, keys, values):
    img_dev = keys.shape[0]
    rows = 2 * img_dev + img_dev // copies
    return pl.pallas_call(
        functools.partial(pack_kernel, copies),
        out_shape=jax.ShapeDtypeStruct((HEADS * copies, rows, HEAD_DIM), jnp.bfloat16),
        in_specs=[VMEM_SPEC] * 3,
        out_specs=VMEM_SPEC,
        compiler_params=params(8),
        cost_estimate=pl.CostEstimate(
            flops=0, bytes_accessed=4 * HEADS * copies * rows * HEAD_DIM, transcendentals=0
        ),
        name="pack",
    )(queries, keys, values)


def unpack_kernel(copies, part_rows, blocks_ref, attended_ref, text_ref):
    share = text_ref.shape[0]
    half = text_ref.shape[1] // 2
    for device in range(blocks_ref.shape[0]):
        head, copy = device // copies, device % copies
        start = head * HEAD_DIM
        rows = slice(copy * part_rows, (copy + 1) * part_rows)
        attended_ref[rows, start : start + HEAD_DIM] = blocks_ref[device, :part_rows, :]
        if copy == 0:
            block = blocks_ref[device, part_rows:, :].astype(jnp.float32)
            text_ref[:, start : start + HEAD_DIM] = block[:share].astype(text_ref.dtype)
            start += half
            text_ref[:, start : start + HEAD_DIM] = block[share:].astype(text_ref.dtype)


def unpack(copies, part_rows, blocks):
    share = (blocks.shape[1] - part_rows) // 2
    return pl.pallas_call(
        functools.partial(unpack_kernel, copies, part_rows),
        out_shape=(
            jax.ShapeDtypeStruct((part_rows * copies, HEADS * HEAD_DIM), jnp.bfloat16),
            jax.ShapeDtypeStruct((share, 2 * HEADS * HEAD_DIM), jnp.bfloat16),
        ),
        in_specs=[VMEM_SPEC],
        out_specs=(VMEM_SPEC, VMEM_SPEC),
        compiler_params=params(8),
        name="unpack",
    )(blocks)


def image_kernel(factor, queries_ref, keys_ref, values_ref, sum_ref, norm_ref):
    contract = (((1,), (1,)), ((), ()))
    queries = queries_ref[...].reshape(-1, HEAD_DIM)
    keys = keys_ref[...].reshape(-1, HEAD_DIM)
    values = values_ref[...].reshape(-1, HEAD_DIM)
    scores = lax.dot_general(queries, keys, contract, preferred_element_type=jnp.float32) * factor
    top = jnp.max(scores, 1, keepdims=True)
    weights = jnp.exp2(scores - top)
    total = jnp.sum(weights, 1, keepdims=True)
    sum_ref[...] = jnp.dot(weights.astype(jnp.bfloat16), values, preferred_element_type=jnp.float32)
    lane = lax.broadcasted_iota(jnp.int32, norm_ref.shape, 1)
    norm_ref[...] = jnp.where(lane < 64, top, total)


def image_attention(packed, img_dev, part_rows, factor, call, calls):
    devices = packed.shape[0]
    count = devices * part_rows // calls
    group = max(1, 256 // part_rows)
    block = group * part_rows
    at = 2 * img_dev // part_rows
    steps = devices // group // calls
    out = jax.ShapeDtypeStruct((count, HEAD_DIM), jnp.float32)
    out_spec = pl.BlockSpec((block, HEAD_DIM), lambda i: (i, 0))
    keys = devices * img_dev
    return pl.pallas_call(
        functools.partial(image_kernel, factor),
        grid=(steps,),
        out_shape=(out, out),
        in_specs=[
            pl.BlockSpec((group, part_rows, HEAD_DIM), lambda i: (call * steps + i, at, 0)),
            pl.BlockSpec((devices, img_dev, HEAD_DIM), lambda i: (0, 0, 0)),
            pl.BlockSpec((devices, img_dev, HEAD_DIM), lambda i: (0, 1, 0)),
        ],
        out_specs=(out_spec, out_spec),
        compiler_params=params(20),
        cost_estimate=pl.CostEstimate(
            flops=4 * count * keys * HEAD_DIM,
            bytes_accessed=4 * keys * HEAD_DIM + 10 * count * HEAD_DIM,
            transcendentals=count * keys,
        ),
        name="image_attention",
    )(packed, packed, packed)


def finish_kernel(factor, calls, place_ref, queries_ref, *refs):
    images, (mine_ref, got_ref, out_ref) = refs[: 2 * calls], refs[2 * calls :]
    core, valid = place_ref[2], place_ref[4]
    devices, part_rows = queries_ref.shape[0], queries_ref.shape[1]
    half = mine_ref.shape[0]
    contract = (((1,), (1,)), ((), ()))
    mine, got = mine_ref[...], got_ref[...]
    keys = jnp.concatenate([mine[:, :HEAD_DIM], got[:, :HEAD_DIM]], 0)
    values = jnp.concatenate([mine[:, HEAD_DIM:], got[:, HEAD_DIM:]], 0)
    lane = lax.broadcasted_iota(jnp.int32, (1, 2 * half), 1)
    text_position = jnp.where((lane >= half) == (core == 0), half, 0) + lane % half
    group = max(1, 512 // part_rows)
    rows = group * part_rows
    each = devices // group // calls
    for step in range(devices // group):
        sum_ref, norm_ref = images[2 * (step // each)], images[2 * (step // each) + 1]
        span = slice(step % each * rows, (step % each + 1) * rows)
        queries = queries_ref[step * group : (step + 1) * group].reshape(rows, HEAD_DIM)
        scores = lax.dot_general(queries, keys, contract, preferred_element_type=jnp.float32) * factor
        scores = jnp.where(text_position < valid, scores, -jnp.inf)
        before = norm_ref[span, 0:1]
        top = jnp.maximum(before, jnp.max(scores, 1, keepdims=True))
        rescale = jnp.exp2(before - top)
        weights = jnp.exp2(scores - top)
        total = norm_ref[span, 64:65] * rescale + jnp.sum(weights, 1, keepdims=True)
        mixed = sum_ref[span, :] * rescale + jnp.dot(
            weights.astype(jnp.bfloat16), values, preferred_element_type=jnp.float32
        )
        mixed = (mixed / total).astype(out_ref.dtype)
        out_ref[step * group : (step + 1) * group, :part_rows, :] = mixed.reshape(group, part_rows, HEAD_DIM)
    low = jnp.where(core == 0, mine.astype(jnp.float32), got.astype(jnp.float32))
    high = jnp.where(core == 0, got.astype(jnp.float32), mine.astype(jnp.float32))
    share = 2 * half // devices
    for device in range(devices):
        source = low if device < devices // 2 else high
        start = device * share % half
        block = source[start : start + share]
        block = jnp.concatenate([block[:, :HEAD_DIM], block[:, HEAD_DIM:]], 0)
        out_ref[device, part_rows:, :] = block.astype(out_ref.dtype)


def finish(place, packed, images, mine, got, img_dev, part_rows, factor):
    devices = packed.shape[0]
    share = 2 * mine.shape[0] // devices
    count = devices * part_rows
    at = 2 * img_dev // part_rows
    return pl.pallas_call(
        functools.partial(finish_kernel, factor, len(images) // 2),
        grid=(1,),
        out_shape=jax.ShapeDtypeStruct((devices, part_rows + 2 * share, HEAD_DIM), jnp.bfloat16),
        in_specs=[SMEM_SPEC, pl.BlockSpec((devices, part_rows, HEAD_DIM), lambda i: (0, at, 0))]
        + [VMEM_SPEC] * (len(images) + 2),
        out_specs=pl.BlockSpec((devices, part_rows + 2 * share, HEAD_DIM), lambda i: (0, 0, 0)),
        compiler_params=params(20),
        cost_estimate=pl.CostEstimate(
            flops=4 * count * 2 * mine.shape[0] * HEAD_DIM,
            bytes_accessed=12 * count * HEAD_DIM,
            transcendentals=count * 2 * mine.shape[0],
        ),
        name="finish",
    )(place, packed, *images, mine, got)


def halves(blocks):
    half = blocks.shape[0] // 2
    return blocks[:half], blocks[half:].astype(jnp.bfloat16)


def local(
    enc_act,
    down_weight,
    norm_gain,
    text_in_weight,
    modulation_weight,
    key_value_weight,
    timesteps,
    lengths,
    image_queries,
    image_key_values,
):
    devices = lax.axis_size("seq")
    chips = devices // 2
    copies = devices // HEADS
    text_len = enc_act.shape[1]
    img_dev = image_queries.shape[1]
    part_rows = img_dev // copies
    factor = math.log2(math.e) / math.sqrt(HEAD_DIM)
    lanes = orders(chips)
    index = lax.axis_index("seq")
    chip, core = index // 2, index % 2
    place = jnp.stack([position(chip, lanes[0]), position(chip, lanes[1]), core, chip, lengths[0]])
    place = place.astype(jnp.int32)

    win0, kv0 = text_in_weight.T, key_value_weight
    win1, kv1 = swap(win0, 1), swap(kv0, 1)
    mod0 = time_embedding(timesteps, modulation_weight)[0]
    mod1 = swap(mod0, 1)

    act = enc_act[0].T
    blocks = []
    for lane, order in enumerate(lanes):
        own, other = encoder(lane, order, place, act, down_weight)
        blocks.append(own.astype(jnp.float32) + swap(other, 1).astype(jnp.float32))
    for step in range(len(lanes[0])):
        keep, sent = zip(*[halves(block) for block in blocks])
        if step == 0:
            sent, image_queries, image_key_values = lax.optimization_barrier(
                (sent, image_queries, image_key_values)
            )
            packed = pack(
                copies, image_queries[0], image_key_values[0, :, 0], image_key_values[0, :, 1]
            )
        got = [swap(part, 2 * order[step]) for part, order in zip(sent, lanes)]
        if step == 0:
            got, packed = lax.optimization_barrier((got, packed))
            packed = lax.all_to_all(packed, "seq", split_axis=0, concat_axis=0, tiled=True)
        blocks = [mine + part.astype(jnp.float32) for mine, part in zip(keep, got)]

    summed = jnp.concatenate([block[0] for block in blocks], 1)
    states = normalize(summed, norm_gain)
    pieces = jnp.split(states, 2, axis=1)
    for step in reversed(range(len(lanes[0]))):
        got = [swap(piece, 2 * order[step]) for piece, order in zip(pieces, lanes)]
        if step > 0:
            pieces = [jnp.concatenate(pair, 0) for pair in zip(pieces, got)]
    pieces = [piece for pair in zip(pieces, got) for piece in pair]

    blocks = project(lanes, place, pieces, win0, win1, kv0, kv1, mod0, mod1)
    calls = 2
    images = []
    for step in range(len(lanes[0])):
        keep, sent = zip(*[halves(block) for block in blocks])
        if step < calls:
            sent, packed = lax.optimization_barrier((sent, packed))
            image = image_attention(packed, img_dev, part_rows, factor, step, calls)
        got = [swap(part, 2 * order[step]) for part, order in zip(sent, lanes)]
        if step < calls:
            got, image = lax.optimization_barrier((got, image))
            images += image
        if step < len(lanes[0]) - 1:
            blocks = [
                mine.astype(jnp.float32) + part.astype(jnp.float32) for mine, part in zip(keep, got)
            ]
    parts = [part[0] for pair in zip(keep, got) for part in pair]
    model_width = text_in_weight.shape[1] * devices
    mine, sent = combine(place, parts, chips, text_len // 2, model_width)
    got = swap(sent, 1)

    back = finish(place, packed, images, mine, got, img_dev, part_rows, factor)
    back = lax.all_to_all(back, "seq", split_axis=0, concat_axis=0, tiled=True)
    attended, text_kv = unpack(copies, part_rows, back)
    return (attended[None], text_kv)


def solution(mesh):
    in_specs = (
        P("dp", None, "seq"),
        P("seq", None),
        P(),
        P(None, "seq"),
        P(None, None, "seq"),
        P("seq", None),
        P("dp"),
        P("dp"),
        P("dp", "seq", None),
        P("dp", "seq", None, None),
    )
    out_specs = (P("dp", "seq", None), P(("dp", "seq"), None))
    return jax.shard_map(local, mesh=mesh, in_specs=in_specs, out_specs=out_specs, check_vma=False)
```

```python
import functools
import math

import jax
import jax.numpy as jnp
from jax import lax
from jax.experimental import pallas as pl
from jax.experimental.pallas import tpu as pltpu
from jax.sharding import PartitionSpec as P

HEAD_DIM = 128
HEADS = 16
TEMB = 256
MIB = 1024 * 1024

epsilon = 1e-06

SMEM_SPEC = pl.BlockSpec(memory_space=pltpu.SMEM)
VMEM_SPEC = pl.BlockSpec(memory_space=pltpu.VMEM)


def params(mib):
    return pltpu.CompilerParams(vmem_limit_bytes=mib * MIB)


def swap(value, mask):
    devices = lax.axis_size("seq")
    return lax.ppermute(value, "seq", [(i, i ^ mask) for i in range(devices)])


def orders(chips):
    bits = [1 << i for i in range(chips.bit_length() - 1)]
    turn = len(bits) // 2
    return (bits, bits[turn:] + bits[:turn])


def position(chip, order):
    last = len(order) - 1
    return sum(((chip >> (bit.bit_length() - 1)) & 1) << (last - i) for i, bit in enumerate(order))


def member(at, order):
    last = len(order) - 1
    return sum(bit for i, bit in enumerate(order) if (at >> (last - i)) & 1)


def normalize(summed, norm_gain):
    scale_rows = lax.rsqrt(jnp.mean(summed * summed, 1, keepdims=True) + epsilon)
    return (summed * scale_rows * norm_gain.astype(jnp.float32)).astype(jnp.bfloat16)


def time_embedding(timesteps, modulation_weight):
    half_width = TEMB // 2
    freqs = jnp.exp(-math.log(10000.0) * jnp.arange(half_width, dtype=jnp.float32) / half_width)
    angles = timesteps.astype(jnp.float32)[:, None] * freqs[None, :]
    embedding = jnp.concatenate([jnp.cos(angles), jnp.sin(angles)], 1)
    embedding = jax.nn.silu(embedding).astype(jnp.bfloat16)
    flat = modulation_weight.reshape(modulation_weight.shape[0], -1)
    product = jnp.dot(embedding, flat, preferred_element_type=jnp.float32)
    return product.reshape(timesteps.shape[0], 2, -1)


def encoder_kernel(lane, order, place_ref, act_ref, weight_ref, own_ref, other_ref, *refs):
    chips = own_ref.shape[0]
    at, core = place_ref[lane], place_ref[2]
    lhs_ref = refs[0] if refs else act_ref

    if refs:

        @pl.when(pl.program_id(0) == 0)
        def _():
            lhs_ref[...] = act_ref[...].T

    result = jnp.dot(lhs_ref[...], weight_ref[...], preferred_element_type=jnp.float32)
    half = result.shape[0] // 2
    share = half // chips
    first = core == 0
    own = jnp.where(first, result[:half], result[half:]).astype(own_ref.dtype)
    other = jnp.where(first, result[half:], result[:half]).astype(own_ref.dtype)
    own = own.reshape(chips, share, -1)
    other = other.reshape(chips, share, -1)
    for block in range(chips):
        own_ref[at ^ position(block, order)] = own[block]
        other_ref[at ^ position(block, order)] = other[block]


def encoder(lane, order, place, act, weight):
    chips = 1 << len(order)
    depth = weight.shape[0]
    rows = act.size // depth
    width = weight.shape[1] // 2
    steps = 2
    turn = act.shape[0] == depth
    tile = width // steps
    share = rows // 2 // chips
    out = jax.ShapeDtypeStruct((chips, share, width), jnp.bfloat16)
    out_spec = pl.BlockSpec((chips, share, tile), lambda i: (0, 0, i))
    return pl.pallas_call(
        functools.partial(encoder_kernel, lane, order),
        grid=(steps,),
        out_shape=(out, out) + (jax.ShapeDtypeStruct((rows, depth), act.dtype),) * turn,
        in_specs=[
            SMEM_SPEC,
            pl.BlockSpec(act.shape, lambda i: (0, 0)),
            pl.BlockSpec((depth, tile), lambda i: (0, lane * steps + i)),
        ],
        out_specs=(out_spec, out_spec) + (pl.BlockSpec((rows, depth), lambda i: (0, 0)),) * turn,
        compiler_params=params(24),
        cost_estimate=pl.CostEstimate(
            flops=2 * rows * depth * width,
            bytes_accessed=2 * (depth * rows + depth * width + rows * width),
            transcendentals=0,
        ),
        name="encoder",
    )(place, act, weight)


def slot_rows(chips, width):
    per_slot = 2 * 128 // width
    return chips * per_slot, -(-(chips * per_slot + 2) // 16) * 16


def project_kernel(lanes, place_ref, *refs):
    pieces, refs = (refs[:2], refs[2:4]), refs[4:]
    win0, win1, kv0, kv1, mod0, mod1, *outs, states, proj0, proj1, sums = refs
    chip = place_ref[3]
    half_chips = outs[0].shape[0]
    chips = 2 * half_chips
    rows = proj0.shape[0]
    share = rows // chips
    depth = states.shape[1]
    contract = (((1,), (1,)), ((), ()))
    for lane, order in enumerate(lanes):
        top, low = pieces[lane]
        states[: rows // 2, :] = top[...]
        states[rows // 2 :, :] = low[...]
        span = slice(lane * depth, (lane + 1) * depth)
        for win, proj in ((win0, proj0), (win1, proj1)):
            part = lax.dot_general(
                states[...], win[:, span], contract, preferred_element_type=jnp.float32
            )
            for at in range(chips):
                start = pl.multiple_of((chip ^ member(at, order)) * share, share)
                block = part[at * share : (at + 1) * share]
                if lane == 0:
                    proj[pl.ds(start, share), :] = block
                else:
                    proj[pl.ds(start, share), :] += block
    value0, value1 = proj0[...], proj1[...]
    first = jnp.sum(value0, 1, keepdims=True) + jnp.sum(value1, 1, keepdims=True)
    second = jnp.sum(value0 * value0, 1, keepdims=True) + jnp.sum(value1 * value1, 1, keepdims=True)
    lane = lax.broadcasted_iota(jnp.int32, sums.shape, 1)
    sums[...] = jnp.where(lane == 0, first, second).T
    left = []
    for value, mod in ((value0, mod0), (value1, mod1)):
        scale, shift = 1.0 + mod[1:2, :], mod[0:1, :]
        row = lax.broadcasted_iota(jnp.int32, (16, value.shape[1]), 0)
        lines = jnp.where(row < 2, scale, shift)
        high = lines.astype(jnp.bfloat16).astype(jnp.float32)
        lines = jnp.where(row % 2 == 0, high, lines - high)
        lines = jnp.where(row < 4, lines, 0.0)
        left.append(jnp.concatenate([value * scale, lines], 0).astype(jnp.bfloat16))
    width = outs[0].shape[2]
    slots, extra = slot_rows(chips, width)
    per_slot = slots // chips
    row = lax.broadcasted_iota(jnp.int32, (extra, width), 0)
    column = lax.broadcasted_iota(jnp.int32, (extra, width), 1)
    half = kv0.shape[1] // 2
    for lane, order in enumerate(lanes):
        line = sums[lane : lane + 1, :]
        high = line.astype(jnp.bfloat16).astype(jnp.float32)
        low = line - high
        if per_slot == 1:
            line = jnp.concatenate([high, low], 1)
        else:
            line = jnp.where(row % 2 == 0, high, low)
        line = jnp.where(row // per_slot == chip, line, 0.0)
        for at in reversed(range(chips)):
            out_ref, to = outs[2 * lane + at // half_chips], at % half_chips
            start = lane * half + (chip ^ member(at, order)) * width
            columns = pl.ds(pl.multiple_of(start, width), width)
            value = jnp.dot(left[0], kv0[:, columns], preferred_element_type=jnp.float32)
            value += jnp.dot(left[1], kv1[:, columns], preferred_element_type=jnp.float32)
            out_ref[to, :rows, :] = value[:rows].astype(out_ref.dtype)
            below = jnp.where(row == slots, value[rows : rows + 1] + value[rows + 1 : rows + 2], line)
            below = jnp.where(
                row == slots + 1, value[rows + 2 : rows + 3] + value[rows + 3 : rows + 4], below
            )
            out_ref[to, rows:, :] = below.astype(out_ref.dtype)


def project(lanes, place, pieces, win0, win1, kv0, kv1, mod0, mod1):
    chips = 1 << len(lanes[0])
    rows = 2 * pieces[0].shape[0]
    features, depth = win0.shape
    total = kv0.shape[1]
    width = total // 2 // chips
    extra = slot_rows(chips, width)[1]
    out = jax.ShapeDtypeStruct((chips // 2, rows + extra, width), jnp.bfloat16)
    return pl.pallas_call(
        functools.partial(project_kernel, lanes),
        out_shape=(out,) * 4,
        in_specs=[SMEM_SPEC] + [VMEM_SPEC] * 10,
        out_specs=(VMEM_SPEC,) * 4,
        scratch_shapes=[
            pltpu.VMEM((rows, depth // 2), jnp.bfloat16),
            pltpu.VMEM((rows, features), jnp.float32),
            pltpu.VMEM((rows, features), jnp.float32),
            pltpu.VMEM((rows, 128), jnp.float32),
        ],
        compiler_params=params(20),
        cost_estimate=pl.CostEstimate(
            flops=4 * rows * features * (depth + total),
            bytes_accessed=2 * (rows * depth + 2 * features * (depth + total) + rows * total),
            transcendentals=0,
        ),
        name="project",
    )(place, *pieces, win0, win1, kv0, kv1, mod0, mod1)


def combine_kernel(chips, model_width, place_ref, *refs):
    refs, mine_ref, sent_ref = refs[:4], refs[4], refs[5]
    core = place_ref[2]
    rows = mine_ref.shape[0]
    width = refs[0].shape[1]
    slots = slot_rows(chips, width)[0]
    totals = [
        refs[2 * lane][...].astype(jnp.float32) + refs[2 * lane + 1][...].astype(jnp.float32)
        for lane in range(2)
    ]
    sums = []
    for total in totals:
        line = jnp.sum(total[rows : rows + slots], 0, keepdims=True)
        if width > 128:
            line = line[:, :128] + line[:, 128:]
        sums.append(line)
    mean_val = sums[0] / model_width
    scale = lax.rsqrt(sums[1] / model_width - mean_val * mean_val + epsilon)
    mean_val = jnp.broadcast_to(mean_val, (rows, rows)).T[:, 0:1]
    scale = jnp.broadcast_to(scale, (rows, rows)).T[:, 0:1]
    texts = []
    for total in totals:
        text = (total[:rows] - mean_val * total[rows + slots : rows + slots + 1]) * scale
        texts.append(text + total[rows + slots + 1 : rows + slots + 2])
    for part, text in enumerate(texts):
        span = slice(part * HEAD_DIM, (part + 1) * HEAD_DIM)
        if width > HEAD_DIM:
            low, high = text[:, :HEAD_DIM], text[:, HEAD_DIM:]
            mine_ref[:, span] = jnp.where(core == 0, low, high).astype(mine_ref.dtype)
            sent_ref[:, span] = jnp.where(core == 0, high, low).astype(mine_ref.dtype)
        else:
            mine_ref[:, span] = text.astype(mine_ref.dtype)
            sent_ref[:, span] = text.astype(mine_ref.dtype)


def combine(place, parts, chips, rows, model_width):
    out = jax.ShapeDtypeStruct((rows, 2 * HEAD_DIM), jnp.bfloat16)
    return pl.pallas_call(
        functools.partial(combine_kernel, chips, model_width),
        out_shape=(out, out),
        in_specs=[SMEM_SPEC] + [VMEM_SPEC] * 4,
        out_specs=(VMEM_SPEC, VMEM_SPEC),
        compiler_params=params(8),
        cost_estimate=pl.CostEstimate(
            flops=8 * rows * 512, bytes_accessed=12 * rows * 512, transcendentals=0
        ),
        name="combine",
    )(place, *parts)


def pack_kernel(copies, place_ref, queries_ref, keys_ref, values_ref, *outs):
    img_dev = keys_ref.shape[0]
    part_rows = img_dev // copies
    for mask, out_ref in enumerate(outs):
        device = (2 * place_ref[3] + place_ref[2]) ^ mask
        head, copy = device // copies, device % copies
        span = pl.ds(pl.multiple_of(head * HEAD_DIM, HEAD_DIM), HEAD_DIM)
        rows = pl.ds(pl.multiple_of(copy * part_rows, part_rows), part_rows)
        out_ref[:img_dev, :] = keys_ref[:, span]
        out_ref[img_dev : 2 * img_dev, :] = values_ref[:, span]
        out_ref[2 * img_dev :, :] = queries_ref[rows, span]


def pack(devices, copies, place, queries, keys, values):
    img_dev = keys.shape[0]
    rows = 2 * img_dev + img_dev // copies
    out = jax.ShapeDtypeStruct((rows, HEAD_DIM), jnp.bfloat16)
    return pl.pallas_call(
        functools.partial(pack_kernel, copies),
        out_shape=(out,) * devices,
        in_specs=[SMEM_SPEC] + [VMEM_SPEC] * 3,
        out_specs=(VMEM_SPEC,) * devices,
        compiler_params=params(8),
        cost_estimate=pl.CostEstimate(
            flops=0, bytes_accessed=4 * devices * rows * HEAD_DIM, transcendentals=0
        ),
        name="pack",
    )(place, queries, keys, values)


def unpack_kernel(copies, part_rows, place_ref, *refs):
    blocks, (attended_ref, text_ref) = refs[:-2], refs[-2:]
    device = 2 * place_ref[3] + place_ref[2]
    share = text_ref.shape[0]
    half = text_ref.shape[1] // 2
    for mask, block_ref in enumerate(blocks):
        head, copy = (device ^ mask) // copies, (device ^ mask) % copies
        start = pl.multiple_of(head * HEAD_DIM, HEAD_DIM)
        rows = pl.ds(pl.multiple_of(copy * part_rows, part_rows), part_rows)
        attended_ref[rows, pl.ds(start, HEAD_DIM)] = block_ref[:part_rows, :]
        block = block_ref[part_rows:, :].astype(jnp.float32)
        text_ref[:, pl.ds(start, HEAD_DIM)] = block[:share].astype(text_ref.dtype)
        start = pl.multiple_of(half + head * HEAD_DIM, HEAD_DIM)
        text_ref[:, pl.ds(start, HEAD_DIM)] = block[share:].astype(text_ref.dtype)


def unpack(copies, part_rows, place, blocks):
    share = (blocks[0].shape[0] - part_rows) // 2
    return pl.pallas_call(
        functools.partial(unpack_kernel, copies, part_rows),
        out_shape=(
            jax.ShapeDtypeStruct((part_rows * copies, HEADS * HEAD_DIM), jnp.bfloat16),
            jax.ShapeDtypeStruct((share, 2 * HEADS * HEAD_DIM), jnp.bfloat16),
        ),
        in_specs=[SMEM_SPEC] + [VMEM_SPEC] * len(blocks),
        out_specs=(VMEM_SPEC, VMEM_SPEC),
        compiler_params=params(8),
        name="unpack",
    )(place, *blocks)


def image_kernel(factor, call, calls, img_dev, *refs):
    pieces, (sum_ref, norm_ref, keys_ref, values_ref) = refs[:-4], refs[-4:]
    contract = (((1,), (1,)), ((), ()))
    for at, piece in enumerate(pieces):
        rows = slice(at * img_dev, (at + 1) * img_dev)
        keys_ref[rows, :] = piece[:img_dev, :]
        values_ref[rows, :] = piece[img_dev : 2 * img_dev, :]
    blocks = pieces[call * len(pieces) // calls : (call + 1) * len(pieces) // calls]
    part_rows = sum_ref.shape[0] // len(blocks)
    group = max(1, 256 // part_rows)
    for step in range(len(blocks) // group):
        span = slice(step * group * part_rows, (step + 1) * group * part_rows)
        queries = [piece[2 * img_dev :, :] for piece in blocks[step * group : (step + 1) * group]]
        queries = jnp.concatenate(queries, 0)
        scores = lax.dot_general(queries, keys_ref[...], contract, preferred_element_type=jnp.float32)
        scores = scores * factor
        top = jnp.max(scores, 1, keepdims=True)
        weights = jnp.exp2(scores - top)
        total = jnp.sum(weights, 1, keepdims=True)
        sum_ref[span, :] = jnp.dot(
            weights.astype(jnp.bfloat16), values_ref[...], preferred_element_type=jnp.float32
        )
        lane = lax.broadcasted_iota(jnp.int32, (queries.shape[0], 128), 1)
        norm_ref[span, :] = jnp.where(lane < 64, top, total)


def image_attention(pieces, img_dev, factor, call, calls):
    part_rows = pieces[0].shape[0] - 2 * img_dev
    keys = len(pieces) * img_dev
    count = len(pieces) * part_rows // calls
    out = jax.ShapeDtypeStruct((count, HEAD_DIM), jnp.float32)
    return pl.pallas_call(
        functools.partial(image_kernel, factor, call, calls, img_dev),
        out_shape=(out, out),
        in_specs=[VMEM_SPEC] * len(pieces),
        out_specs=(VMEM_SPEC, VMEM_SPEC),
        scratch_shapes=[pltpu.VMEM((keys, HEAD_DIM), jnp.bfloat16)] * 2,
        compiler_params=params(24),
        cost_estimate=pl.CostEstimate(
            flops=4 * count * keys * HEAD_DIM,
            bytes_accessed=4 * keys * HEAD_DIM + 10 * count * HEAD_DIM,
            transcendentals=count * keys,
        ),
        name="image_attention",
    )(*pieces)


def finish_kernel(factor, masks, img_dev, place_ref, *refs):
    pieces, refs = refs[: len(masks)], refs[len(masks) :]
    sum_ref, norm_ref, mine_ref, got_ref, *outs, text_ref = refs
    chip, core, valid = place_ref[3], place_ref[2], place_ref[4]
    half = mine_ref.shape[0]
    contract = (((1,), (1,)), ((), ()))
    mine, got = mine_ref[...], got_ref[...]
    keys = jnp.concatenate([mine[:, :HEAD_DIM], got[:, :HEAD_DIM]], 0)
    values = jnp.concatenate([mine[:, HEAD_DIM:], got[:, HEAD_DIM:]], 0)
    lane = lax.broadcasted_iota(jnp.int32, (1, 2 * half), 1)
    text_position = jnp.where((lane >= half) == (core == 0), half, 0) + lane % half
    part_rows = sum_ref.shape[0] // len(pieces)
    group = max(1, 512 // part_rows)
    for step in range(len(pieces) // group):
        span = slice(step * group * part_rows, (step + 1) * group * part_rows)
        queries = [piece[2 * img_dev :, :] for piece in pieces[step * group : (step + 1) * group]]
        queries = jnp.concatenate(queries, 0)
        scores = lax.dot_general(queries, keys, contract, preferred_element_type=jnp.float32) * factor
        scores = jnp.where(text_position < valid, scores, -jnp.inf)
        before = norm_ref[span, 0:1]
        top = jnp.maximum(before, jnp.max(scores, 1, keepdims=True))
        rescale = jnp.exp2(before - top)
        weights = jnp.exp2(scores - top)
        total = norm_ref[span, 64:65] * rescale + jnp.sum(weights, 1, keepdims=True)
        mixed = sum_ref[span, :] * rescale + jnp.dot(
            weights.astype(jnp.bfloat16), values, preferred_element_type=jnp.float32
        )
        mixed = (mixed / total).astype(jnp.bfloat16)
        for at in range(group):
            outs[step * group + at][:part_rows, :] = mixed[at * part_rows : (at + 1) * part_rows]
    low, high = mine.astype(jnp.float32), got.astype(jnp.float32)
    text_ref[:half, :] = jnp.where(core == 0, low, high)
    text_ref[half:, :] = jnp.where(core == 0, high, low)
    share = (outs[0].shape[0] - part_rows) // 2
    for at, out_ref in enumerate(outs):
        device = (2 * chip + core) ^ masks[at]
        block = text_ref[pl.ds(pl.multiple_of(device * share, share), share), :]
        block = jnp.concatenate([block[:, :HEAD_DIM], block[:, HEAD_DIM:]], 0)
        out_ref[part_rows:, :] = block.astype(out_ref.dtype)


def finish(place, masks, pieces, image, mine, got, img_dev, factor):
    devices = len(pieces)
    part_rows = pieces[0].shape[0] - 2 * img_dev
    half = mine.shape[0]
    share = 2 * half // devices
    count = len(masks) * part_rows
    out = jax.ShapeDtypeStruct((part_rows + 2 * share, HEAD_DIM), jnp.bfloat16)
    return pl.pallas_call(
        functools.partial(finish_kernel, factor, masks, img_dev),
        out_shape=(out,) * len(masks),
        in_specs=[SMEM_SPEC] + [VMEM_SPEC] * (len(masks) + 4),
        out_specs=(VMEM_SPEC,) * len(masks),
        scratch_shapes=[pltpu.VMEM((2 * half, 2 * HEAD_DIM), jnp.float32)],
        compiler_params=params(16),
        cost_estimate=pl.CostEstimate(
            flops=8 * count * half * HEAD_DIM,
            bytes_accessed=12 * count * HEAD_DIM,
            transcendentals=2 * count * half,
        ),
        name="finish",
    )(place, *[pieces[mask] for mask in masks], *image, mine, got)


def add(one, other, dtype):
    return (one.astype(jnp.float32) + other.astype(jnp.float32)).astype(dtype)


ROUND = {12: 1, 3: 2, 4: 2, 13: 3, 1: 3, 10: 4, 5: 4, 6: 5, 7: 5, 14: 6, 11: 7, 15: 7}


def local(
    enc_act,
    down_weight,
    norm_gain,
    text_in_weight,
    modulation_weight,
    key_value_weight,
    timesteps,
    lengths,
    image_queries,
    image_key_values,
):
    devices = lax.axis_size("seq")
    chips = devices // 2
    copies = devices // HEADS
    text_len = enc_act.shape[1]
    img_dev = image_queries.shape[1]
    part_rows = img_dev // copies
    factor = math.log2(math.e) / math.sqrt(HEAD_DIM)
    lanes = orders(chips)
    index = lax.axis_index("seq")
    chip, core = index // 2, index % 2
    place = jnp.stack([position(chip, lanes[0]), position(chip, lanes[1]), core, chip, lengths[0]])
    place = place.astype(jnp.int32)

    win0, kv0 = text_in_weight.T, key_value_weight
    win1, kv1 = swap(win0, 1), swap(kv0, 1)
    mod0 = time_embedding(timesteps, modulation_weight)[0]
    mod1 = swap(mod0, 1)

    rounds = len(lanes[0])
    tie = lax.optimization_barrier

    pieces = pack(
        devices, copies, place, image_queries[0], image_key_values[0, :, 0], image_key_values[0, :, 1]
    )
    pieces = list(pieces)
    masks = [[m for m in range(1, devices) if ROUND.get(m, 0) == at] for at in range(8)]

    def send_pieces(at, chain):
        chain, held = tie((chain, [pieces[mask] for mask in masks[at]]))
        for mask, piece in zip(masks[at], held):
            pieces[mask] = swap(piece, mask)
        return chain

    def take_pieces(at, chain):
        chain, held = tie((chain, [pieces[mask] for mask in masks[at]]))
        for mask, piece in zip(masks[at], held):
            pieces[mask] = piece
        return chain

    act = send_pieces(0, enc_act[0].T)
    keep, sent = [], []
    for lane, order in enumerate(lanes):
        own, other, *turned = encoder(lane, order, place, act, down_weight)
        if lane == 0:
            act = turned[0]
        else:
            other = take_pieces(0, other)
        got = swap(other, 1)
        sent.append(add(own[chips // 2 :], got[chips // 2 :], jnp.bfloat16))
        keep.append(add(own[: chips // 2], got[: chips // 2], jnp.float32))
    for step in range(rounds):
        if step < 3:
            sent = send_pieces(1 + step, sent)
        got = [swap(part, 2 * order[step]) for part, order in zip(sent, lanes)]
        if step == 0:
            got, win1, kv1 = tie((got, win1, kv1))
        elif step < 3:
            got = take_pieces(step, got)
        half = keep[0].shape[0] // 2
        if half:
            sent = [add(mine[half:], part[half:], jnp.bfloat16) for mine, part in zip(keep, got)]
            keep = [add(mine[:half], part[:half], jnp.float32) for mine, part in zip(keep, got)]
    summed = [add(mine[0], part[0], jnp.float32) for mine, part in zip(keep, got)]

    width = summed[0].shape[1]
    square = sum(jnp.sum(part * part, 1, keepdims=True) for part in summed)
    scale_rows = lax.rsqrt(square / (2 * width) + epsilon)
    gains = norm_gain.astype(jnp.float32)
    states = [
        (part * scale_rows * gains[lane * width : (lane + 1) * width]).astype(jnp.bfloat16)
        for lane, part in enumerate(summed)
    ]
    for step in range(rounds):
        if step < 3:
            states = send_pieces(4 + step, states)
        bit = rounds - 1 - step
        got = [swap(state, 2 * order[bit]) for state, order in zip(states, lanes)]
        if step < 3:
            got = take_pieces(3 + step, got)
        if bit:
            states = [jnp.concatenate(pair, 0) for pair in zip(states, got)]
    got = send_pieces(7, got)
    states = [state for pair in zip(states, got) for state in pair]

    blocks = project(lanes, place, states, win0, win1, kv0, kv1, mod0, mod1)
    keep, sent = [blocks[0], blocks[2]], [blocks[1], blocks[3]]
    images = []
    for step in range(rounds):
        got = [swap(part, 2 * order[step]) for part, order in zip(sent, lanes)]
        if step == 0:
            got = take_pieces(6, got)
            got = take_pieces(7, got)
        elif step <= 2:
            sent, pieces = tie((sent, pieces))
            image = image_attention(pieces, img_dev, factor, step - 1, 2)
            got, image = tie((got, image))
            images.append(image)
        half = keep[0].shape[0] // 2
        if half:
            sent = [add(mine[half:], part[half:], jnp.bfloat16) for mine, part in zip(keep, got)]
            keep = [add(mine[:half], part[:half], jnp.float32) for mine, part in zip(keep, got)]
    parts = [part[0] for pair in zip(keep, got) for part in pair]
    model_width = text_in_weight.shape[1] * devices
    mine, sent = combine(place, parts, chips, text_len // 2, model_width)
    got = swap(sent, 1)

    back = [None] * devices
    for call in (1, 0):
        masks = range(call * devices // 2, (call + 1) * devices // 2)
        blocks = finish(place, masks, pieces, images[call], mine, got, img_dev, factor)
        for mask, block in zip(masks, blocks):
            back[mask] = swap(block, mask) if mask else block
    attended, text_kv = unpack(copies, part_rows, place, back)
    return (attended[None], text_kv)


def solution(mesh):
    in_specs = (
        P("dp", None, "seq"),
        P("seq", None),
        P(),
        P(None, "seq"),
        P(None, None, "seq"),
        P("seq", None),
        P("dp"),
        P("dp"),
        P("dp", "seq", None),
        P("dp", "seq", None, None),
    )
    out_specs = (P("dp", "seq", None), P(("dp", "seq"), None))
    return jax.shard_map(local, mesh=mesh, in_specs=in_specs, out_specs=out_specs, check_vma=False)
```

```python
import functools
import math

import jax
import jax.numpy as jnp
from jax import lax
from jax.experimental import pallas as pl
from jax.experimental.pallas import tpu as pltpu
from jax.sharding import PartitionSpec as P

HEAD_DIM = 128
HEADS = 16
TEMB = 256
MIB = 1024 * 1024

epsilon = 1e-06

SMEM_SPEC = pl.BlockSpec(memory_space=pltpu.SMEM)
VMEM_SPEC = pl.BlockSpec(memory_space=pltpu.VMEM)


def params(mib):
    return pltpu.CompilerParams(vmem_limit_bytes=mib * MIB)


def swap(value, mask):
    devices = lax.axis_size("seq")
    return lax.ppermute(value, "seq", [(i, i ^ mask) for i in range(devices)])


def orders(chips):
    bits = [1 << i for i in range(chips.bit_length() - 1)]
    turn = len(bits) // 2
    return (bits, bits[turn:] + bits[:turn])


def position(chip, order):
    last = len(order) - 1
    return sum(((chip >> (bit.bit_length() - 1)) & 1) << (last - i) for i, bit in enumerate(order))


def member(at, order):
    last = len(order) - 1
    return sum(bit for i, bit in enumerate(order) if (at >> (last - i)) & 1)


def normalize(summed, norm_gain):
    scale_rows = lax.rsqrt(jnp.mean(summed * summed, 1, keepdims=True) + epsilon)
    return (summed * scale_rows * norm_gain.astype(jnp.float32)).astype(jnp.bfloat16)


def time_embedding(timesteps):
    half_width = TEMB // 2
    freqs = jnp.exp(-math.log(10000.0) * jnp.arange(half_width, dtype=jnp.float32) / half_width)
    angles = timesteps.astype(jnp.float32)[:, None] * freqs[None, :]
    embedding = jnp.concatenate([jnp.cos(angles), jnp.sin(angles)], 1)
    return jax.nn.silu(embedding).astype(jnp.bfloat16)


def encoder_kernel(lane, order, place_ref, act_ref, weight_ref, own_ref, other_ref, *refs):
    *turned, held_ref, arrived = refs
    chips, share, width = own_ref.shape
    at, core = place_ref[lane], place_ref[2]
    depth = weight_ref.shape[0]
    tile = 256
    loads = []
    for start in range(0, width, tile):
        load = pltpu.make_async_copy(
            weight_ref.at[:, pl.ds(lane * width + start, tile)],
            held_ref.at[:, pl.ds(start, tile)],
            arrived.at[start // tile],
        )
        load.start()
        loads.append(load)
    lhs_ref = act_ref
    if turned:
        (lhs_ref,) = turned
        lhs_ref[...] = act_ref[...].T
    cut = depth // 256 * 256
    half = chips * share
    first = core == 0
    for start in range(0, width, tile):
        columns = slice(start, start + tile)
        loads[start // tile].wait()
        result = jnp.dot(
            lhs_ref[:, :cut], held_ref[:cut, columns], preferred_element_type=jnp.float32
        )
        if cut < depth:
            result += jnp.dot(
                lhs_ref[:, cut:], held_ref[cut:, columns], preferred_element_type=jnp.float32
            )
        own = jnp.where(first, result[:half], result[half:]).astype(own_ref.dtype)
        other = jnp.where(first, result[half:], result[:half]).astype(own_ref.dtype)
        own = own.reshape(chips, share, tile)
        other = other.reshape(chips, share, tile)
        for block in range(chips):
            to = at ^ position(block, order)
            own_ref[to, :, start : start + tile] = own[block]
            other_ref[to, :, start : start + tile] = other[block]


def encoder(lane, order, place, act, weight):
    chips = 1 << len(order)
    depth = weight.shape[0]
    rows = act.size // depth
    width = weight.shape[1] // 2
    turn = act.shape[0] == depth
    out = jax.ShapeDtypeStruct((chips, rows // 2 // chips, width), jnp.bfloat16)
    return pl.pallas_call(
        functools.partial(encoder_kernel, lane, order),
        out_shape=(out, out) + (jax.ShapeDtypeStruct((rows, depth), act.dtype),) * turn,
        in_specs=[SMEM_SPEC, VMEM_SPEC, pl.BlockSpec(memory_space=pl.ANY)],
        out_specs=(VMEM_SPEC,) * (2 + turn),
        scratch_shapes=[
            pltpu.VMEM((depth, width), weight.dtype),
            pltpu.SemaphoreType.DMA((width // 256,)),
        ],
        compiler_params=params(60),
        cost_estimate=pl.CostEstimate(
            flops=2 * rows * depth * width,
            bytes_accessed=2 * (depth * rows + depth * width + rows * width),
            transcendentals=0,
        ),
        name="encoder",
    )(place, act, weight)


def slot_rows(chips, width):
    per_slot = 2 * 128 // width
    return chips * per_slot, -(-(chips * per_slot + 2) // 16) * 16


def project_kernel(lanes, place_ref, *refs):
    pieces, refs = (refs[:2], refs[2:4]), refs[4:]
    time, win0, win1, kv0, kv1, mod0, mod1, *outs, states, proj0, proj1, sums = refs
    chip = place_ref[3]
    half_chips = outs[0].shape[0]
    chips = 2 * half_chips
    rows = proj0.shape[0]
    share = rows // chips
    depth = states.shape[1]
    contract = (((1,), (1,)), ((), ()))
    for lane, order in enumerate(lanes):
        top, low = pieces[lane]
        states[: rows // 2, :] = top[...]
        states[rows // 2 :, :] = low[...]
        span = slice(lane * depth, (lane + 1) * depth)
        for win, proj in ((win0, proj0), (win1, proj1)):
            part = lax.dot_general(
                states[...], win[:, span], contract, preferred_element_type=jnp.float32
            )
            for at in range(chips):
                start = pl.multiple_of((chip ^ member(at, order)) * share, share)
                block = part[at * share : (at + 1) * share]
                if lane == 0:
                    proj[pl.ds(start, share), :] = block
                else:
                    proj[pl.ds(start, share), :] += block
    value0, value1 = proj0[...], proj1[...]
    first = jnp.sum(value0, 1, keepdims=True) + jnp.sum(value1, 1, keepdims=True)
    second = jnp.sum(value0 * value0, 1, keepdims=True) + jnp.sum(value1 * value1, 1, keepdims=True)
    lane = lax.broadcasted_iota(jnp.int32, sums.shape, 1)
    sums[...] = jnp.where(lane == 0, first, second).T
    left = []
    embedding = jnp.broadcast_to(time[...].astype(jnp.float32), (16, time.shape[1]))
    embedding = embedding.astype(jnp.bfloat16)
    for value, mod in ((value0, mod0), (value1, mod1)):
        shift, scale = [
            lax.dot_general(embedding, mod[at], contract, preferred_element_type=jnp.float32)[:1]
            for at in range(2)
        ]
        scale = 1.0 + scale
        row = lax.broadcasted_iota(jnp.int32, (16, value.shape[1]), 0)
        lines = jnp.where(row < 2, scale, shift)
        high = lines.astype(jnp.bfloat16).astype(jnp.float32)
        lines = jnp.where(row % 2 == 0, high, lines - high)
        lines = jnp.where(row < 4, lines, 0.0)
        left.append(jnp.concatenate([value * scale, lines], 0).astype(jnp.bfloat16))
    width = outs[0].shape[2]
    slots, extra = slot_rows(chips, width)
    per_slot = slots // chips
    row = lax.broadcasted_iota(jnp.int32, (extra, width), 0)
    column = lax.broadcasted_iota(jnp.int32, (extra, width), 1)
    half = kv0.shape[1] // 2
    for lane, order in enumerate(lanes):
        line = sums[lane : lane + 1, :]
        high = line.astype(jnp.bfloat16).astype(jnp.float32)
        low = line - high
        if per_slot == 1:
            line = jnp.concatenate([high, low], 1)
        else:
            line = jnp.where(row % 2 == 0, high, low)
        line = jnp.where(row // per_slot == chip, line, 0.0)
        for at in reversed(range(chips)):
            out_ref, to = outs[2 * lane + at // half_chips], at % half_chips
            start = lane * half + (chip ^ member(at, order)) * width
            columns = pl.ds(pl.multiple_of(start, width), width)
            value = jnp.dot(left[0], kv0[:, columns], preferred_element_type=jnp.float32)
            value += jnp.dot(left[1], kv1[:, columns], preferred_element_type=jnp.float32)
            out_ref[to, :rows, :] = value[:rows].astype(out_ref.dtype)
            below = jnp.where(row == slots, value[rows : rows + 1] + value[rows + 1 : rows + 2], line)
            below = jnp.where(
                row == slots + 1, value[rows + 2 : rows + 3] + value[rows + 3 : rows + 4], below
            )
            out_ref[to, rows:, :] = below.astype(out_ref.dtype)


def project(lanes, place, pieces, time, win0, win1, kv0, kv1, mod0, mod1):
    chips = 1 << len(lanes[0])
    rows = 2 * pieces[0].shape[0]
    features, depth = win0.shape
    total = kv0.shape[1]
    width = total // 2 // chips
    extra = slot_rows(chips, width)[1]
    out = jax.ShapeDtypeStruct((chips // 2, rows + extra, width), jnp.bfloat16)
    return pl.pallas_call(
        functools.partial(project_kernel, lanes),
        out_shape=(out,) * 4,
        in_specs=[SMEM_SPEC] + [VMEM_SPEC] * 11,
        out_specs=(VMEM_SPEC,) * 4,
        scratch_shapes=[
            pltpu.VMEM((rows, depth // 2), jnp.bfloat16),
            pltpu.VMEM((rows, features), jnp.float32),
            pltpu.VMEM((rows, features), jnp.float32),
            pltpu.VMEM((rows, 128), jnp.float32),
        ],
        compiler_params=params(20),
        cost_estimate=pl.CostEstimate(
            flops=4 * rows * features * (depth + total),
            bytes_accessed=2 * (rows * depth + 2 * features * (depth + total) + rows * total),
            transcendentals=0,
        ),
        name="project",
    )(place, *pieces, time, win0, win1, kv0, kv1, mod0, mod1)


def combine_kernel(chips, model_width, place_ref, *refs):
    refs, mine_ref, sent_ref = refs[:4], refs[4], refs[5]
    core = place_ref[2]
    rows = mine_ref.shape[0]
    width = refs[0].shape[1]
    slots = slot_rows(chips, width)[0]
    totals = [
        refs[2 * lane][...].astype(jnp.float32) + refs[2 * lane + 1][...].astype(jnp.float32)
        for lane in range(2)
    ]
    sums = []
    for total in totals:
        line = jnp.sum(total[rows : rows + slots], 0, keepdims=True)
        if width > 128:
            line = line[:, :128] + line[:, 128:]
        sums.append(line)
    mean_val = sums[0] / model_width
    scale = lax.rsqrt(sums[1] / model_width - mean_val * mean_val + epsilon)
    mean_val = jnp.broadcast_to(mean_val, (rows, rows)).T[:, 0:1]
    scale = jnp.broadcast_to(scale, (rows, rows)).T[:, 0:1]
    texts = []
    for total in totals:
        text = (total[:rows] - mean_val * total[rows + slots : rows + slots + 1]) * scale
        texts.append(text + total[rows + slots + 1 : rows + slots + 2])
    for part, text in enumerate(texts):
        span = slice(part * HEAD_DIM, (part + 1) * HEAD_DIM)
        if width > HEAD_DIM:
            low, high = text[:, :HEAD_DIM], text[:, HEAD_DIM:]
            mine_ref[:, span] = jnp.where(core == 0, low, high).astype(mine_ref.dtype)
            sent_ref[:, span] = jnp.where(core == 0, high, low).astype(mine_ref.dtype)
        else:
            mine_ref[:, span] = text.astype(mine_ref.dtype)
            sent_ref[:, span] = text.astype(mine_ref.dtype)


def combine(place, parts, chips, rows, model_width):
    out = jax.ShapeDtypeStruct((rows, 2 * HEAD_DIM), jnp.bfloat16)
    return pl.pallas_call(
        functools.partial(combine_kernel, chips, model_width),
        out_shape=(out, out),
        in_specs=[SMEM_SPEC] + [VMEM_SPEC] * 4,
        out_specs=(VMEM_SPEC, VMEM_SPEC),
        compiler_params=params(8),
        cost_estimate=pl.CostEstimate(
            flops=8 * rows * 512, bytes_accessed=12 * rows * 512, transcendentals=0
        ),
        name="combine",
    )(place, *parts)


def pack_kernel(copies, rows_ref, out_ref):
    count = out_ref.shape[1]
    for device in range(out_ref.shape[0]):
        head, copy = device // copies, device % copies
        span = slice(head * HEAD_DIM, (head + 1) * HEAD_DIM)
        start = copy * count if count < rows_ref.shape[0] else 0
        out_ref[device] = rows_ref[start : start + count, span]


def pack(copies, rows, count):
    return pl.pallas_call(
        functools.partial(pack_kernel, copies),
        out_shape=jax.ShapeDtypeStruct((HEADS * copies, count, HEAD_DIM), jnp.bfloat16),
        in_specs=[VMEM_SPEC],
        out_specs=VMEM_SPEC,
        compiler_params=params(8),
        cost_estimate=pl.CostEstimate(flops=0, bytes_accessed=4 * rows.size, transcendentals=0),
        name="pack",
    )(rows)


def unpack_kernel(copies, part_rows, blocks_ref, attended_ref, text_ref):
    share = text_ref.shape[0]
    half = text_ref.shape[1] // 2
    for device in range(blocks_ref.shape[0]):
        head, copy = device // copies, device % copies
        start = head * HEAD_DIM
        rows = slice(copy * part_rows, (copy + 1) * part_rows)
        attended_ref[rows, start : start + HEAD_DIM] = blocks_ref[device, :part_rows, :]
        if copy == 0:
            block = blocks_ref[device, part_rows:, :].astype(jnp.float32)
            text_ref[:, start : start + HEAD_DIM] = block[:share].astype(text_ref.dtype)
            start += half
            text_ref[:, start : start + HEAD_DIM] = block[share:].astype(text_ref.dtype)


def unpack(copies, part_rows, blocks):
    share = (blocks.shape[1] - part_rows) // 2
    return pl.pallas_call(
        functools.partial(unpack_kernel, copies, part_rows),
        out_shape=(
            jax.ShapeDtypeStruct((part_rows * copies, HEADS * HEAD_DIM), jnp.bfloat16),
            jax.ShapeDtypeStruct((share, 2 * HEADS * HEAD_DIM), jnp.bfloat16),
        ),
        in_specs=[VMEM_SPEC],
        out_specs=(VMEM_SPEC, VMEM_SPEC),
        compiler_params=params(8),
        name="unpack",
    )(blocks)


def image_kernel(factor, call, queries_ref, keys_ref, values_ref, sum_ref, norm_ref):
    part_rows = queries_ref.shape[1]
    group = max(1, 256 // part_rows)
    rows = group * part_rows
    contract = (((1,), (1,)), ((), ()))
    keys = keys_ref[...].reshape(-1, HEAD_DIM)
    values = values_ref[...].reshape(-1, HEAD_DIM)
    steps = sum_ref.shape[0] // rows
    for step in range(steps):
        at = (call * steps + step) * group
        span = slice(step * rows, (step + 1) * rows)
        queries = queries_ref[at : at + group].reshape(rows, HEAD_DIM)
        scores = lax.dot_general(queries, keys, contract, preferred_element_type=jnp.float32) * factor
        top = jnp.max(scores, 1, keepdims=True)
        weights = jnp.exp2(scores - top)
        total = jnp.sum(weights, 1, keepdims=True)
        sum_ref[span, :] = jnp.dot(
            weights.astype(jnp.bfloat16), values, preferred_element_type=jnp.float32
        )
        lane = lax.broadcasted_iota(jnp.int32, (rows, 128), 1)
        norm_ref[span, :] = jnp.where(lane < 64, top, total)


def image_attention(queries, keys, values, factor, call, calls):
    count = queries.shape[0] * queries.shape[1] // calls
    total = keys.shape[0] * keys.shape[1]
    out = jax.ShapeDtypeStruct((count, HEAD_DIM), jnp.float32)
    return pl.pallas_call(
        functools.partial(image_kernel, factor, call),
        out_shape=(out, out),
        in_specs=[VMEM_SPEC] * 3,
        out_specs=(VMEM_SPEC, VMEM_SPEC),
        compiler_params=params(24),
        cost_estimate=pl.CostEstimate(
            flops=4 * count * total * HEAD_DIM,
            bytes_accessed=4 * total * HEAD_DIM + 10 * count * HEAD_DIM,
            transcendentals=count * total,
        ),
        name="image_attention",
    )(queries, keys, values)


def finish_kernel(factor, calls, place_ref, queries_ref, *refs):
    images, (mine_ref, got_ref, out_ref) = refs[: 2 * calls], refs[2 * calls :]
    core, valid = place_ref[2], place_ref[4]
    devices, part_rows = queries_ref.shape[0], queries_ref.shape[1]
    half = mine_ref.shape[0]
    contract = (((1,), (1,)), ((), ()))
    mine, got = mine_ref[...], got_ref[...]
    keys = jnp.concatenate([mine[:, :HEAD_DIM], got[:, :HEAD_DIM]], 0)
    values = jnp.concatenate([mine[:, HEAD_DIM:], got[:, HEAD_DIM:]], 0)
    lane = lax.broadcasted_iota(jnp.int32, (1, 2 * half), 1)
    text_position = jnp.where((lane >= half) == (core == 0), half, 0) + lane % half
    group = max(1, 512 // part_rows)
    rows = group * part_rows
    each = devices // group // calls
    for step in range(devices // group):
        sum_ref, norm_ref = images[2 * (step // each)], images[2 * (step // each) + 1]
        span = slice(step % each * rows, (step % each + 1) * rows)
        queries = queries_ref[step * group : (step + 1) * group].reshape(rows, HEAD_DIM)
        scores = lax.dot_general(queries, keys, contract, preferred_element_type=jnp.float32) * factor
        scores = jnp.where(text_position < valid, scores, -jnp.inf)
        before = norm_ref[span, 0:1]
        top = jnp.maximum(before, jnp.max(scores, 1, keepdims=True))
        rescale = jnp.exp2(before - top)
        weights = jnp.exp2(scores - top)
        total = norm_ref[span, 64:65] * rescale + jnp.sum(weights, 1, keepdims=True)
        mixed = sum_ref[span, :] * rescale + jnp.dot(
            weights.astype(jnp.bfloat16), values, preferred_element_type=jnp.float32
        )
        mixed = (mixed / total).astype(out_ref.dtype)
        out_ref[step * group : (step + 1) * group, :part_rows, :] = mixed.reshape(group, part_rows, HEAD_DIM)
    low = jnp.where(core == 0, mine.astype(jnp.float32), got.astype(jnp.float32))
    high = jnp.where(core == 0, got.astype(jnp.float32), mine.astype(jnp.float32))
    share = 2 * half // devices
    for device in range(devices):
        source = low if device < devices // 2 else high
        start = device * share % half
        block = source[start : start + share]
        block = jnp.concatenate([block[:, :HEAD_DIM], block[:, HEAD_DIM:]], 0)
        out_ref[device, part_rows:, :] = block.astype(out_ref.dtype)


def finish(place, queries, images, mine, got, factor):
    devices, part_rows = queries.shape[0], queries.shape[1]
    share = 2 * mine.shape[0] // devices
    count = devices * part_rows
    return pl.pallas_call(
        functools.partial(finish_kernel, factor, len(images) // 2),
        out_shape=jax.ShapeDtypeStruct((devices, part_rows + 2 * share, HEAD_DIM), jnp.bfloat16),
        in_specs=[SMEM_SPEC] + [VMEM_SPEC] * (len(images) + 3),
        out_specs=VMEM_SPEC,
        compiler_params=params(16),
        cost_estimate=pl.CostEstimate(
            flops=4 * count * 2 * mine.shape[0] * HEAD_DIM,
            bytes_accessed=12 * count * HEAD_DIM,
            transcendentals=count * 2 * mine.shape[0],
        ),
        name="finish",
    )(place, queries, *images, mine, got)


def add(one, other, dtype):
    return (one.astype(jnp.float32) + other.astype(jnp.float32)).astype(dtype)


def local(
    enc_act,
    down_weight,
    norm_gain,
    text_in_weight,
    modulation_weight,
    key_value_weight,
    timesteps,
    lengths,
    image_queries,
    image_key_values,
):
    devices = lax.axis_size("seq")
    chips = devices // 2
    copies = devices // HEADS
    text_len = enc_act.shape[1]
    img_dev = image_queries.shape[1]
    part_rows = img_dev // copies
    factor = math.log2(math.e) / math.sqrt(HEAD_DIM)
    lanes = orders(chips)
    index = lax.axis_index("seq")
    chip, core = index // 2, index % 2
    place = jnp.stack([position(chip, lanes[0]), position(chip, lanes[1]), core, chip, lengths[0]])
    place = place.astype(jnp.int32)

    win0, kv0 = text_in_weight.T, key_value_weight
    mod0 = modulation_weight.transpose(1, 2, 0)
    win1, kv1, mod1 = swap(win0, 1), swap(kv0, 1), swap(mod0, 1)
    time = time_embedding(timesteps)

    rounds = len(lanes[0])
    tie = lax.optimization_barrier

    def exchange(rows):
        return lax.all_to_all(rows, "seq", split_axis=0, concat_axis=0, tiled=True)

    act = enc_act[0].T
    act, queries = tie((act, pack(copies, image_queries[0], part_rows)))
    queries = exchange(queries)
    keep, sent = [], []
    for lane, order in enumerate(lanes):
        own, other, *turned = encoder(lane, order, place, act, down_weight)
        if lane == 0:
            act = turned[0]
        got = swap(other, 1)
        sent.append(add(own[chips // 2 :], got[chips // 2 :], jnp.bfloat16))
        keep.append(add(own[: chips // 2], got[: chips // 2], jnp.float32))
    for step in range(rounds):
        if step == 0:
            sent, image_key_values = tie((sent, image_key_values))
            keys = exchange(pack(copies, image_key_values[0, :, 0], img_dev))
        got = [swap(part, 2 * order[step]) for part, order in zip(sent, lanes)]
        if step == 0:
            got, win1, kv1, mod1, queries = tie((got, win1, kv1, mod1, queries))
        if step == 2:
            got, keys = tie((got, keys))
        half = keep[0].shape[0] // 2
        if half:
            sent = [add(mine[half:], part[half:], jnp.bfloat16) for mine, part in zip(keep, got)]
            keep = [add(mine[:half], part[:half], jnp.float32) for mine, part in zip(keep, got)]
    summed = [add(mine[0], part[0], jnp.float32) for mine, part in zip(keep, got)]

    width = summed[0].shape[1]
    square = sum(jnp.sum(part * part, 1, keepdims=True) for part in summed)
    scale_rows = lax.rsqrt(square / (2 * width) + epsilon)
    gains = norm_gain.astype(jnp.float32)
    states = [
        (part * scale_rows * gains[lane * width : (lane + 1) * width]).astype(jnp.bfloat16)
        for lane, part in enumerate(summed)
    ]
    for step in reversed(range(rounds)):
        if step == 1:
            states, image_key_values = tie((states, image_key_values))
            values = pack(copies, image_key_values[0, :, 1], img_dev)
        if step == 0:
            states, values = tie((states, values))
            values = exchange(values)
        got = [swap(state, 2 * order[step]) for state, order in zip(states, lanes)]
        if step:
            states = [jnp.concatenate(pair, 0) for pair in zip(states, got)]
    states = [state for pair in zip(states, got) for state in pair]

    blocks = project(lanes, place, states, time, win0, win1, kv0, kv1, mod0, mod1)
    keep, sent = [blocks[0], blocks[2]], [blocks[1], blocks[3]]
    images = []
    for step in range(rounds):
        got = [swap(part, 2 * order[step]) for part, order in zip(sent, lanes)]
        if step == 0:
            got, values = tie((got, values))
        elif step <= 2:
            sent, queries = tie((sent, queries))
            image = image_attention(queries, keys, values, factor, step - 1, 2)
            got, image = tie((got, image))
            images += image
        half = keep[0].shape[0] // 2
        if half:
            sent = [add(mine[half:], part[half:], jnp.bfloat16) for mine, part in zip(keep, got)]
            keep = [add(mine[:half], part[:half], jnp.float32) for mine, part in zip(keep, got)]
    parts = [part[0] for pair in zip(keep, got) for part in pair]
    model_width = text_in_weight.shape[1] * devices
    mine, sent = combine(place, parts, chips, text_len // 2, model_width)
    got = swap(sent, 1)

    back = exchange(finish(place, queries, images, mine, got, factor))
    attended, text_kv = unpack(copies, part_rows, back)
    return (attended[None], text_kv)


def solution(mesh):
    in_specs = (
        P("dp", None, "seq"),
        P("seq", None),
        P(),
        P(None, "seq"),
        P(None, None, "seq"),
        P("seq", None),
        P("dp"),
        P("dp"),
        P("dp", "seq", None),
        P("dp", "seq", None, None),
    )
    out_specs = (P("dp", "seq", None), P(("dp", "seq"), None))
    return jax.shard_map(local, mesh=mesh, in_specs=in_specs, out_specs=out_specs, check_vma=False)
```

```python
import functools
import math

import jax
import jax.numpy as jnp
from jax import lax
from jax.experimental import pallas as pl
from jax.experimental.pallas import tpu as pltpu
from jax.sharding import PartitionSpec as P

HEAD_DIM = 128
HEADS = 16
TEMB = 256
MIB = 1024 * 1024
DEPTH_BLOCK = 512

epsilon = 1e-06

SMEM_SPEC = pl.BlockSpec(memory_space=pltpu.SMEM)
VMEM_SPEC = pl.BlockSpec(memory_space=pltpu.VMEM)


def params(mib):
    return pltpu.CompilerParams(vmem_limit_bytes=mib * MIB)


def swap(value, mask):
    devices = lax.axis_size("seq")
    return lax.ppermute(value, "seq", [(i, i ^ mask) for i in range(devices)])


def orders(chips):
    bits = [1 << i for i in range(chips.bit_length() - 1)]
    return (bits, [bits[1], bits[0]] + bits[2:])


def position(chip, order):
    last = len(order) - 1
    return sum(((chip >> (bit.bit_length() - 1)) & 1) << (last - i) for i, bit in enumerate(order))


def member(at, order):
    last = len(order) - 1
    return sum(bit for i, bit in enumerate(order) if (at >> (last - i)) & 1)


def normalize(summed, norm_gain):
    scale_rows = lax.rsqrt(jnp.mean(summed * summed, 1, keepdims=True) + epsilon)
    return (summed * scale_rows * norm_gain.astype(jnp.float32)).astype(jnp.bfloat16)


def time_embedding(timesteps):
    half_width = TEMB // 2
    freqs = jnp.exp(-math.log(10000.0) * jnp.arange(half_width, dtype=jnp.float32) / half_width)
    angles = timesteps.astype(jnp.float32)[:, None] * freqs[None, :]
    embedding = jnp.concatenate([jnp.cos(angles), jnp.sin(angles)], 1)
    return jax.nn.silu(embedding).astype(jnp.bfloat16)


def encoder_kernel(lane, order, place_ref, act_ref, weight_ref, own_ref, other_ref, *refs):
    *turned, held_ref, total_ref, arrived = refs
    chips, share, width = own_ref.shape
    at, core = place_ref[lane], place_ref[2]
    depth = weight_ref.shape[0]
    starts = range(0, depth, DEPTH_BLOCK)
    loads = []
    for step, start in enumerate(starts):
        rows = pl.ds(start, min(DEPTH_BLOCK, depth - start))
        load = pltpu.make_async_copy(
            weight_ref.at[rows, pl.ds(lane * width, width)], held_ref.at[rows, :], arrived.at[step]
        )
        load.start()
        loads.append(load)
    lhs_ref = act_ref
    if turned:
        (lhs_ref,) = turned
        lhs_ref[...] = act_ref[...].T
    half = chips * share
    first = core == 0
    tile = 256
    for step, start in enumerate(starts):
        rows = slice(start, min(start + DEPTH_BLOCK, depth))
        loads[step].wait()
        for column in range(0, width, tile):
            columns = slice(column, column + tile)
            result = jnp.dot(
                lhs_ref[:, rows], held_ref[rows, columns], preferred_element_type=jnp.float32
            )
            if step > 0:
                result += total_ref[:, columns]
            if rows.stop < depth:
                total_ref[:, columns] = result
                continue
            own = jnp.where(first, result[:half], result[half:]).astype(own_ref.dtype)
            other = jnp.where(first, result[half:], result[:half]).astype(own_ref.dtype)
            own = own.reshape(chips, share, tile)
            other = other.reshape(chips, share, tile)
            for block in range(chips):
                to = at ^ position(block, order)
                own_ref[to, :, columns] = own[block]
                other_ref[to, :, columns] = other[block]


def encoder(lane, order, place, act, weight):
    chips = 1 << len(order)
    depth = weight.shape[0]
    rows = act.size // depth
    width = weight.shape[1] // 2
    turn = act.shape[0] == depth
    out = jax.ShapeDtypeStruct((chips, rows // 2 // chips, width), jnp.bfloat16)
    return pl.pallas_call(
        functools.partial(encoder_kernel, lane, order),
        out_shape=(out, out) + (jax.ShapeDtypeStruct((rows, depth), act.dtype),) * turn,
        in_specs=[SMEM_SPEC, VMEM_SPEC, pl.BlockSpec(memory_space=pl.ANY)],
        out_specs=(VMEM_SPEC,) * (2 + turn),
        scratch_shapes=[
            pltpu.VMEM((depth, width), weight.dtype),
            pltpu.VMEM((rows, width), jnp.float32),
            pltpu.SemaphoreType.DMA((-(-depth // DEPTH_BLOCK),)),
        ],
        compiler_params=params(60),
        cost_estimate=pl.CostEstimate(
            flops=2 * rows * depth * width,
            bytes_accessed=2 * (depth * rows + depth * width + rows * width),
            transcendentals=0,
        ),
        name="encoder",
    )(place, act, weight)


def slot_rows(chips, width):
    per_slot = 2 * 128 // width
    return chips * per_slot, -(-(chips * per_slot + 2) // 16) * 16


def project_kernel(lanes, place_ref, *refs):
    pieces, refs = (refs[:2], refs[2:4]), refs[4:]
    time, win0, win1, kv0, kv1, mod0, mod1, *outs, states, proj0, proj1, sums = refs
    chip = place_ref[3]
    half_chips = outs[0].shape[0]
    chips = 2 * half_chips
    rows = proj0.shape[0]
    share = rows // chips
    depth = states.shape[1]
    contract = (((1,), (1,)), ((), ()))
    for lane, order in enumerate(lanes):
        top, low = pieces[lane]
        states[: rows // 2, :] = top[...]
        states[rows // 2 :, :] = low[...]
        span = slice(lane * depth, (lane + 1) * depth)
        for win, proj in ((win0, proj0), (win1, proj1)):
            part = lax.dot_general(
                states[...], win[:, span], contract, preferred_element_type=jnp.float32
            )
            for at in range(chips):
                start = pl.multiple_of((chip ^ member(at, order)) * share, share)
                block = part[at * share : (at + 1) * share]
                if lane == 0:
                    proj[pl.ds(start, share), :] = block
                else:
                    proj[pl.ds(start, share), :] += block
    value0, value1 = proj0[...], proj1[...]
    first = jnp.sum(value0, 1, keepdims=True) + jnp.sum(value1, 1, keepdims=True)
    second = jnp.sum(value0 * value0, 1, keepdims=True) + jnp.sum(value1 * value1, 1, keepdims=True)
    lane = lax.broadcasted_iota(jnp.int32, sums.shape, 1)
    sums[...] = jnp.where(lane == 0, first, second).T
    left = []
    embedding = jnp.broadcast_to(time[...].astype(jnp.float32), (16, time.shape[1]))
    embedding = embedding.astype(jnp.bfloat16)
    for value, mod in ((value0, mod0), (value1, mod1)):
        shift, scale = [
            lax.dot_general(embedding, mod[at], contract, preferred_element_type=jnp.float32)[:1]
            for at in range(2)
        ]
        scale = 1.0 + scale
        row = lax.broadcasted_iota(jnp.int32, (16, value.shape[1]), 0)
        lines = jnp.where(row < 2, scale, shift)
        high = lines.astype(jnp.bfloat16).astype(jnp.float32)
        lines = jnp.where(row % 2 == 0, high, lines - high)
        lines = jnp.where(row < 4, lines, 0.0)
        left.append(jnp.concatenate([value * scale, lines], 0).astype(jnp.bfloat16))
    width = outs[0].shape[2]
    slots, extra = slot_rows(chips, width)
    per_slot = slots // chips
    row = lax.broadcasted_iota(jnp.int32, (extra, width), 0)
    column = lax.broadcasted_iota(jnp.int32, (extra, width), 1)
    half = kv0.shape[1] // 2
    for lane, order in enumerate(lanes):
        line = sums[lane : lane + 1, :]
        high = line.astype(jnp.bfloat16).astype(jnp.float32)
        low = line - high
        if per_slot == 1:
            line = jnp.concatenate([high, low], 1)
        else:
            line = jnp.where(row % 2 == 0, high, low)
        line = jnp.where(row // per_slot == chip, line, 0.0)
        for at in reversed(range(chips)):
            out_ref, to = outs[2 * lane + at // half_chips], at % half_chips
            start = lane * half + (chip ^ member(at, order)) * width
            columns = pl.ds(pl.multiple_of(start, width), width)
            value = jnp.dot(left[0], kv0[:, columns], preferred_element_type=jnp.float32)
            value += jnp.dot(left[1], kv1[:, columns], preferred_element_type=jnp.float32)
            out_ref[to, :rows, :] = value[:rows].astype(out_ref.dtype)
            below = jnp.where(row == slots, value[rows : rows + 1] + value[rows + 1 : rows + 2], line)
            below = jnp.where(
                row == slots + 1, value[rows + 2 : rows + 3] + value[rows + 3 : rows + 4], below
            )
            out_ref[to, rows:, :] = below.astype(out_ref.dtype)


def project(lanes, place, pieces, time, win0, win1, kv0, kv1, mod0, mod1):
    chips = 1 << len(lanes[0])
    rows = 2 * pieces[0].shape[0]
    features, depth = win0.shape
    total = kv0.shape[1]
    width = total // 2 // chips
    extra = slot_rows(chips, width)[1]
    out = jax.ShapeDtypeStruct((chips // 2, rows + extra, width), jnp.bfloat16)
    return pl.pallas_call(
        functools.partial(project_kernel, lanes),
        out_shape=(out,) * 4,
        in_specs=[SMEM_SPEC] + [VMEM_SPEC] * 11,
        out_specs=(VMEM_SPEC,) * 4,
        scratch_shapes=[
            pltpu.VMEM((rows, depth // 2), jnp.bfloat16),
            pltpu.VMEM((rows, features), jnp.float32),
            pltpu.VMEM((rows, features), jnp.float32),
            pltpu.VMEM((rows, 128), jnp.float32),
        ],
        compiler_params=params(20),
        cost_estimate=pl.CostEstimate(
            flops=4 * rows * features * (depth + total),
            bytes_accessed=2 * (rows * depth + 2 * features * (depth + total) + rows * total),
            transcendentals=0,
        ),
        name="project",
    )(place, *pieces, time, win0, win1, kv0, kv1, mod0, mod1)


def combine_kernel(chips, model_width, place_ref, *refs):
    refs, mine_ref, sent_ref = refs[:4], refs[4], refs[5]
    core = place_ref[2]
    rows = mine_ref.shape[0]
    width = refs[0].shape[1]
    slots = slot_rows(chips, width)[0]
    totals = [
        refs[2 * lane][...].astype(jnp.float32) + refs[2 * lane + 1][...].astype(jnp.float32)
        for lane in range(2)
    ]
    sums = []
    for total in totals:
        line = jnp.sum(total[rows : rows + slots], 0, keepdims=True)
        if width > 128:
            line = line[:, :128] + line[:, 128:]
        sums.append(line)
    mean_val = sums[0] / model_width
    scale = lax.rsqrt(sums[1] / model_width - mean_val * mean_val + epsilon)
    mean_val = jnp.broadcast_to(mean_val, (rows, rows)).T[:, 0:1]
    scale = jnp.broadcast_to(scale, (rows, rows)).T[:, 0:1]
    texts = []
    for total in totals:
        text = (total[:rows] - mean_val * total[rows + slots : rows + slots + 1]) * scale
        texts.append(text + total[rows + slots + 1 : rows + slots + 2])
    for part, text in enumerate(texts):
        span = slice(part * HEAD_DIM, (part + 1) * HEAD_DIM)
        if width > HEAD_DIM:
            low, high = text[:, :HEAD_DIM], text[:, HEAD_DIM:]
            mine_ref[:, span] = jnp.where(core == 0, low, high).astype(mine_ref.dtype)
            sent_ref[:, span] = jnp.where(core == 0, high, low).astype(mine_ref.dtype)
        else:
            mine_ref[:, span] = text.astype(mine_ref.dtype)
            sent_ref[:, span] = text.astype(mine_ref.dtype)


def combine(place, parts, chips, rows, model_width):
    out = jax.ShapeDtypeStruct((rows, 2 * HEAD_DIM), jnp.bfloat16)
    return pl.pallas_call(
        functools.partial(combine_kernel, chips, model_width),
        out_shape=(out, out),
        in_specs=[SMEM_SPEC] + [VMEM_SPEC] * 4,
        out_specs=(VMEM_SPEC, VMEM_SPEC),
        compiler_params=params(8),
        cost_estimate=pl.CostEstimate(
            flops=8 * rows * 512, bytes_accessed=12 * rows * 512, transcendentals=0
        ),
        name="combine",
    )(place, *parts)


def pack_kernel(copies, queries_ref, keys_ref, values_ref, out_ref):
    img_dev = keys_ref.shape[0]
    part_rows = img_dev // copies
    for device in range(out_ref.shape[0]):
        head, copy = device // copies, device % copies
        span = slice(head * HEAD_DIM, (head + 1) * HEAD_DIM)
        out_ref[device, :img_dev, :] = keys_ref[:, span]
        out_ref[device, img_dev : 2 * img_dev, :] = values_ref[:, span]
        out_ref[device, 2 * img_dev :, :] = queries_ref[copy * part_rows : (copy + 1) * part_rows, span]


def pack(copies, queries, keys, values):
    img_dev = keys.shape[0]
    rows = 2 * img_dev + img_dev // copies
    return pl.pallas_call(
        functools.partial(pack_kernel, copies),
        out_shape=jax.ShapeDtypeStruct((HEADS * copies, rows, HEAD_DIM), jnp.bfloat16),
        in_specs=[VMEM_SPEC] * 3,
        out_specs=VMEM_SPEC,
        compiler_params=params(8),
        cost_estimate=pl.CostEstimate(
            flops=0, bytes_accessed=4 * HEADS * copies * rows * HEAD_DIM, transcendentals=0
        ),
        name="pack",
    )(queries, keys, values)


def unpack_kernel(copies, part_rows, blocks_ref, attended_ref, text_ref):
    share = text_ref.shape[0]
    half = text_ref.shape[1] // 2
    for device in range(blocks_ref.shape[0]):
        head, copy = device // copies, device % copies
        start = head * HEAD_DIM
        rows = slice(copy * part_rows, (copy + 1) * part_rows)
        attended_ref[rows, start : start + HEAD_DIM] = blocks_ref[device, :part_rows, :]
        if copy == 0:
            block = blocks_ref[device, part_rows:, :].astype(jnp.float32)
            text_ref[:, start : start + HEAD_DIM] = block[:share].astype(text_ref.dtype)
            start += half
            text_ref[:, start : start + HEAD_DIM] = block[share:].astype(text_ref.dtype)


def unpack(copies, part_rows, blocks):
    share = (blocks.shape[1] - part_rows) // 2
    return pl.pallas_call(
        functools.partial(unpack_kernel, copies, part_rows),
        out_shape=(
            jax.ShapeDtypeStruct((part_rows * copies, HEADS * HEAD_DIM), jnp.bfloat16),
            jax.ShapeDtypeStruct((share, 2 * HEADS * HEAD_DIM), jnp.bfloat16),
        ),
        in_specs=[VMEM_SPEC],
        out_specs=(VMEM_SPEC, VMEM_SPEC),
        compiler_params=params(8),
        name="unpack",
    )(blocks)


def image_kernel(factor, call, img_dev, packed_ref, sum_ref, norm_ref, keys_ref, values_ref):
    devices = packed_ref.shape[0]
    part_rows = packed_ref.shape[1] - 2 * img_dev
    for device in range(devices):
        rows = slice(device * img_dev, (device + 1) * img_dev)
        keys_ref[rows, :] = packed_ref[device, :img_dev, :]
        values_ref[rows, :] = packed_ref[device, img_dev : 2 * img_dev, :]
    group = max(1, 256 // part_rows)
    rows = group * part_rows
    contract = (((1,), (1,)), ((), ()))
    steps = sum_ref.shape[0] // rows
    for step in range(steps):
        at = (call * steps + step) * group
        span = slice(step * rows, (step + 1) * rows)
        queries = packed_ref[at : at + group, 2 * img_dev :, :].reshape(rows, HEAD_DIM)
        scores = lax.dot_general(queries, keys_ref[...], contract, preferred_element_type=jnp.float32)
        scores = scores * factor
        top = jnp.max(scores, 1, keepdims=True)
        weights = jnp.exp2(scores - top)
        total = jnp.sum(weights, 1, keepdims=True)
        sum_ref[span, :] = jnp.dot(
            weights.astype(jnp.bfloat16), values_ref[...], preferred_element_type=jnp.float32
        )
        lane = lax.broadcasted_iota(jnp.int32, (rows, 128), 1)
        norm_ref[span, :] = jnp.where(lane < 64, top, total)


def image_attention(packed, img_dev, factor, call, calls):
    devices = packed.shape[0]
    keys = devices * img_dev
    count = devices * (packed.shape[1] - 2 * img_dev) // calls
    out = jax.ShapeDtypeStruct((count, HEAD_DIM), jnp.float32)
    return pl.pallas_call(
        functools.partial(image_kernel, factor, call, img_dev),
        out_shape=(out, out),
        in_specs=[VMEM_SPEC],
        out_specs=(VMEM_SPEC, VMEM_SPEC),
        scratch_shapes=[pltpu.VMEM((keys, HEAD_DIM), jnp.bfloat16)] * 2,
        compiler_params=params(24),
        cost_estimate=pl.CostEstimate(
            flops=4 * count * keys * HEAD_DIM,
            bytes_accessed=4 * keys * HEAD_DIM + 10 * count * HEAD_DIM,
            transcendentals=count * keys,
        ),
        name="image_attention",
    )(packed)


def finish_kernel(factor, calls, img_dev, place_ref, packed_ref, *refs):
    images, (mine_ref, got_ref, out_ref) = refs[: 2 * calls], refs[2 * calls :]
    core, valid = place_ref[2], place_ref[4]
    devices, part_rows = packed_ref.shape[0], packed_ref.shape[1] - 2 * img_dev
    half = mine_ref.shape[0]
    contract = (((1,), (1,)), ((), ()))
    mine, got = mine_ref[...], got_ref[...]
    keys = jnp.concatenate([mine[:, :HEAD_DIM], got[:, :HEAD_DIM]], 0)
    values = jnp.concatenate([mine[:, HEAD_DIM:], got[:, HEAD_DIM:]], 0)
    lane = lax.broadcasted_iota(jnp.int32, (1, 2 * half), 1)
    text_position = jnp.where((lane >= half) == (core == 0), half, 0) + lane % half
    group = max(1, 512 // part_rows)
    rows = group * part_rows
    each = devices // group // calls
    for step in range(devices // group):
        sum_ref, norm_ref = images[2 * (step // each)], images[2 * (step // each) + 1]
        span = slice(step % each * rows, (step % each + 1) * rows)
        queries = packed_ref[step * group : (step + 1) * group, 2 * img_dev :, :]
        queries = queries.reshape(rows, HEAD_DIM)
        scores = lax.dot_general(queries, keys, contract, preferred_element_type=jnp.float32) * factor
        scores = jnp.where(text_position < valid, scores, -jnp.inf)
        before = norm_ref[span, 0:1]
        top = jnp.maximum(before, jnp.max(scores, 1, keepdims=True))
        rescale = jnp.exp2(before - top)
        weights = jnp.exp2(scores - top)
        total = norm_ref[span, 64:65] * rescale + jnp.sum(weights, 1, keepdims=True)
        mixed = sum_ref[span, :] * rescale + jnp.dot(
            weights.astype(jnp.bfloat16), values, preferred_element_type=jnp.float32
        )
        mixed = (mixed / total).astype(out_ref.dtype)
        out_ref[step * group : (step + 1) * group, :part_rows, :] = mixed.reshape(group, part_rows, HEAD_DIM)
    low = jnp.where(core == 0, mine.astype(jnp.float32), got.astype(jnp.float32))
    high = jnp.where(core == 0, got.astype(jnp.float32), mine.astype(jnp.float32))
    share = 2 * half // devices
    for device in range(devices):
        source = low if device < devices // 2 else high
        start = device * share % half
        block = source[start : start + share]
        block = jnp.concatenate([block[:, :HEAD_DIM], block[:, HEAD_DIM:]], 0)
        out_ref[device, part_rows:, :] = block.astype(out_ref.dtype)


def finish(place, packed, images, mine, got, img_dev, factor):
    devices, part_rows = packed.shape[0], packed.shape[1] - 2 * img_dev
    share = 2 * mine.shape[0] // devices
    count = devices * part_rows
    return pl.pallas_call(
        functools.partial(finish_kernel, factor, len(images) // 2, img_dev),
        out_shape=jax.ShapeDtypeStruct((devices, part_rows + 2 * share, HEAD_DIM), jnp.bfloat16),
        in_specs=[SMEM_SPEC] + [VMEM_SPEC] * (len(images) + 3),
        out_specs=VMEM_SPEC,
        compiler_params=params(16),
        cost_estimate=pl.CostEstimate(
            flops=4 * count * 2 * mine.shape[0] * HEAD_DIM,
            bytes_accessed=12 * count * HEAD_DIM,
            transcendentals=count * 2 * mine.shape[0],
        ),
        name="finish",
    )(place, packed, *images, mine, got)


def add(one, other, dtype):
    return (one.astype(jnp.float32) + other.astype(jnp.float32)).astype(dtype)


def local(
    enc_act,
    down_weight,
    norm_gain,
    text_in_weight,
    modulation_weight,
    key_value_weight,
    timesteps,
    lengths,
    image_queries,
    image_key_values,
):
    devices = lax.axis_size("seq")
    chips = devices // 2
    copies = devices // HEADS
    text_len = enc_act.shape[1]
    img_dev = image_queries.shape[1]
    part_rows = img_dev // copies
    factor = math.log2(math.e) / math.sqrt(HEAD_DIM)
    lanes = orders(chips)
    index = lax.axis_index("seq")
    chip, core = index // 2, index % 2
    place = jnp.stack([position(chip, lanes[0]), position(chip, lanes[1]), core, chip, lengths[0]])
    place = place.astype(jnp.int32)

    win0, kv0 = text_in_weight.T, key_value_weight
    mod0 = modulation_weight.transpose(1, 2, 0)
    win1, kv1, mod1 = swap(win0, 1), swap(kv0, 1), swap(mod0, 1)
    time = time_embedding(timesteps)

    rounds = len(lanes[0])
    tie = lax.optimization_barrier

    def exchange(rows):
        return lax.all_to_all(rows, "seq", split_axis=0, concat_axis=0, tiled=True)

    act = enc_act[0].T
    keep, sent = [], []
    for lane, order in enumerate(lanes):
        own, other, *turned = encoder(lane, order, place, act, down_weight)
        if lane == 0:
            act = turned[0]
        got = swap(other, 1)
        sent.append(add(own[chips // 2 :], got[chips // 2 :], jnp.bfloat16))
        keep.append(add(own[: chips // 2], got[: chips // 2], jnp.float32))
    for step in range(rounds):
        if step == 0:
            sent, image_key_values, image_queries = tie((sent, image_key_values, image_queries))
            packed = pack(
                copies, image_queries[0], image_key_values[0, :, 0], image_key_values[0, :, 1]
            )
            packed = exchange(packed)
        got = [swap(part, 2 * order[step]) for part, order in zip(sent, lanes)]
        if step == 0:
            got, win1, kv1, mod1 = tie((got, win1, kv1, mod1))
        half = keep[0].shape[0] // 2
        if half:
            sent = [add(mine[half:], part[half:], jnp.bfloat16) for mine, part in zip(keep, got)]
            keep = [add(mine[:half], part[:half], jnp.float32) for mine, part in zip(keep, got)]
    summed = [add(mine[0], part[0], jnp.float32) for mine, part in zip(keep, got)]

    width = summed[0].shape[1]
    square = sum(jnp.sum(part * part, 1, keepdims=True) for part in summed)
    scale_rows = lax.rsqrt(square / (2 * width) + epsilon)
    gains = norm_gain.astype(jnp.float32)
    states = [
        (part * scale_rows * gains[lane * width : (lane + 1) * width]).astype(jnp.bfloat16)
        for lane, part in enumerate(summed)
    ]
    images = []

    for step in reversed(range(rounds)):
        if step == 0:
            states, packed = tie((states, packed))
            image = image_attention(packed, img_dev, factor, 0, 2)
        got = [swap(state, 2 * order[step]) for state, order in zip(states, lanes)]
        if step:
            states = [jnp.concatenate(pair, 0) for pair in zip(states, got)]
    got, image = tie((got, image))
    images += image
    states = [state for pair in zip(states, got) for state in pair]

    blocks = project(lanes, place, states, time, win0, win1, kv0, kv1, mod0, mod1)
    keep, sent = [blocks[0], blocks[2]], [blocks[1], blocks[3]]
    for step in range(rounds):
        if step == 0:
            sent, packed = tie((sent, packed))
            image = image_attention(packed, img_dev, factor, 1, 2)
        got = [swap(part, 2 * order[step]) for part, order in zip(sent, lanes)]
        if step == 0:
            got, image = tie((got, image))
            images += image
        half = keep[0].shape[0] // 2
        if half:
            sent = [add(mine[half:], part[half:], jnp.bfloat16) for mine, part in zip(keep, got)]
            keep = [add(mine[:half], part[:half], jnp.float32) for mine, part in zip(keep, got)]
    parts = [part[0] for pair in zip(keep, got) for part in pair]
    model_width = text_in_weight.shape[1] * devices
    mine, sent = combine(place, parts, chips, text_len // 2, model_width)
    got = swap(sent, 1)

    back = exchange(finish(place, packed, images, mine, got, img_dev, factor))
    attended, text_kv = unpack(copies, part_rows, back)
    return (attended[None], text_kv)


def solution(mesh):
    in_specs = (
        P("dp", None, "seq"),
        P("seq", None),
        P(),
        P(None, "seq"),
        P(None, None, "seq"),
        P("seq", None),
        P("dp"),
        P("dp"),
        P("dp", "seq", None),
        P("dp", "seq", None, None),
    )
    out_specs = (P("dp", "seq", None), P(("dp", "seq"), None))
    return jax.shard_map(local, mesh=mesh, in_specs=in_specs, out_specs=out_specs, check_vma=False)
```

```python
import functools
import math

import jax
import jax.numpy as jnp
from jax import lax
from jax.experimental import pallas as pl
from jax.experimental.pallas import tpu as pltpu
from jax.sharding import PartitionSpec as P

HEAD_DIM = 128
HEADS = 16
TEMB = 256
MIB = 1024 * 1024
DEPTH_BLOCK = 512

epsilon = 1e-06

SMEM_SPEC = pl.BlockSpec(memory_space=pltpu.SMEM)
VMEM_SPEC = pl.BlockSpec(memory_space=pltpu.VMEM)


def params(mib):
    return pltpu.CompilerParams(vmem_limit_bytes=mib * MIB)


def swap(value, mask):
    devices = lax.axis_size("seq")
    return lax.ppermute(value, "seq", [(i, i ^ mask) for i in range(devices)])


def orders(chips):
    bits = [1 << i for i in range(chips.bit_length() - 1)]
    return (bits, [bits[1], bits[0]] + bits[2:])


def position(chip, order):
    last = len(order) - 1
    return sum(((chip >> (bit.bit_length() - 1)) & 1) << (last - i) for i, bit in enumerate(order))


def member(at, order):
    last = len(order) - 1
    return sum(bit for i, bit in enumerate(order) if (at >> (last - i)) & 1)


def normalize(summed, norm_gain):
    scale_rows = lax.rsqrt(jnp.mean(summed * summed, 1, keepdims=True) + epsilon)
    return (summed * scale_rows * norm_gain.astype(jnp.float32)).astype(jnp.bfloat16)


def time_embedding(timesteps):
    half_width = TEMB // 2
    freqs = jnp.exp(-math.log(10000.0) * jnp.arange(half_width, dtype=jnp.float32) / half_width)
    angles = timesteps.astype(jnp.float32)[:, None] * freqs[None, :]
    embedding = jnp.concatenate([jnp.cos(angles), jnp.sin(angles)], 1)
    return jax.nn.silu(embedding).astype(jnp.bfloat16)


def encoder_kernel(lane, order, place_ref, act_ref, weight_ref, own_ref, other_ref, *refs):
    *turned, held_ref, total_ref, arrived = refs
    chips, share, width = own_ref.shape
    at, core = place_ref[lane], place_ref[2]
    depth = weight_ref.shape[0]
    starts = range(0, depth, DEPTH_BLOCK)
    loads = []
    for step, start in enumerate(starts):
        rows = pl.ds(start, min(DEPTH_BLOCK, depth - start))
        load = pltpu.make_async_copy(
            weight_ref.at[rows, pl.ds(lane * width, width)], held_ref.at[rows, :], arrived.at[step]
        )
        load.start()
        loads.append(load)
    lhs_ref = act_ref
    if turned:
        (lhs_ref,) = turned
        lhs_ref[...] = act_ref[...].T
    half = chips * share
    first = core == 0
    tile = width // 2
    for step, start in enumerate(starts):
        rows = slice(start, min(start + DEPTH_BLOCK, depth))
        loads[step].wait()
        for column in range(0, width, tile):
            columns = slice(column, column + tile)
            result = jnp.dot(
                lhs_ref[:, rows], held_ref[rows, columns], preferred_element_type=jnp.float32
            )
            if step > 0:
                result += total_ref[:, columns]
            if rows.stop < depth:
                total_ref[:, columns] = result
                continue
            own = jnp.where(first, result[:half], result[half:]).astype(own_ref.dtype)
            other = jnp.where(first, result[half:], result[:half]).astype(own_ref.dtype)
            own = own.reshape(chips, share, tile)
            other = other.reshape(chips, share, tile)
            for block in range(chips):
                to = at ^ position(block, order)
                own_ref[to, :, columns] = own[block]
                other_ref[to, :, columns] = other[block]


def encoder(lane, order, place, act, weight):
    chips = 1 << len(order)
    depth = weight.shape[0]
    rows = act.size // depth
    width = weight.shape[1] // 2
    turn = act.shape[0] == depth
    out = jax.ShapeDtypeStruct((chips, rows // 2 // chips, width), jnp.bfloat16)
    return pl.pallas_call(
        functools.partial(encoder_kernel, lane, order),
        out_shape=(out, out) + (jax.ShapeDtypeStruct((rows, depth), act.dtype),) * turn,
        in_specs=[SMEM_SPEC, VMEM_SPEC, pl.BlockSpec(memory_space=pl.ANY)],
        out_specs=(VMEM_SPEC,) * (2 + turn),
        scratch_shapes=[
            pltpu.VMEM((depth, width), weight.dtype),
            pltpu.VMEM((rows, width), jnp.float32),
            pltpu.SemaphoreType.DMA((-(-depth // DEPTH_BLOCK),)),
        ],
        compiler_params=params(60),
        cost_estimate=pl.CostEstimate(
            flops=2 * rows * depth * width,
            bytes_accessed=2 * (depth * rows + depth * width + rows * width),
            transcendentals=0,
        ),
        name="encoder",
    )(place, act, weight)


def modulation_kernel(time_ref, mod0_ref, mod1_ref, out_ref):
    contract = (((1,), (1,)), ((), ()))
    embedding = jnp.broadcast_to(time_ref[...].astype(jnp.float32), (16, time_ref.shape[1]))
    embedding = embedding.astype(jnp.bfloat16)
    row = lax.broadcasted_iota(jnp.int32, (16, mod0_ref.shape[1]), 0)
    for side, mod in enumerate((mod0_ref, mod1_ref)):
        shift, scale = [
            lax.dot_general(embedding, mod[at], contract, preferred_element_type=jnp.float32)
            for at in range(2)
        ]
        lines = jnp.where(row < 2, 1.0 + scale, shift)
        high = lines.astype(jnp.bfloat16).astype(jnp.float32)
        low = jnp.where(row % 2 == 0, high, lines - high)
        out_ref[side] = jnp.where(row < 4, low, 1.0 + scale)


def modulation(time, mod0, mod1):
    return pl.pallas_call(
        modulation_kernel,
        out_shape=jax.ShapeDtypeStruct((2, 16, mod0.shape[1]), jnp.float32),
        in_specs=[VMEM_SPEC] * 3,
        out_specs=VMEM_SPEC,
        compiler_params=params(8),
        name="modulation",
    )(time, mod0, mod1)


def slot_rows(chips, width):
    per_slot = 2 * 128 // width
    return chips * per_slot, -(-(chips * per_slot + 2) // 16) * 16


def project_kernel(lanes, place_ref, *refs):
    pieces, refs = (refs[:2], refs[2:4]), refs[4:]
    lines_ref, win0, win1, kv0, kv1, *outs, states, proj0, proj1, sums = refs
    chip = place_ref[3]
    half_chips = outs[0].shape[0]
    chips = 2 * half_chips
    rows = proj0.shape[0]
    share = rows // chips
    depth = states.shape[1]
    contract = (((1,), (1,)), ((), ()))
    for lane, order in enumerate(lanes):
        top, low = pieces[lane]
        states[: rows // 2, :] = top[...]
        states[rows // 2 :, :] = low[...]
        span = slice(lane * depth, (lane + 1) * depth)
        for win, proj in ((win0, proj0), (win1, proj1)):
            part = lax.dot_general(
                states[...], win[:, span], contract, preferred_element_type=jnp.float32
            )
            for at in range(chips):
                start = pl.multiple_of((chip ^ member(at, order)) * share, share)
                block = part[at * share : (at + 1) * share]
                if lane == 0:
                    proj[pl.ds(start, share), :] = block
                else:
                    proj[pl.ds(start, share), :] += block
    value0, value1 = proj0[...], proj1[...]
    first = jnp.sum(value0, 1, keepdims=True) + jnp.sum(value1, 1, keepdims=True)
    second = jnp.sum(value0 * value0, 1, keepdims=True) + jnp.sum(value1 * value1, 1, keepdims=True)
    lane = lax.broadcasted_iota(jnp.int32, sums.shape, 1)
    sums[...] = jnp.where(lane == 0, first, second).T
    left = []
    for side, value in enumerate((value0, value1)):
        lines = lines_ref[side]
        row = lax.broadcasted_iota(jnp.int32, lines.shape, 0)
        lines, scale = jnp.where(row < 4, lines, 0.0), lines[4:5]
        left.append(jnp.concatenate([value * scale, lines], 0).astype(jnp.bfloat16))
    width = outs[0].shape[2]
    slots, extra = slot_rows(chips, width)
    per_slot = slots // chips
    row = lax.broadcasted_iota(jnp.int32, (extra, width), 0)
    column = lax.broadcasted_iota(jnp.int32, (extra, width), 1)
    half = kv0.shape[1] // 2
    for lane, order in enumerate(lanes):
        line = sums[lane : lane + 1, :]
        high = line.astype(jnp.bfloat16).astype(jnp.float32)
        low = line - high
        if per_slot == 1:
            line = jnp.concatenate([high, low], 1)
        else:
            line = jnp.where(row % 2 == 0, high, low)
        line = jnp.where(row // per_slot == chip, line, 0.0)
        for at in reversed(range(chips)):
            out_ref, to = outs[2 * lane + at // half_chips], at % half_chips
            start = lane * half + (chip ^ member(at, order)) * width
            columns = pl.ds(pl.multiple_of(start, width), width)
            value = jnp.dot(left[0], kv0[:, columns], preferred_element_type=jnp.float32)
            value += jnp.dot(left[1], kv1[:, columns], preferred_element_type=jnp.float32)
            out_ref[to, :rows, :] = value[:rows].astype(out_ref.dtype)
            below = jnp.where(row == slots, value[rows : rows + 1] + value[rows + 1 : rows + 2], line)
            below = jnp.where(
                row == slots + 1, value[rows + 2 : rows + 3] + value[rows + 3 : rows + 4], below
            )
            out_ref[to, rows:, :] = below.astype(out_ref.dtype)


def project(lanes, place, pieces, lines, win0, win1, kv0, kv1):
    chips = 1 << len(lanes[0])
    rows = 2 * pieces[0].shape[0]
    features, depth = win0.shape
    total = kv0.shape[1]
    width = total // 2 // chips
    extra = slot_rows(chips, width)[1]
    out = jax.ShapeDtypeStruct((chips // 2, rows + extra, width), jnp.bfloat16)
    return pl.pallas_call(
        functools.partial(project_kernel, lanes),
        out_shape=(out,) * 4,
        in_specs=[SMEM_SPEC] + [VMEM_SPEC] * 9,
        out_specs=(VMEM_SPEC,) * 4,
        scratch_shapes=[
            pltpu.VMEM((rows, depth // 2), jnp.bfloat16),
            pltpu.VMEM((rows, features), jnp.float32),
            pltpu.VMEM((rows, features), jnp.float32),
            pltpu.VMEM((rows, 128), jnp.float32),
        ],
        compiler_params=params(20),
        cost_estimate=pl.CostEstimate(
            flops=4 * rows * features * (depth + total),
            bytes_accessed=2 * (rows * depth + 2 * features * (depth + total) + rows * total),
            transcendentals=0,
        ),
        name="project",
    )(place, *pieces, lines, win0, win1, kv0, kv1)


def combine_kernel(chips, model_width, place_ref, *refs):
    refs, mine_ref, sent_ref = refs[:4], refs[4], refs[5]
    core = place_ref[2]
    rows = mine_ref.shape[0]
    width = refs[0].shape[1]
    slots = slot_rows(chips, width)[0]
    totals = [
        refs[2 * lane][...].astype(jnp.float32) + refs[2 * lane + 1][...].astype(jnp.float32)
        for lane in range(2)
    ]
    sums = []
    for total in totals:
        line = jnp.sum(total[rows : rows + slots], 0, keepdims=True)
        if width > 128:
            line = line[:, :128] + line[:, 128:]
        sums.append(line)
    mean_val = sums[0] / model_width
    scale = lax.rsqrt(sums[1] / model_width - mean_val * mean_val + epsilon)
    mean_val = jnp.broadcast_to(mean_val, (rows, rows)).T[:, 0:1]
    scale = jnp.broadcast_to(scale, (rows, rows)).T[:, 0:1]
    texts = []
    for total in totals:
        text = (total[:rows] - mean_val * total[rows + slots : rows + slots + 1]) * scale
        texts.append(text + total[rows + slots + 1 : rows + slots + 2])
    for part, text in enumerate(texts):
        span = slice(part * HEAD_DIM, (part + 1) * HEAD_DIM)
        if width > HEAD_DIM:
            low, high = text[:, :HEAD_DIM], text[:, HEAD_DIM:]
            mine_ref[:, span] = jnp.where(core == 0, low, high).astype(mine_ref.dtype)
            sent_ref[:, span] = jnp.where(core == 0, high, low).astype(mine_ref.dtype)
        else:
            mine_ref[:, span] = text.astype(mine_ref.dtype)
            sent_ref[:, span] = text.astype(mine_ref.dtype)


def combine(place, parts, chips, rows, model_width):
    out = jax.ShapeDtypeStruct((rows, 2 * HEAD_DIM), jnp.bfloat16)
    return pl.pallas_call(
        functools.partial(combine_kernel, chips, model_width),
        out_shape=(out, out),
        in_specs=[SMEM_SPEC] + [VMEM_SPEC] * 4,
        out_specs=(VMEM_SPEC, VMEM_SPEC),
        compiler_params=params(8),
        cost_estimate=pl.CostEstimate(
            flops=8 * rows * 512, bytes_accessed=12 * rows * 512, transcendentals=0
        ),
        name="combine",
    )(place, *parts)


def pack_kernel(copies, queries_ref, keys_ref, values_ref, out_ref):
    img_dev = keys_ref.shape[0]
    part_rows = img_dev // copies
    for device in range(out_ref.shape[0]):
        head, copy = device // copies, device % copies
        span = slice(head * HEAD_DIM, (head + 1) * HEAD_DIM)
        out_ref[device, :img_dev, :] = keys_ref[:, span]
        out_ref[device, img_dev : 2 * img_dev, :] = values_ref[:, span]
        out_ref[device, 2 * img_dev :, :] = queries_ref[copy * part_rows : (copy + 1) * part_rows, span]


def pack(copies, queries, keys, values):
    img_dev = keys.shape[0]
    rows = 2 * img_dev + img_dev // copies
    return pl.pallas_call(
        functools.partial(pack_kernel, copies),
        out_shape=jax.ShapeDtypeStruct((HEADS * copies, rows, HEAD_DIM), jnp.bfloat16),
        in_specs=[VMEM_SPEC] * 3,
        out_specs=VMEM_SPEC,
        compiler_params=params(8),
        cost_estimate=pl.CostEstimate(
            flops=0, bytes_accessed=4 * HEADS * copies * rows * HEAD_DIM, transcendentals=0
        ),
        name="pack",
    )(queries, keys, values)


def unpack_kernel(copies, part_rows, blocks_ref, attended_ref, text_ref):
    share = text_ref.shape[0]
    half = text_ref.shape[1] // 2
    for device in range(blocks_ref.shape[0]):
        head, copy = device // copies, device % copies
        start = head * HEAD_DIM
        rows = slice(copy * part_rows, (copy + 1) * part_rows)
        attended_ref[rows, start : start + HEAD_DIM] = blocks_ref[device, :part_rows, :]
        if copy == 0:
            block = blocks_ref[device, part_rows:, :].astype(jnp.float32)
            text_ref[:, start : start + HEAD_DIM] = block[:share].astype(text_ref.dtype)
            start += half
            text_ref[:, start : start + HEAD_DIM] = block[share:].astype(text_ref.dtype)


def unpack(copies, part_rows, blocks):
    share = (blocks.shape[1] - part_rows) // 2
    return pl.pallas_call(
        functools.partial(unpack_kernel, copies, part_rows),
        out_shape=(
            jax.ShapeDtypeStruct((part_rows * copies, HEADS * HEAD_DIM), jnp.bfloat16),
            jax.ShapeDtypeStruct((share, 2 * HEADS * HEAD_DIM), jnp.bfloat16),
        ),
        in_specs=[VMEM_SPEC],
        out_specs=(VMEM_SPEC, VMEM_SPEC),
        compiler_params=params(8),
        name="unpack",
    )(blocks)


def image_kernel(factor, call, img_dev, packed_ref, sum_ref, norm_ref, keys_ref, values_ref):
    devices = packed_ref.shape[0]
    part_rows = packed_ref.shape[1] - 2 * img_dev
    for device in range(devices):
        rows = slice(device * img_dev, (device + 1) * img_dev)
        keys_ref[rows, :] = packed_ref[device, :img_dev, :]
        values_ref[rows, :] = packed_ref[device, img_dev : 2 * img_dev, :]
    group = max(1, 256 // part_rows)
    rows = group * part_rows
    contract = (((1,), (1,)), ((), ()))
    steps = sum_ref.shape[0] // rows
    for step in range(steps):
        at = (call * steps + step) * group
        span = slice(step * rows, (step + 1) * rows)
        queries = packed_ref[at : at + group, 2 * img_dev :, :].reshape(rows, HEAD_DIM)
        scores = lax.dot_general(queries, keys_ref[...], contract, preferred_element_type=jnp.float32)
        scores = scores * factor
        top = jnp.max(scores, 1, keepdims=True)
        weights = jnp.exp2(scores - top)
        total = jnp.sum(weights, 1, keepdims=True)
        sum_ref[span, :] = jnp.dot(
            weights.astype(jnp.bfloat16), values_ref[...], preferred_element_type=jnp.float32
        )
        lane = lax.broadcasted_iota(jnp.int32, (rows, 128), 1)
        norm_ref[span, :] = jnp.where(lane < 64, top, total)


def image_attention(packed, img_dev, factor, call, calls):
    devices = packed.shape[0]
    keys = devices * img_dev
    count = devices * (packed.shape[1] - 2 * img_dev) // calls
    out = jax.ShapeDtypeStruct((count, HEAD_DIM), jnp.float32)
    return pl.pallas_call(
        functools.partial(image_kernel, factor, call, img_dev),
        out_shape=(out, out),
        in_specs=[VMEM_SPEC],
        out_specs=(VMEM_SPEC, VMEM_SPEC),
        scratch_shapes=[pltpu.VMEM((keys, HEAD_DIM), jnp.bfloat16)] * 2,
        compiler_params=params(24),
        cost_estimate=pl.CostEstimate(
            flops=4 * count * keys * HEAD_DIM,
            bytes_accessed=4 * keys * HEAD_DIM + 10 * count * HEAD_DIM,
            transcendentals=count * keys,
        ),
        name="image_attention",
    )(packed)


def finish_kernel(factor, calls, img_dev, place_ref, packed_ref, *refs):
    images, (mine_ref, got_ref, out_ref) = refs[: 2 * calls], refs[2 * calls :]
    core, valid = place_ref[2], place_ref[4]
    devices, part_rows = packed_ref.shape[0], packed_ref.shape[1] - 2 * img_dev
    half = mine_ref.shape[0]
    contract = (((1,), (1,)), ((), ()))
    mine, got = mine_ref[...], got_ref[...]
    keys = jnp.concatenate([mine[:, :HEAD_DIM], got[:, :HEAD_DIM]], 0)
    values = jnp.concatenate([mine[:, HEAD_DIM:], got[:, HEAD_DIM:]], 0)
    lane = lax.broadcasted_iota(jnp.int32, (1, 2 * half), 1)
    text_position = jnp.where((lane >= half) == (core == 0), half, 0) + lane % half
    group = max(1, 512 // part_rows)
    rows = group * part_rows
    each = devices // group // calls
    for step in range(devices // group):
        sum_ref, norm_ref = images[2 * (step // each)], images[2 * (step // each) + 1]
        span = slice(step % each * rows, (step % each + 1) * rows)
        queries = packed_ref[step * group : (step + 1) * group, 2 * img_dev :, :]
        queries = queries.reshape(rows, HEAD_DIM)
        scores = lax.dot_general(queries, keys, contract, preferred_element_type=jnp.float32) * factor
        scores = jnp.where(text_position < valid, scores, -jnp.inf)
        before = norm_ref[span, 0:1]
        top = jnp.maximum(before, jnp.max(scores, 1, keepdims=True))
        rescale = jnp.exp2(before - top)
        weights = jnp.exp2(scores - top)
        total = norm_ref[span, 64:65] * rescale + jnp.sum(weights, 1, keepdims=True)
        mixed = sum_ref[span, :] * rescale + jnp.dot(
            weights.astype(jnp.bfloat16), values, preferred_element_type=jnp.float32
        )
        mixed = (mixed / total).astype(out_ref.dtype)
        out_ref[step * group : (step + 1) * group, :part_rows, :] = mixed.reshape(group, part_rows, HEAD_DIM)
    low = jnp.where(core == 0, mine.astype(jnp.float32), got.astype(jnp.float32))
    high = jnp.where(core == 0, got.astype(jnp.float32), mine.astype(jnp.float32))
    share = 2 * half // devices
    for device in range(devices):
        source = low if device < devices // 2 else high
        start = device * share % half
        block = source[start : start + share]
        block = jnp.concatenate([block[:, :HEAD_DIM], block[:, HEAD_DIM:]], 0)
        out_ref[device, part_rows:, :] = block.astype(out_ref.dtype)


def finish(place, packed, images, mine, got, img_dev, factor):
    devices, part_rows = packed.shape[0], packed.shape[1] - 2 * img_dev
    share = 2 * mine.shape[0] // devices
    count = devices * part_rows
    return pl.pallas_call(
        functools.partial(finish_kernel, factor, len(images) // 2, img_dev),
        out_shape=jax.ShapeDtypeStruct((devices, part_rows + 2 * share, HEAD_DIM), jnp.bfloat16),
        in_specs=[SMEM_SPEC] + [VMEM_SPEC] * (len(images) + 3),
        out_specs=VMEM_SPEC,
        compiler_params=params(16),
        cost_estimate=pl.CostEstimate(
            flops=4 * count * 2 * mine.shape[0] * HEAD_DIM,
            bytes_accessed=12 * count * HEAD_DIM,
            transcendentals=count * 2 * mine.shape[0],
        ),
        name="finish",
    )(place, packed, *images, mine, got)


def add(one, other, dtype):
    return (one.astype(jnp.float32) + other.astype(jnp.float32)).astype(dtype)


def local(
    enc_act,
    down_weight,
    norm_gain,
    text_in_weight,
    modulation_weight,
    key_value_weight,
    timesteps,
    lengths,
    image_queries,
    image_key_values,
):
    devices = lax.axis_size("seq")
    chips = devices // 2
    copies = devices // HEADS
    text_len = enc_act.shape[1]
    img_dev = image_queries.shape[1]
    part_rows = img_dev // copies
    factor = math.log2(math.e) / math.sqrt(HEAD_DIM)
    lanes = orders(chips)
    index = lax.axis_index("seq")
    chip, core = index // 2, index % 2
    place = jnp.stack([position(chip, lanes[0]), position(chip, lanes[1]), core, chip, lengths[0]])
    place = place.astype(jnp.int32)

    win0, kv0 = text_in_weight.T, key_value_weight
    mod0 = modulation_weight.transpose(1, 2, 0)
    win1, kv1, mod1 = swap(win0, 1), swap(kv0, 1), swap(mod0, 1)
    time = time_embedding(timesteps)

    rounds = len(lanes[0])
    tie = lax.optimization_barrier

    def exchange(rows):
        return lax.all_to_all(rows, "seq", split_axis=0, concat_axis=0, tiled=True)

    image_key_values, image_queries = tie((image_key_values, image_queries))
    packed = pack(copies, image_queries[0], image_key_values[0, :, 0], image_key_values[0, :, 1])
    act, packed = tie((enc_act[0].T, packed))
    packed = exchange(packed)
    keep, sent = [], []
    for lane, order in enumerate(lanes):
        own, other, *turned = encoder(lane, order, place, act, down_weight)
        if lane == 0:
            act = turned[0]
        got = swap(other, 1)
        sent.append(add(own[chips // 2 :], got[chips // 2 :], jnp.bfloat16))
        keep.append(add(own[: chips // 2], got[: chips // 2], jnp.float32))
    for step in range(rounds):
        got = [swap(part, 2 * order[step]) for part, order in zip(sent, lanes)]
        if step == 0:
            got, win1, kv1, mod1 = tie((got, win1, kv1, mod1))
            lines = modulation(time, mod0, mod1)
        if step == 1:
            got, lines = tie((got, lines))
        half = keep[0].shape[0] // 2
        if half:
            sent = [add(mine[half:], part[half:], jnp.bfloat16) for mine, part in zip(keep, got)]
            keep = [add(mine[:half], part[:half], jnp.float32) for mine, part in zip(keep, got)]
    summed = [add(mine[0], part[0], jnp.float32) for mine, part in zip(keep, got)]

    width = summed[0].shape[1]
    square = sum(jnp.sum(part * part, 1, keepdims=True) for part in summed)
    scale_rows = lax.rsqrt(square / (2 * width) + epsilon)
    gains = norm_gain.astype(jnp.float32)
    states = [
        (part * scale_rows * gains[lane * width : (lane + 1) * width]).astype(jnp.bfloat16)
        for lane, part in enumerate(summed)
    ]
    images = []

    for step in reversed(range(rounds)):
        if step == 0:
            states, packed = tie((states, packed))
            image = image_attention(packed, img_dev, factor, 0, 2)
        got = [swap(state, 2 * order[step]) for state, order in zip(states, lanes)]
        if step:
            states = [jnp.concatenate(pair, 0) for pair in zip(states, got)]
    got, image = tie((got, image))
    images += image
    states = [state for pair in zip(states, got) for state in pair]

    blocks = project(lanes, place, states, lines, win0, win1, kv0, kv1)
    keep, sent = [blocks[0], blocks[2]], [blocks[1], blocks[3]]
    for step in range(rounds):
        if step == 0:
            sent, packed = tie((sent, packed))
            image = image_attention(packed, img_dev, factor, 1, 2)
        got = [swap(part, 2 * order[step]) for part, order in zip(sent, lanes)]
        if step == 0:
            got, image = tie((got, image))
            images += image
        half = keep[0].shape[0] // 2
        if half:
            sent = [add(mine[half:], part[half:], jnp.bfloat16) for mine, part in zip(keep, got)]
            keep = [add(mine[:half], part[:half], jnp.float32) for mine, part in zip(keep, got)]
    parts = [part[0] for pair in zip(keep, got) for part in pair]
    model_width = text_in_weight.shape[1] * devices
    mine, sent = combine(place, parts, chips, text_len // 2, model_width)
    got = swap(sent, 1)

    back = exchange(finish(place, packed, images, mine, got, img_dev, factor))
    attended, text_kv = unpack(copies, part_rows, back)
    return (attended[None], text_kv)


def solution(mesh):
    in_specs = (
        P("dp", None, "seq"),
        P("seq", None),
        P(),
        P(None, "seq"),
        P(None, None, "seq"),
        P("seq", None),
        P("dp"),
        P("dp"),
        P("dp", "seq", None),
        P("dp", "seq", None, None),
    )
    out_specs = (P("dp", "seq", None), P(("dp", "seq"), None))
    return jax.shard_map(local, mesh=mesh, in_specs=in_specs, out_specs=out_specs, check_vma=False)
```

```python
import functools
import math

import jax
import jax.numpy as jnp
from jax import lax
from jax.experimental import pallas as pl
from jax.experimental.pallas import tpu as pltpu
from jax.sharding import PartitionSpec as P

HEAD_DIM = 128
HEADS = 16
TEMB = 256
MIB = 1024 * 1024

epsilon = 1e-06

SMEM_SPEC = pl.BlockSpec(memory_space=pltpu.SMEM)
VMEM_SPEC = pl.BlockSpec(memory_space=pltpu.VMEM)


def params(mib):
    return pltpu.CompilerParams(vmem_limit_bytes=mib * MIB)


def swap(value, mask):
    devices = lax.axis_size("seq")
    return lax.ppermute(value, "seq", [(i, i ^ mask) for i in range(devices)])


def orders(chips):
    bits = [1 << i for i in range(chips.bit_length() - 1)]
    return (bits, [bits[1], bits[0]] + bits[2:])


def position(chip, order):
    last = len(order) - 1
    return sum(((chip >> (bit.bit_length() - 1)) & 1) << (last - i) for i, bit in enumerate(order))


def member(at, order):
    last = len(order) - 1
    return sum(bit for i, bit in enumerate(order) if (at >> (last - i)) & 1)


def normalize(summed, norm_gain):
    scale_rows = lax.rsqrt(jnp.mean(summed * summed, 1, keepdims=True) + epsilon)
    return (summed * scale_rows * norm_gain.astype(jnp.float32)).astype(jnp.bfloat16)


def time_embedding(timesteps):
    half_width = TEMB // 2
    freqs = jnp.exp(-math.log(10000.0) * jnp.arange(half_width, dtype=jnp.float32) / half_width)
    angles = timesteps.astype(jnp.float32)[:, None] * freqs[None, :]
    embedding = jnp.concatenate([jnp.cos(angles), jnp.sin(angles)], 1)
    return jax.nn.silu(embedding).astype(jnp.bfloat16)


def encoder_kernel(lanes, place_ref, act_ref, weight_ref, *refs):
    outs, lhs_ref = refs[:-1], refs[-1]
    chips, share, width = outs[0].shape
    core = place_ref[2]
    half = chips * share
    first = core == 0
    tile = width // 2
    lhs_ref[...] = act_ref[...].T
    for lane, order in enumerate(lanes):
        own_ref, other_ref = outs[2 * lane], outs[2 * lane + 1]
        for column in range(0, width, tile):
            start = lane * width + column
            result = jnp.dot(
                lhs_ref[...], weight_ref[:, start : start + tile], preferred_element_type=jnp.float32
            )
            own = jnp.where(first, result[:half], result[half:]).astype(own_ref.dtype)
            other = jnp.where(first, result[half:], result[:half]).astype(own_ref.dtype)
            own = own.reshape(chips, share, tile)
            other = other.reshape(chips, share, tile)
            for block in range(chips):
                to = place_ref[lane] ^ position(block, order)
                own_ref[to, :, column : column + tile] = own[block]
                other_ref[to, :, column : column + tile] = other[block]


def encoder(lanes, place, act, weight):
    chips = 1 << len(lanes[0])
    depth, rows = act.shape
    width = weight.shape[1]
    out = jax.ShapeDtypeStruct((chips, rows // 2 // chips, width // 2), jnp.bfloat16)
    return pl.pallas_call(
        functools.partial(encoder_kernel, lanes),
        out_shape=(out,) * 4,
        in_specs=[SMEM_SPEC, VMEM_SPEC, VMEM_SPEC],
        out_specs=(VMEM_SPEC,) * 4,
        scratch_shapes=[pltpu.VMEM((rows, depth), jnp.bfloat16)],
        compiler_params=params(24),
        cost_estimate=pl.CostEstimate(
            flops=2 * rows * depth * width,
            bytes_accessed=2 * (depth * rows + depth * width + rows * width),
            transcendentals=0,
        ),
        name="encoder",
    )(place, act, weight)


def modulation_kernel(time_ref, mod0_ref, mod1_ref, out_ref):
    contract = (((1,), (1,)), ((), ()))
    embedding = jnp.broadcast_to(time_ref[...].astype(jnp.float32), (16, time_ref.shape[1]))
    embedding = embedding.astype(jnp.bfloat16)
    row = lax.broadcasted_iota(jnp.int32, (16, mod0_ref.shape[1]), 0)
    for side, mod in enumerate((mod0_ref, mod1_ref)):
        shift, scale = [
            lax.dot_general(embedding, mod[at], contract, preferred_element_type=jnp.float32)
            for at in range(2)
        ]
        lines = jnp.where(row < 2, 1.0 + scale, shift)
        high = lines.astype(jnp.bfloat16).astype(jnp.float32)
        low = jnp.where(row % 2 == 0, high, lines - high)
        out_ref[side] = jnp.where(row < 4, low, 1.0 + scale)


def modulation(time, mod0, mod1):
    return pl.pallas_call(
        modulation_kernel,
        out_shape=jax.ShapeDtypeStruct((2, 16, mod0.shape[1]), jnp.float32),
        in_specs=[VMEM_SPEC] * 3,
        out_specs=VMEM_SPEC,
        compiler_params=params(8),
        name="modulation",
    )(time, mod0, mod1)


def slot_rows(chips, width):
    per_slot = 2 * 128 // width
    return chips * per_slot, -(-(chips * per_slot + 2) // 16) * 16


def project_kernel(lanes, place_ref, *refs):
    pieces, refs = (refs[:2], refs[2:4]), refs[4:]
    lines_ref, win0, win1, kv0, kv1, *outs, states, proj0, proj1, sums = refs
    chip = place_ref[3]
    half_chips = outs[0].shape[0]
    chips = 2 * half_chips
    rows = proj0.shape[0]
    share = rows // chips
    depth = states.shape[1]
    contract = (((1,), (1,)), ((), ()))
    for lane, order in enumerate(lanes):
        top, low = pieces[lane]
        states[: rows // 2, :] = top[...]
        states[rows // 2 :, :] = low[...]
        span = slice(lane * depth, (lane + 1) * depth)
        for win, proj in ((win0, proj0), (win1, proj1)):
            part = lax.dot_general(
                states[...], win[:, span], contract, preferred_element_type=jnp.float32
            )
            for at in range(chips):
                start = pl.multiple_of((chip ^ member(at, order)) * share, share)
                block = part[at * share : (at + 1) * share]
                if lane == 0:
                    proj[pl.ds(start, share), :] = block
                else:
                    proj[pl.ds(start, share), :] += block
    value0, value1 = proj0[...], proj1[...]
    first = jnp.sum(value0, 1, keepdims=True) + jnp.sum(value1, 1, keepdims=True)
    second = jnp.sum(value0 * value0, 1, keepdims=True) + jnp.sum(value1 * value1, 1, keepdims=True)
    lane = lax.broadcasted_iota(jnp.int32, sums.shape, 1)
    sums[...] = jnp.where(lane == 0, first, second).T
    left = []
    for side, value in enumerate((value0, value1)):
        lines = lines_ref[side]
        row = lax.broadcasted_iota(jnp.int32, lines.shape, 0)
        lines, scale = jnp.where(row < 4, lines, 0.0), lines[4:5]
        left.append(jnp.concatenate([value * scale, lines], 0).astype(jnp.bfloat16))
    width = outs[0].shape[2]
    slots, extra = slot_rows(chips, width)
    per_slot = slots // chips
    row = lax.broadcasted_iota(jnp.int32, (extra, width), 0)
    column = lax.broadcasted_iota(jnp.int32, (extra, width), 1)
    half = kv0.shape[1] // 2
    for lane, order in enumerate(lanes):
        line = sums[lane : lane + 1, :]
        high = line.astype(jnp.bfloat16).astype(jnp.float32)
        low = line - high
        if per_slot == 1:
            line = jnp.concatenate([high, low], 1)
        else:
            line = jnp.where(row % 2 == 0, high, low)
        line = jnp.where(row // per_slot == chip, line, 0.0)
        for at in reversed(range(chips)):
            out_ref, to = outs[2 * lane + at // half_chips], at % half_chips
            start = lane * half + (chip ^ member(at, order)) * width
            columns = pl.ds(pl.multiple_of(start, width), width)
            value = jnp.dot(left[0], kv0[:, columns], preferred_element_type=jnp.float32)
            value += jnp.dot(left[1], kv1[:, columns], preferred_element_type=jnp.float32)
            out_ref[to, :rows, :] = value[:rows].astype(out_ref.dtype)
            below = jnp.where(row == slots, value[rows : rows + 1] + value[rows + 1 : rows + 2], line)
            below = jnp.where(
                row == slots + 1, value[rows + 2 : rows + 3] + value[rows + 3 : rows + 4], below
            )
            out_ref[to, rows:, :] = below.astype(out_ref.dtype)


def project(lanes, place, pieces, lines, win0, win1, kv0, kv1):
    chips = 1 << len(lanes[0])
    rows = 2 * pieces[0].shape[0]
    features, depth = win0.shape
    total = kv0.shape[1]
    width = total // 2 // chips
    extra = slot_rows(chips, width)[1]
    out = jax.ShapeDtypeStruct((chips // 2, rows + extra, width), jnp.bfloat16)
    return pl.pallas_call(
        functools.partial(project_kernel, lanes),
        out_shape=(out,) * 4,
        in_specs=[SMEM_SPEC] + [VMEM_SPEC] * 9,
        out_specs=(VMEM_SPEC,) * 4,
        scratch_shapes=[
            pltpu.VMEM((rows, depth // 2), jnp.bfloat16),
            pltpu.VMEM((rows, features), jnp.float32),
            pltpu.VMEM((rows, features), jnp.float32),
            pltpu.VMEM((rows, 128), jnp.float32),
        ],
        compiler_params=params(20),
        cost_estimate=pl.CostEstimate(
            flops=4 * rows * features * (depth + total),
            bytes_accessed=2 * (rows * depth + 2 * features * (depth + total) + rows * total),
            transcendentals=0,
        ),
        name="project",
    )(place, *pieces, lines, win0, win1, kv0, kv1)


def combine_kernel(chips, model_width, place_ref, *refs):
    refs, mine_ref, sent_ref = refs[:4], refs[4], refs[5]
    core = place_ref[2]
    rows = mine_ref.shape[0]
    width = refs[0].shape[1]
    slots = slot_rows(chips, width)[0]
    totals = [
        refs[2 * lane][...].astype(jnp.float32) + refs[2 * lane + 1][...].astype(jnp.float32)
        for lane in range(2)
    ]
    sums = []
    for total in totals:
        line = jnp.sum(total[rows : rows + slots], 0, keepdims=True)
        if width > 128:
            line = line[:, :128] + line[:, 128:]
        sums.append(line)
    mean_val = sums[0] / model_width
    scale = lax.rsqrt(sums[1] / model_width - mean_val * mean_val + epsilon)
    mean_val = jnp.broadcast_to(mean_val, (rows, rows)).T[:, 0:1]
    scale = jnp.broadcast_to(scale, (rows, rows)).T[:, 0:1]
    texts = []
    for total in totals:
        text = (total[:rows] - mean_val * total[rows + slots : rows + slots + 1]) * scale
        texts.append(text + total[rows + slots + 1 : rows + slots + 2])
    for part, text in enumerate(texts):
        span = slice(part * HEAD_DIM, (part + 1) * HEAD_DIM)
        if width > HEAD_DIM:
            low, high = text[:, :HEAD_DIM], text[:, HEAD_DIM:]
            mine_ref[:, span] = jnp.where(core == 0, low, high).astype(mine_ref.dtype)
            sent_ref[:, span] = jnp.where(core == 0, high, low).astype(mine_ref.dtype)
        else:
            mine_ref[:, span] = text.astype(mine_ref.dtype)
            sent_ref[:, span] = text.astype(mine_ref.dtype)


def combine(place, parts, chips, rows, model_width):
    out = jax.ShapeDtypeStruct((rows, 2 * HEAD_DIM), jnp.bfloat16)
    return pl.pallas_call(
        functools.partial(combine_kernel, chips, model_width),
        out_shape=(out, out),
        in_specs=[SMEM_SPEC] + [VMEM_SPEC] * 4,
        out_specs=(VMEM_SPEC, VMEM_SPEC),
        compiler_params=params(8),
        cost_estimate=pl.CostEstimate(
            flops=8 * rows * 512, bytes_accessed=12 * rows * 512, transcendentals=0
        ),
        name="combine",
    )(place, *parts)


def pack_kernel(copies, queries_ref, keys_ref, values_ref, out_ref):
    img_dev = keys_ref.shape[0]
    part_rows = img_dev // copies
    for device in range(out_ref.shape[0]):
        head, copy = device // copies, device % copies
        span = slice(head * HEAD_DIM, (head + 1) * HEAD_DIM)
        out_ref[device, :img_dev, :] = keys_ref[:, span]
        out_ref[device, img_dev : 2 * img_dev, :] = values_ref[:, span]
        out_ref[device, 2 * img_dev :, :] = queries_ref[copy * part_rows : (copy + 1) * part_rows, span]


def pack(copies, queries, keys, values):
    img_dev = keys.shape[0]
    rows = 2 * img_dev + img_dev // copies
    return pl.pallas_call(
        functools.partial(pack_kernel, copies),
        out_shape=jax.ShapeDtypeStruct((HEADS * copies, rows, HEAD_DIM), jnp.bfloat16),
        in_specs=[VMEM_SPEC] * 3,
        out_specs=VMEM_SPEC,
        compiler_params=params(8),
        cost_estimate=pl.CostEstimate(
            flops=0, bytes_accessed=4 * HEADS * copies * rows * HEAD_DIM, transcendentals=0
        ),
        name="pack",
    )(queries, keys, values)


def unpack_kernel(copies, part_rows, blocks_ref, attended_ref, text_ref):
    share = text_ref.shape[0]
    half = text_ref.shape[1] // 2
    for device in range(blocks_ref.shape[0]):
        head, copy = device // copies, device % copies
        start = head * HEAD_DIM
        rows = slice(copy * part_rows, (copy + 1) * part_rows)
        attended_ref[rows, start : start + HEAD_DIM] = blocks_ref[device, :part_rows, :]
        if copy == 0:
            block = blocks_ref[device, part_rows:, :].astype(jnp.float32)
            text_ref[:, start : start + HEAD_DIM] = block[:share].astype(text_ref.dtype)
            start += half
            text_ref[:, start : start + HEAD_DIM] = block[share:].astype(text_ref.dtype)


def unpack(copies, part_rows, blocks):
    share = (blocks.shape[1] - part_rows) // 2
    return pl.pallas_call(
        functools.partial(unpack_kernel, copies, part_rows),
        out_shape=(
            jax.ShapeDtypeStruct((part_rows * copies, HEADS * HEAD_DIM), jnp.bfloat16),
            jax.ShapeDtypeStruct((share, 2 * HEADS * HEAD_DIM), jnp.bfloat16),
        ),
        in_specs=[VMEM_SPEC],
        out_specs=(VMEM_SPEC, VMEM_SPEC),
        compiler_params=params(8),
        name="unpack",
    )(blocks)


def image_kernel(factor, call, img_dev, packed_ref, sum_ref, norm_ref, keys_ref, values_ref):
    devices = packed_ref.shape[0]
    part_rows = packed_ref.shape[1] - 2 * img_dev
    for device in range(devices):
        rows = slice(device * img_dev, (device + 1) * img_dev)
        keys_ref[rows, :] = packed_ref[device, :img_dev, :]
        values_ref[rows, :] = packed_ref[device, img_dev : 2 * img_dev, :]
    group = max(1, 256 // part_rows)
    rows = group * part_rows
    contract = (((1,), (1,)), ((), ()))
    steps = sum_ref.shape[0] // rows
    for step in range(steps):
        at = (call * steps + step) * group
        span = slice(step * rows, (step + 1) * rows)
        queries = packed_ref[at : at + group, 2 * img_dev :, :].reshape(rows, HEAD_DIM)
        scores = lax.dot_general(queries, keys_ref[...], contract, preferred_element_type=jnp.float32)
        scores = scores * factor
        top = jnp.max(scores, 1, keepdims=True)
        weights = jnp.exp2(scores - top)
        total = jnp.sum(weights, 1, keepdims=True)
        sum_ref[span, :] = jnp.dot(
            weights.astype(jnp.bfloat16), values_ref[...], preferred_element_type=jnp.float32
        )
        lane = lax.broadcasted_iota(jnp.int32, (rows, 128), 1)
        norm_ref[span, :] = jnp.where(lane < 64, top, total)


def image_attention(packed, img_dev, factor, call, calls):
    devices = packed.shape[0]
    keys = devices * img_dev
    count = devices * (packed.shape[1] - 2 * img_dev) // calls
    out = jax.ShapeDtypeStruct((count, HEAD_DIM), jnp.float32)
    return pl.pallas_call(
        functools.partial(image_kernel, factor, call, img_dev),
        out_shape=(out, out),
        in_specs=[VMEM_SPEC],
        out_specs=(VMEM_SPEC, VMEM_SPEC),
        scratch_shapes=[pltpu.VMEM((keys, HEAD_DIM), jnp.bfloat16)] * 2,
        compiler_params=params(24),
        cost_estimate=pl.CostEstimate(
            flops=4 * count * keys * HEAD_DIM,
            bytes_accessed=4 * keys * HEAD_DIM + 10 * count * HEAD_DIM,
            transcendentals=count * keys,
        ),
        name="image_attention",
    )(packed)


def finish_kernel(factor, calls, img_dev, place_ref, packed_ref, *refs):
    images, (mine_ref, got_ref, out_ref) = refs[: 2 * calls], refs[2 * calls :]
    core, valid = place_ref[2], place_ref[4]
    devices, part_rows = packed_ref.shape[0], packed_ref.shape[1] - 2 * img_dev
    half = mine_ref.shape[0]
    contract = (((1,), (1,)), ((), ()))
    mine, got = mine_ref[...], got_ref[...]
    keys = jnp.concatenate([mine[:, :HEAD_DIM], got[:, :HEAD_DIM]], 0)
    values = jnp.concatenate([mine[:, HEAD_DIM:], got[:, HEAD_DIM:]], 0)
    lane = lax.broadcasted_iota(jnp.int32, (1, 2 * half), 1)
    text_position = jnp.where((lane >= half) == (core == 0), half, 0) + lane % half
    group = max(1, 512 // part_rows)
    rows = group * part_rows
    each = devices // group // calls
    for step in range(devices // group):
        sum_ref, norm_ref = images[2 * (step // each)], images[2 * (step // each) + 1]
        span = slice(step % each * rows, (step % each + 1) * rows)
        queries = packed_ref[step * group : (step + 1) * group, 2 * img_dev :, :]
        queries = queries.reshape(rows, HEAD_DIM)
        scores = lax.dot_general(queries, keys, contract, preferred_element_type=jnp.float32) * factor
        scores = jnp.where(text_position < valid, scores, -jnp.inf)
        before = norm_ref[span, 0:1]
        top = jnp.maximum(before, jnp.max(scores, 1, keepdims=True))
        rescale = jnp.exp2(before - top)
        weights = jnp.exp2(scores - top)
        total = norm_ref[span, 64:65] * rescale + jnp.sum(weights, 1, keepdims=True)
        mixed = sum_ref[span, :] * rescale + jnp.dot(
            weights.astype(jnp.bfloat16), values, preferred_element_type=jnp.float32
        )
        mixed = (mixed / total).astype(out_ref.dtype)
        out_ref[step * group : (step + 1) * group, :part_rows, :] = mixed.reshape(group, part_rows, HEAD_DIM)
    low = jnp.where(core == 0, mine.astype(jnp.float32), got.astype(jnp.float32))
    high = jnp.where(core == 0, got.astype(jnp.float32), mine.astype(jnp.float32))
    share = 2 * half // devices
    for device in range(devices):
        source = low if device < devices // 2 else high
        start = device * share % half
        block = source[start : start + share]
        block = jnp.concatenate([block[:, :HEAD_DIM], block[:, HEAD_DIM:]], 0)
        out_ref[device, part_rows:, :] = block.astype(out_ref.dtype)


def finish(place, packed, images, mine, got, img_dev, factor):
    devices, part_rows = packed.shape[0], packed.shape[1] - 2 * img_dev
    share = 2 * mine.shape[0] // devices
    count = devices * part_rows
    return pl.pallas_call(
        functools.partial(finish_kernel, factor, len(images) // 2, img_dev),
        out_shape=jax.ShapeDtypeStruct((devices, part_rows + 2 * share, HEAD_DIM), jnp.bfloat16),
        in_specs=[SMEM_SPEC] + [VMEM_SPEC] * (len(images) + 3),
        out_specs=VMEM_SPEC,
        compiler_params=params(16),
        cost_estimate=pl.CostEstimate(
            flops=4 * count * 2 * mine.shape[0] * HEAD_DIM,
            bytes_accessed=12 * count * HEAD_DIM,
            transcendentals=count * 2 * mine.shape[0],
        ),
        name="finish",
    )(place, packed, *images, mine, got)


def add(one, other, dtype):
    return (one.astype(jnp.float32) + other.astype(jnp.float32)).astype(dtype)


def local(
    enc_act,
    down_weight,
    norm_gain,
    text_in_weight,
    modulation_weight,
    key_value_weight,
    timesteps,
    lengths,
    image_queries,
    image_key_values,
):
    devices = lax.axis_size("seq")
    chips = devices // 2
    copies = devices // HEADS
    text_len = enc_act.shape[1]
    img_dev = image_queries.shape[1]
    part_rows = img_dev // copies
    factor = math.log2(math.e) / math.sqrt(HEAD_DIM)
    lanes = orders(chips)
    index = lax.axis_index("seq")
    chip, core = index // 2, index % 2
    place = jnp.stack([position(chip, lanes[0]), position(chip, lanes[1]), core, chip, lengths[0]])
    place = place.astype(jnp.int32)

    win0, kv0 = text_in_weight.T, key_value_weight
    mod0 = modulation_weight.transpose(1, 2, 0)
    win1, kv1, mod1 = swap(win0, 1), swap(kv0, 1), swap(mod0, 1)
    time = time_embedding(timesteps)

    rounds = len(lanes[0])
    tie = lax.optimization_barrier

    def exchange(rows):
        return lax.all_to_all(rows, "seq", split_axis=0, concat_axis=0, tiled=True)

    image_key_values, image_queries = tie((image_key_values, image_queries))
    packed = pack(copies, image_queries[0], image_key_values[0, :, 0], image_key_values[0, :, 1])
    act, packed = tie((enc_act[0].T, packed))
    packed = exchange(packed)
    keep, sent = [], []
    encoded = encoder(lanes, place, act, down_weight)
    for own, other in (encoded[:2], encoded[2:]):
        got = swap(other, 1)
        sent.append(add(own[chips // 2 :], got[chips // 2 :], jnp.bfloat16))
        keep.append(add(own[: chips // 2], got[: chips // 2], jnp.float32))
    for step in range(rounds):
        got = [swap(part, 2 * order[step]) for part, order in zip(sent, lanes)]
        if step == 0:
            got, win1, kv1, mod1, packed = tie((got, win1, kv1, mod1, packed))
            lines = modulation(time, mod0, mod1)
        if step == 1:
            got, lines = tie((got, lines))
        half = keep[0].shape[0] // 2
        if half:
            sent = [add(mine[half:], part[half:], jnp.bfloat16) for mine, part in zip(keep, got)]
            keep = [add(mine[:half], part[:half], jnp.float32) for mine, part in zip(keep, got)]
    summed = [add(mine[0], part[0], jnp.float32) for mine, part in zip(keep, got)]

    width = summed[0].shape[1]
    square = sum(jnp.sum(part * part, 1, keepdims=True) for part in summed)
    scale_rows = lax.rsqrt(square / (2 * width) + epsilon)
    gains = norm_gain.astype(jnp.float32)
    states = [
        (part * scale_rows * gains[lane * width : (lane + 1) * width]).astype(jnp.bfloat16)
        for lane, part in enumerate(summed)
    ]
    images = []

    for step in reversed(range(rounds)):
        if step == 0:
            states, packed = tie((states, packed))
            image = image_attention(packed, img_dev, factor, 0, 2)
        got = [swap(state, 2 * order[step]) for state, order in zip(states, lanes)]
        if step:
            states = [jnp.concatenate(pair, 0) for pair in zip(states, got)]
    got, image = tie((got, image))
    images += image
    states = [state for pair in zip(states, got) for state in pair]

    blocks = project(lanes, place, states, lines, win0, win1, kv0, kv1)
    keep, sent = [blocks[0], blocks[2]], [blocks[1], blocks[3]]
    for step in range(rounds):
        if step == 0:
            sent, packed = tie((sent, packed))
            image = image_attention(packed, img_dev, factor, 1, 2)
        got = [swap(part, 2 * order[step]) for part, order in zip(sent, lanes)]
        if step == 0:
            got, image = tie((got, image))
            images += image
        half = keep[0].shape[0] // 2
        if half:
            sent = [add(mine[half:], part[half:], jnp.bfloat16) for mine, part in zip(keep, got)]
            keep = [add(mine[:half], part[:half], jnp.float32) for mine, part in zip(keep, got)]
    parts = [part[0] for pair in zip(keep, got) for part in pair]
    model_width = text_in_weight.shape[1] * devices
    mine, sent = combine(place, parts, chips, text_len // 2, model_width)
    got = swap(sent, 1)

    back = exchange(finish(place, packed, images, mine, got, img_dev, factor))
    attended, text_kv = unpack(copies, part_rows, back)
    return (attended[None], text_kv)


def solution(mesh):
    in_specs = (
        P("dp", None, "seq"),
        P("seq", None),
        P(),
        P(None, "seq"),
        P(None, None, "seq"),
        P("seq", None),
        P("dp"),
        P("dp"),
        P("dp", "seq", None),
        P("dp", "seq", None, None),
    )
    out_specs = (P("dp", "seq", None), P(("dp", "seq"), None))
    return jax.shard_map(local, mesh=mesh, in_specs=in_specs, out_specs=out_specs, check_vma=False)
```

```python
import functools
import math

import jax
import jax.numpy as jnp
from jax import lax
from jax.experimental import pallas as pl
from jax.experimental.pallas import tpu as pltpu
from jax.sharding import PartitionSpec as P

HEAD_DIM = 128
HEADS = 16
TEMB = 256
MIB = 1024 * 1024

epsilon = 1e-06

SMEM_SPEC = pl.BlockSpec(memory_space=pltpu.SMEM)
VMEM_SPEC = pl.BlockSpec(memory_space=pltpu.VMEM)


def params(mib):
    return pltpu.CompilerParams(vmem_limit_bytes=mib * MIB)


def swap(value, mask):
    devices = lax.axis_size("seq")
    return lax.ppermute(value, "seq", [(i, i ^ mask) for i in range(devices)])


def orders(chips):
    bits = [1 << i for i in range(chips.bit_length() - 1)]
    return (bits, [bits[1], bits[0]] + bits[2:])


def position(chip, order):
    last = len(order) - 1
    return sum(((chip >> (bit.bit_length() - 1)) & 1) << (last - i) for i, bit in enumerate(order))


def member(at, order):
    last = len(order) - 1
    return sum(bit for i, bit in enumerate(order) if (at >> (last - i)) & 1)


def normalize(summed, norm_gain):
    scale_rows = lax.rsqrt(jnp.mean(summed * summed, 1, keepdims=True) + epsilon)
    return (summed * scale_rows * norm_gain.astype(jnp.float32)).astype(jnp.bfloat16)


def time_embedding(timesteps):
    half_width = TEMB // 2
    freqs = jnp.exp(-math.log(10000.0) * jnp.arange(half_width, dtype=jnp.float32) / half_width)
    angles = timesteps.astype(jnp.float32)[:, None] * freqs[None, :]
    embedding = jnp.concatenate([jnp.cos(angles), jnp.sin(angles)], 1)
    return jax.nn.silu(embedding).astype(jnp.bfloat16)


def encoder_kernel(lanes, place_ref, act_ref, weight_ref, *refs):
    outs, lhs_ref = refs[:-1], refs[-1]
    chips, share, width = outs[0].shape
    core = place_ref[2]
    half = chips * share
    first = core == 0
    tile = width // 2
    lhs_ref[...] = act_ref[...].T
    for lane, order in enumerate(lanes):
        own_ref, other_ref = outs[2 * lane], outs[2 * lane + 1]
        for column in range(0, width, tile):
            start = lane * width + column
            result = jnp.dot(
                lhs_ref[...], weight_ref[:, start : start + tile], preferred_element_type=jnp.float32
            )
            own = jnp.where(first, result[:half], result[half:]).astype(own_ref.dtype)
            other = jnp.where(first, result[half:], result[:half]).astype(own_ref.dtype)
            own = own.reshape(chips, share, tile)
            other = other.reshape(chips, share, tile)
            for block in range(chips):
                to = place_ref[lane] ^ position(block, order)
                own_ref[to, :, column : column + tile] = own[block]
                other_ref[to, :, column : column + tile] = other[block]


def encoder(lanes, place, act, weight):
    chips = 1 << len(lanes[0])
    depth, rows = act.shape
    width = weight.shape[1]
    out = jax.ShapeDtypeStruct((chips, rows // 2 // chips, width // 2), jnp.bfloat16)
    return pl.pallas_call(
        functools.partial(encoder_kernel, lanes),
        out_shape=(out,) * 4,
        in_specs=[SMEM_SPEC, VMEM_SPEC, VMEM_SPEC],
        out_specs=(VMEM_SPEC,) * 4,
        scratch_shapes=[pltpu.VMEM((rows, depth), jnp.bfloat16)],
        compiler_params=params(24),
        cost_estimate=pl.CostEstimate(
            flops=2 * rows * depth * width,
            bytes_accessed=2 * (depth * rows + depth * width + rows * width),
            transcendentals=0,
        ),
        name="encoder",
    )(place, act, weight)


def modulation_kernel(time_ref, mod0_ref, mod1_ref, out_ref):
    contract = (((1,), (1,)), ((), ()))
    embedding = jnp.broadcast_to(time_ref[...].astype(jnp.float32), (16, time_ref.shape[1]))
    embedding = embedding.astype(jnp.bfloat16)
    row = lax.broadcasted_iota(jnp.int32, (16, mod0_ref.shape[1]), 0)
    for side, mod in enumerate((mod0_ref, mod1_ref)):
        shift, scale = [
            lax.dot_general(embedding, mod[at], contract, preferred_element_type=jnp.float32)
            for at in range(2)
        ]
        lines = jnp.where(row < 2, 1.0 + scale, shift)
        high = lines.astype(jnp.bfloat16).astype(jnp.float32)
        low = jnp.where(row % 2 == 0, high, lines - high)
        out_ref[side] = jnp.where(row < 4, low, 1.0 + scale)


def modulation(time, mod0, mod1):
    return pl.pallas_call(
        modulation_kernel,
        out_shape=jax.ShapeDtypeStruct((2, 16, mod0.shape[1]), jnp.float32),
        in_specs=[VMEM_SPEC] * 3,
        out_specs=VMEM_SPEC,
        compiler_params=params(8),
        name="modulation",
    )(time, mod0, mod1)


def slot_rows(chips, width):
    per_slot = 2 * 128 // width
    return chips * per_slot, -(-(chips * per_slot + 2) // 16) * 16


def project_kernel(lanes, place_ref, *refs):
    pieces, refs = (refs[:2], refs[2:4]), refs[4:]
    lines_ref, win0, win1, kv0, kv1, *outs, states, proj0, proj1, sums = refs
    chip = place_ref[3]
    half_chips = outs[0].shape[0]
    chips = 2 * half_chips
    rows = proj0.shape[0]
    share = rows // chips
    depth = states.shape[1]
    contract = (((1,), (1,)), ((), ()))
    for lane, order in enumerate(lanes):
        top, low = pieces[lane]
        states[: rows // 2, :] = top[...]
        states[rows // 2 :, :] = low[...]
        span = slice(lane * depth, (lane + 1) * depth)
        for win, proj in ((win0, proj0), (win1, proj1)):
            part = lax.dot_general(
                states[...], win[:, span], contract, preferred_element_type=jnp.float32
            )
            for at in range(chips):
                start = pl.multiple_of((chip ^ member(at, order)) * share, share)
                block = part[at * share : (at + 1) * share]
                if lane == 0:
                    proj[pl.ds(start, share), :] = block
                else:
                    proj[pl.ds(start, share), :] += block
    value0, value1 = proj0[...], proj1[...]
    first = jnp.sum(value0, 1, keepdims=True) + jnp.sum(value1, 1, keepdims=True)
    second = jnp.sum(value0 * value0, 1, keepdims=True) + jnp.sum(value1 * value1, 1, keepdims=True)
    lane = lax.broadcasted_iota(jnp.int32, sums.shape, 1)
    sums[...] = jnp.where(lane == 0, first, second).T
    left = []
    for side, value in enumerate((value0, value1)):
        lines = lines_ref[side]
        row = lax.broadcasted_iota(jnp.int32, lines.shape, 0)
        lines, scale = jnp.where(row < 4, lines, 0.0), lines[4:5]
        left.append(jnp.concatenate([value * scale, lines], 0).astype(jnp.bfloat16))
    width = outs[0].shape[2]
    slots, extra = slot_rows(chips, width)
    per_slot = slots // chips
    row = lax.broadcasted_iota(jnp.int32, (extra, width), 0)
    column = lax.broadcasted_iota(jnp.int32, (extra, width), 1)
    half = kv0.shape[1] // 2
    for lane, order in enumerate(lanes):
        line = sums[lane : lane + 1, :]
        high = line.astype(jnp.bfloat16).astype(jnp.float32)
        low = line - high
        if per_slot == 1:
            line = jnp.concatenate([high, low], 1)
        else:
            line = jnp.where(row % 2 == 0, high, low)
        line = jnp.where(row // per_slot == chip, line, 0.0)
        for at in reversed(range(chips)):
            out_ref, to = outs[2 * lane + at // half_chips], at % half_chips
            start = lane * half + (chip ^ member(at, order)) * width
            columns = pl.ds(pl.multiple_of(start, width), width)
            value = jnp.dot(left[0], kv0[:, columns], preferred_element_type=jnp.float32)
            value += jnp.dot(left[1], kv1[:, columns], preferred_element_type=jnp.float32)
            out_ref[to, :rows, :] = value[:rows].astype(out_ref.dtype)
            below = jnp.where(row == slots, value[rows : rows + 1] + value[rows + 1 : rows + 2], line)
            below = jnp.where(
                row == slots + 1, value[rows + 2 : rows + 3] + value[rows + 3 : rows + 4], below
            )
            out_ref[to, rows:, :] = below.astype(out_ref.dtype)


def project(lanes, place, pieces, lines, win0, win1, kv0, kv1):
    chips = 1 << len(lanes[0])
    rows = 2 * pieces[0].shape[0]
    features, depth = win0.shape
    total = kv0.shape[1]
    width = total // 2 // chips
    extra = slot_rows(chips, width)[1]
    out = jax.ShapeDtypeStruct((chips // 2, rows + extra, width), jnp.bfloat16)
    return pl.pallas_call(
        functools.partial(project_kernel, lanes),
        out_shape=(out,) * 4,
        in_specs=[SMEM_SPEC] + [VMEM_SPEC] * 9,
        out_specs=(VMEM_SPEC,) * 4,
        scratch_shapes=[
            pltpu.VMEM((rows, depth // 2), jnp.bfloat16),
            pltpu.VMEM((rows, features), jnp.float32),
            pltpu.VMEM((rows, features), jnp.float32),
            pltpu.VMEM((rows, 128), jnp.float32),
        ],
        compiler_params=params(20),
        cost_estimate=pl.CostEstimate(
            flops=4 * rows * features * (depth + total),
            bytes_accessed=2 * (rows * depth + 2 * features * (depth + total) + rows * total),
            transcendentals=0,
        ),
        name="project",
    )(place, *pieces, lines, win0, win1, kv0, kv1)


def combine_kernel(chips, model_width, place_ref, *refs):
    refs, mine_ref, sent_ref = refs[:4], refs[4], refs[5]
    core = place_ref[2]
    rows = mine_ref.shape[0]
    width = refs[0].shape[1]
    slots = slot_rows(chips, width)[0]
    totals = [
        refs[2 * lane][...].astype(jnp.float32) + refs[2 * lane + 1][...].astype(jnp.float32)
        for lane in range(2)
    ]
    sums = []
    for total in totals:
        line = jnp.sum(total[rows : rows + slots], 0, keepdims=True)
        if width > 128:
            line = line[:, :128] + line[:, 128:]
        sums.append(line)
    mean_val = sums[0] / model_width
    scale = lax.rsqrt(sums[1] / model_width - mean_val * mean_val + epsilon)
    mean_val = jnp.broadcast_to(mean_val, (rows, rows)).T[:, 0:1]
    scale = jnp.broadcast_to(scale, (rows, rows)).T[:, 0:1]
    texts = []
    for total in totals:
        text = (total[:rows] - mean_val * total[rows + slots : rows + slots + 1]) * scale
        texts.append(text + total[rows + slots + 1 : rows + slots + 2])
    for part, text in enumerate(texts):
        span = slice(part * HEAD_DIM, (part + 1) * HEAD_DIM)
        if width > HEAD_DIM:
            low, high = text[:, :HEAD_DIM], text[:, HEAD_DIM:]
            mine_ref[:, span] = jnp.where(core == 0, low, high).astype(mine_ref.dtype)
            sent_ref[:, span] = jnp.where(core == 0, high, low).astype(mine_ref.dtype)
        else:
            mine_ref[:, span] = text.astype(mine_ref.dtype)
            sent_ref[:, span] = text.astype(mine_ref.dtype)


def combine(place, parts, chips, rows, model_width):
    out = jax.ShapeDtypeStruct((rows, 2 * HEAD_DIM), jnp.bfloat16)
    return pl.pallas_call(
        functools.partial(combine_kernel, chips, model_width),
        out_shape=(out, out),
        in_specs=[SMEM_SPEC] + [VMEM_SPEC] * 4,
        out_specs=(VMEM_SPEC, VMEM_SPEC),
        compiler_params=params(8),
        cost_estimate=pl.CostEstimate(
            flops=8 * rows * 512, bytes_accessed=12 * rows * 512, transcendentals=0
        ),
        name="combine",
    )(place, *parts)


def pack_kernel(copies, place_ref, queries_ref, keys_ref, values_ref, *outs):
    chip, core = place_ref[3], place_ref[2]
    img_dev = keys_ref.shape[0]
    part_rows = img_dev // copies
    for mask, out_ref in enumerate(outs):
        for side in range(2):
            device = 2 * (chip ^ mask) + (core ^ side)
            head, copy = device // copies, device % copies
            span = pl.ds(pl.multiple_of(head * HEAD_DIM, HEAD_DIM), HEAD_DIM)
            rows = pl.ds(pl.multiple_of(copy * part_rows, part_rows), part_rows)
            out_ref[side, :img_dev, :] = keys_ref[:, span]
            out_ref[side, img_dev : 2 * img_dev, :] = values_ref[:, span]
            out_ref[side, 2 * img_dev :, :] = queries_ref[rows, span]


def pack(chips, copies, place, queries, keys, values):
    img_dev = keys.shape[0]
    rows = 2 * img_dev + img_dev // copies
    out = jax.ShapeDtypeStruct((2, rows, HEAD_DIM), jnp.bfloat16)
    return pl.pallas_call(
        functools.partial(pack_kernel, copies),
        out_shape=(out,) * chips,
        in_specs=[SMEM_SPEC] + [VMEM_SPEC] * 3,
        out_specs=(VMEM_SPEC,) * chips,
        compiler_params=params(8),
        cost_estimate=pl.CostEstimate(
            flops=0, bytes_accessed=8 * chips * rows * HEAD_DIM, transcendentals=0
        ),
        name="pack",
    )(place, queries, keys, values)


def gather_kernel(*refs):
    for at, piece in enumerate(refs[:-1]):
        refs[-1][at] = piece[1]


def gather_other(pieces):
    shape = (len(pieces),) + pieces[0].shape[1:]
    return pl.pallas_call(
        gather_kernel,
        out_shape=jax.ShapeDtypeStruct(shape, pieces[0].dtype),
        in_specs=[VMEM_SPEC] * len(pieces),
        out_specs=VMEM_SPEC,
        compiler_params=params(8),
        cost_estimate=pl.CostEstimate(
            flops=0, bytes_accessed=4 * len(pieces) * pieces[0].size // 2, transcendentals=0
        ),
        name="gather_other",
    )(*pieces)


def by_distance(pieces, early, late, early_ref, late_ref):
    passed = {mask: (early_ref, at) for at, mask in enumerate(early)}
    passed.update({mask: (late_ref, at) for at, mask in enumerate(late)})
    return [block for mask, piece in enumerate(pieces) for block in ((piece, 0), passed[mask])]


def unpack_kernel(copies, part_rows, blocks_ref, attended_ref, text_ref):
    share = text_ref.shape[0]
    half = text_ref.shape[1] // 2
    for device in range(blocks_ref.shape[0]):
        head, copy = device // copies, device % copies
        start = head * HEAD_DIM
        rows = slice(copy * part_rows, (copy + 1) * part_rows)
        attended_ref[rows, start : start + HEAD_DIM] = blocks_ref[device, :part_rows, :]
        if copy == 0:
            block = blocks_ref[device, part_rows:, :].astype(jnp.float32)
            text_ref[:, start : start + HEAD_DIM] = block[:share].astype(text_ref.dtype)
            start += half
            text_ref[:, start : start + HEAD_DIM] = block[share:].astype(text_ref.dtype)


def unpack(copies, part_rows, blocks):
    share = (blocks.shape[1] - part_rows) // 2
    return pl.pallas_call(
        functools.partial(unpack_kernel, copies, part_rows),
        out_shape=(
            jax.ShapeDtypeStruct((part_rows * copies, HEADS * HEAD_DIM), jnp.bfloat16),
            jax.ShapeDtypeStruct((share, 2 * HEADS * HEAD_DIM), jnp.bfloat16),
        ),
        in_specs=[VMEM_SPEC],
        out_specs=(VMEM_SPEC, VMEM_SPEC),
        compiler_params=params(8),
        name="unpack",
    )(blocks)


def image_kernel(factor, call, early, late, img_dev, *refs):
    *pieces, early_ref, late_ref, sum_ref, top_ref, keys_ref, values_ref = refs
    blocks = by_distance(pieces, early, late, early_ref, late_ref)
    values_ref[:, HEAD_DIM:] = jnp.ones((values_ref.shape[0], HEAD_DIM), values_ref.dtype)
    for at, (piece, side) in enumerate(blocks):
        rows = slice(at * img_dev, (at + 1) * img_dev)
        keys_ref[rows, :] = piece[side, :img_dev, :]
        values_ref[rows, :HEAD_DIM] = piece[side, img_dev : 2 * img_dev, :]
    part_rows = pieces[0].shape[1] - 2 * img_dev
    group = max(1, 256 // part_rows)
    rows = group * part_rows
    contract = (((1,), (1,)), ((), ()))
    steps = sum_ref.shape[0] // rows
    for step in range(steps):
        at = (call * steps + step) * group
        span = slice(step * rows, (step + 1) * rows)
        queries = [piece[side, 2 * img_dev :, :] for piece, side in blocks[at : at + group]]
        queries = jnp.concatenate(queries, 0)
        scores = lax.dot_general(queries, keys_ref[...], contract, preferred_element_type=jnp.float32)
        scores = scores * factor
        top = jnp.max(scores, 1, keepdims=True)
        weights = jnp.exp2(scores - top).astype(jnp.bfloat16)
        sum_ref[span, :] = jnp.dot(weights, values_ref[...], preferred_element_type=jnp.float32)
        top_ref[span, :] = jnp.broadcast_to(top, (rows, HEAD_DIM))


def image_attention(pieces, passed, early, late, img_dev, factor, call, calls):
    devices = 2 * len(pieces)
    keys = devices * img_dev
    count = devices * (pieces[0].shape[1] - 2 * img_dev) // calls
    return pl.pallas_call(
        functools.partial(image_kernel, factor, call, early, late, img_dev),
        out_shape=(
            jax.ShapeDtypeStruct((count, 2 * HEAD_DIM), jnp.float32),
            jax.ShapeDtypeStruct((count, HEAD_DIM), jnp.float32),
        ),
        in_specs=[VMEM_SPEC] * (len(pieces) + 2),
        out_specs=(VMEM_SPEC, VMEM_SPEC),
        scratch_shapes=[
            pltpu.VMEM((keys, HEAD_DIM), jnp.bfloat16),
            pltpu.VMEM((keys, 2 * HEAD_DIM), jnp.bfloat16),
        ],
        compiler_params=params(24),
        cost_estimate=pl.CostEstimate(
            flops=4 * count * keys * HEAD_DIM,
            bytes_accessed=4 * keys * HEAD_DIM + 10 * count * HEAD_DIM,
            transcendentals=count * keys,
        ),
        name="image_attention",
    )(*pieces, *passed)


def finish_kernel(factor, calls, early, late, img_dev, place_ref, *refs):
    *pieces, early_ref, late_ref = refs[: -3 - 2 * calls]
    images, (mine_ref, got_ref, out_ref) = refs[-3 - 2 * calls : -3], refs[-3:]
    blocks = by_distance(pieces, early, late, early_ref, late_ref)
    core, valid = place_ref[2], place_ref[4]
    me = 2 * place_ref[3] + core
    devices, part_rows = len(blocks), pieces[0].shape[1] - 2 * img_dev
    half = mine_ref.shape[0]
    contract = (((1,), (1,)), ((), ()))
    mine, got = mine_ref[...], got_ref[...]
    keys = jnp.concatenate([mine[:, :HEAD_DIM], got[:, :HEAD_DIM]], 0)
    values = jnp.concatenate([mine[:, HEAD_DIM:], got[:, HEAD_DIM:]], 0)
    values = jnp.concatenate([values, jnp.ones(values.shape, values.dtype)], 1)
    lane = lax.broadcasted_iota(jnp.int32, (1, 2 * half), 1)
    text_position = jnp.where((lane >= half) == (core == 0), half, 0) + lane % half
    bias = jnp.where(text_position < valid, 0.0, -jnp.inf)
    group = max(1, 512 // part_rows)
    rows = group * part_rows
    each = devices // group // calls
    for step in range(devices // group):
        sum_ref, top_ref = images[2 * (step // each)], images[2 * (step // each) + 1]
        span = slice(step % each * rows, (step % each + 1) * rows)
        queries = blocks[step * group : (step + 1) * group]
        queries = jnp.concatenate([piece[side, 2 * img_dev :, :] for piece, side in queries], 0)
        scores = lax.dot_general(queries, keys, contract, preferred_element_type=jnp.float32)
        scores = scores * factor + bias
        before = top_ref[span, :]
        top = jnp.maximum(before, jnp.max(scores, 1, keepdims=True))
        rescale = jnp.exp2(before - top)
        weights = jnp.exp2(scores - jnp.concatenate([top] * (2 * half // HEAD_DIM), 1))
        total = jnp.dot(weights.astype(jnp.bfloat16), values, preferred_element_type=jnp.float32)
        mixed = sum_ref[span, :HEAD_DIM] * rescale + total[:, :HEAD_DIM]
        total = sum_ref[span, HEAD_DIM:] * rescale + total[:, HEAD_DIM:]
        mixed = (mixed / total).astype(out_ref.dtype)
        for at in range(group):
            to = me ^ (step * group + at)
            out_ref[to, :part_rows, :] = mixed[at * part_rows : (at + 1) * part_rows]
    low = jnp.where(core == 0, mine.astype(jnp.float32), got.astype(jnp.float32))
    high = jnp.where(core == 0, got.astype(jnp.float32), mine.astype(jnp.float32))
    share = 2 * half // devices
    for device in range(devices):
        source = low if device < devices // 2 else high
        start = device * share % half
        block = source[start : start + share]
        block = jnp.concatenate([block[:, :HEAD_DIM], block[:, HEAD_DIM:]], 0)
        out_ref[device, part_rows:, :] = block.astype(out_ref.dtype)


def finish(place, pieces, passed, early, late, images, mine, got, img_dev, factor):
    devices, part_rows = 2 * len(pieces), pieces[0].shape[1] - 2 * img_dev
    share = 2 * mine.shape[0] // devices
    count = devices * part_rows
    return pl.pallas_call(
        functools.partial(finish_kernel, factor, len(images) // 2, early, late, img_dev),
        out_shape=jax.ShapeDtypeStruct((devices, part_rows + 2 * share, HEAD_DIM), jnp.bfloat16),
        in_specs=[SMEM_SPEC] + [VMEM_SPEC] * (len(pieces) + len(images) + 4),
        out_specs=VMEM_SPEC,
        compiler_params=params(16),
        cost_estimate=pl.CostEstimate(
            flops=4 * count * 2 * mine.shape[0] * HEAD_DIM,
            bytes_accessed=12 * count * HEAD_DIM,
            transcendentals=count * 2 * mine.shape[0],
        ),
        name="finish",
    )(place, *pieces, *passed, *images, mine, got)


def add(one, other, dtype):
    return (one.astype(jnp.float32) + other.astype(jnp.float32)).astype(dtype)


def local(
    enc_act,
    down_weight,
    norm_gain,
    text_in_weight,
    modulation_weight,
    key_value_weight,
    timesteps,
    lengths,
    image_queries,
    image_key_values,
):
    devices = lax.axis_size("seq")
    chips = devices // 2
    copies = devices // HEADS
    text_len = enc_act.shape[1]
    img_dev = image_queries.shape[1]
    part_rows = img_dev // copies
    factor = math.log2(math.e) / math.sqrt(HEAD_DIM)
    lanes = orders(chips)
    index = lax.axis_index("seq")
    chip, core = index // 2, index % 2
    place = jnp.stack([position(chip, lanes[0]), position(chip, lanes[1]), core, chip, lengths[0]])
    place = place.astype(jnp.int32)

    win0, kv0 = text_in_weight.T, key_value_weight
    mod0 = modulation_weight.transpose(1, 2, 0)
    win1, kv1, mod1 = swap(win0, 1), swap(kv0, 1), swap(mod0, 1)
    time = time_embedding(timesteps)

    rounds = len(lanes[0])
    tie = lax.optimization_barrier

    def exchange(rows):
        return lax.all_to_all(rows, "seq", split_axis=0, concat_axis=0, tiled=True)

    image_key_values, image_queries = tie((image_key_values, image_queries))
    pieces = pack(
        chips, copies, place, image_queries[0], image_key_values[0, :, 0], image_key_values[0, :, 1]
    )
    pieces = list(pieces)
    act, pieces = tie((enc_act[0].T, pieces))
    late = [6, 7]
    early = [mask for mask in range(chips) if mask not in late]

    def send_piece(mask, chain):
        chain, piece = tie((chain, pieces[mask]))
        pieces[mask] = swap(piece, 2 * mask)
        return chain

    def take_pieces(masks, chain):
        chain, taken = tie((chain, [pieces[mask] for mask in masks]))
        for mask, piece in zip(masks, taken):
            pieces[mask] = piece
        return chain

    first, second = [4, 1, 2], [mask for mask in early if mask in (3, 5) or mask > 7]
    for mask in first:
        act = send_piece(mask, act)
    keep, sent = [], []
    encoded = list(encoder(lanes, place, act, down_weight))
    encoded[1::2] = take_pieces(first[:2], encoded[1::2])
    for mask in second:
        encoded = send_piece(mask, encoded)
    for own, other in (encoded[:2], encoded[2:]):
        got = swap(other, 1)
        sent.append(add(own[chips // 2 :], got[chips // 2 :], jnp.bfloat16))
        keep.append(add(own[: chips // 2], got[: chips // 2], jnp.float32))
    sent = take_pieces(first[2:], sent)
    for step in range(rounds):
        got = [swap(part, 2 * order[step]) for part, order in zip(sent, lanes)]
        if step == 0:
            got = take_pieces(second, got)
        if step == 1:
            passed_early = gather_other([pieces[mask] for mask in early])
        if step == 2:
            got, win1, kv1, mod1 = tie((got, win1, kv1, mod1))
            lines = modulation(time, mod0, mod1)
        half = keep[0].shape[0] // 2
        if half:
            sent = [add(mine[half:], part[half:], jnp.bfloat16) for mine, part in zip(keep, got)]
            keep = [add(mine[:half], part[:half], jnp.float32) for mine, part in zip(keep, got)]
    summed = [add(mine[0], part[0], jnp.float32) for mine, part in zip(keep, got)]

    width = summed[0].shape[1]
    square = sum(jnp.sum(part * part, 1, keepdims=True) for part in summed)
    scale_rows = lax.rsqrt(square / (2 * width) + epsilon)
    gains = norm_gain.astype(jnp.float32)
    states = [
        (part * scale_rows * gains[lane * width : (lane + 1) * width]).astype(jnp.bfloat16)
        for lane, part in enumerate(summed)
    ]
    images = []

    for step in reversed(range(rounds)):
        if step < 2:
            states = send_piece(late[1 - step], states)
        got = [swap(state, 2 * order[step]) for state, order in zip(states, lanes)]
        if step == rounds - 1:
            passed_early = swap(passed_early, 1)
            got, lines = tie((got, lines))
        if step == rounds - 2:
            got, passed_early = tie((got, passed_early))
        if step:
            states = [jnp.concatenate(pair, 0) for pair in zip(states, got)]
    got = take_pieces(late[:1], got)
    states = [state for pair in zip(states, got) for state in pair]

    blocks = project(lanes, place, states, lines, win0, win1, kv0, kv1)
    keep, sent = [blocks[0], blocks[2]], [blocks[1], blocks[3]]
    for step in range(rounds):
        got = [swap(part, 2 * order[step]) for part, order in zip(sent, lanes)]
        if step == 0:
            passed_late = swap(gather_other([pieces[mask] for mask in late]), 1)
            got, passed_late = tie((got, passed_late))
            passed = (passed_early, passed_late)
        elif step <= 2:
            sent, passed = tie((sent, passed))
            image = image_attention(pieces, passed, early, late, img_dev, factor, step - 1, 2)
            got, image = tie((got, image))
            images += image
        half = keep[0].shape[0] // 2
        if half:
            sent = [add(mine[half:], part[half:], jnp.bfloat16) for mine, part in zip(keep, got)]
            keep = [add(mine[:half], part[:half], jnp.float32) for mine, part in zip(keep, got)]
    parts = [part[0] for pair in zip(keep, got) for part in pair]
    model_width = text_in_weight.shape[1] * devices
    mine, sent = combine(place, parts, chips, text_len // 2, model_width)
    got = swap(sent, 1)

    back = exchange(finish(place, pieces, passed, early, late, images, mine, got, img_dev, factor))
    attended, text_kv = unpack(copies, part_rows, back)
    return (attended[None], text_kv)


def solution(mesh):
    in_specs = (
        P("dp", None, "seq"),
        P("seq", None),
        P(),
        P(None, "seq"),
        P(None, None, "seq"),
        P("seq", None),
        P("dp"),
        P("dp"),
        P("dp", "seq", None),
        P("dp", "seq", None, None),
    )
    out_specs = (P("dp", "seq", None), P(("dp", "seq"), None))
    return jax.shard_map(local, mesh=mesh, in_specs=in_specs, out_specs=out_specs, check_vma=False)
```

```python
import functools
import math

import jax
import jax.numpy as jnp
from jax import lax
from jax.experimental import pallas as pl
from jax.experimental.pallas import tpu as pltpu
from jax.sharding import PartitionSpec as P

HEAD_DIM = 128
HEADS = 16
TEMB = 256
MIB = 1024 * 1024

epsilon = 1e-06

SMEM_SPEC = pl.BlockSpec(memory_space=pltpu.SMEM)
VMEM_SPEC = pl.BlockSpec(memory_space=pltpu.VMEM)


def params(mib):
    return pltpu.CompilerParams(vmem_limit_bytes=mib * MIB)


def swap(value, mask):
    devices = lax.axis_size("seq")
    return lax.ppermute(value, "seq", [(i, i ^ mask) for i in range(devices)])


def orders(chips):
    bits = [1 << i for i in range(chips.bit_length() - 1)]
    return (bits, [bits[1], bits[0]] + bits[2:])


def position(chip, order):
    last = len(order) - 1
    return sum(((chip >> (bit.bit_length() - 1)) & 1) << (last - i) for i, bit in enumerate(order))


def member(at, order):
    last = len(order) - 1
    return sum(bit for i, bit in enumerate(order) if (at >> (last - i)) & 1)


def normalize(summed, norm_gain):
    scale_rows = lax.rsqrt(jnp.mean(summed * summed, 1, keepdims=True) + epsilon)
    return (summed * scale_rows * norm_gain.astype(jnp.float32)).astype(jnp.bfloat16)


def time_embedding(timesteps):
    half_width = TEMB // 2
    freqs = jnp.exp(-math.log(10000.0) * jnp.arange(half_width, dtype=jnp.float32) / half_width)
    angles = timesteps.astype(jnp.float32)[:, None] * freqs[None, :]
    embedding = jnp.concatenate([jnp.cos(angles), jnp.sin(angles)], 1)
    return jax.nn.silu(embedding).astype(jnp.bfloat16)


def encoder_kernel(lanes, place_ref, act_ref, weight_ref, *refs):
    outs, lhs_ref = refs[:-1], refs[-1]
    chips, share, width = outs[0].shape
    core = place_ref[2]
    half = chips * share
    first = core == 0
    tile = width // 2
    lhs_ref[...] = act_ref[...].T
    for lane, order in enumerate(lanes):
        own_ref, other_ref = outs[2 * lane], outs[2 * lane + 1]
        for column in range(0, width, tile):
            start = lane * width + column
            result = jnp.dot(
                lhs_ref[...], weight_ref[:, start : start + tile], preferred_element_type=jnp.float32
            )
            own = jnp.where(first, result[:half], result[half:]).astype(own_ref.dtype)
            other = jnp.where(first, result[half:], result[:half]).astype(own_ref.dtype)
            own = own.reshape(chips, share, tile)
            other = other.reshape(chips, share, tile)
            for block in range(chips):
                to = place_ref[lane] ^ position(block, order)
                own_ref[to, :, column : column + tile] = own[block]
                other_ref[to, :, column : column + tile] = other[block]


def encoder(lanes, place, act, weight):
    chips = 1 << len(lanes[0])
    depth, rows = act.shape
    width = weight.shape[1]
    out = jax.ShapeDtypeStruct((chips, rows // 2 // chips, width // 2), jnp.bfloat16)
    return pl.pallas_call(
        functools.partial(encoder_kernel, lanes),
        out_shape=(out,) * 4,
        in_specs=[SMEM_SPEC, VMEM_SPEC, VMEM_SPEC],
        out_specs=(VMEM_SPEC,) * 4,
        scratch_shapes=[pltpu.VMEM((rows, depth), jnp.bfloat16)],
        compiler_params=params(24),
        cost_estimate=pl.CostEstimate(
            flops=2 * rows * depth * width,
            bytes_accessed=2 * (depth * rows + depth * width + rows * width),
            transcendentals=0,
        ),
        name="encoder",
    )(place, act, weight)


def modulation_kernel(time_ref, mod0_ref, mod1_ref, out_ref):
    contract = (((1,), (1,)), ((), ()))
    embedding = jnp.broadcast_to(time_ref[...].astype(jnp.float32), (16, time_ref.shape[1]))
    embedding = embedding.astype(jnp.bfloat16)
    row = lax.broadcasted_iota(jnp.int32, (16, mod0_ref.shape[1]), 0)
    for side, mod in enumerate((mod0_ref, mod1_ref)):
        shift, scale = [
            lax.dot_general(embedding, mod[at], contract, preferred_element_type=jnp.float32)
            for at in range(2)
        ]
        lines = jnp.where(row < 2, 1.0 + scale, shift)
        high = lines.astype(jnp.bfloat16).astype(jnp.float32)
        low = jnp.where(row % 2 == 0, high, lines - high)
        out_ref[side] = jnp.where(row < 4, low, 1.0 + scale)


def modulation(time, mod0, mod1):
    return pl.pallas_call(
        modulation_kernel,
        out_shape=jax.ShapeDtypeStruct((2, 16, mod0.shape[1]), jnp.float32),
        in_specs=[VMEM_SPEC] * 3,
        out_specs=VMEM_SPEC,
        compiler_params=params(8),
        name="modulation",
    )(time, mod0, mod1)


def slot_rows(chips, width):
    per_slot = 2 * 128 // width
    return chips * per_slot, -(-(chips * per_slot + 2) // 16) * 16


def project_kernel(lanes, place_ref, *refs):
    pieces, refs = (refs[:2], refs[2:4]), refs[4:]
    lines_ref, win0, win1, kv0, kv1, *outs, states, proj0, proj1, sums = refs
    chip = place_ref[3]
    half_chips = outs[0].shape[0]
    chips = 2 * half_chips
    rows = proj0.shape[0]
    share = rows // chips
    depth = states.shape[1]
    contract = (((1,), (1,)), ((), ()))
    for lane, order in enumerate(lanes):
        top, low = pieces[lane]
        states[: rows // 2, :] = top[...]
        states[rows // 2 :, :] = low[...]
        span = slice(lane * depth, (lane + 1) * depth)
        for win, proj in ((win0, proj0), (win1, proj1)):
            part = lax.dot_general(
                states[...], win[:, span], contract, preferred_element_type=jnp.float32
            )
            for at in range(chips):
                start = pl.multiple_of((chip ^ member(at, order)) * share, share)
                block = part[at * share : (at + 1) * share]
                if lane == 0:
                    proj[pl.ds(start, share), :] = block
                else:
                    proj[pl.ds(start, share), :] += block
    value0, value1 = proj0[...], proj1[...]
    first = jnp.sum(value0, 1, keepdims=True) + jnp.sum(value1, 1, keepdims=True)
    second = jnp.sum(value0 * value0, 1, keepdims=True) + jnp.sum(value1 * value1, 1, keepdims=True)
    lane = lax.broadcasted_iota(jnp.int32, sums.shape, 1)
    sums[...] = jnp.where(lane == 0, first, second).T
    left = []
    for side, value in enumerate((value0, value1)):
        lines = lines_ref[side]
        row = lax.broadcasted_iota(jnp.int32, lines.shape, 0)
        lines, scale = jnp.where(row < 4, lines, 0.0), lines[4:5]
        left.append(jnp.concatenate([value * scale, lines], 0).astype(jnp.bfloat16))
    width = outs[0].shape[2]
    slots, extra = slot_rows(chips, width)
    per_slot = slots // chips
    row = lax.broadcasted_iota(jnp.int32, (extra, width), 0)
    column = lax.broadcasted_iota(jnp.int32, (extra, width), 1)
    half = kv0.shape[1] // 2
    for lane, order in enumerate(lanes):
        line = sums[lane : lane + 1, :]
        high = line.astype(jnp.bfloat16).astype(jnp.float32)
        low = line - high
        if per_slot == 1:
            line = jnp.concatenate([high, low], 1)
        else:
            line = jnp.where(row % 2 == 0, high, low)
        line = jnp.where(row // per_slot == chip, line, 0.0)
        for at in reversed(range(chips)):
            out_ref, to = outs[2 * lane + at // half_chips], at % half_chips
            start = lane * half + (chip ^ member(at, order)) * width
            columns = pl.ds(pl.multiple_of(start, width), width)
            value = jnp.dot(left[0], kv0[:, columns], preferred_element_type=jnp.float32)
            value += jnp.dot(left[1], kv1[:, columns], preferred_element_type=jnp.float32)
            out_ref[to, :rows, :] = value[:rows].astype(out_ref.dtype)
            below = jnp.where(row == slots, value[rows : rows + 1] + value[rows + 1 : rows + 2], line)
            below = jnp.where(
                row == slots + 1, value[rows + 2 : rows + 3] + value[rows + 3 : rows + 4], below
            )
            out_ref[to, rows:, :] = below.astype(out_ref.dtype)


def project(lanes, place, pieces, lines, win0, win1, kv0, kv1):
    chips = 1 << len(lanes[0])
    rows = 2 * pieces[0].shape[0]
    features, depth = win0.shape
    total = kv0.shape[1]
    width = total // 2 // chips
    extra = slot_rows(chips, width)[1]
    out = jax.ShapeDtypeStruct((chips // 2, rows + extra, width), jnp.bfloat16)
    return pl.pallas_call(
        functools.partial(project_kernel, lanes),
        out_shape=(out,) * 4,
        in_specs=[SMEM_SPEC] + [VMEM_SPEC] * 9,
        out_specs=(VMEM_SPEC,) * 4,
        scratch_shapes=[
            pltpu.VMEM((rows, depth // 2), jnp.bfloat16),
            pltpu.VMEM((rows, features), jnp.float32),
            pltpu.VMEM((rows, features), jnp.float32),
            pltpu.VMEM((rows, 128), jnp.float32),
        ],
        compiler_params=params(20),
        cost_estimate=pl.CostEstimate(
            flops=4 * rows * features * (depth + total),
            bytes_accessed=2 * (rows * depth + 2 * features * (depth + total) + rows * total),
            transcendentals=0,
        ),
        name="project",
    )(place, *pieces, lines, win0, win1, kv0, kv1)


def combine_kernel(chips, model_width, place_ref, *refs):
    refs, mine_ref, sent_ref = refs[:4], refs[4], refs[5]
    core = place_ref[2]
    rows = mine_ref.shape[0]
    width = refs[0].shape[1]
    slots = slot_rows(chips, width)[0]
    totals = [
        refs[2 * lane][...].astype(jnp.float32) + refs[2 * lane + 1][...].astype(jnp.float32)
        for lane in range(2)
    ]
    sums = []
    for total in totals:
        line = jnp.sum(total[rows : rows + slots], 0, keepdims=True)
        if width > 128:
            line = line[:, :128] + line[:, 128:]
        sums.append(line)
    mean_val = sums[0] / model_width
    scale = lax.rsqrt(sums[1] / model_width - mean_val * mean_val + epsilon)
    mean_val = jnp.broadcast_to(mean_val, (rows, rows)).T[:, 0:1]
    scale = jnp.broadcast_to(scale, (rows, rows)).T[:, 0:1]
    texts = []
    for total in totals:
        text = (total[:rows] - mean_val * total[rows + slots : rows + slots + 1]) * scale
        texts.append(text + total[rows + slots + 1 : rows + slots + 2])
    for part, text in enumerate(texts):
        span = slice(part * HEAD_DIM, (part + 1) * HEAD_DIM)
        if width > HEAD_DIM:
            low, high = text[:, :HEAD_DIM], text[:, HEAD_DIM:]
            mine_ref[:, span] = jnp.where(core == 0, low, high).astype(mine_ref.dtype)
            sent_ref[:, span] = jnp.where(core == 0, high, low).astype(mine_ref.dtype)
        else:
            mine_ref[:, span] = text.astype(mine_ref.dtype)
            sent_ref[:, span] = text.astype(mine_ref.dtype)


def combine(place, parts, chips, rows, model_width):
    out = jax.ShapeDtypeStruct((rows, 2 * HEAD_DIM), jnp.bfloat16)
    return pl.pallas_call(
        functools.partial(combine_kernel, chips, model_width),
        out_shape=(out, out),
        in_specs=[SMEM_SPEC] + [VMEM_SPEC] * 4,
        out_specs=(VMEM_SPEC, VMEM_SPEC),
        compiler_params=params(8),
        cost_estimate=pl.CostEstimate(
            flops=8 * rows * 512, bytes_accessed=12 * rows * 512, transcendentals=0
        ),
        name="combine",
    )(place, *parts)


def pack_kernel(copies, place_ref, queries_ref, keys_ref, values_ref, out_ref):
    chip, core = place_ref[3], place_ref[2]
    img_dev = keys_ref.shape[0]
    part_rows = img_dev // copies
    half_chips = out_ref.shape[1]
    for top in range(2):
        for mask in range(half_chips):
            for side in range(2):
                device = 2 * (top * half_chips + (chip % half_chips) ^ mask) + (core ^ side)
                head, copy = device // copies, device % copies
                span = pl.ds(pl.multiple_of(head * HEAD_DIM, HEAD_DIM), HEAD_DIM)
                rows = pl.ds(pl.multiple_of(copy * part_rows, part_rows), part_rows)
                out_ref[top, mask, side, :img_dev, :] = keys_ref[:, span]
                out_ref[top, mask, side, img_dev : 2 * img_dev, :] = values_ref[:, span]
                out_ref[top, mask, side, 2 * img_dev :, :] = queries_ref[rows, span]


def pack(chips, copies, place, queries, keys, values):
    img_dev = keys.shape[0]
    shape = (2, chips // 2, 2, 2 * img_dev + img_dev // copies, HEAD_DIM)
    return pl.pallas_call(
        functools.partial(pack_kernel, copies),
        out_shape=jax.ShapeDtypeStruct(shape, jnp.bfloat16),
        in_specs=[SMEM_SPEC] + [VMEM_SPEC] * 3,
        out_specs=VMEM_SPEC,
        compiler_params=params(8),
        cost_estimate=pl.CostEstimate(
            flops=0, bytes_accessed=4 * math.prod(shape), transcendentals=0
        ),
        name="pack",
    )(place, queries, keys, values)


def gather_kernel(*refs):
    for at, piece in enumerate(refs[:-1]):
        refs[-1][at] = piece[1]


def gather_other(pieces):
    shape = (len(pieces),) + pieces[0].shape[1:]
    return pl.pallas_call(
        gather_kernel,
        out_shape=jax.ShapeDtypeStruct(shape, pieces[0].dtype),
        in_specs=[VMEM_SPEC] * len(pieces),
        out_specs=VMEM_SPEC,
        compiler_params=params(8),
        cost_estimate=pl.CostEstimate(
            flops=0, bytes_accessed=4 * len(pieces) * pieces[0].size // 2, transcendentals=0
        ),
        name="gather_other",
    )(*pieces)


def all_blocks(pieces, passed_ref):
    views = [(piece.at[0], passed_ref.at[at]) for at, piece in enumerate(pieces)]
    return [view for pair in views for view in pair]


def origin(at, count, chip, core):
    half_chips = count // 4
    mask, top, side = at // 4, at // 2 % 2, at % 2
    return 2 * (top * half_chips + (chip % half_chips) ^ mask) + (core ^ side)


def unpack_kernel(copies, part_rows, blocks_ref, attended_ref, text_ref):
    share = text_ref.shape[0]
    half = text_ref.shape[1] // 2
    for device in range(blocks_ref.shape[0]):
        head, copy = device // copies, device % copies
        start = head * HEAD_DIM
        rows = slice(copy * part_rows, (copy + 1) * part_rows)
        attended_ref[rows, start : start + HEAD_DIM] = blocks_ref[device, :part_rows, :]
        if copy == 0:
            block = blocks_ref[device, part_rows:, :].astype(jnp.float32)
            text_ref[:, start : start + HEAD_DIM] = block[:share].astype(text_ref.dtype)
            start += half
            text_ref[:, start : start + HEAD_DIM] = block[share:].astype(text_ref.dtype)


def unpack(copies, part_rows, blocks):
    share = (blocks.shape[1] - part_rows) // 2
    return pl.pallas_call(
        functools.partial(unpack_kernel, copies, part_rows),
        out_shape=(
            jax.ShapeDtypeStruct((part_rows * copies, HEADS * HEAD_DIM), jnp.bfloat16),
            jax.ShapeDtypeStruct((share, 2 * HEADS * HEAD_DIM), jnp.bfloat16),
        ),
        in_specs=[VMEM_SPEC],
        out_specs=(VMEM_SPEC, VMEM_SPEC),
        compiler_params=params(8),
        name="unpack",
    )(blocks)


def image_kernel(factor, call, img_dev, *refs):
    *pieces, passed_ref, sum_ref, top_ref, keys_ref, values_ref = refs
    blocks = all_blocks(pieces, passed_ref)
    values_ref[:, HEAD_DIM:] = jnp.ones((values_ref.shape[0], HEAD_DIM), values_ref.dtype)
    for at, block in enumerate(blocks):
        rows = slice(at * img_dev, (at + 1) * img_dev)
        keys_ref[rows, :] = block[:img_dev, :]
        values_ref[rows, :HEAD_DIM] = block[img_dev : 2 * img_dev, :]
    part_rows = pieces[0].shape[1] - 2 * img_dev
    group = max(1, 256 // part_rows)
    rows = group * part_rows
    contract = (((1,), (1,)), ((), ()))
    steps = sum_ref.shape[0] // rows
    for step in range(steps):
        at = (call * steps + step) * group
        span = slice(step * rows, (step + 1) * rows)
        queries = [block[2 * img_dev :, :] for block in blocks[at : at + group]]
        queries = jnp.concatenate(queries, 0)
        scores = lax.dot_general(queries, keys_ref[...], contract, preferred_element_type=jnp.float32)
        scores = scores * factor
        top = jnp.max(scores, 1, keepdims=True)
        weights = jnp.exp2(scores - top).astype(jnp.bfloat16)
        sum_ref[span, :] = jnp.dot(weights, values_ref[...], preferred_element_type=jnp.float32)
        top_ref[span, :] = jnp.broadcast_to(top, (rows, HEAD_DIM))


def image_attention(pieces, passed, img_dev, factor, call, calls):
    devices = 2 * len(pieces)
    keys = devices * img_dev
    count = devices * (pieces[0].shape[1] - 2 * img_dev) // calls
    return pl.pallas_call(
        functools.partial(image_kernel, factor, call, img_dev),
        out_shape=(
            jax.ShapeDtypeStruct((count, 2 * HEAD_DIM), jnp.float32),
            jax.ShapeDtypeStruct((count, HEAD_DIM), jnp.float32),
        ),
        in_specs=[VMEM_SPEC] * (len(pieces) + 1),
        out_specs=(VMEM_SPEC, VMEM_SPEC),
        scratch_shapes=[
            pltpu.VMEM((keys, HEAD_DIM), jnp.bfloat16),
            pltpu.VMEM((keys, 2 * HEAD_DIM), jnp.bfloat16),
        ],
        compiler_params=params(24),
        cost_estimate=pl.CostEstimate(
            flops=4 * count * keys * HEAD_DIM,
            bytes_accessed=4 * keys * HEAD_DIM + 10 * count * HEAD_DIM,
            transcendentals=count * keys,
        ),
        name="image_attention",
    )(*pieces, passed)


def finish_kernel(factor, calls, img_dev, place_ref, *refs):
    *pieces, passed_ref = refs[: -3 - 2 * calls]
    images, (mine_ref, got_ref, out_ref) = refs[-3 - 2 * calls : -3], refs[-3:]
    blocks = all_blocks(pieces, passed_ref)
    core, valid = place_ref[2], place_ref[4]
    devices, part_rows = len(blocks), pieces[0].shape[1] - 2 * img_dev
    half = mine_ref.shape[0]
    contract = (((1,), (1,)), ((), ()))
    mine, got = mine_ref[...], got_ref[...]
    keys = jnp.concatenate([mine[:, :HEAD_DIM], got[:, :HEAD_DIM]], 0)
    values = jnp.concatenate([mine[:, HEAD_DIM:], got[:, HEAD_DIM:]], 0)
    values = jnp.concatenate([values, jnp.ones(values.shape, values.dtype)], 1)
    lane = lax.broadcasted_iota(jnp.int32, (1, 2 * half), 1)
    text_position = jnp.where((lane >= half) == (core == 0), half, 0) + lane % half
    bias = jnp.where(text_position < valid, 0.0, -jnp.inf)
    group = max(1, 512 // part_rows)
    rows = group * part_rows
    each = devices // group // calls
    for step in range(devices // group):
        sum_ref, top_ref = images[2 * (step // each)], images[2 * (step // each) + 1]
        span = slice(step % each * rows, (step % each + 1) * rows)
        queries = blocks[step * group : (step + 1) * group]
        queries = jnp.concatenate([block[2 * img_dev :, :] for block in queries], 0)
        scores = lax.dot_general(queries, keys, contract, preferred_element_type=jnp.float32)
        scores = scores * factor + bias
        before = top_ref[span, :]
        top = jnp.maximum(before, jnp.max(scores, 1, keepdims=True))
        rescale = jnp.exp2(before - top)
        weights = jnp.exp2(scores - jnp.concatenate([top] * (2 * half // HEAD_DIM), 1))
        total = jnp.dot(weights.astype(jnp.bfloat16), values, preferred_element_type=jnp.float32)
        mixed = sum_ref[span, :HEAD_DIM] * rescale + total[:, :HEAD_DIM]
        total = sum_ref[span, HEAD_DIM:] * rescale + total[:, HEAD_DIM:]
        mixed = (mixed / total).astype(out_ref.dtype)
        for at in range(group):
            to = origin(step * group + at, devices, place_ref[3], core)
            out_ref[to, :part_rows, :] = mixed[at * part_rows : (at + 1) * part_rows]
    low = jnp.where(core == 0, mine.astype(jnp.float32), got.astype(jnp.float32))
    high = jnp.where(core == 0, got.astype(jnp.float32), mine.astype(jnp.float32))
    share = 2 * half // devices
    for device in range(devices):
        source = low if device < devices // 2 else high
        start = device * share % half
        block = source[start : start + share]
        block = jnp.concatenate([block[:, :HEAD_DIM], block[:, HEAD_DIM:]], 0)
        out_ref[device, part_rows:, :] = block.astype(out_ref.dtype)


def finish(place, pieces, passed, images, mine, got, img_dev, factor):
    devices, part_rows = 2 * len(pieces), pieces[0].shape[1] - 2 * img_dev
    share = 2 * mine.shape[0] // devices
    count = devices * part_rows
    return pl.pallas_call(
        functools.partial(finish_kernel, factor, len(images) // 2, img_dev),
        out_shape=jax.ShapeDtypeStruct((devices, part_rows + 2 * share, HEAD_DIM), jnp.bfloat16),
        in_specs=[SMEM_SPEC] + [VMEM_SPEC] * (len(pieces) + len(images) + 3),
        out_specs=VMEM_SPEC,
        compiler_params=params(16),
        cost_estimate=pl.CostEstimate(
            flops=4 * count * 2 * mine.shape[0] * HEAD_DIM,
            bytes_accessed=12 * count * HEAD_DIM,
            transcendentals=count * 2 * mine.shape[0],
        ),
        name="finish",
    )(place, *pieces, passed, *images, mine, got)


def add(one, other, dtype):
    return (one.astype(jnp.float32) + other.astype(jnp.float32)).astype(dtype)


def local(
    enc_act,
    down_weight,
    norm_gain,
    text_in_weight,
    modulation_weight,
    key_value_weight,
    timesteps,
    lengths,
    image_queries,
    image_key_values,
):
    devices = lax.axis_size("seq")
    chips = devices // 2
    copies = devices // HEADS
    text_len = enc_act.shape[1]
    img_dev = image_queries.shape[1]
    part_rows = img_dev // copies
    factor = math.log2(math.e) / math.sqrt(HEAD_DIM)
    lanes = orders(chips)
    index = lax.axis_index("seq")
    chip, core = index // 2, index % 2
    place = jnp.stack([position(chip, lanes[0]), position(chip, lanes[1]), core, chip, lengths[0]])
    place = place.astype(jnp.int32)

    win0, kv0 = text_in_weight.T, key_value_weight
    mod0 = modulation_weight.transpose(1, 2, 0)
    win1, kv1, mod1 = swap(win0, 1), swap(kv0, 1), swap(mod0, 1)
    time = time_embedding(timesteps)

    rounds = len(lanes[0])
    tie = lax.optimization_barrier

    def exchange(rows):
        return lax.all_to_all(rows, "seq", split_axis=0, concat_axis=0, tiled=True)

    image_key_values, image_queries = tie((image_key_values, image_queries))
    packed = pack(
        chips, copies, place, image_queries[0], image_key_values[0, :, 0], image_key_values[0, :, 1]
    )
    half_chips = chips // 2
    pairs = [[i, i + half_chips * 2] for i in range(half_chips * 2)]
    act, packed = tie((enc_act[0].T, packed))
    packed = lax.all_to_all(
        packed, "seq", split_axis=0, concat_axis=0, axis_index_groups=pairs, tiled=True
    )

    def move(chain, array, mask):
        chain, array = tie((chain, array))
        return chain, swap(array, 2 * mask)

    encoded = list(encoder(lanes, place, act, down_weight))
    keep, sent = [], []
    for own, other in (encoded[:2], encoded[2:]):
        got = swap(other, 1)
        sent.append(add(own[chips // 2 :], got[chips // 2 :], jnp.bfloat16))
        keep.append(add(own[: chips // 2], got[: chips // 2], jnp.float32))
    for step in range(rounds):
        got = [swap(part, 2 * order[step]) for part, order in zip(sent, lanes)]
        if step == 0:
            got, win1 = tie((got, win1))
        if step == 1:
            got, kv1, mod1 = tie((got, kv1, mod1))
            lines = modulation(time, mod0, mod1)
        if step == 2:
            got, packed = tie((got, packed))
        half = keep[0].shape[0] // 2
        if half:
            sent = [add(mine[half:], part[half:], jnp.bfloat16) for mine, part in zip(keep, got)]
            keep = [add(mine[:half], part[:half], jnp.float32) for mine, part in zip(keep, got)]
    summed = [add(mine[0], part[0], jnp.float32) for mine, part in zip(keep, got)]
    pieces = {(mask, top): packed[top, mask] for mask in range(half_chips) for top in range(2)}

    width = summed[0].shape[1]
    square = sum(jnp.sum(part * part, 1, keepdims=True) for part in summed)
    scale_rows = lax.rsqrt(square / (2 * width) + epsilon)
    gains = norm_gain.astype(jnp.float32)
    states = [
        (part * scale_rows * gains[lane * width : (lane + 1) * width]).astype(jnp.bfloat16)
        for lane, part in enumerate(summed)
    ]
    images = []

    for step in reversed(range(rounds)):
        if step > 0:
            top = step % 2
            for mask in (1, 2):
                if step > rounds - 3:
                    states, pieces[mask, top] = move(states, pieces[mask, top], mask)
        if step == 0:
            for mask in range(3, half_chips):
                for top in range(2):
                    states, pieces[mask, top] = move(states, pieces[mask, top], mask)
        got = [swap(state, 2 * order[step]) for state, order in zip(states, lanes)]
        if step > rounds - 3 and step > 0:
            got, pieces[1, top], pieces[2, top] = tie((got, pieces[1, top], pieces[2, top]))
        if step == rounds - 1:
            got, lines = tie((got, lines))
        if step == 0:
            for mask in range(3, half_chips):
                got, pieces[mask, 0] = tie((got, pieces[mask, 0]))
        if step:
            states = [jnp.concatenate(pair, 0) for pair in zip(states, got)]
    pieces = [pieces[mask, top] for mask in range(half_chips) for top in range(2)]
    states = [state for pair in zip(states, got) for state in pair]

    blocks = project(lanes, place, states, lines, win0, win1, kv0, kv1)
    blocks, pieces = tie((blocks, pieces))
    keep, sent = [blocks[0], blocks[2]], [blocks[1], blocks[3]]
    for step in range(rounds):
        got = [swap(part, 2 * order[step]) for part, order in zip(sent, lanes)]
        if step == 0:
            passed = swap(gather_other(pieces), 1)
            got, passed = tie((got, passed))
        elif step <= 2:
            sent, passed = tie((sent, passed))
            image = image_attention(pieces, passed, img_dev, factor, step - 1, 2)
            got, image = tie((got, image))
            images += image
        half = keep[0].shape[0] // 2
        if half:
            sent = [add(mine[half:], part[half:], jnp.bfloat16) for mine, part in zip(keep, got)]
            keep = [add(mine[:half], part[:half], jnp.float32) for mine, part in zip(keep, got)]
    parts = [part[0] for pair in zip(keep, got) for part in pair]
    model_width = text_in_weight.shape[1] * devices
    mine, sent = combine(place, parts, chips, text_len // 2, model_width)
    got = swap(sent, 1)

    back = exchange(finish(place, pieces, passed, images, mine, got, img_dev, factor))
    attended, text_kv = unpack(copies, part_rows, back)
    return (attended[None], text_kv)


def solution(mesh):
    in_specs = (
        P("dp", None, "seq"),
        P("seq", None),
        P(),
        P(None, "seq"),
        P(None, None, "seq"),
        P("seq", None),
        P("dp"),
        P("dp"),
        P("dp", "seq", None),
        P("dp", "seq", None, None),
    )
    out_specs = (P("dp", "seq", None), P(("dp", "seq"), None))
    return jax.shard_map(local, mesh=mesh, in_specs=in_specs, out_specs=out_specs, check_vma=False)
```

```python
import functools
import math

import jax
import jax.numpy as jnp
from jax import lax
from jax.experimental import pallas as pl
from jax.experimental.pallas import tpu as pltpu
from jax.sharding import PartitionSpec as P

HEAD_DIM = 128
HEADS = 16
TEMB = 256
MIB = 1024 * 1024

epsilon = 1e-06

SMEM_SPEC = pl.BlockSpec(memory_space=pltpu.SMEM)
VMEM_SPEC = pl.BlockSpec(memory_space=pltpu.VMEM)


def params(mib):
    return pltpu.CompilerParams(vmem_limit_bytes=mib * MIB)


def swap(value, mask):
    devices = lax.axis_size("seq")
    return lax.ppermute(value, "seq", [(i, i ^ mask) for i in range(devices)])


def orders(chips):
    bits = [1 << i for i in range(chips.bit_length() - 1)]
    return (bits, [bits[1], bits[0]] + bits[2:])


def position(chip, order):
    last = len(order) - 1
    return sum(((chip >> (bit.bit_length() - 1)) & 1) << (last - i) for i, bit in enumerate(order))


def member(at, order):
    last = len(order) - 1
    return sum(bit for i, bit in enumerate(order) if (at >> (last - i)) & 1)


def normalize(summed, norm_gain):
    scale_rows = lax.rsqrt(jnp.mean(summed * summed, 1, keepdims=True) + epsilon)
    return (summed * scale_rows * norm_gain.astype(jnp.float32)).astype(jnp.bfloat16)


def time_embedding(timesteps):
    half_width = TEMB // 2
    freqs = jnp.exp(-math.log(10000.0) * jnp.arange(half_width, dtype=jnp.float32) / half_width)
    angles = timesteps.astype(jnp.float32)[:, None] * freqs[None, :]
    embedding = jnp.concatenate([jnp.cos(angles), jnp.sin(angles)], 1)
    return jax.nn.silu(embedding).astype(jnp.bfloat16)


def encoder_kernel(lanes, place_ref, act_ref, weight_ref, *refs):
    outs, lhs_ref = refs[:-1], refs[-1]
    chips, share, width = outs[0].shape
    core = place_ref[2]
    half = chips * share
    first = core == 0
    tile = width // 2
    lhs_ref[...] = act_ref[...].T
    for lane, order in enumerate(lanes):
        own_ref, other_ref = outs[2 * lane], outs[2 * lane + 1]
        for column in range(0, width, tile):
            start = lane * width + column
            result = jnp.dot(
                lhs_ref[...], weight_ref[:, start : start + tile], preferred_element_type=jnp.float32
            )
            own = jnp.where(first, result[:half], result[half:]).astype(own_ref.dtype)
            other = jnp.where(first, result[half:], result[:half]).astype(own_ref.dtype)
            own = own.reshape(chips, share, tile)
            other = other.reshape(chips, share, tile)
            for block in range(chips):
                to = place_ref[lane] ^ position(block, order)
                own_ref[to, :, column : column + tile] = own[block]
                other_ref[to, :, column : column + tile] = other[block]


def encoder(lanes, place, act, weight):
    chips = 1 << len(lanes[0])
    depth, rows = act.shape
    width = weight.shape[1]
    out = jax.ShapeDtypeStruct((chips, rows // 2 // chips, width // 2), jnp.bfloat16)
    return pl.pallas_call(
        functools.partial(encoder_kernel, lanes),
        out_shape=(out,) * 4,
        in_specs=[SMEM_SPEC, VMEM_SPEC, VMEM_SPEC],
        out_specs=(VMEM_SPEC,) * 4,
        scratch_shapes=[pltpu.VMEM((rows, depth), jnp.bfloat16)],
        compiler_params=params(24),
        cost_estimate=pl.CostEstimate(
            flops=2 * rows * depth * width,
            bytes_accessed=2 * (depth * rows + depth * width + rows * width),
            transcendentals=0,
        ),
        name="encoder",
    )(place, act, weight)


def modulation_kernel(time_ref, mod0_ref, mod1_ref, out_ref):
    contract = (((1,), (1,)), ((), ()))
    embedding = jnp.broadcast_to(time_ref[...].astype(jnp.float32), (16, time_ref.shape[1]))
    embedding = embedding.astype(jnp.bfloat16)
    row = lax.broadcasted_iota(jnp.int32, (16, mod0_ref.shape[1]), 0)
    for side, mod in enumerate((mod0_ref, mod1_ref)):
        shift, scale = [
            lax.dot_general(embedding, mod[at], contract, preferred_element_type=jnp.float32)
            for at in range(2)
        ]
        lines = jnp.where(row < 2, 1.0 + scale, shift)
        high = lines.astype(jnp.bfloat16).astype(jnp.float32)
        low = jnp.where(row % 2 == 0, high, lines - high)
        out_ref[side] = jnp.where(row < 4, low, 1.0 + scale)


def modulation(time, mod0, mod1):
    return pl.pallas_call(
        modulation_kernel,
        out_shape=jax.ShapeDtypeStruct((2, 16, mod0.shape[1]), jnp.float32),
        in_specs=[VMEM_SPEC] * 3,
        out_specs=VMEM_SPEC,
        compiler_params=params(8),
        name="modulation",
    )(time, mod0, mod1)


def slot_rows(chips, width):
    per_slot = 2 * 128 // width
    return chips * per_slot, -(-(chips * per_slot + 2) // 16) * 16


def project_kernel(lanes, place_ref, *refs):
    pieces, refs = (refs[:2], refs[2:4]), refs[4:]
    lines_ref, win0, win1, kv0, kv1, *outs, states, proj0, proj1, sums = refs
    chip = place_ref[3]
    half_chips = outs[0].shape[0]
    chips = 2 * half_chips
    rows = proj0.shape[0]
    share = rows // chips
    depth = states.shape[1]
    contract = (((1,), (1,)), ((), ()))
    for lane, order in enumerate(lanes):
        top, low = pieces[lane]
        states[: rows // 2, :] = top[...]
        states[rows // 2 :, :] = low[...]
        span = slice(lane * depth, (lane + 1) * depth)
        for win, proj in ((win0, proj0), (win1, proj1)):
            part = lax.dot_general(
                states[...], win[:, span], contract, preferred_element_type=jnp.float32
            )
            for at in range(chips):
                start = pl.multiple_of((chip ^ member(at, order)) * share, share)
                block = part[at * share : (at + 1) * share]
                if lane == 0:
                    proj[pl.ds(start, share), :] = block
                else:
                    proj[pl.ds(start, share), :] += block
    value0, value1 = proj0[...], proj1[...]
    first = jnp.sum(value0, 1, keepdims=True) + jnp.sum(value1, 1, keepdims=True)
    second = jnp.sum(value0 * value0, 1, keepdims=True) + jnp.sum(value1 * value1, 1, keepdims=True)
    lane = lax.broadcasted_iota(jnp.int32, sums.shape, 1)
    sums[...] = jnp.where(lane == 0, first, second).T
    left = []
    for side, value in enumerate((value0, value1)):
        lines = lines_ref[side]
        row = lax.broadcasted_iota(jnp.int32, lines.shape, 0)
        lines, scale = jnp.where(row < 4, lines, 0.0), lines[4:5]
        left.append(jnp.concatenate([value * scale, lines], 0).astype(jnp.bfloat16))
    width = outs[0].shape[2]
    slots, extra = slot_rows(chips, width)
    per_slot = slots // chips
    row = lax.broadcasted_iota(jnp.int32, (extra, width), 0)
    column = lax.broadcasted_iota(jnp.int32, (extra, width), 1)
    half = kv0.shape[1] // 2
    for lane, order in enumerate(lanes):
        line = sums[lane : lane + 1, :]
        high = line.astype(jnp.bfloat16).astype(jnp.float32)
        low = line - high
        if per_slot == 1:
            line = jnp.concatenate([high, low], 1)
        else:
            line = jnp.where(row % 2 == 0, high, low)
        line = jnp.where(row // per_slot == chip, line, 0.0)
        for at in reversed(range(chips)):
            out_ref, to = outs[2 * lane + at // half_chips], at % half_chips
            start = lane * half + (chip ^ member(at, order)) * width
            columns = pl.ds(pl.multiple_of(start, width), width)
            value = jnp.dot(left[0], kv0[:, columns], preferred_element_type=jnp.float32)
            value += jnp.dot(left[1], kv1[:, columns], preferred_element_type=jnp.float32)
            out_ref[to, :rows, :] = value[:rows].astype(out_ref.dtype)
            below = jnp.where(row == slots, value[rows : rows + 1] + value[rows + 1 : rows + 2], line)
            below = jnp.where(
                row == slots + 1, value[rows + 2 : rows + 3] + value[rows + 3 : rows + 4], below
            )
            out_ref[to, rows:, :] = below.astype(out_ref.dtype)


def project(lanes, place, pieces, lines, win0, win1, kv0, kv1):
    chips = 1 << len(lanes[0])
    rows = 2 * pieces[0].shape[0]
    features, depth = win0.shape
    total = kv0.shape[1]
    width = total // 2 // chips
    extra = slot_rows(chips, width)[1]
    out = jax.ShapeDtypeStruct((chips // 2, rows + extra, width), jnp.bfloat16)
    return pl.pallas_call(
        functools.partial(project_kernel, lanes),
        out_shape=(out,) * 4,
        in_specs=[SMEM_SPEC] + [VMEM_SPEC] * 9,
        out_specs=(VMEM_SPEC,) * 4,
        scratch_shapes=[
            pltpu.VMEM((rows, depth // 2), jnp.bfloat16),
            pltpu.VMEM((rows, features), jnp.float32),
            pltpu.VMEM((rows, features), jnp.float32),
            pltpu.VMEM((rows, 128), jnp.float32),
        ],
        compiler_params=params(20),
        cost_estimate=pl.CostEstimate(
            flops=4 * rows * features * (depth + total),
            bytes_accessed=2 * (rows * depth + 2 * features * (depth + total) + rows * total),
            transcendentals=0,
        ),
        name="project",
    )(place, *pieces, lines, win0, win1, kv0, kv1)


def combine_kernel(chips, model_width, place_ref, *refs):
    refs, mine_ref, sent_ref = refs[:4], refs[4], refs[5]
    core = place_ref[2]
    rows = mine_ref.shape[0]
    width = refs[0].shape[1]
    slots = slot_rows(chips, width)[0]
    totals = [
        refs[2 * lane][...].astype(jnp.float32) + refs[2 * lane + 1][...].astype(jnp.float32)
        for lane in range(2)
    ]
    sums = []
    for total in totals:
        line = jnp.sum(total[rows : rows + slots], 0, keepdims=True)
        if width > 128:
            line = line[:, :128] + line[:, 128:]
        sums.append(line)
    mean_val = sums[0] / model_width
    scale = lax.rsqrt(sums[1] / model_width - mean_val * mean_val + epsilon)
    mean_val = jnp.broadcast_to(mean_val, (rows, rows)).T[:, 0:1]
    scale = jnp.broadcast_to(scale, (rows, rows)).T[:, 0:1]
    texts = []
    for total in totals:
        text = (total[:rows] - mean_val * total[rows + slots : rows + slots + 1]) * scale
        texts.append(text + total[rows + slots + 1 : rows + slots + 2])
    for part, text in enumerate(texts):
        span = slice(part * HEAD_DIM, (part + 1) * HEAD_DIM)
        if width > HEAD_DIM:
            low, high = text[:, :HEAD_DIM], text[:, HEAD_DIM:]
            mine_ref[:, span] = jnp.where(core == 0, low, high).astype(mine_ref.dtype)
            sent_ref[:, span] = jnp.where(core == 0, high, low).astype(mine_ref.dtype)
        else:
            mine_ref[:, span] = text.astype(mine_ref.dtype)
            sent_ref[:, span] = text.astype(mine_ref.dtype)


def combine(place, parts, chips, rows, model_width):
    out = jax.ShapeDtypeStruct((rows, 2 * HEAD_DIM), jnp.bfloat16)
    return pl.pallas_call(
        functools.partial(combine_kernel, chips, model_width),
        out_shape=(out, out),
        in_specs=[SMEM_SPEC] + [VMEM_SPEC] * 4,
        out_specs=(VMEM_SPEC, VMEM_SPEC),
        compiler_params=params(8),
        cost_estimate=pl.CostEstimate(
            flops=8 * rows * 512, bytes_accessed=12 * rows * 512, transcendentals=0
        ),
        name="combine",
    )(place, *parts)


def pack_kernel(copies, rows_ref, out_ref):
    count = out_ref.shape[1]
    for device in range(out_ref.shape[0]):
        head, copy = device // copies, device % copies
        span = slice(head * HEAD_DIM, (head + 1) * HEAD_DIM)
        start = copy * count if count < rows_ref.shape[0] else 0
        out_ref[device] = rows_ref[start : start + count, span]


def pack(copies, rows, count):
    return pl.pallas_call(
        functools.partial(pack_kernel, copies),
        out_shape=jax.ShapeDtypeStruct((HEADS * copies, count, HEAD_DIM), jnp.bfloat16),
        in_specs=[VMEM_SPEC],
        out_specs=VMEM_SPEC,
        compiler_params=params(8),
        cost_estimate=pl.CostEstimate(flops=0, bytes_accessed=4 * rows.size, transcendentals=0),
        name="pack",
    )(rows)


def unpack_kernel(copies, part_rows, blocks_ref, attended_ref, text_ref):
    share = text_ref.shape[0]
    half = text_ref.shape[1] // 2
    for device in range(blocks_ref.shape[0]):
        head, copy = device // copies, device % copies
        start = head * HEAD_DIM
        rows = slice(copy * part_rows, (copy + 1) * part_rows)
        attended_ref[rows, start : start + HEAD_DIM] = blocks_ref[device, :part_rows, :]
        if copy == 0:
            block = blocks_ref[device, part_rows:, :].astype(jnp.float32)
            text_ref[:, start : start + HEAD_DIM] = block[:share].astype(text_ref.dtype)
            start += half
            text_ref[:, start : start + HEAD_DIM] = block[share:].astype(text_ref.dtype)


def unpack(copies, part_rows, blocks):
    share = (blocks.shape[1] - part_rows) // 2
    return pl.pallas_call(
        functools.partial(unpack_kernel, copies, part_rows),
        out_shape=(
            jax.ShapeDtypeStruct((part_rows * copies, HEADS * HEAD_DIM), jnp.bfloat16),
            jax.ShapeDtypeStruct((share, 2 * HEADS * HEAD_DIM), jnp.bfloat16),
        ),
        in_specs=[VMEM_SPEC],
        out_specs=(VMEM_SPEC, VMEM_SPEC),
        compiler_params=params(8),
        name="unpack",
    )(blocks)


def image_kernel(factor, call, queries_ref, keys_ref, values_ref, sum_ref, top_ref, wide_ref):
    wide_ref[:, :HEAD_DIM] = values_ref[...]
    wide_ref[:, HEAD_DIM:] = jnp.ones(values_ref.shape, values_ref.dtype)
    rows = 256
    contract = (((1,), (1,)), ((), ()))
    count = sum_ref.shape[0]
    for start in range(0, count, rows):
        span = slice(start, start + rows)
        queries = queries_ref[call * count + start : call * count + start + rows, :]
        scores = lax.dot_general(queries, keys_ref[...], contract, preferred_element_type=jnp.float32)
        scores = scores * factor
        top = jnp.max(scores, 1, keepdims=True)
        weights = jnp.exp2(scores - top).astype(jnp.bfloat16)
        sum_ref[span, :] = jnp.dot(weights, wide_ref[...], preferred_element_type=jnp.float32)
        top_ref[span, :] = jnp.broadcast_to(top, (rows, HEAD_DIM))


def image_attention(queries, keys, values, factor, call, calls):
    count = queries.shape[0] // calls
    total = keys.shape[0]
    return pl.pallas_call(
        functools.partial(image_kernel, factor, call),
        out_shape=(
            jax.ShapeDtypeStruct((count, 2 * HEAD_DIM), jnp.float32),
            jax.ShapeDtypeStruct((count, HEAD_DIM), jnp.float32),
        ),
        in_specs=[VMEM_SPEC] * 3,
        out_specs=(VMEM_SPEC, VMEM_SPEC),
        scratch_shapes=[pltpu.VMEM((total, 2 * HEAD_DIM), jnp.bfloat16)],
        compiler_params=params(24),
        cost_estimate=pl.CostEstimate(
            flops=4 * count * total * HEAD_DIM,
            bytes_accessed=4 * total * HEAD_DIM + 10 * count * HEAD_DIM,
            transcendentals=count * total,
        ),
        name="image_attention",
    )(queries, keys, values)


def finish_kernel(factor, calls, place_ref, queries_ref, *refs):
    images, (mine_ref, got_ref, out_ref) = refs[: 2 * calls], refs[2 * calls :]
    core, valid = place_ref[2], place_ref[4]
    devices = out_ref.shape[0]
    part_rows = queries_ref.shape[0] // devices
    half = mine_ref.shape[0]
    contract = (((1,), (1,)), ((), ()))
    mine, got = mine_ref[...], got_ref[...]
    keys = jnp.concatenate([mine[:, :HEAD_DIM], got[:, :HEAD_DIM]], 0)
    values = jnp.concatenate([mine[:, HEAD_DIM:], got[:, HEAD_DIM:]], 0)
    values = jnp.concatenate([values, jnp.ones(values.shape, values.dtype)], 1)
    lane = lax.broadcasted_iota(jnp.int32, (1, 2 * half), 1)
    text_position = jnp.where((lane >= half) == (core == 0), half, 0) + lane % half
    bias = jnp.where(text_position < valid, 0.0, -jnp.inf)
    group = max(1, 512 // part_rows)
    rows = group * part_rows
    each = devices // group // calls
    for step in range(devices // group):
        sum_ref, top_ref = images[2 * (step // each)], images[2 * (step // each) + 1]
        span = slice(step % each * rows, (step % each + 1) * rows)
        queries = queries_ref[step * rows : (step + 1) * rows, :]
        scores = lax.dot_general(queries, keys, contract, preferred_element_type=jnp.float32)
        scores = scores * factor + bias
        before = top_ref[span, :]
        top = jnp.maximum(before, jnp.max(scores, 1, keepdims=True))
        rescale = jnp.exp2(before - top)
        weights = jnp.exp2(scores - jnp.concatenate([top] * (2 * half // HEAD_DIM), 1))
        total = jnp.dot(weights.astype(jnp.bfloat16), values, preferred_element_type=jnp.float32)
        mixed = sum_ref[span, :HEAD_DIM] * rescale + total[:, :HEAD_DIM]
        total = sum_ref[span, HEAD_DIM:] * rescale + total[:, HEAD_DIM:]
        mixed = (mixed / total).astype(out_ref.dtype)
        out_ref[step * group : (step + 1) * group, :part_rows, :] = mixed.reshape(group, part_rows, HEAD_DIM)
    low = jnp.where(core == 0, mine.astype(jnp.float32), got.astype(jnp.float32))
    high = jnp.where(core == 0, got.astype(jnp.float32), mine.astype(jnp.float32))
    share = 2 * half // devices
    for device in range(devices):
        source = low if device < devices // 2 else high
        start = device * share % half
        block = source[start : start + share]
        block = jnp.concatenate([block[:, :HEAD_DIM], block[:, HEAD_DIM:]], 0)
        out_ref[device, part_rows:, :] = block.astype(out_ref.dtype)


def finish(place, devices, queries, images, mine, got, factor):
    count = queries.shape[0]
    part_rows = count // devices
    share = 2 * mine.shape[0] // devices
    return pl.pallas_call(
        functools.partial(finish_kernel, factor, len(images) // 2),
        out_shape=jax.ShapeDtypeStruct((devices, part_rows + 2 * share, HEAD_DIM), jnp.bfloat16),
        in_specs=[SMEM_SPEC] + [VMEM_SPEC] * (len(images) + 3),
        out_specs=VMEM_SPEC,
        compiler_params=params(16),
        cost_estimate=pl.CostEstimate(
            flops=4 * count * 2 * mine.shape[0] * HEAD_DIM,
            bytes_accessed=12 * count * HEAD_DIM,
            transcendentals=count * 2 * mine.shape[0],
        ),
        name="finish",
    )(place, queries, *images, mine, got)


def add(one, other, dtype):
    return (one.astype(jnp.float32) + other.astype(jnp.float32)).astype(dtype)


def local(
    enc_act,
    down_weight,
    norm_gain,
    text_in_weight,
    modulation_weight,
    key_value_weight,
    timesteps,
    lengths,
    image_queries,
    image_key_values,
):
    devices = lax.axis_size("seq")
    chips = devices // 2
    copies = devices // HEADS
    text_len = enc_act.shape[1]
    img_dev = image_queries.shape[1]
    part_rows = img_dev // copies
    factor = math.log2(math.e) / math.sqrt(HEAD_DIM)
    lanes = orders(chips)
    index = lax.axis_index("seq")
    chip, core = index // 2, index % 2
    place = jnp.stack([position(chip, lanes[0]), position(chip, lanes[1]), core, chip, lengths[0]])
    place = place.astype(jnp.int32)

    win0, kv0 = text_in_weight.T, key_value_weight
    mod0 = modulation_weight.transpose(1, 2, 0)
    win1, kv1, mod1 = swap(win0, 1), swap(kv0, 1), swap(mod0, 1)
    time = time_embedding(timesteps)

    rounds = len(lanes[0])
    tie = lax.optimization_barrier

    def exchange(rows):
        return lax.all_to_all(rows, "seq", split_axis=0, concat_axis=0, tiled=True)

    act, queries = tie((enc_act[0].T, pack(copies, image_queries[0], part_rows)))
    queries = exchange(queries)
    keep, sent = [], []
    encoded = encoder(lanes, place, act, down_weight)
    for own, other in (encoded[:2], encoded[2:]):
        got = swap(other, 1)
        sent.append(add(own[chips // 2 :], got[chips // 2 :], jnp.bfloat16))
        keep.append(add(own[: chips // 2], got[: chips // 2], jnp.float32))
    sent, queries, image_key_values = tie((sent, queries, image_key_values))
    keys = exchange(pack(copies, image_key_values[0, :, 0], img_dev))
    for step in range(rounds):
        got = [swap(part, 2 * order[step]) for part, order in zip(sent, lanes)]
        if step == 0:
            got, win1, kv1, mod1 = tie((got, win1, kv1, mod1))
            lines = modulation(time, mod0, mod1)
        if step == 1:
            got, lines, keys = tie((got, lines, keys))
        half = keep[0].shape[0] // 2
        if half:
            sent = [add(mine[half:], part[half:], jnp.bfloat16) for mine, part in zip(keep, got)]
            keep = [add(mine[:half], part[:half], jnp.float32) for mine, part in zip(keep, got)]
    summed = [add(mine[0], part[0], jnp.float32) for mine, part in zip(keep, got)]

    width = summed[0].shape[1]
    square = sum(jnp.sum(part * part, 1, keepdims=True) for part in summed)
    scale_rows = lax.rsqrt(square / (2 * width) + epsilon)
    gains = norm_gain.astype(jnp.float32)
    states = [
        (part * scale_rows * gains[lane * width : (lane + 1) * width]).astype(jnp.bfloat16)
        for lane, part in enumerate(summed)
    ]
    images = []

    for step in reversed(range(rounds)):
        if step == 0:
            states, image_key_values = tie((states, image_key_values))
            values = exchange(pack(copies, image_key_values[0, :, 1], img_dev))
        got = [swap(state, 2 * order[step]) for state, order in zip(states, lanes)]
        if step:
            states = [jnp.concatenate(pair, 0) for pair in zip(states, got)]
    states = [state for pair in zip(states, got) for state in pair]

    blocks = project(lanes, place, states, lines, win0, win1, kv0, kv1)
    keep, sent = [blocks[0], blocks[2]], [blocks[1], blocks[3]]
    for step in range(rounds):
        got = [swap(part, 2 * order[step]) for part, order in zip(sent, lanes)]
        if step == 0:
            got, values = tie((got, values))
            queries, keys, values = [part.reshape(-1, HEAD_DIM) for part in (queries, keys, values)]
        elif step <= 2:
            sent, queries = tie((sent, queries))
            image = image_attention(queries, keys, values, factor, step - 1, 2)
            got, image = tie((got, image))
            images += image
        half = keep[0].shape[0] // 2
        if half:
            sent = [add(mine[half:], part[half:], jnp.bfloat16) for mine, part in zip(keep, got)]
            keep = [add(mine[:half], part[:half], jnp.float32) for mine, part in zip(keep, got)]
    parts = [part[0] for pair in zip(keep, got) for part in pair]
    model_width = text_in_weight.shape[1] * devices
    mine, sent = combine(place, parts, chips, text_len // 2, model_width)
    got = swap(sent, 1)

    back = exchange(finish(place, devices, queries, images, mine, got, factor))
    attended, text_kv = unpack(copies, part_rows, back)
    return (attended[None], text_kv)


def solution(mesh):
    in_specs = (
        P("dp", None, "seq"),
        P("seq", None),
        P(),
        P(None, "seq"),
        P(None, None, "seq"),
        P("seq", None),
        P("dp"),
        P("dp"),
        P("dp", "seq", None),
        P("dp", "seq", None, None),
    )
    out_specs = (P("dp", "seq", None), P(("dp", "seq"), None))
    return jax.shard_map(local, mesh=mesh, in_specs=in_specs, out_specs=out_specs, check_vma=False)
```

```python
import functools
import math

import jax
import jax.numpy as jnp
from jax import lax
from jax.experimental import pallas as pl
from jax.experimental.pallas import tpu as pltpu
from jax.sharding import PartitionSpec as P

HEAD_DIM = 128
HEADS = 16
TEMB = 256
MIB = 1024 * 1024

epsilon = 1e-06

SMEM_SPEC = pl.BlockSpec(memory_space=pltpu.SMEM)
VMEM_SPEC = pl.BlockSpec(memory_space=pltpu.VMEM)


def params(mib):
    return pltpu.CompilerParams(vmem_limit_bytes=mib * MIB)


def swap(value, mask):
    devices = lax.axis_size("seq")
    return lax.ppermute(value, "seq", [(i, i ^ mask) for i in range(devices)])


def orders(chips):
    bits = [1 << i for i in range(chips.bit_length() - 1)]
    return (bits, [bits[1], bits[0]] + bits[2:])


def position(chip, order):
    last = len(order) - 1
    return sum(((chip >> (bit.bit_length() - 1)) & 1) << (last - i) for i, bit in enumerate(order))


def member(at, order):
    last = len(order) - 1
    return sum(bit for i, bit in enumerate(order) if (at >> (last - i)) & 1)


def normalize(summed, norm_gain):
    scale_rows = lax.rsqrt(jnp.mean(summed * summed, 1, keepdims=True) + epsilon)
    return (summed * scale_rows * norm_gain.astype(jnp.float32)).astype(jnp.bfloat16)


def time_embedding(timesteps):
    half_width = TEMB // 2
    freqs = jnp.exp(-math.log(10000.0) * jnp.arange(half_width, dtype=jnp.float32) / half_width)
    angles = timesteps.astype(jnp.float32)[:, None] * freqs[None, :]
    embedding = jnp.concatenate([jnp.cos(angles), jnp.sin(angles)], 1)
    return jax.nn.silu(embedding).astype(jnp.bfloat16)


def encoder_kernel(lanes, place_ref, act_ref, weight_ref, *refs):
    outs, lhs_ref = refs[:-1], refs[-1]
    chips, share, width = outs[0].shape
    core = place_ref[2]
    half = chips * share
    first = core == 0
    tile = width // 2
    lhs_ref[...] = act_ref[...].T
    for lane, order in enumerate(lanes):
        own_ref, other_ref = outs[2 * lane], outs[2 * lane + 1]
        for column in range(0, width, tile):
            start = lane * width + column
            result = jnp.dot(
                lhs_ref[...], weight_ref[:, start : start + tile], preferred_element_type=jnp.float32
            )
            own = jnp.where(first, result[:half], result[half:]).astype(own_ref.dtype)
            other = jnp.where(first, result[half:], result[:half]).astype(own_ref.dtype)
            own = own.reshape(chips, share, tile)
            other = other.reshape(chips, share, tile)
            for block in range(chips):
                to = place_ref[lane] ^ position(block, order)
                own_ref[to, :, column : column + tile] = own[block]
                other_ref[to, :, column : column + tile] = other[block]


def encoder(lanes, place, act, weight):
    chips = 1 << len(lanes[0])
    depth, rows = act.shape
    width = weight.shape[1]
    out = jax.ShapeDtypeStruct((chips, rows // 2 // chips, width // 2), jnp.bfloat16)
    return pl.pallas_call(
        functools.partial(encoder_kernel, lanes),
        out_shape=(out,) * 4,
        in_specs=[SMEM_SPEC, VMEM_SPEC, VMEM_SPEC],
        out_specs=(VMEM_SPEC,) * 4,
        scratch_shapes=[pltpu.VMEM((rows, depth), jnp.bfloat16)],
        compiler_params=params(24),
        cost_estimate=pl.CostEstimate(
            flops=2 * rows * depth * width,
            bytes_accessed=2 * (depth * rows + depth * width + rows * width),
            transcendentals=0,
        ),
        name="encoder",
    )(place, act, weight)


def modulation_kernel(time_ref, mod0_ref, mod1_ref, out_ref):
    contract = (((1,), (1,)), ((), ()))
    embedding = jnp.broadcast_to(time_ref[...].astype(jnp.float32), (16, time_ref.shape[1]))
    embedding = embedding.astype(jnp.bfloat16)
    row = lax.broadcasted_iota(jnp.int32, (16, mod0_ref.shape[1]), 0)
    for side, mod in enumerate((mod0_ref, mod1_ref)):
        shift, scale = [
            lax.dot_general(embedding, mod[at], contract, preferred_element_type=jnp.float32)
            for at in range(2)
        ]
        lines = jnp.where(row < 2, 1.0 + scale, shift)
        high = lines.astype(jnp.bfloat16).astype(jnp.float32)
        low = jnp.where(row % 2 == 0, high, lines - high)
        out_ref[side] = jnp.where(row < 4, low, 1.0 + scale)


def modulation(time, mod0, mod1):
    return pl.pallas_call(
        modulation_kernel,
        out_shape=jax.ShapeDtypeStruct((2, 16, mod0.shape[1]), jnp.float32),
        in_specs=[VMEM_SPEC] * 3,
        out_specs=VMEM_SPEC,
        compiler_params=params(8),
        name="modulation",
    )(time, mod0, mod1)


def slot_rows(chips, width):
    per_slot = 2 * 128 // width
    return chips * per_slot, -(-(chips * per_slot + 2) // 16) * 16


def project_kernel(lanes, place_ref, *refs):
    pieces, refs = (refs[:2], refs[2:4]), refs[4:]
    lines_ref, win0, win1, kv0, kv1, *outs, states, proj0, proj1, sums = refs
    chip = place_ref[3]
    half_chips = outs[0].shape[0]
    chips = 2 * half_chips
    rows = proj0.shape[0]
    share = rows // chips
    depth = states.shape[1]
    contract = (((1,), (1,)), ((), ()))
    for lane, order in enumerate(lanes):
        top, low = pieces[lane]
        states[: rows // 2, :] = top[...]
        states[rows // 2 :, :] = low[...]
        span = slice(lane * depth, (lane + 1) * depth)
        for win, proj in ((win0, proj0), (win1, proj1)):
            part = lax.dot_general(
                states[...], win[:, span], contract, preferred_element_type=jnp.float32
            )
            for at in range(chips):
                start = pl.multiple_of((chip ^ member(at, order)) * share, share)
                block = part[at * share : (at + 1) * share]
                if lane == 0:
                    proj[pl.ds(start, share), :] = block
                else:
                    proj[pl.ds(start, share), :] += block
    value0, value1 = proj0[...], proj1[...]
    first = jnp.sum(value0, 1, keepdims=True) + jnp.sum(value1, 1, keepdims=True)
    second = jnp.sum(value0 * value0, 1, keepdims=True) + jnp.sum(value1 * value1, 1, keepdims=True)
    lane = lax.broadcasted_iota(jnp.int32, sums.shape, 1)
    sums[...] = jnp.where(lane == 0, first, second).T
    left = []
    for side, value in enumerate((value0, value1)):
        lines = lines_ref[side]
        row = lax.broadcasted_iota(jnp.int32, lines.shape, 0)
        lines, scale = jnp.where(row < 4, lines, 0.0), lines[4:5]
        left.append(jnp.concatenate([value * scale, lines], 0).astype(jnp.bfloat16))
    width = outs[0].shape[2]
    slots, extra = slot_rows(chips, width)
    per_slot = slots // chips
    row = lax.broadcasted_iota(jnp.int32, (extra, width), 0)
    column = lax.broadcasted_iota(jnp.int32, (extra, width), 1)
    half = kv0.shape[1] // 2
    for lane, order in enumerate(lanes):
        line = sums[lane : lane + 1, :]
        high = line.astype(jnp.bfloat16).astype(jnp.float32)
        low = line - high
        if per_slot == 1:
            line = jnp.concatenate([high, low], 1)
        else:
            line = jnp.where(row % 2 == 0, high, low)
        line = jnp.where(row // per_slot == chip, line, 0.0)
        for at in reversed(range(chips)):
            out_ref, to = outs[2 * lane + at // half_chips], at % half_chips
            start = lane * half + (chip ^ member(at, order)) * width
            columns = pl.ds(pl.multiple_of(start, width), width)
            value = jnp.dot(left[0], kv0[:, columns], preferred_element_type=jnp.float32)
            value += jnp.dot(left[1], kv1[:, columns], preferred_element_type=jnp.float32)
            out_ref[to, :rows, :] = value[:rows].astype(out_ref.dtype)
            below = jnp.where(row == slots, value[rows : rows + 1] + value[rows + 1 : rows + 2], line)
            below = jnp.where(
                row == slots + 1, value[rows + 2 : rows + 3] + value[rows + 3 : rows + 4], below
            )
            out_ref[to, rows:, :] = below.astype(out_ref.dtype)


def project(lanes, place, pieces, lines, win0, win1, kv0, kv1):
    chips = 1 << len(lanes[0])
    rows = 2 * pieces[0].shape[0]
    features, depth = win0.shape
    total = kv0.shape[1]
    width = total // 2 // chips
    extra = slot_rows(chips, width)[1]
    out = jax.ShapeDtypeStruct((chips // 2, rows + extra, width), jnp.bfloat16)
    return pl.pallas_call(
        functools.partial(project_kernel, lanes),
        out_shape=(out,) * 4,
        in_specs=[SMEM_SPEC] + [VMEM_SPEC] * 9,
        out_specs=(VMEM_SPEC,) * 4,
        scratch_shapes=[
            pltpu.VMEM((rows, depth // 2), jnp.bfloat16),
            pltpu.VMEM((rows, features), jnp.float32),
            pltpu.VMEM((rows, features), jnp.float32),
            pltpu.VMEM((rows, 128), jnp.float32),
        ],
        compiler_params=params(20),
        cost_estimate=pl.CostEstimate(
            flops=4 * rows * features * (depth + total),
            bytes_accessed=2 * (rows * depth + 2 * features * (depth + total) + rows * total),
            transcendentals=0,
        ),
        name="project",
    )(place, *pieces, lines, win0, win1, kv0, kv1)


def combine_kernel(chips, model_width, place_ref, *refs):
    refs, mine_ref, sent_ref = refs[:4], refs[4], refs[5]
    core = place_ref[2]
    rows = mine_ref.shape[0]
    width = refs[0].shape[1]
    slots = slot_rows(chips, width)[0]
    totals = [
        refs[2 * lane][...].astype(jnp.float32) + refs[2 * lane + 1][...].astype(jnp.float32)
        for lane in range(2)
    ]
    sums = []
    for total in totals:
        line = jnp.sum(total[rows : rows + slots], 0, keepdims=True)
        if width > 128:
            line = line[:, :128] + line[:, 128:]
        sums.append(line)
    mean_val = sums[0] / model_width
    scale = lax.rsqrt(sums[1] / model_width - mean_val * mean_val + epsilon)
    mean_val = jnp.broadcast_to(mean_val, (rows, rows)).T[:, 0:1]
    scale = jnp.broadcast_to(scale, (rows, rows)).T[:, 0:1]
    texts = []
    for total in totals:
        text = (total[:rows] - mean_val * total[rows + slots : rows + slots + 1]) * scale
        texts.append(text + total[rows + slots + 1 : rows + slots + 2])
    for part, text in enumerate(texts):
        span = slice(part * HEAD_DIM, (part + 1) * HEAD_DIM)
        if width > HEAD_DIM:
            low, high = text[:, :HEAD_DIM], text[:, HEAD_DIM:]
            mine_ref[:, span] = jnp.where(core == 0, low, high).astype(mine_ref.dtype)
            sent_ref[:, span] = jnp.where(core == 0, high, low).astype(mine_ref.dtype)
        else:
            mine_ref[:, span] = text.astype(mine_ref.dtype)
            sent_ref[:, span] = text.astype(mine_ref.dtype)


def combine(place, parts, chips, rows, model_width):
    out = jax.ShapeDtypeStruct((rows, 2 * HEAD_DIM), jnp.bfloat16)
    return pl.pallas_call(
        functools.partial(combine_kernel, chips, model_width),
        out_shape=(out, out),
        in_specs=[SMEM_SPEC] + [VMEM_SPEC] * 4,
        out_specs=(VMEM_SPEC, VMEM_SPEC),
        compiler_params=params(8),
        cost_estimate=pl.CostEstimate(
            flops=8 * rows * 512, bytes_accessed=12 * rows * 512, transcendentals=0
        ),
        name="combine",
    )(place, *parts)


def pack_kernel(copies, queries_ref, keys_ref, values_ref, out_ref):
    img_dev = keys_ref.shape[0]
    part_rows = img_dev // copies
    for device in range(out_ref.shape[0]):
        head, copy = device // copies, device % copies
        span = slice(head * HEAD_DIM, (head + 1) * HEAD_DIM)
        out_ref[device, :img_dev, :] = keys_ref[:, span]
        out_ref[device, img_dev : 2 * img_dev, :] = values_ref[:, span]
        out_ref[device, 2 * img_dev :, :] = queries_ref[copy * part_rows : (copy + 1) * part_rows, span]


def pack(copies, queries, keys, values):
    img_dev = keys.shape[0]
    rows = 2 * img_dev + img_dev // copies
    return pl.pallas_call(
        functools.partial(pack_kernel, copies),
        out_shape=jax.ShapeDtypeStruct((HEADS * copies, rows, HEAD_DIM), jnp.bfloat16),
        in_specs=[VMEM_SPEC] * 3,
        out_specs=VMEM_SPEC,
        compiler_params=params(8),
        cost_estimate=pl.CostEstimate(
            flops=0, bytes_accessed=4 * HEADS * copies * rows * HEAD_DIM, transcendentals=0
        ),
        name="pack",
    )(queries, keys, values)


def unpack_kernel(copies, part_rows, blocks_ref, attended_ref, text_ref):
    share = text_ref.shape[0]
    half = text_ref.shape[1] // 2
    for device in range(blocks_ref.shape[0]):
        head, copy = device // copies, device % copies
        start = head * HEAD_DIM
        rows = slice(copy * part_rows, (copy + 1) * part_rows)
        attended_ref[rows, start : start + HEAD_DIM] = blocks_ref[device, :part_rows, :]
        if copy == 0:
            block = blocks_ref[device, part_rows:, :].astype(jnp.float32)
            text_ref[:, start : start + HEAD_DIM] = block[:share].astype(text_ref.dtype)
            start += half
            text_ref[:, start : start + HEAD_DIM] = block[share:].astype(text_ref.dtype)


def unpack(copies, part_rows, blocks):
    share = (blocks.shape[1] - part_rows) // 2
    return pl.pallas_call(
        functools.partial(unpack_kernel, copies, part_rows),
        out_shape=(
            jax.ShapeDtypeStruct((part_rows * copies, HEADS * HEAD_DIM), jnp.bfloat16),
            jax.ShapeDtypeStruct((share, 2 * HEADS * HEAD_DIM), jnp.bfloat16),
        ),
        in_specs=[VMEM_SPEC],
        out_specs=(VMEM_SPEC, VMEM_SPEC),
        compiler_params=params(8),
        name="unpack",
    )(blocks)


def image_kernel(factor, call, img_dev, packed_ref, sum_ref, top_ref, keys_ref, wide_ref):
    wide_ref[:, HEAD_DIM:] = jnp.ones((wide_ref.shape[0], HEAD_DIM), wide_ref.dtype)
    for device in range(packed_ref.shape[0]):
        rows = slice(device * img_dev, (device + 1) * img_dev)
        keys_ref[rows, :] = packed_ref[device, :img_dev, :]
        wide_ref[rows, :HEAD_DIM] = packed_ref[device, img_dev : 2 * img_dev, :]
    group = max(1, 256 // (packed_ref.shape[1] - 2 * img_dev))
    rows = 256
    contract = (((1,), (1,)), ((), ()))
    count = sum_ref.shape[0]
    for start in range(0, count, rows):
        span = slice(start, start + rows)
        at = (call * count + start) // rows * group
        queries = packed_ref[at : at + group, 2 * img_dev :, :].reshape(rows, HEAD_DIM)
        scores = lax.dot_general(queries, keys_ref[...], contract, preferred_element_type=jnp.float32)
        scores = scores * factor
        top = jnp.max(scores, 1, keepdims=True)
        weights = jnp.exp2(scores - top).astype(jnp.bfloat16)
        sum_ref[span, :] = jnp.dot(weights, wide_ref[...], preferred_element_type=jnp.float32)
        top_ref[span, :] = jnp.broadcast_to(top, (rows, HEAD_DIM))


def image_attention(packed, img_dev, factor, call, calls):
    count = packed.shape[0] * (packed.shape[1] - 2 * img_dev) // calls
    total = packed.shape[0] * img_dev
    return pl.pallas_call(
        functools.partial(image_kernel, factor, call, img_dev),
        out_shape=(
            jax.ShapeDtypeStruct((count, 2 * HEAD_DIM), jnp.float32),
            jax.ShapeDtypeStruct((count, HEAD_DIM), jnp.float32),
        ),
        in_specs=[VMEM_SPEC],
        out_specs=(VMEM_SPEC, VMEM_SPEC),
        scratch_shapes=[
            pltpu.VMEM((total, HEAD_DIM), jnp.bfloat16),
            pltpu.VMEM((total, 2 * HEAD_DIM), jnp.bfloat16),
        ],
        compiler_params=params(24),
        cost_estimate=pl.CostEstimate(
            flops=4 * count * total * HEAD_DIM,
            bytes_accessed=4 * total * HEAD_DIM + 10 * count * HEAD_DIM,
            transcendentals=count * total,
        ),
        name="image_attention",
    )(packed)


def finish_kernel(factor, calls, img_dev, place_ref, packed_ref, *refs):
    images, (mine_ref, got_ref, out_ref) = refs[: 2 * calls], refs[2 * calls :]
    core, valid = place_ref[2], place_ref[4]
    devices = out_ref.shape[0]
    part_rows = packed_ref.shape[1] - 2 * img_dev
    half = mine_ref.shape[0]
    contract = (((1,), (1,)), ((), ()))
    mine, got = mine_ref[...], got_ref[...]
    keys = jnp.concatenate([mine[:, :HEAD_DIM], got[:, :HEAD_DIM]], 0)
    values = jnp.concatenate([mine[:, HEAD_DIM:], got[:, HEAD_DIM:]], 0)
    values = jnp.concatenate([values, jnp.ones(values.shape, values.dtype)], 1)
    lane = lax.broadcasted_iota(jnp.int32, (1, 2 * half), 1)
    text_position = jnp.where((lane >= half) == (core == 0), half, 0) + lane % half
    bias = jnp.where(text_position < valid, 0.0, -jnp.inf)
    group = max(1, 512 // part_rows)
    rows = group * part_rows
    each = devices // group // calls
    for step in range(devices // group):
        sum_ref, top_ref = images[2 * (step // each)], images[2 * (step // each) + 1]
        span = slice(step % each * rows, (step % each + 1) * rows)
        queries = packed_ref[step * group : (step + 1) * group, 2 * img_dev :, :]
        queries = queries.reshape(rows, HEAD_DIM)
        scores = lax.dot_general(queries, keys, contract, preferred_element_type=jnp.float32)
        scores = scores * factor + bias
        before = top_ref[span, :]
        top = jnp.maximum(before, jnp.max(scores, 1, keepdims=True))
        rescale = jnp.exp2(before - top)
        weights = jnp.exp2(scores - jnp.concatenate([top] * (2 * half // HEAD_DIM), 1))
        total = jnp.dot(weights.astype(jnp.bfloat16), values, preferred_element_type=jnp.float32)
        mixed = sum_ref[span, :HEAD_DIM] * rescale + total[:, :HEAD_DIM]
        total = sum_ref[span, HEAD_DIM:] * rescale + total[:, HEAD_DIM:]
        mixed = (mixed / total).astype(out_ref.dtype)
        out_ref[step * group : (step + 1) * group, :part_rows, :] = mixed.reshape(group, part_rows, HEAD_DIM)
    low = jnp.where(core == 0, mine.astype(jnp.float32), got.astype(jnp.float32))
    high = jnp.where(core == 0, got.astype(jnp.float32), mine.astype(jnp.float32))
    share = 2 * half // devices
    for device in range(devices):
        source = low if device < devices // 2 else high
        start = device * share % half
        block = source[start : start + share]
        block = jnp.concatenate([block[:, :HEAD_DIM], block[:, HEAD_DIM:]], 0)
        out_ref[device, part_rows:, :] = block.astype(out_ref.dtype)


def finish(place, packed, images, mine, got, img_dev, factor):
    devices, part_rows = packed.shape[0], packed.shape[1] - 2 * img_dev
    count = devices * part_rows
    share = 2 * mine.shape[0] // devices
    return pl.pallas_call(
        functools.partial(finish_kernel, factor, len(images) // 2, img_dev),
        out_shape=jax.ShapeDtypeStruct((devices, part_rows + 2 * share, HEAD_DIM), jnp.bfloat16),
        in_specs=[SMEM_SPEC] + [VMEM_SPEC] * (len(images) + 3),
        out_specs=VMEM_SPEC,
        compiler_params=params(16),
        cost_estimate=pl.CostEstimate(
            flops=4 * count * 2 * mine.shape[0] * HEAD_DIM,
            bytes_accessed=12 * count * HEAD_DIM,
            transcendentals=count * 2 * mine.shape[0],
        ),
        name="finish",
    )(place, packed, *images, mine, got)


def add(one, other, dtype):
    return (one.astype(jnp.float32) + other.astype(jnp.float32)).astype(dtype)


def local(
    enc_act,
    down_weight,
    norm_gain,
    text_in_weight,
    modulation_weight,
    key_value_weight,
    timesteps,
    lengths,
    image_queries,
    image_key_values,
):
    devices = lax.axis_size("seq")
    chips = devices // 2
    copies = devices // HEADS
    text_len = enc_act.shape[1]
    img_dev = image_queries.shape[1]
    part_rows = img_dev // copies
    factor = math.log2(math.e) / math.sqrt(HEAD_DIM)
    lanes = orders(chips)
    index = lax.axis_index("seq")
    chip, core = index // 2, index % 2
    place = jnp.stack([position(chip, lanes[0]), position(chip, lanes[1]), core, chip, lengths[0]])
    place = place.astype(jnp.int32)

    win0, kv0 = text_in_weight.T, key_value_weight
    mod0 = modulation_weight.transpose(1, 2, 0)
    win1, kv1, mod1 = swap(win0, 1), swap(kv0, 1), swap(mod0, 1)
    time = time_embedding(timesteps)

    rounds = len(lanes[0])
    tie = lax.optimization_barrier

    def exchange(rows):
        return lax.all_to_all(rows, "seq", split_axis=0, concat_axis=0, tiled=True)

    image_key_values, image_queries = tie((image_key_values, image_queries))
    packed = pack(copies, image_queries[0], image_key_values[0, :, 0], image_key_values[0, :, 1])
    act, packed = tie((enc_act[0].T, packed))
    packed = exchange(packed)
    keep, sent = [], []
    encoded = encoder(lanes, place, act, down_weight)
    for own, other in (encoded[:2], encoded[2:]):
        got = swap(other, 1)
        sent.append(add(own[chips // 2 :], got[chips // 2 :], jnp.bfloat16))
        keep.append(add(own[: chips // 2], got[: chips // 2], jnp.float32))
    for step in range(rounds):
        got = [swap(part, 2 * order[step]) for part, order in zip(sent, lanes)]
        if step == 0:
            got, packed = tie((got, packed))
            lines = modulation(time, mod0, mod1)
        if step == 1:
            got, lines = tie((got, lines))
        half = keep[0].shape[0] // 2
        if half:
            sent = [add(mine[half:], part[half:], jnp.bfloat16) for mine, part in zip(keep, got)]
            keep = [add(mine[:half], part[:half], jnp.float32) for mine, part in zip(keep, got)]
    summed = [add(mine[0], part[0], jnp.float32) for mine, part in zip(keep, got)]

    width = summed[0].shape[1]
    square = sum(jnp.sum(part * part, 1, keepdims=True) for part in summed)
    scale_rows = lax.rsqrt(square / (2 * width) + epsilon)
    gains = norm_gain.astype(jnp.float32)
    states = [
        (part * scale_rows * gains[lane * width : (lane + 1) * width]).astype(jnp.bfloat16)
        for lane, part in enumerate(summed)
    ]
    images = []

    for step in reversed(range(rounds)):
        if step == 0:
            states, packed = tie((states, packed))
            image = image_attention(packed, img_dev, factor, 0, 2)
        got = [swap(state, 2 * order[step]) for state, order in zip(states, lanes)]
        if step:
            states = [jnp.concatenate(pair, 0) for pair in zip(states, got)]
    got, image = tie((got, image))
    images += image
    states = [state for pair in zip(states, got) for state in pair]

    blocks = project(lanes, place, states, lines, win0, win1, kv0, kv1)
    keep, sent = [blocks[0], blocks[2]], [blocks[1], blocks[3]]
    for step in range(rounds):
        if step == 0:
            sent, packed = tie((sent, packed))
            image = image_attention(packed, img_dev, factor, 1, 2)
        got = [swap(part, 2 * order[step]) for part, order in zip(sent, lanes)]
        if step == 0:
            got, image = tie((got, image))
            images += image
        half = keep[0].shape[0] // 2
        if half:
            sent = [add(mine[half:], part[half:], jnp.bfloat16) for mine, part in zip(keep, got)]
            keep = [add(mine[:half], part[:half], jnp.float32) for mine, part in zip(keep, got)]
    parts = [part[0] for pair in zip(keep, got) for part in pair]
    model_width = text_in_weight.shape[1] * devices
    mine, sent = combine(place, parts, chips, text_len // 2, model_width)
    got = swap(sent, 1)

    back = exchange(finish(place, packed, images, mine, got, img_dev, factor))
    attended, text_kv = unpack(copies, part_rows, back)
    return (attended[None], text_kv)


def solution(mesh):
    in_specs = (
        P("dp", None, "seq"),
        P("seq", None),
        P(),
        P(None, "seq"),
        P(None, None, "seq"),
        P("seq", None),
        P("dp"),
        P("dp"),
        P("dp", "seq", None),
        P("dp", "seq", None, None),
    )
    out_specs = (P("dp", "seq", None), P(("dp", "seq"), None))
    return jax.shard_map(local, mesh=mesh, in_specs=in_specs, out_specs=out_specs, check_vma=False)
```

```python
import functools
import math

import jax
import jax.numpy as jnp
from jax import lax
from jax.experimental import pallas as pl
from jax.experimental.pallas import tpu as pltpu
from jax.sharding import PartitionSpec as P

HEAD_DIM = 128
HEADS = 16
TEMB = 256
MIB = 1024 * 1024

epsilon = 1e-06

SMEM_SPEC = pl.BlockSpec(memory_space=pltpu.SMEM)
VMEM_SPEC = pl.BlockSpec(memory_space=pltpu.VMEM)


def params(mib):
    return pltpu.CompilerParams(vmem_limit_bytes=mib * MIB)


def swap(value, mask):
    devices = lax.axis_size("seq")
    return lax.ppermute(value, "seq", [(i, i ^ mask) for i in range(devices)])


def orders(chips):
    bits = [1 << i for i in range(chips.bit_length() - 1)]
    return (bits, [bits[1], bits[0]] + bits[2:])


def position(chip, order):
    last = len(order) - 1
    return sum(((chip >> (bit.bit_length() - 1)) & 1) << (last - i) for i, bit in enumerate(order))


def member(at, order):
    last = len(order) - 1
    return sum(bit for i, bit in enumerate(order) if (at >> (last - i)) & 1)


def time_embedding(timesteps):
    half_width = TEMB // 2
    freqs = jnp.exp(-math.log(10000.0) * jnp.arange(half_width, dtype=jnp.float32) / half_width)
    angles = timesteps.astype(jnp.float32)[:, None] * freqs[None, :]
    embedding = jnp.concatenate([jnp.cos(angles), jnp.sin(angles)], 1)
    return jax.nn.silu(embedding).astype(jnp.bfloat16)


def encoder_kernel(lanes, place_ref, act_ref, weight_ref, *refs):
    outs, lhs_ref = refs[:-1], refs[-1]
    chips, share, width = outs[0].shape
    core = place_ref[2]
    half = chips * share
    first = core == 0
    tile = width // 2
    lhs_ref[...] = act_ref[...].T
    for lane, order in enumerate(lanes):
        own_ref, other_ref = outs[2 * lane], outs[2 * lane + 1]
        for column in range(0, width, tile):
            start = lane * width + column
            result = jnp.dot(
                lhs_ref[...], weight_ref[:, start : start + tile], preferred_element_type=jnp.float32
            )
            own = jnp.where(first, result[:half], result[half:]).astype(own_ref.dtype)
            other = jnp.where(first, result[half:], result[:half]).astype(own_ref.dtype)
            own = own.reshape(chips, share, tile)
            other = other.reshape(chips, share, tile)
            for block in range(chips):
                to = place_ref[lane] ^ position(block, order)
                own_ref[to, :, column : column + tile] = own[block]
                other_ref[to, :, column : column + tile] = other[block]


def encoder(lanes, place, act, weight):
    chips = 1 << len(lanes[0])
    depth, rows = act.shape
    width = weight.shape[1]
    out = jax.ShapeDtypeStruct((chips, rows // 2 // chips, width // 2), jnp.bfloat16)
    return pl.pallas_call(
        functools.partial(encoder_kernel, lanes),
        out_shape=(out,) * 4,
        in_specs=[SMEM_SPEC, VMEM_SPEC, VMEM_SPEC],
        out_specs=(VMEM_SPEC,) * 4,
        scratch_shapes=[pltpu.VMEM((rows, depth), jnp.bfloat16)],
        compiler_params=params(24),
        cost_estimate=pl.CostEstimate(
            flops=2 * rows * depth * width,
            bytes_accessed=2 * (depth * rows + depth * width + rows * width),
            transcendentals=0,
        ),
        name="encoder",
    )(place, act, weight)


def modulation_kernel(time_ref, mod0_ref, mod1_ref, out_ref):
    contract = (((1,), (1,)), ((), ()))
    embedding = jnp.broadcast_to(time_ref[...].astype(jnp.float32), (16, time_ref.shape[1]))
    embedding = embedding.astype(jnp.bfloat16)
    row = lax.broadcasted_iota(jnp.int32, (16, mod0_ref.shape[1]), 0)
    for side, mod in enumerate((mod0_ref, mod1_ref)):
        shift, scale = [
            lax.dot_general(embedding, mod[at], contract, preferred_element_type=jnp.float32)
            for at in range(2)
        ]
        lines = jnp.where(row < 2, 1.0 + scale, shift)
        high = lines.astype(jnp.bfloat16).astype(jnp.float32)
        low = jnp.where(row % 2 == 0, high, lines - high)
        out_ref[side] = jnp.where(row < 4, low, 1.0 + scale)


def modulation(time, mod0, mod1):
    return pl.pallas_call(
        modulation_kernel,
        out_shape=jax.ShapeDtypeStruct((2, 16, mod0.shape[1]), jnp.float32),
        in_specs=[VMEM_SPEC] * 3,
        out_specs=VMEM_SPEC,
        compiler_params=params(8),
        name="modulation",
    )(time, mod0, mod1)


def slot_rows(chips, width):
    per_slot = 2 * 128 // width
    return chips * per_slot, -(-(chips * per_slot + 2) // 16) * 16


def project_kernel(lanes, place_ref, *refs):
    pieces, refs = (refs[:2], refs[2:4]), refs[4:]
    lines_ref, win0, win1, kv0, kv1, *outs, states, proj0, proj1, sums = refs
    chip = place_ref[3]
    half_chips = outs[0].shape[0]
    chips = 2 * half_chips
    rows = proj0.shape[0]
    share = rows // chips
    depth = states.shape[1]
    contract = (((1,), (1,)), ((), ()))
    for lane, order in enumerate(lanes):
        top, low = pieces[lane]
        states[: rows // 2, :] = top[...]
        states[rows // 2 :, :] = low[...]
        span = slice(lane * depth, (lane + 1) * depth)
        for win, proj in ((win0, proj0), (win1, proj1)):
            part = lax.dot_general(
                states[...], win[:, span], contract, preferred_element_type=jnp.float32
            )
            for at in range(chips):
                start = pl.multiple_of((chip ^ member(at, order)) * share, share)
                block = part[at * share : (at + 1) * share]
                if lane == 0:
                    proj[pl.ds(start, share), :] = block
                else:
                    proj[pl.ds(start, share), :] += block
    value0, value1 = proj0[...], proj1[...]
    first = jnp.sum(value0, 1, keepdims=True) + jnp.sum(value1, 1, keepdims=True)
    second = jnp.sum(value0 * value0, 1, keepdims=True) + jnp.sum(value1 * value1, 1, keepdims=True)
    lane = lax.broadcasted_iota(jnp.int32, sums.shape, 1)
    sums[...] = jnp.where(lane == 0, first, second).T
    left = []
    for side, value in enumerate((value0, value1)):
        lines = lines_ref[side]
        row = lax.broadcasted_iota(jnp.int32, lines.shape, 0)
        lines, scale = jnp.where(row < 4, lines, 0.0), lines[4:5]
        left.append(jnp.concatenate([value * scale, lines], 0).astype(jnp.bfloat16))
    width = outs[0].shape[2]
    slots, extra = slot_rows(chips, width)
    per_slot = slots // chips
    row = lax.broadcasted_iota(jnp.int32, (extra, width), 0)
    column = lax.broadcasted_iota(jnp.int32, (extra, width), 1)
    half = kv0.shape[1] // 2
    for lane, order in enumerate(lanes):
        line = sums[lane : lane + 1, :]
        high = line.astype(jnp.bfloat16).astype(jnp.float32)
        low = line - high
        if per_slot == 1:
            line = jnp.concatenate([high, low], 1)
        else:
            line = jnp.where(row % 2 == 0, high, low)
        line = jnp.where(row // per_slot == chip, line, 0.0)
        for at in reversed(range(chips)):
            out_ref, to = outs[2 * lane + at // half_chips], at % half_chips
            start = lane * half + (chip ^ member(at, order)) * width
            columns = pl.ds(pl.multiple_of(start, width), width)
            value = jnp.dot(left[0], kv0[:, columns], preferred_element_type=jnp.float32)
            value += jnp.dot(left[1], kv1[:, columns], preferred_element_type=jnp.float32)
            out_ref[to, :rows, :] = value[:rows].astype(out_ref.dtype)
            below = jnp.where(row == slots, value[rows : rows + 1] + value[rows + 1 : rows + 2], line)
            below = jnp.where(
                row == slots + 1, value[rows + 2 : rows + 3] + value[rows + 3 : rows + 4], below
            )
            out_ref[to, rows:, :] = below.astype(out_ref.dtype)


def project(lanes, place, pieces, lines, win0, win1, kv0, kv1):
    chips = 1 << len(lanes[0])
    rows = 2 * pieces[0].shape[0]
    features, depth = win0.shape
    total = kv0.shape[1]
    width = total // 2 // chips
    extra = slot_rows(chips, width)[1]
    out = jax.ShapeDtypeStruct((chips // 2, rows + extra, width), jnp.bfloat16)
    return pl.pallas_call(
        functools.partial(project_kernel, lanes),
        out_shape=(out,) * 4,
        in_specs=[SMEM_SPEC] + [VMEM_SPEC] * 9,
        out_specs=(VMEM_SPEC,) * 4,
        scratch_shapes=[
            pltpu.VMEM((rows, depth // 2), jnp.bfloat16),
            pltpu.VMEM((rows, features), jnp.float32),
            pltpu.VMEM((rows, features), jnp.float32),
            pltpu.VMEM((rows, 128), jnp.float32),
        ],
        compiler_params=params(20),
        cost_estimate=pl.CostEstimate(
            flops=4 * rows * features * (depth + total),
            bytes_accessed=2 * (rows * depth + 2 * features * (depth + total) + rows * total),
            transcendentals=0,
        ),
        name="project",
    )(place, *pieces, lines, win0, win1, kv0, kv1)


def combine_kernel(chips, model_width, place_ref, *refs):
    refs, mine_ref, sent_ref = refs[:4], refs[4], refs[5]
    core = place_ref[2]
    rows = mine_ref.shape[0]
    width = refs[0].shape[1]
    slots = slot_rows(chips, width)[0]
    totals = [
        refs[2 * lane][...].astype(jnp.float32) + refs[2 * lane + 1][...].astype(jnp.float32)
        for lane in range(2)
    ]
    sums = []
    for total in totals:
        line = jnp.sum(total[rows : rows + slots], 0, keepdims=True)
        if width > 128:
            line = line[:, :128] + line[:, 128:]
        sums.append(line)
    mean_val = sums[0] / model_width
    scale = lax.rsqrt(sums[1] / model_width - mean_val * mean_val + epsilon)
    mean_val = jnp.broadcast_to(mean_val, (rows, rows)).T[:, 0:1]
    scale = jnp.broadcast_to(scale, (rows, rows)).T[:, 0:1]
    texts = []
    for total in totals:
        text = (total[:rows] - mean_val * total[rows + slots : rows + slots + 1]) * scale
        texts.append(text + total[rows + slots + 1 : rows + slots + 2])
    for part, text in enumerate(texts):
        span = slice(part * HEAD_DIM, (part + 1) * HEAD_DIM)
        if width > HEAD_DIM:
            low, high = text[:, :HEAD_DIM], text[:, HEAD_DIM:]
            mine_ref[:, span] = jnp.where(core == 0, low, high).astype(mine_ref.dtype)
            sent_ref[:, span] = jnp.where(core == 0, high, low).astype(mine_ref.dtype)
        else:
            mine_ref[:, span] = text.astype(mine_ref.dtype)
            sent_ref[:, span] = text.astype(mine_ref.dtype)


def combine(place, parts, chips, rows, model_width):
    out = jax.ShapeDtypeStruct((rows, 2 * HEAD_DIM), jnp.bfloat16)
    return pl.pallas_call(
        functools.partial(combine_kernel, chips, model_width),
        out_shape=(out, out),
        in_specs=[SMEM_SPEC] + [VMEM_SPEC] * 4,
        out_specs=(VMEM_SPEC, VMEM_SPEC),
        compiler_params=params(8),
        cost_estimate=pl.CostEstimate(
            flops=8 * rows * 512, bytes_accessed=12 * rows * 512, transcendentals=0
        ),
        name="combine",
    )(place, *parts)


def pack_kernel(copies, queries_ref, keys_ref, values_ref, out_ref):
    img_dev = keys_ref.shape[0]
    part_rows = img_dev // copies
    for device in range(out_ref.shape[0]):
        head, copy = device // copies, device % copies
        span = slice(head * HEAD_DIM, (head + 1) * HEAD_DIM)
        out_ref[device, :img_dev, :] = keys_ref[:, span]
        out_ref[device, img_dev : 2 * img_dev, :] = values_ref[:, span]
        out_ref[device, 2 * img_dev :, :] = queries_ref[copy * part_rows : (copy + 1) * part_rows, span]


def pack(copies, queries, keys, values):
    img_dev = keys.shape[0]
    rows = 2 * img_dev + img_dev // copies
    return pl.pallas_call(
        functools.partial(pack_kernel, copies),
        out_shape=jax.ShapeDtypeStruct((HEADS * copies, rows, HEAD_DIM), jnp.bfloat16),
        in_specs=[VMEM_SPEC] * 3,
        out_specs=VMEM_SPEC,
        compiler_params=params(8),
        cost_estimate=pl.CostEstimate(
            flops=0, bytes_accessed=4 * HEADS * copies * rows * HEAD_DIM, transcendentals=0
        ),
        name="pack",
    )(queries, keys, values)


def unpack_kernel(copies, part_rows, blocks_ref, attended_ref, text_ref):
    share = text_ref.shape[0]
    half = text_ref.shape[1] // 2
    for device in range(blocks_ref.shape[0]):
        head, copy = device // copies, device % copies
        start = head * HEAD_DIM
        rows = slice(copy * part_rows, (copy + 1) * part_rows)
        attended_ref[rows, start : start + HEAD_DIM] = blocks_ref[device, :part_rows, :]
        if copy == 0:
            block = blocks_ref[device, part_rows:, :].astype(jnp.float32)
            text_ref[:, start : start + HEAD_DIM] = block[:share].astype(text_ref.dtype)
            start += half
            text_ref[:, start : start + HEAD_DIM] = block[share:].astype(text_ref.dtype)


def unpack(copies, part_rows, blocks):
    share = (blocks.shape[1] - part_rows) // 2
    return pl.pallas_call(
        functools.partial(unpack_kernel, copies, part_rows),
        out_shape=(
            jax.ShapeDtypeStruct((part_rows * copies, HEADS * HEAD_DIM), jnp.bfloat16),
            jax.ShapeDtypeStruct((share, 2 * HEADS * HEAD_DIM), jnp.bfloat16),
        ),
        in_specs=[VMEM_SPEC],
        out_specs=(VMEM_SPEC, VMEM_SPEC),
        compiler_params=params(8),
        name="unpack",
    )(blocks)


def image_kernel(factor, call, img_dev, packed_ref, sum_ref, top_ref, keys_ref, wide_ref):
    wide_ref[:, HEAD_DIM:] = jnp.ones((wide_ref.shape[0], HEAD_DIM), wide_ref.dtype)
    for device in range(packed_ref.shape[0]):
        rows = slice(device * img_dev, (device + 1) * img_dev)
        keys_ref[rows, :] = packed_ref[device, :img_dev, :]
        wide_ref[rows, :HEAD_DIM] = packed_ref[device, img_dev : 2 * img_dev, :]
    group = max(1, 256 // (packed_ref.shape[1] - 2 * img_dev))
    rows = 256
    contract = (((1,), (1,)), ((), ()))
    count = sum_ref.shape[0]
    for start in range(0, count, rows):
        span = slice(start, start + rows)
        at = (call * count + start) // rows * group
        queries = packed_ref[at : at + group, 2 * img_dev :, :].reshape(rows, HEAD_DIM)
        scores = lax.dot_general(queries, keys_ref[...], contract, preferred_element_type=jnp.float32)
        scores = scores * factor
        top = jnp.max(scores, 1, keepdims=True)
        weights = jnp.exp2(scores - top).astype(jnp.bfloat16)
        sum_ref[span, :] = jnp.dot(weights, wide_ref[...], preferred_element_type=jnp.float32)
        top_ref[span, :] = jnp.broadcast_to(top, (rows, HEAD_DIM))


def image_attention(packed, img_dev, factor, call, calls):
    count = packed.shape[0] * (packed.shape[1] - 2 * img_dev) // calls
    total = packed.shape[0] * img_dev
    return pl.pallas_call(
        functools.partial(image_kernel, factor, call, img_dev),
        out_shape=(
            jax.ShapeDtypeStruct((count, 2 * HEAD_DIM), jnp.float32),
            jax.ShapeDtypeStruct((count, HEAD_DIM), jnp.float32),
        ),
        in_specs=[VMEM_SPEC],
        out_specs=(VMEM_SPEC, VMEM_SPEC),
        scratch_shapes=[
            pltpu.VMEM((total, HEAD_DIM), jnp.bfloat16),
            pltpu.VMEM((total, 2 * HEAD_DIM), jnp.bfloat16),
        ],
        compiler_params=params(24),
        cost_estimate=pl.CostEstimate(
            flops=4 * count * total * HEAD_DIM,
            bytes_accessed=4 * total * HEAD_DIM + 10 * count * HEAD_DIM,
            transcendentals=count * total,
        ),
        name="image_attention",
    )(packed)


def finish_kernel(factor, calls, img_dev, place_ref, packed_ref, *refs):
    images, (mine_ref, got_ref, out_ref) = refs[: 2 * calls], refs[2 * calls :]
    core, valid = place_ref[2], place_ref[4]
    devices = out_ref.shape[0]
    part_rows = packed_ref.shape[1] - 2 * img_dev
    half = mine_ref.shape[0]
    contract = (((1,), (1,)), ((), ()))
    mine, got = mine_ref[...], got_ref[...]
    keys = jnp.concatenate([mine[:, :HEAD_DIM], got[:, :HEAD_DIM]], 0)
    values = jnp.concatenate([mine[:, HEAD_DIM:], got[:, HEAD_DIM:]], 0)
    values = jnp.concatenate([values, jnp.ones(values.shape, values.dtype)], 1)
    lane = lax.broadcasted_iota(jnp.int32, (1, 2 * half), 1)
    text_position = jnp.where((lane >= half) == (core == 0), half, 0) + lane % half
    bias = jnp.where(text_position < valid, 0.0, -jnp.inf)
    group = max(1, 512 // part_rows)
    rows = group * part_rows
    each = devices // group // calls
    for step in range(devices // group):
        sum_ref, top_ref = images[2 * (step // each)], images[2 * (step // each) + 1]
        span = slice(step % each * rows, (step % each + 1) * rows)
        queries = packed_ref[step * group : (step + 1) * group, 2 * img_dev :, :]
        queries = queries.reshape(rows, HEAD_DIM)
        scores = lax.dot_general(queries, keys, contract, preferred_element_type=jnp.float32)
        scores = scores * factor + bias
        before = top_ref[span, :]
        top = jnp.maximum(before, jnp.max(scores, 1, keepdims=True))
        rescale = jnp.exp2(before - top)
        weights = jnp.exp2(scores - jnp.concatenate([top] * (2 * half // HEAD_DIM), 1))
        total = jnp.dot(weights.astype(jnp.bfloat16), values, preferred_element_type=jnp.float32)
        mixed = sum_ref[span, :HEAD_DIM] * rescale + total[:, :HEAD_DIM]
        total = sum_ref[span, HEAD_DIM:] * rescale + total[:, HEAD_DIM:]
        mixed = (mixed / total).astype(out_ref.dtype)
        out_ref[step * group : (step + 1) * group, :part_rows, :] = mixed.reshape(group, part_rows, HEAD_DIM)
    low = jnp.where(core == 0, mine.astype(jnp.float32), got.astype(jnp.float32))
    high = jnp.where(core == 0, got.astype(jnp.float32), mine.astype(jnp.float32))
    share = 2 * half // devices
    for device in range(devices):
        source = low if device < devices // 2 else high
        start = device * share % half
        block = source[start : start + share]
        block = jnp.concatenate([block[:, :HEAD_DIM], block[:, HEAD_DIM:]], 0)
        out_ref[device, part_rows:, :] = block.astype(out_ref.dtype)


def finish(place, packed, images, mine, got, img_dev, factor):
    devices, part_rows = packed.shape[0], packed.shape[1] - 2 * img_dev
    count = devices * part_rows
    share = 2 * mine.shape[0] // devices
    return pl.pallas_call(
        functools.partial(finish_kernel, factor, len(images) // 2, img_dev),
        out_shape=jax.ShapeDtypeStruct((devices, part_rows + 2 * share, HEAD_DIM), jnp.bfloat16),
        in_specs=[SMEM_SPEC] + [VMEM_SPEC] * (len(images) + 3),
        out_specs=VMEM_SPEC,
        compiler_params=params(16),
        cost_estimate=pl.CostEstimate(
            flops=4 * count * 2 * mine.shape[0] * HEAD_DIM,
            bytes_accessed=12 * count * HEAD_DIM,
            transcendentals=count * 2 * mine.shape[0],
        ),
        name="finish",
    )(place, packed, *images, mine, got)


def add_kernel(*refs):
    ins, outs = refs[:4], refs[4:]
    for lane in range(2):
        mine, got = ins[2 * lane], ins[2 * lane + 1]
        half = mine.shape[0] // 2
        outs[2 * lane][...] = (
            mine[half:].astype(jnp.float32) + got[half:].astype(jnp.float32)
        ).astype(jnp.bfloat16)
        outs[2 * lane + 1][...] = mine[:half].astype(jnp.float32) + got[:half].astype(jnp.float32)


def add_halves(mine, got):
    shape = (mine[0].shape[0] // 2,) + mine[0].shape[1:]
    outs = (jax.ShapeDtypeStruct(shape, jnp.bfloat16), jax.ShapeDtypeStruct(shape, jnp.float32))
    sent0, keep0, sent1, keep1 = pl.pallas_call(
        add_kernel,
        out_shape=outs * 2,
        in_specs=[VMEM_SPEC] * 4,
        out_specs=(VMEM_SPEC,) * 4,
        compiler_params=params(8),
        cost_estimate=pl.CostEstimate(
            flops=2 * mine[0].size, bytes_accessed=12 * mine[0].size, transcendentals=0
        ),
        name="add_halves",
    )(mine[0], got[0], mine[1], got[1])
    return [sent0, sent1], [keep0, keep1]


def norm_kernel(keep0, got0, keep1, got1, gain_ref, out0, out1):
    totals = [keep0[0] + got0[0].astype(jnp.float32), keep1[0] + got1[0].astype(jnp.float32)]
    width = totals[0].shape[1]
    square = sum(jnp.sum(total * total, 1, keepdims=True) for total in totals)
    scale_rows = lax.rsqrt(square / (2 * width) + epsilon)
    for lane, (total, out_ref) in enumerate(zip(totals, (out0, out1))):
        gain = gain_ref[:, lane * width : (lane + 1) * width].astype(jnp.float32)
        out_ref[...] = (total * scale_rows * gain).astype(out_ref.dtype)


def normalize(keep, got, norm_gain):
    out = jax.ShapeDtypeStruct(keep[0].shape[1:], jnp.bfloat16)
    return pl.pallas_call(
        norm_kernel,
        out_shape=(out, out),
        in_specs=[VMEM_SPEC] * 5,
        out_specs=(VMEM_SPEC,) * 2,
        compiler_params=params(8),
        cost_estimate=pl.CostEstimate(
            flops=8 * keep[0].size, bytes_accessed=16 * keep[0].size, transcendentals=0
        ),
        name="normalize",
    )(keep[0], got[0], keep[1], got[1], norm_gain)


def join_kernel(mine0, got0, mine1, got1, out0, out1):
    for mine, got, out_ref in ((mine0, got0, out0), (mine1, got1, out1)):
        rows = mine.shape[0]
        if rows % 16:
            both = [mine[...].astype(jnp.float32), got[...].astype(jnp.float32)]
            out_ref[...] = jnp.concatenate(both, 0).astype(out_ref.dtype)
        else:
            out_ref[:rows, :] = mine[...]
            out_ref[rows:, :] = got[...]


def join(mine, got):
    rows, width = mine[0].shape
    out = jax.ShapeDtypeStruct((2 * rows, width), mine[0].dtype)
    return pl.pallas_call(
        join_kernel,
        out_shape=(out, out),
        in_specs=[VMEM_SPEC] * 4,
        out_specs=(VMEM_SPEC,) * 2,
        compiler_params=params(8),
        cost_estimate=pl.CostEstimate(
            flops=0, bytes_accessed=16 * rows * width, transcendentals=0
        ),
        name="join",
    )(mine[0], got[0], mine[1], got[1])


def local(
    enc_act,
    down_weight,
    norm_gain,
    text_in_weight,
    modulation_weight,
    key_value_weight,
    timesteps,
    lengths,
    image_queries,
    image_key_values,
):
    devices = lax.axis_size("seq")
    chips = devices // 2
    copies = devices // HEADS
    text_len = enc_act.shape[1]
    img_dev = image_queries.shape[1]
    part_rows = img_dev // copies
    factor = math.log2(math.e) / math.sqrt(HEAD_DIM)
    lanes = orders(chips)
    index = lax.axis_index("seq")
    chip, core = index // 2, index % 2
    place = jnp.stack([position(chip, lanes[0]), position(chip, lanes[1]), core, chip, lengths[0]])
    place = place.astype(jnp.int32)

    win0, kv0 = text_in_weight.T, key_value_weight
    mod0 = modulation_weight.transpose(1, 2, 0)
    win1, kv1, mod1 = swap(win0, 1), swap(kv0, 1), swap(mod0, 1)
    time = time_embedding(timesteps)

    rounds = len(lanes[0])
    tie = lax.optimization_barrier

    def exchange(rows):
        return lax.all_to_all(rows, "seq", split_axis=0, concat_axis=0, tiled=True)

    image_key_values, image_queries = tie((image_key_values, image_queries))
    packed = pack(copies, image_queries[0], image_key_values[0, :, 0], image_key_values[0, :, 1])
    act, packed = tie((enc_act[0].T, packed))
    packed = exchange(packed)
    encoded = encoder(lanes, place, act, down_weight)
    keep, got = encoded[::2], [swap(other, 1) for other in encoded[1::2]]
    for step in range(rounds):
        sent, keep = add_halves(keep, got)
        got = [swap(part, 2 * order[step]) for part, order in zip(sent, lanes)]
        if step == 0:
            got, win1, kv1, mod1, packed = tie((got, win1, kv1, mod1, packed))
            lines = modulation(time, mod0, mod1)
        if step == 1:
            got, lines = tie((got, lines))

    states = normalize(keep, got, norm_gain[None, :])
    images = []

    for step in reversed(range(rounds)):
        if step == 0:
            states, packed = tie((states, packed))
            image = image_attention(packed, img_dev, factor, 0, 2)
        got = [swap(state, 2 * order[step]) for state, order in zip(states, lanes)]
        if step:
            states = join(states, got)
    got, image = tie((got, image))
    images += image
    states = [state for pair in zip(states, got) for state in pair]

    blocks = project(lanes, place, states, lines, win0, win1, kv0, kv1)
    keep, sent = [blocks[0], blocks[2]], [blocks[1], blocks[3]]
    for step in range(rounds):
        if step == 0:
            sent, packed = tie((sent, packed))
            image = image_attention(packed, img_dev, factor, 1, 2)
        got = [swap(part, 2 * order[step]) for part, order in zip(sent, lanes)]
        if step == 0:
            got, image = tie((got, image))
            images += image
        if step < rounds - 1:
            sent, keep = add_halves(keep, got)
    parts = [part[0] for pair in zip(keep, got) for part in pair]
    model_width = text_in_weight.shape[1] * devices
    mine, sent = combine(place, parts, chips, text_len // 2, model_width)
    got = swap(sent, 1)

    back = exchange(finish(place, packed, images, mine, got, img_dev, factor))
    attended, text_kv = unpack(copies, part_rows, back)
    return (attended[None], text_kv)


def solution(mesh):
    in_specs = (
        P("dp", None, "seq"),
        P("seq", None),
        P(),
        P(None, "seq"),
        P(None, None, "seq"),
        P("seq", None),
        P("dp"),
        P("dp"),
        P("dp", "seq", None),
        P("dp", "seq", None, None),
    )
    out_specs = (P("dp", "seq", None), P(("dp", "seq"), None))
    return jax.shard_map(local, mesh=mesh, in_specs=in_specs, out_specs=out_specs, check_vma=False)
```

```python
import functools
import math

import jax
import jax.numpy as jnp
from jax import lax
from jax.experimental import pallas as pl
from jax.experimental.pallas import tpu as pltpu
from jax.sharding import PartitionSpec as P

HEAD_DIM = 128
HEADS = 16
TEMB = 256
MIB = 1024 * 1024

epsilon = 1e-06

SMEM_SPEC = pl.BlockSpec(memory_space=pltpu.SMEM)
VMEM_SPEC = pl.BlockSpec(memory_space=pltpu.VMEM)


def params(mib):
    return pltpu.CompilerParams(vmem_limit_bytes=mib * MIB)


def swap(value, mask):
    devices = lax.axis_size("seq")
    return lax.ppermute(value, "seq", [(i, i ^ mask) for i in range(devices)])


def orders(chips):
    bits = [1 << i for i in range(chips.bit_length() - 1)]
    return (bits, [bits[1], bits[0]] + bits[2:])


def position(chip, order):
    last = len(order) - 1
    return sum(((chip >> (bit.bit_length() - 1)) & 1) << (last - i) for i, bit in enumerate(order))


def member(at, order):
    last = len(order) - 1
    return sum(bit for i, bit in enumerate(order) if (at >> (last - i)) & 1)


def time_embedding(timesteps):
    half_width = TEMB // 2
    freqs = jnp.exp(-math.log(10000.0) * jnp.arange(half_width, dtype=jnp.float32) / half_width)
    angles = timesteps.astype(jnp.float32)[:, None] * freqs[None, :]
    embedding = jnp.concatenate([jnp.cos(angles), jnp.sin(angles)], 1)
    return jax.nn.silu(embedding).astype(jnp.bfloat16)


def encoder_kernel(lanes, place_ref, act_ref, weight_ref, *refs):
    outs, lhs_ref = refs[:-1], refs[-1]
    chips, share, width = outs[0].shape
    core = place_ref[2]
    half = chips * share
    first = core == 0
    tile = width // 2
    lhs_ref[...] = act_ref[...].T
    for lane, order in enumerate(lanes):
        own_ref, other_ref = outs[2 * lane], outs[2 * lane + 1]
        for column in range(0, width, tile):
            start = lane * width + column
            result = jnp.dot(
                lhs_ref[...], weight_ref[:, start : start + tile], preferred_element_type=jnp.float32
            )
            own = jnp.where(first, result[:half], result[half:]).astype(own_ref.dtype)
            other = jnp.where(first, result[half:], result[:half]).astype(own_ref.dtype)
            own = own.reshape(chips, share, tile)
            other = other.reshape(chips, share, tile)
            for block in range(chips):
                to = place_ref[lane] ^ position(block, order)
                own_ref[to, :, column : column + tile] = own[block]
                other_ref[to, :, column : column + tile] = other[block]


def encoder(lanes, place, act, weight):
    chips = 1 << len(lanes[0])
    depth, rows = act.shape
    width = weight.shape[1]
    out = jax.ShapeDtypeStruct((chips, rows // 2 // chips, width // 2), jnp.bfloat16)
    return pl.pallas_call(
        functools.partial(encoder_kernel, lanes),
        out_shape=(out,) * 4,
        in_specs=[SMEM_SPEC, VMEM_SPEC, VMEM_SPEC],
        out_specs=(VMEM_SPEC,) * 4,
        scratch_shapes=[pltpu.VMEM((rows, depth), jnp.bfloat16)],
        compiler_params=params(16),
        cost_estimate=pl.CostEstimate(
            flops=2 * rows * depth * width,
            bytes_accessed=2 * (depth * rows + depth * width + rows * width),
            transcendentals=0,
        ),
        name="encoder",
    )(place, act, weight)


def modulation_kernel(time_ref, mod0_ref, mod1_ref, out_ref):
    contract = (((1,), (1,)), ((), ()))
    embedding = jnp.broadcast_to(time_ref[...].astype(jnp.float32), (16, time_ref.shape[1]))
    embedding = embedding.astype(jnp.bfloat16)
    row = lax.broadcasted_iota(jnp.int32, (16, mod0_ref.shape[1]), 0)
    for side, mod in enumerate((mod0_ref, mod1_ref)):
        shift, scale = [
            lax.dot_general(embedding, mod[at], contract, preferred_element_type=jnp.float32)
            for at in range(2)
        ]
        lines = jnp.where(row < 2, 1.0 + scale, shift)
        high = lines.astype(jnp.bfloat16).astype(jnp.float32)
        low = jnp.where(row % 2 == 0, high, lines - high)
        out_ref[side] = jnp.where(row < 4, low, 1.0 + scale)


def modulation(time, mod0, mod1):
    return pl.pallas_call(
        modulation_kernel,
        out_shape=jax.ShapeDtypeStruct((2, 16, mod0.shape[1]), jnp.float32),
        in_specs=[VMEM_SPEC] * 3,
        out_specs=VMEM_SPEC,
        compiler_params=params(4),
        name="modulation",
    )(time, mod0, mod1)


def slot_rows(chips, width):
    per_slot = 2 * 128 // width
    return chips * per_slot, -(-(chips * per_slot + 2) // 16) * 16


def project_kernel(lanes, place_ref, *refs):
    pieces, refs = (refs[:2], refs[2:4]), refs[4:]
    lines_ref, win0, win1, kv0, kv1, *outs, states, proj0, proj1, sums = refs
    chip = place_ref[3]
    half_chips = outs[0].shape[0]
    chips = 2 * half_chips
    rows = proj0.shape[0]
    share = rows // chips
    depth = states.shape[1]
    contract = (((1,), (1,)), ((), ()))
    for lane, order in enumerate(lanes):
        top, low = pieces[lane]
        states[: rows // 2, :] = top[...]
        states[rows // 2 :, :] = low[...]
        span = slice(lane * depth, (lane + 1) * depth)
        for win, proj in ((win0, proj0), (win1, proj1)):
            part = lax.dot_general(
                states[...], win[:, span], contract, preferred_element_type=jnp.float32
            )
            for at in range(chips):
                start = pl.multiple_of((chip ^ member(at, order)) * share, share)
                block = part[at * share : (at + 1) * share]
                if lane == 0:
                    proj[pl.ds(start, share), :] = block
                else:
                    proj[pl.ds(start, share), :] += block
    value0, value1 = proj0[...], proj1[...]
    first = jnp.sum(value0, 1, keepdims=True) + jnp.sum(value1, 1, keepdims=True)
    second = jnp.sum(value0 * value0, 1, keepdims=True) + jnp.sum(value1 * value1, 1, keepdims=True)
    lane = lax.broadcasted_iota(jnp.int32, sums.shape, 1)
    sums[...] = jnp.where(lane == 0, first, second).T
    left = []
    for side, value in enumerate((value0, value1)):
        lines = lines_ref[side]
        row = lax.broadcasted_iota(jnp.int32, lines.shape, 0)
        lines, scale = jnp.where(row < 4, lines, 0.0), lines[4:5]
        left.append(jnp.concatenate([value * scale, lines], 0).astype(jnp.bfloat16))
    width = outs[0].shape[2]
    slots, extra = slot_rows(chips, width)
    per_slot = slots // chips
    row = lax.broadcasted_iota(jnp.int32, (extra, width), 0)
    column = lax.broadcasted_iota(jnp.int32, (extra, width), 1)
    half = kv0.shape[1] // 2
    for lane, order in enumerate(lanes):
        line = sums[lane : lane + 1, :]
        high = line.astype(jnp.bfloat16).astype(jnp.float32)
        low = line - high
        if per_slot == 1:
            line = jnp.concatenate([high, low], 1)
        else:
            line = jnp.where(row % 2 == 0, high, low)
        line = jnp.where(row // per_slot == chip, line, 0.0)
        for at in reversed(range(chips)):
            out_ref, to = outs[2 * lane + at // half_chips], at % half_chips
            start = lane * half + (chip ^ member(at, order)) * width
            columns = pl.ds(pl.multiple_of(start, width), width)
            value = jnp.dot(left[0], kv0[:, columns], preferred_element_type=jnp.float32)
            value += jnp.dot(left[1], kv1[:, columns], preferred_element_type=jnp.float32)
            out_ref[to, :rows, :] = value[:rows].astype(out_ref.dtype)
            below = jnp.where(row == slots, value[rows : rows + 1] + value[rows + 1 : rows + 2], line)
            below = jnp.where(
                row == slots + 1, value[rows + 2 : rows + 3] + value[rows + 3 : rows + 4], below
            )
            out_ref[to, rows:, :] = below.astype(out_ref.dtype)


def project(lanes, place, pieces, lines, win0, win1, kv0, kv1):
    chips = 1 << len(lanes[0])
    rows = 2 * pieces[0].shape[0]
    features, depth = win0.shape
    total = kv0.shape[1]
    width = total // 2 // chips
    extra = slot_rows(chips, width)[1]
    out = jax.ShapeDtypeStruct((chips // 2, rows + extra, width), jnp.bfloat16)
    return pl.pallas_call(
        functools.partial(project_kernel, lanes),
        out_shape=(out,) * 4,
        in_specs=[SMEM_SPEC] + [VMEM_SPEC] * 9,
        out_specs=(VMEM_SPEC,) * 4,
        scratch_shapes=[
            pltpu.VMEM((rows, depth // 2), jnp.bfloat16),
            pltpu.VMEM((rows, features), jnp.float32),
            pltpu.VMEM((rows, features), jnp.float32),
            pltpu.VMEM((rows, 128), jnp.float32),
        ],
        compiler_params=params(14),
        cost_estimate=pl.CostEstimate(
            flops=4 * rows * features * (depth + total),
            bytes_accessed=2 * (rows * depth + 2 * features * (depth + total) + rows * total),
            transcendentals=0,
        ),
        name="project",
    )(place, *pieces, lines, win0, win1, kv0, kv1)


def combine_kernel(chips, model_width, place_ref, *refs):
    refs, mine_ref, sent_ref = refs[:4], refs[4], refs[5]
    core = place_ref[2]
    rows = mine_ref.shape[0]
    width = refs[0].shape[1]
    slots = slot_rows(chips, width)[0]
    totals = [
        refs[2 * lane][...].astype(jnp.float32) + refs[2 * lane + 1][...].astype(jnp.float32)
        for lane in range(2)
    ]
    sums = []
    for total in totals:
        line = jnp.sum(total[rows : rows + slots], 0, keepdims=True)
        if width > 128:
            line = line[:, :128] + line[:, 128:]
        sums.append(line)
    mean_val = sums[0] / model_width
    scale = lax.rsqrt(sums[1] / model_width - mean_val * mean_val + epsilon)
    mean_val = jnp.broadcast_to(mean_val, (rows, rows)).T[:, 0:1]
    scale = jnp.broadcast_to(scale, (rows, rows)).T[:, 0:1]
    texts = []
    for total in totals:
        text = (total[:rows] - mean_val * total[rows + slots : rows + slots + 1]) * scale
        texts.append(text + total[rows + slots + 1 : rows + slots + 2])
    for part, text in enumerate(texts):
        span = slice(part * HEAD_DIM, (part + 1) * HEAD_DIM)
        if width > HEAD_DIM:
            low, high = text[:, :HEAD_DIM], text[:, HEAD_DIM:]
            mine_ref[:, span] = jnp.where(core == 0, low, high).astype(mine_ref.dtype)
            sent_ref[:, span] = jnp.where(core == 0, high, low).astype(mine_ref.dtype)
        else:
            mine_ref[:, span] = text.astype(mine_ref.dtype)
            sent_ref[:, span] = text.astype(mine_ref.dtype)


def combine(place, parts, chips, rows, model_width):
    out = jax.ShapeDtypeStruct((rows, 2 * HEAD_DIM), jnp.bfloat16)
    return pl.pallas_call(
        functools.partial(combine_kernel, chips, model_width),
        out_shape=(out, out),
        in_specs=[SMEM_SPEC] + [VMEM_SPEC] * 4,
        out_specs=(VMEM_SPEC, VMEM_SPEC),
        compiler_params=params(4),
        cost_estimate=pl.CostEstimate(
            flops=8 * rows * 512, bytes_accessed=12 * rows * 512, transcendentals=0
        ),
        name="combine",
    )(place, *parts)


def pack_kernel(copies, queries_ref, keys_ref, values_ref, out_ref):
    img_dev = keys_ref.shape[0]
    part_rows = img_dev // copies
    for device in range(out_ref.shape[0]):
        head, copy = device // copies, device % copies
        span = slice(head * HEAD_DIM, (head + 1) * HEAD_DIM)
        out_ref[device, :img_dev, :] = keys_ref[:, span]
        out_ref[device, img_dev : 2 * img_dev, :] = values_ref[:, span]
        out_ref[device, 2 * img_dev :, :] = queries_ref[copy * part_rows : (copy + 1) * part_rows, span]


def pack(copies, queries, keys, values):
    img_dev = keys.shape[0]
    rows = 2 * img_dev + img_dev // copies
    return pl.pallas_call(
        functools.partial(pack_kernel, copies),
        out_shape=jax.ShapeDtypeStruct((HEADS * copies, rows, HEAD_DIM), jnp.bfloat16),
        in_specs=[VMEM_SPEC] * 3,
        out_specs=VMEM_SPEC,
        compiler_params=params(8),
        cost_estimate=pl.CostEstimate(
            flops=0, bytes_accessed=4 * HEADS * copies * rows * HEAD_DIM, transcendentals=0
        ),
        name="pack",
    )(queries, keys, values)


def unpack_kernel(copies, part_rows, blocks_ref, attended_ref, text_ref):
    share = text_ref.shape[0]
    half = text_ref.shape[1] // 2
    for device in range(blocks_ref.shape[0]):
        head, copy = device // copies, device % copies
        start = head * HEAD_DIM
        rows = slice(copy * part_rows, (copy + 1) * part_rows)
        attended_ref[rows, start : start + HEAD_DIM] = blocks_ref[device, :part_rows, :]
        if copy == 0:
            block = blocks_ref[device, part_rows:, :].astype(jnp.float32)
            text_ref[:, start : start + HEAD_DIM] = block[:share].astype(text_ref.dtype)
            start += half
            text_ref[:, start : start + HEAD_DIM] = block[share:].astype(text_ref.dtype)


def unpack(copies, part_rows, blocks):
    share = (blocks.shape[1] - part_rows) // 2
    return pl.pallas_call(
        functools.partial(unpack_kernel, copies, part_rows),
        out_shape=(
            jax.ShapeDtypeStruct((part_rows * copies, HEADS * HEAD_DIM), jnp.bfloat16),
            jax.ShapeDtypeStruct((share, 2 * HEADS * HEAD_DIM), jnp.bfloat16),
        ),
        in_specs=[VMEM_SPEC],
        out_specs=(VMEM_SPEC, VMEM_SPEC),
        compiler_params=params(4),
        name="unpack",
    )(blocks)


def image_kernel(factor, call, img_dev, packed_ref, sum_ref, top_ref, keys_ref, wide_ref):
    wide_ref[:, HEAD_DIM:] = jnp.ones((wide_ref.shape[0], HEAD_DIM), wide_ref.dtype)
    for device in range(packed_ref.shape[0]):
        rows = slice(device * img_dev, (device + 1) * img_dev)
        keys_ref[rows, :] = packed_ref[device, :img_dev, :]
        wide_ref[rows, :HEAD_DIM] = packed_ref[device, img_dev : 2 * img_dev, :]
    group = max(1, 256 // (packed_ref.shape[1] - 2 * img_dev))
    rows = 256
    contract = (((1,), (1,)), ((), ()))
    count = sum_ref.shape[0]
    for start in range(0, count, rows):
        span = slice(start, start + rows)
        at = (call * count + start) // rows * group
        queries = packed_ref[at : at + group, 2 * img_dev :, :].reshape(rows, HEAD_DIM)
        scores = lax.dot_general(queries, keys_ref[...], contract, preferred_element_type=jnp.float32)
        scores = scores * factor
        top = jnp.max(scores, 1, keepdims=True)
        weights = jnp.exp2(scores - top).astype(jnp.bfloat16)
        sum_ref[span, :] = jnp.dot(weights, wide_ref[...], preferred_element_type=jnp.float32)
        top_ref[span, :] = jnp.broadcast_to(top, (rows, HEAD_DIM))


def image_attention(packed, img_dev, factor, call, calls):
    count = packed.shape[0] * (packed.shape[1] - 2 * img_dev) // calls
    total = packed.shape[0] * img_dev
    return pl.pallas_call(
        functools.partial(image_kernel, factor, call, img_dev),
        out_shape=(
            jax.ShapeDtypeStruct((count, 2 * HEAD_DIM), jnp.float32),
            jax.ShapeDtypeStruct((count, HEAD_DIM), jnp.float32),
        ),
        in_specs=[VMEM_SPEC],
        out_specs=(VMEM_SPEC, VMEM_SPEC),
        scratch_shapes=[
            pltpu.VMEM((total, HEAD_DIM), jnp.bfloat16),
            pltpu.VMEM((total, 2 * HEAD_DIM), jnp.bfloat16),
        ],
        compiler_params=params(14),
        cost_estimate=pl.CostEstimate(
            flops=4 * count * total * HEAD_DIM,
            bytes_accessed=4 * total * HEAD_DIM + 10 * count * HEAD_DIM,
            transcendentals=count * total,
        ),
        name="image_attention",
    )(packed)


def finish_kernel(factor, calls, img_dev, place_ref, packed_ref, *refs):
    images, (mine_ref, got_ref, out_ref) = refs[: 2 * calls], refs[2 * calls :]
    core, valid = place_ref[2], place_ref[4]
    devices = out_ref.shape[0]
    part_rows = packed_ref.shape[1] - 2 * img_dev
    half = mine_ref.shape[0]
    contract = (((1,), (1,)), ((), ()))
    mine, got = mine_ref[...], got_ref[...]
    keys = jnp.concatenate([mine[:, :HEAD_DIM], got[:, :HEAD_DIM]], 0)
    values = jnp.concatenate([mine[:, HEAD_DIM:], got[:, HEAD_DIM:]], 0)
    values = jnp.concatenate([values, jnp.ones(values.shape, values.dtype)], 1)
    lane = lax.broadcasted_iota(jnp.int32, (1, 2 * half), 1)
    text_position = jnp.where((lane >= half) == (core == 0), half, 0) + lane % half
    bias = jnp.where(text_position < valid, 0.0, -jnp.inf)
    group = max(1, 512 // part_rows)
    rows = group * part_rows
    each = devices // group // calls
    for step in range(devices // group):
        sum_ref, top_ref = images[2 * (step // each)], images[2 * (step // each) + 1]
        span = slice(step % each * rows, (step % each + 1) * rows)
        queries = packed_ref[step * group : (step + 1) * group, 2 * img_dev :, :]
        queries = queries.reshape(rows, HEAD_DIM)
        scores = lax.dot_general(queries, keys, contract, preferred_element_type=jnp.float32)
        scores = scores * factor + bias
        before = top_ref[span, :]
        top = jnp.maximum(before, jnp.max(scores, 1, keepdims=True))
        rescale = jnp.exp2(before - top)
        weights = jnp.exp2(scores - jnp.concatenate([top] * (2 * half // HEAD_DIM), 1))
        total = jnp.dot(weights.astype(jnp.bfloat16), values, preferred_element_type=jnp.float32)
        mixed = sum_ref[span, :HEAD_DIM] * rescale + total[:, :HEAD_DIM]
        total = sum_ref[span, HEAD_DIM:] * rescale + total[:, HEAD_DIM:]
        mixed = (mixed / total).astype(out_ref.dtype)
        out_ref[step * group : (step + 1) * group, :part_rows, :] = mixed.reshape(group, part_rows, HEAD_DIM)
    low = jnp.where(core == 0, mine.astype(jnp.float32), got.astype(jnp.float32))
    high = jnp.where(core == 0, got.astype(jnp.float32), mine.astype(jnp.float32))
    share = 2 * half // devices
    for device in range(devices):
        source = low if device < devices // 2 else high
        start = device * share % half
        block = source[start : start + share]
        block = jnp.concatenate([block[:, :HEAD_DIM], block[:, HEAD_DIM:]], 0)
        out_ref[device, part_rows:, :] = block.astype(out_ref.dtype)


def finish(place, packed, images, mine, got, img_dev, factor):
    devices, part_rows = packed.shape[0], packed.shape[1] - 2 * img_dev
    count = devices * part_rows
    share = 2 * mine.shape[0] // devices
    return pl.pallas_call(
        functools.partial(finish_kernel, factor, len(images) // 2, img_dev),
        out_shape=jax.ShapeDtypeStruct((devices, part_rows + 2 * share, HEAD_DIM), jnp.bfloat16),
        in_specs=[SMEM_SPEC] + [VMEM_SPEC] * (len(images) + 3),
        out_specs=VMEM_SPEC,
        compiler_params=params(10),
        cost_estimate=pl.CostEstimate(
            flops=4 * count * 2 * mine.shape[0] * HEAD_DIM,
            bytes_accessed=12 * count * HEAD_DIM,
            transcendentals=count * 2 * mine.shape[0],
        ),
        name="finish",
    )(place, packed, *images, mine, got)


def add_kernel(*refs):
    ins, outs = refs[:4], refs[4:]
    for lane in range(2):
        mine, got = ins[2 * lane], ins[2 * lane + 1]
        half = mine.shape[0] // 2
        outs[2 * lane][...] = (
            mine[half:].astype(jnp.float32) + got[half:].astype(jnp.float32)
        ).astype(jnp.bfloat16)
        outs[2 * lane + 1][...] = mine[:half].astype(jnp.float32) + got[:half].astype(jnp.float32)


def add_halves(mine, got):
    shape = (mine[0].shape[0] // 2,) + mine[0].shape[1:]
    outs = (jax.ShapeDtypeStruct(shape, jnp.bfloat16), jax.ShapeDtypeStruct(shape, jnp.float32))
    sent0, keep0, sent1, keep1 = pl.pallas_call(
        add_kernel,
        out_shape=outs * 2,
        in_specs=[VMEM_SPEC] * 4,
        out_specs=(VMEM_SPEC,) * 4,
        compiler_params=params(6),
        cost_estimate=pl.CostEstimate(
            flops=2 * mine[0].size, bytes_accessed=12 * mine[0].size, transcendentals=0
        ),
        name="add_halves",
    )(mine[0], got[0], mine[1], got[1])
    return [sent0, sent1], [keep0, keep1]


def norm_kernel(keep0, got0, keep1, got1, gain_ref, out0, out1):
    totals = [keep0[0] + got0[0].astype(jnp.float32), keep1[0] + got1[0].astype(jnp.float32)]
    width = totals[0].shape[1]
    square = sum(jnp.sum(total * total, 1, keepdims=True) for total in totals)
    scale_rows = lax.rsqrt(square / (2 * width) + epsilon)
    for lane, (total, out_ref) in enumerate(zip(totals, (out0, out1))):
        gain = gain_ref[:, lane * width : (lane + 1) * width].astype(jnp.float32)
        out_ref[...] = (total * scale_rows * gain).astype(out_ref.dtype)


def normalize(keep, got, norm_gain):
    out = jax.ShapeDtypeStruct(keep[0].shape[1:], jnp.bfloat16)
    return pl.pallas_call(
        norm_kernel,
        out_shape=(out, out),
        in_specs=[VMEM_SPEC] * 5,
        out_specs=(VMEM_SPEC,) * 2,
        compiler_params=params(4),
        cost_estimate=pl.CostEstimate(
            flops=8 * keep[0].size, bytes_accessed=16 * keep[0].size, transcendentals=0
        ),
        name="normalize",
    )(keep[0], got[0], keep[1], got[1], norm_gain)


def join_kernel(mine0, got0, mine1, got1, out0, out1):
    for mine, got, out_ref in ((mine0, got0, out0), (mine1, got1, out1)):
        rows = mine.shape[0]
        if rows % 16:
            both = [mine[...].astype(jnp.float32), got[...].astype(jnp.float32)]
            out_ref[...] = jnp.concatenate(both, 0).astype(out_ref.dtype)
        else:
            out_ref[:rows, :] = mine[...]
            out_ref[rows:, :] = got[...]


def join(mine, got):
    rows, width = mine[0].shape
    out = jax.ShapeDtypeStruct((2 * rows, width), mine[0].dtype)
    return pl.pallas_call(
        join_kernel,
        out_shape=(out, out),
        in_specs=[VMEM_SPEC] * 4,
        out_specs=(VMEM_SPEC,) * 2,
        compiler_params=params(4),
        cost_estimate=pl.CostEstimate(
            flops=0, bytes_accessed=16 * rows * width, transcendentals=0
        ),
        name="join",
    )(mine[0], got[0], mine[1], got[1])


def local(
    enc_act,
    down_weight,
    norm_gain,
    text_in_weight,
    modulation_weight,
    key_value_weight,
    timesteps,
    lengths,
    image_queries,
    image_key_values,
):
    devices = lax.axis_size("seq")
    chips = devices // 2
    copies = devices // HEADS
    text_len = enc_act.shape[1]
    img_dev = image_queries.shape[1]
    part_rows = img_dev // copies
    factor = math.log2(math.e) / math.sqrt(HEAD_DIM)
    lanes = orders(chips)
    index = lax.axis_index("seq")
    chip, core = index // 2, index % 2
    place = jnp.stack([position(chip, lanes[0]), position(chip, lanes[1]), core, chip, lengths[0]])
    place = place.astype(jnp.int32)

    win0, kv0 = text_in_weight.T, key_value_weight
    mod0 = modulation_weight.transpose(1, 2, 0)
    time = time_embedding(timesteps)

    rounds = len(lanes[0])
    tie = lax.optimization_barrier

    def exchange(rows):
        return lax.all_to_all(rows, "seq", split_axis=0, concat_axis=0, tiled=True)

    image_key_values, image_queries = tie((image_key_values, image_queries))
    packed = pack(copies, image_queries[0], image_key_values[0, :, 0], image_key_values[0, :, 1])
    act, packed = tie((enc_act[0].T, packed))
    packed = exchange(packed)
    encoded = encoder(lanes, place, act, down_weight)
    keep, got = encoded[::2], [swap(other, 1) for other in encoded[1::2]]
    for step in range(rounds):
        sent, keep = add_halves(keep, got)
        got = [swap(part, 2 * order[step]) for part, order in zip(sent, lanes)]
        if step == 0:
            got, packed = tie((got, packed))

    states = normalize(keep, got, norm_gain[None, :])
    images = []

    for step in reversed(range(rounds)):
        if step == rounds - 1:
            states, held, mod1 = tie((states, win0, mod0))
            win1, mod1 = swap(held, 1), swap(mod1, 1)
        if step == rounds - 2:
            states, held = tie((states, kv0))
            kv1 = swap(held, 1)
            lines = modulation(time, mod0, mod1)
        if step == 0:
            states, packed = tie((states, packed))
            image = image_attention(packed, img_dev, factor, 0, 2)
        got = [swap(state, 2 * order[step]) for state, order in zip(states, lanes)]
        if step == rounds - 2:
            got, lines = tie((got, lines))
        if step:
            states = join(states, got)
    got, image = tie((got, image))
    images += image
    states = [state for pair in zip(states, got) for state in pair]

    blocks = project(lanes, place, states, lines, win0, win1, kv0, kv1)
    keep, sent = [blocks[0], blocks[2]], [blocks[1], blocks[3]]
    for step in range(rounds):
        if step == 0:
            sent, packed = tie((sent, packed))
            image = image_attention(packed, img_dev, factor, 1, 2)
        got = [swap(part, 2 * order[step]) for part, order in zip(sent, lanes)]
        if step == 0:
            got, image = tie((got, image))
            images += image
        if step < rounds - 1:
            sent, keep = add_halves(keep, got)
    parts = [part[0] for pair in zip(keep, got) for part in pair]
    model_width = text_in_weight.shape[1] * devices
    mine, sent = combine(place, parts, chips, text_len // 2, model_width)
    got = swap(sent, 1)

    back = exchange(finish(place, packed, images, mine, got, img_dev, factor))
    attended, text_kv = unpack(copies, part_rows, back)
    return (attended[None], text_kv)


def solution(mesh):
    in_specs = (
        P("dp", None, "seq"),
        P("seq", None),
        P(),
        P(None, "seq"),
        P(None, None, "seq"),
        P("seq", None),
        P("dp"),
        P("dp"),
        P("dp", "seq", None),
        P("dp", "seq", None, None),
    )
    out_specs = (P("dp", "seq", None), P(("dp", "seq"), None))
    return jax.shard_map(local, mesh=mesh, in_specs=in_specs, out_specs=out_specs, check_vma=False)
```

```python
import functools
import math

import jax
import jax.numpy as jnp
from jax import lax
from jax.experimental import pallas as pl
from jax.experimental.pallas import tpu as pltpu
from jax.sharding import PartitionSpec as P

HEAD_DIM = 128
HEADS = 16
TEMB = 256
MIB = 1024 * 1024

epsilon = 1e-06

SMEM_SPEC = pl.BlockSpec(memory_space=pltpu.SMEM)
VMEM_SPEC = pl.BlockSpec(memory_space=pltpu.VMEM)


def params(mib):
    return pltpu.CompilerParams(vmem_limit_bytes=mib * MIB)


def swap(value, mask):
    devices = lax.axis_size("seq")
    return lax.ppermute(value, "seq", [(i, i ^ mask) for i in range(devices)])


def orders(chips):
    bits = [1 << i for i in range(chips.bit_length() - 1)]
    return (bits, [bits[1], bits[0]] + bits[2:])


def position(chip, order):
    last = len(order) - 1
    return sum(((chip >> (bit.bit_length() - 1)) & 1) << (last - i) for i, bit in enumerate(order))


def member(at, order):
    last = len(order) - 1
    return sum(bit for i, bit in enumerate(order) if (at >> (last - i)) & 1)


def time_embedding(timesteps):
    half_width = TEMB // 2
    freqs = jnp.exp(-math.log(10000.0) * jnp.arange(half_width, dtype=jnp.float32) / half_width)
    angles = timesteps.astype(jnp.float32)[:, None] * freqs[None, :]
    embedding = jnp.concatenate([jnp.cos(angles), jnp.sin(angles)], 1)
    return jax.nn.silu(embedding).astype(jnp.bfloat16)


def encoder_kernel(lanes, place_ref, act_ref, weight_ref, *refs):
    outs, lhs_ref = refs[:-1], refs[-1]
    chips, share, width = outs[0].shape
    core = place_ref[2]
    half = chips * share
    first = core == 0
    tile = width // 2
    lhs_ref[...] = act_ref[...].T
    for lane, order in enumerate(lanes):
        own_ref, other_ref = outs[2 * lane], outs[2 * lane + 1]
        for column in range(0, width, tile):
            start = lane * width + column
            result = jnp.dot(
                lhs_ref[...], weight_ref[:, start : start + tile], preferred_element_type=jnp.float32
            )
            own = jnp.where(first, result[:half], result[half:]).astype(own_ref.dtype)
            other = jnp.where(first, result[half:], result[:half]).astype(own_ref.dtype)
            own = own.reshape(chips, share, tile)
            other = other.reshape(chips, share, tile)
            for block in range(chips):
                to = place_ref[lane] ^ position(block, order)
                own_ref[to, :, column : column + tile] = own[block]
                other_ref[to, :, column : column + tile] = other[block]


def encoder(lanes, place, act, weight):
    chips = 1 << len(lanes[0])
    depth, rows = act.shape
    width = weight.shape[1]
    out = jax.ShapeDtypeStruct((chips, rows // 2 // chips, width // 2), jnp.bfloat16)
    return pl.pallas_call(
        functools.partial(encoder_kernel, lanes),
        out_shape=(out,) * 4,
        in_specs=[SMEM_SPEC, VMEM_SPEC, VMEM_SPEC],
        out_specs=(VMEM_SPEC,) * 4,
        scratch_shapes=[pltpu.VMEM((rows, depth), jnp.bfloat16)],
        compiler_params=params(16),
        cost_estimate=pl.CostEstimate(
            flops=2 * rows * depth * width,
            bytes_accessed=2 * (depth * rows + depth * width + rows * width),
            transcendentals=0,
        ),
        name="encoder",
    )(place, act, weight)


def modulation_kernel(time_ref, mod0_ref, mod1_ref, out_ref):
    contract = (((1,), (1,)), ((), ()))
    embedding = jnp.broadcast_to(time_ref[...].astype(jnp.float32), (16, time_ref.shape[1]))
    embedding = embedding.astype(jnp.bfloat16)
    row = lax.broadcasted_iota(jnp.int32, (16, mod0_ref.shape[1]), 0)
    for side, mod in enumerate((mod0_ref, mod1_ref)):
        shift, scale = [
            lax.dot_general(embedding, mod[at], contract, preferred_element_type=jnp.float32)
            for at in range(2)
        ]
        lines = jnp.where(row < 2, 1.0 + scale, shift)
        high = lines.astype(jnp.bfloat16).astype(jnp.float32)
        low = jnp.where(row % 2 == 0, high, lines - high)
        out_ref[side] = jnp.where(row < 4, low, 1.0 + scale)


def modulation(time, mod0, mod1):
    return pl.pallas_call(
        modulation_kernel,
        out_shape=jax.ShapeDtypeStruct((2, 16, mod0.shape[1]), jnp.float32),
        in_specs=[VMEM_SPEC] * 3,
        out_specs=VMEM_SPEC,
        compiler_params=params(4),
        name="modulation",
    )(time, mod0, mod1)


def slot_rows(chips, width):
    per_slot = 2 * 128 // width
    return chips * per_slot, -(-(chips * per_slot + 2) // 16) * 16


def project_kernel(lanes, place_ref, *refs):
    pieces, refs = (refs[:2], refs[2:4]), refs[4:]
    lines_ref, win0, win1, kv0, kv1, *outs, states, proj0, proj1, sums = refs
    chip = place_ref[3]
    half_chips = outs[0].shape[0]
    chips = 2 * half_chips
    rows = proj0.shape[0]
    share = rows // chips
    depth = states.shape[1]
    contract = (((1,), (1,)), ((), ()))
    for lane, order in enumerate(lanes):
        top, low = pieces[lane]
        states[: rows // 2, :] = top[...]
        states[rows // 2 :, :] = low[...]
        span = slice(lane * depth, (lane + 1) * depth)
        for win, proj in ((win0, proj0), (win1, proj1)):
            part = lax.dot_general(
                states[...], win[:, span], contract, preferred_element_type=jnp.float32
            )
            for at in range(chips):
                start = pl.multiple_of((chip ^ member(at, order)) * share, share)
                block = part[at * share : (at + 1) * share]
                if lane == 0:
                    proj[pl.ds(start, share), :] = block
                else:
                    proj[pl.ds(start, share), :] += block
    value0, value1 = proj0[...], proj1[...]
    first = jnp.sum(value0, 1, keepdims=True) + jnp.sum(value1, 1, keepdims=True)
    second = jnp.sum(value0 * value0, 1, keepdims=True) + jnp.sum(value1 * value1, 1, keepdims=True)
    lane = lax.broadcasted_iota(jnp.int32, sums.shape, 1)
    sums[...] = jnp.where(lane == 0, first, second).T
    left = []
    for side, value in enumerate((value0, value1)):
        lines = lines_ref[side]
        row = lax.broadcasted_iota(jnp.int32, lines.shape, 0)
        lines, scale = jnp.where(row < 4, lines, 0.0), lines[4:5]
        left.append(jnp.concatenate([value * scale, lines], 0).astype(jnp.bfloat16))
    width = outs[0].shape[2]
    slots, extra = slot_rows(chips, width)
    per_slot = slots // chips
    row = lax.broadcasted_iota(jnp.int32, (extra, width), 0)
    column = lax.broadcasted_iota(jnp.int32, (extra, width), 1)
    half = kv0.shape[1] // 2
    for lane, order in enumerate(lanes):
        line = sums[lane : lane + 1, :]
        high = line.astype(jnp.bfloat16).astype(jnp.float32)
        low = line - high
        if per_slot == 1:
            line = jnp.concatenate([high, low], 1)
        else:
            line = jnp.where(row % 2 == 0, high, low)
        line = jnp.where(row // per_slot == chip, line, 0.0)
        for at in reversed(range(chips)):
            out_ref, to = outs[2 * lane + at // half_chips], at % half_chips
            start = lane * half + (chip ^ member(at, order)) * width
            columns = pl.ds(pl.multiple_of(start, width), width)
            value = jnp.dot(left[0], kv0[:, columns], preferred_element_type=jnp.float32)
            value += jnp.dot(left[1], kv1[:, columns], preferred_element_type=jnp.float32)
            out_ref[to, :rows, :] = value[:rows].astype(out_ref.dtype)
            below = jnp.where(row == slots, value[rows : rows + 1] + value[rows + 1 : rows + 2], line)
            below = jnp.where(
                row == slots + 1, value[rows + 2 : rows + 3] + value[rows + 3 : rows + 4], below
            )
            out_ref[to, rows:, :] = below.astype(out_ref.dtype)


def project(lanes, place, pieces, lines, win0, win1, kv0, kv1):
    chips = 1 << len(lanes[0])
    rows = 2 * pieces[0].shape[0]
    features, depth = win0.shape
    total = kv0.shape[1]
    width = total // 2 // chips
    extra = slot_rows(chips, width)[1]
    out = jax.ShapeDtypeStruct((chips // 2, rows + extra, width), jnp.bfloat16)
    return pl.pallas_call(
        functools.partial(project_kernel, lanes),
        out_shape=(out,) * 4,
        in_specs=[SMEM_SPEC] + [VMEM_SPEC] * 9,
        out_specs=(VMEM_SPEC,) * 4,
        scratch_shapes=[
            pltpu.VMEM((rows, depth // 2), jnp.bfloat16),
            pltpu.VMEM((rows, features), jnp.float32),
            pltpu.VMEM((rows, features), jnp.float32),
            pltpu.VMEM((rows, 128), jnp.float32),
        ],
        compiler_params=params(14),
        cost_estimate=pl.CostEstimate(
            flops=4 * rows * features * (depth + total),
            bytes_accessed=2 * (rows * depth + 2 * features * (depth + total) + rows * total),
            transcendentals=0,
        ),
        name="project",
    )(place, *pieces, lines, win0, win1, kv0, kv1)


def combine_kernel(chips, model_width, place_ref, *refs):
    refs, mine_ref, sent_ref = refs[:4], refs[4], refs[5]
    core = place_ref[2]
    rows = mine_ref.shape[0]
    width = refs[0].shape[1]
    slots = slot_rows(chips, width)[0]
    totals = [
        refs[2 * lane][...].astype(jnp.float32) + refs[2 * lane + 1][...].astype(jnp.float32)
        for lane in range(2)
    ]
    sums = []
    for total in totals:
        line = jnp.sum(total[rows : rows + slots], 0, keepdims=True)
        if width > 128:
            line = line[:, :128] + line[:, 128:]
        sums.append(line)
    mean_val = sums[0] / model_width
    scale = lax.rsqrt(sums[1] / model_width - mean_val * mean_val + epsilon)
    mean_val = jnp.broadcast_to(mean_val, (rows, rows)).T[:, 0:1]
    scale = jnp.broadcast_to(scale, (rows, rows)).T[:, 0:1]
    texts = []
    for total in totals:
        text = (total[:rows] - mean_val * total[rows + slots : rows + slots + 1]) * scale
        texts.append(text + total[rows + slots + 1 : rows + slots + 2])
    for part, text in enumerate(texts):
        span = slice(part * HEAD_DIM, (part + 1) * HEAD_DIM)
        if width > HEAD_DIM:
            low, high = text[:, :HEAD_DIM], text[:, HEAD_DIM:]
            mine_ref[:, span] = jnp.where(core == 0, low, high).astype(mine_ref.dtype)
            sent_ref[:, span] = jnp.where(core == 0, high, low).astype(mine_ref.dtype)
        else:
            mine_ref[:, span] = text.astype(mine_ref.dtype)
            sent_ref[:, span] = text.astype(mine_ref.dtype)


def combine(place, parts, chips, rows, model_width):
    out = jax.ShapeDtypeStruct((rows, 2 * HEAD_DIM), jnp.bfloat16)
    return pl.pallas_call(
        functools.partial(combine_kernel, chips, model_width),
        out_shape=(out, out),
        in_specs=[SMEM_SPEC] + [VMEM_SPEC] * 4,
        out_specs=(VMEM_SPEC, VMEM_SPEC),
        compiler_params=params(4),
        cost_estimate=pl.CostEstimate(
            flops=8 * rows * 512, bytes_accessed=12 * rows * 512, transcendentals=0
        ),
        name="combine",
    )(place, *parts)


def pack_kernel(copies, rows_ref, out_ref):
    count = out_ref.shape[1]
    for device in range(out_ref.shape[0]):
        head, copy = device // copies, device % copies
        span = slice(head * HEAD_DIM, (head + 1) * HEAD_DIM)
        start = copy * count if count < rows_ref.shape[0] else 0
        out_ref[device] = rows_ref[start : start + count, span]


def pack(copies, rows, count):
    return pl.pallas_call(
        functools.partial(pack_kernel, copies),
        out_shape=jax.ShapeDtypeStruct((HEADS * copies, count, HEAD_DIM), jnp.bfloat16),
        in_specs=[VMEM_SPEC],
        out_specs=VMEM_SPEC,
        compiler_params=params(8),
        cost_estimate=pl.CostEstimate(flops=0, bytes_accessed=4 * rows.size, transcendentals=0),
        name="pack",
    )(rows)


def split_kernel(copies, place_ref, queries_ref, values_ref, *outs):
    chip, core = place_ref[3], place_ref[2]
    img_dev = values_ref.shape[0]
    part_rows = img_dev // copies
    for mask, out_ref in enumerate(outs):
        for side in range(2):
            device = 2 * (chip ^ mask) + (core ^ side)
            head, copy = device // copies, device % copies
            span = pl.ds(pl.multiple_of(head * HEAD_DIM, HEAD_DIM), HEAD_DIM)
            rows = pl.ds(pl.multiple_of(copy * part_rows, part_rows), part_rows)
            out_ref[side, :img_dev, :] = values_ref[:, span]
            out_ref[side, img_dev:, :] = queries_ref[rows, span]


def split(chips, copies, place, queries, values):
    img_dev = values.shape[0]
    rows = img_dev + img_dev // copies
    out = jax.ShapeDtypeStruct((2, rows, HEAD_DIM), jnp.bfloat16)
    return pl.pallas_call(
        functools.partial(split_kernel, copies),
        out_shape=(out,) * chips,
        in_specs=[SMEM_SPEC] + [VMEM_SPEC] * 2,
        out_specs=(VMEM_SPEC,) * chips,
        compiler_params=params(6),
        cost_estimate=pl.CostEstimate(
            flops=0, bytes_accessed=8 * chips * rows * HEAD_DIM, transcendentals=0
        ),
        name="split",
    )(place, queries, values)


def gather_kernel(*refs):
    for at, piece in enumerate(refs[:-1]):
        refs[-1][at] = piece[1]


def gather_other(pieces):
    shape = (len(pieces),) + pieces[0].shape[1:]
    return pl.pallas_call(
        gather_kernel,
        out_shape=jax.ShapeDtypeStruct(shape, pieces[0].dtype),
        in_specs=[VMEM_SPEC] * len(pieces),
        out_specs=VMEM_SPEC,
        compiler_params=params(6),
        cost_estimate=pl.CostEstimate(
            flops=0, bytes_accessed=2 * len(pieces) * pieces[0].size, transcendentals=0
        ),
        name="gather_other",
    )(*pieces)


def by_distance(pieces, passed_ref):
    views = [(piece.at[0], passed_ref.at[at]) for at, piece in enumerate(pieces)]
    return [view for pair in views for view in pair]


def unpack_kernel(copies, part_rows, blocks_ref, attended_ref, text_ref):
    share = text_ref.shape[0]
    half = text_ref.shape[1] // 2
    for device in range(blocks_ref.shape[0]):
        head, copy = device // copies, device % copies
        start = head * HEAD_DIM
        rows = slice(copy * part_rows, (copy + 1) * part_rows)
        attended_ref[rows, start : start + HEAD_DIM] = blocks_ref[device, :part_rows, :]
        if copy == 0:
            block = blocks_ref[device, part_rows:, :].astype(jnp.float32)
            text_ref[:, start : start + HEAD_DIM] = block[:share].astype(text_ref.dtype)
            start += half
            text_ref[:, start : start + HEAD_DIM] = block[share:].astype(text_ref.dtype)


def unpack(copies, part_rows, blocks):
    share = (blocks.shape[1] - part_rows) // 2
    return pl.pallas_call(
        functools.partial(unpack_kernel, copies, part_rows),
        out_shape=(
            jax.ShapeDtypeStruct((part_rows * copies, HEADS * HEAD_DIM), jnp.bfloat16),
            jax.ShapeDtypeStruct((share, 2 * HEADS * HEAD_DIM), jnp.bfloat16),
        ),
        in_specs=[VMEM_SPEC],
        out_specs=(VMEM_SPEC, VMEM_SPEC),
        compiler_params=params(4),
        name="unpack",
    )(blocks)


def image_kernel(factor, call, place_ref, keys_ref, *refs):
    *pieces, passed_ref, sum_ref, top_ref, wide_ref = refs
    blocks = by_distance(pieces, passed_ref)
    me = 2 * place_ref[3] + place_ref[2]
    img_dev = keys_ref.shape[0] // len(blocks)
    wide_ref[:, HEAD_DIM:] = jnp.ones((wide_ref.shape[0], HEAD_DIM), wide_ref.dtype)
    for at, block in enumerate(blocks):
        start = pl.multiple_of((me ^ at) * img_dev, img_dev)
        wide_ref[pl.ds(start, img_dev), :HEAD_DIM] = block[:img_dev, :]
    group = max(1, 256 // (pieces[0].shape[1] - img_dev))
    rows = 256
    contract = (((1,), (1,)), ((), ()))
    count = sum_ref.shape[0]
    for start in range(0, count, rows):
        span = slice(start, start + rows)
        at = (call * count + start) // rows * group
        queries = jnp.concatenate([block[img_dev:, :] for block in blocks[at : at + group]], 0)
        scores = lax.dot_general(queries, keys_ref[...], contract, preferred_element_type=jnp.float32)
        scores = scores * factor
        top = jnp.max(scores, 1, keepdims=True)
        weights = jnp.exp2(scores - top).astype(jnp.bfloat16)
        sum_ref[span, :] = jnp.dot(weights, wide_ref[...], preferred_element_type=jnp.float32)
        top_ref[span, :] = jnp.broadcast_to(top, (rows, HEAD_DIM))


def image_attention(place, keys, pieces, passed, factor, call, calls):
    total = keys.shape[0]
    part_rows = passed.shape[1] - total // (2 * len(pieces))
    count = 2 * len(pieces) * part_rows // calls
    return pl.pallas_call(
        functools.partial(image_kernel, factor, call),
        out_shape=(
            jax.ShapeDtypeStruct((count, 2 * HEAD_DIM), jnp.float32),
            jax.ShapeDtypeStruct((count, HEAD_DIM), jnp.float32),
        ),
        in_specs=[SMEM_SPEC] + [VMEM_SPEC] * (len(pieces) + 2),
        out_specs=(VMEM_SPEC, VMEM_SPEC),
        scratch_shapes=[pltpu.VMEM((total, 2 * HEAD_DIM), jnp.bfloat16)],
        compiler_params=params(14),
        cost_estimate=pl.CostEstimate(
            flops=4 * count * total * HEAD_DIM,
            bytes_accessed=4 * total * HEAD_DIM + 10 * count * HEAD_DIM,
            transcendentals=count * total,
        ),
        name="image_attention",
    )(place, keys, *pieces, passed)


def finish_kernel(factor, calls, img_dev, place_ref, *refs):
    *pieces, passed_ref = refs[: -3 - 2 * calls]
    images, (mine_ref, got_ref, out_ref) = refs[-3 - 2 * calls : -3], refs[-3:]
    blocks = by_distance(pieces, passed_ref)
    me = 2 * place_ref[3] + place_ref[2]
    core, valid = place_ref[2], place_ref[4]
    devices = out_ref.shape[0]
    part_rows = passed_ref.shape[1] - img_dev
    half = mine_ref.shape[0]
    contract = (((1,), (1,)), ((), ()))
    mine, got = mine_ref[...], got_ref[...]
    keys = jnp.concatenate([mine[:, :HEAD_DIM], got[:, :HEAD_DIM]], 0)
    values = jnp.concatenate([mine[:, HEAD_DIM:], got[:, HEAD_DIM:]], 0)
    values = jnp.concatenate([values, jnp.ones(values.shape, values.dtype)], 1)
    lane = lax.broadcasted_iota(jnp.int32, (1, 2 * half), 1)
    text_position = jnp.where((lane >= half) == (core == 0), half, 0) + lane % half
    bias = jnp.where(text_position < valid, 0.0, -jnp.inf)
    group = max(1, 512 // part_rows)
    rows = group * part_rows
    each = devices // group // calls
    for step in range(devices // group):
        sum_ref, top_ref = images[2 * (step // each)], images[2 * (step // each) + 1]
        span = slice(step % each * rows, (step % each + 1) * rows)
        queries = blocks[step * group : (step + 1) * group]
        queries = jnp.concatenate([block[img_dev:, :] for block in queries], 0)
        scores = lax.dot_general(queries, keys, contract, preferred_element_type=jnp.float32)
        scores = scores * factor + bias
        before = top_ref[span, :]
        top = jnp.maximum(before, jnp.max(scores, 1, keepdims=True))
        rescale = jnp.exp2(before - top)
        weights = jnp.exp2(scores - jnp.concatenate([top] * (2 * half // HEAD_DIM), 1))
        total = jnp.dot(weights.astype(jnp.bfloat16), values, preferred_element_type=jnp.float32)
        mixed = sum_ref[span, :HEAD_DIM] * rescale + total[:, :HEAD_DIM]
        total = sum_ref[span, HEAD_DIM:] * rescale + total[:, HEAD_DIM:]
        mixed = (mixed / total).astype(out_ref.dtype)
        for at in range(group):
            to = me ^ (step * group + at)
            out_ref[to, :part_rows, :] = mixed[at * part_rows : (at + 1) * part_rows]
    low = jnp.where(core == 0, mine.astype(jnp.float32), got.astype(jnp.float32))
    high = jnp.where(core == 0, got.astype(jnp.float32), mine.astype(jnp.float32))
    share = 2 * half // devices
    for device in range(devices):
        source = low if device < devices // 2 else high
        start = device * share % half
        block = source[start : start + share]
        block = jnp.concatenate([block[:, :HEAD_DIM], block[:, HEAD_DIM:]], 0)
        out_ref[device, part_rows:, :] = block.astype(out_ref.dtype)


def finish(place, pieces, passed, images, mine, got, img_dev, factor):
    devices, part_rows = 2 * len(pieces), passed.shape[1] - img_dev
    count = devices * part_rows
    share = 2 * mine.shape[0] // devices
    return pl.pallas_call(
        functools.partial(finish_kernel, factor, len(images) // 2, img_dev),
        out_shape=jax.ShapeDtypeStruct((devices, part_rows + 2 * share, HEAD_DIM), jnp.bfloat16),
        in_specs=[SMEM_SPEC] + [VMEM_SPEC] * (len(pieces) + len(images) + 3),
        out_specs=VMEM_SPEC,
        compiler_params=params(10),
        cost_estimate=pl.CostEstimate(
            flops=4 * count * 2 * mine.shape[0] * HEAD_DIM,
            bytes_accessed=12 * count * HEAD_DIM,
            transcendentals=count * 2 * mine.shape[0],
        ),
        name="finish",
    )(place, *pieces, passed, *images, mine, got)


def add_kernel(*refs):
    ins, outs = refs[:4], refs[4:]
    for lane in range(2):
        mine, got = ins[2 * lane], ins[2 * lane + 1]
        half = mine.shape[0] // 2
        outs[2 * lane][...] = (
            mine[half:].astype(jnp.float32) + got[half:].astype(jnp.float32)
        ).astype(jnp.bfloat16)
        outs[2 * lane + 1][...] = mine[:half].astype(jnp.float32) + got[:half].astype(jnp.float32)


def add_halves(mine, got):
    shape = (mine[0].shape[0] // 2,) + mine[0].shape[1:]
    outs = (jax.ShapeDtypeStruct(shape, jnp.bfloat16), jax.ShapeDtypeStruct(shape, jnp.float32))
    sent0, keep0, sent1, keep1 = pl.pallas_call(
        add_kernel,
        out_shape=outs * 2,
        in_specs=[VMEM_SPEC] * 4,
        out_specs=(VMEM_SPEC,) * 4,
        compiler_params=params(6),
        cost_estimate=pl.CostEstimate(
            flops=2 * mine[0].size, bytes_accessed=12 * mine[0].size, transcendentals=0
        ),
        name="add_halves",
    )(mine[0], got[0], mine[1], got[1])
    return [sent0, sent1], [keep0, keep1]


def total_kernel(mine0, got0, mine1, got1, out0, out1):
    for mine, got, out_ref in ((mine0, got0, out0), (mine1, got1, out1)):
        out_ref[...] = (mine[...] + got[...].astype(jnp.float32)).astype(out_ref.dtype)


def add_all(mine, got):
    out = jax.ShapeDtypeStruct(mine[0].shape, jnp.bfloat16)
    return pl.pallas_call(
        total_kernel,
        out_shape=(out, out),
        in_specs=[VMEM_SPEC] * 4,
        out_specs=(VMEM_SPEC,) * 2,
        compiler_params=params(4),
        cost_estimate=pl.CostEstimate(
            flops=2 * mine[0].size, bytes_accessed=16 * mine[0].size, transcendentals=0
        ),
        name="add_all",
    )(mine[0], got[0], mine[1], got[1])


def norm_kernel(mine0, got0, mine1, got1, gain_ref, out0, out1):
    share, width = mine0.shape[1:]
    for at in range(2):
        totals = [
            mine[at].astype(jnp.float32) + got[1 - at].astype(jnp.float32)
            for mine, got in ((mine0, got0), (mine1, got1))
        ]
        square = sum(jnp.sum(total * total, 1, keepdims=True) for total in totals)
        scale_rows = lax.rsqrt(square / (2 * width) + epsilon)
        for lane, (total, out_ref) in enumerate(zip(totals, (out0, out1))):
            gain = gain_ref[:, lane * width : (lane + 1) * width].astype(jnp.float32)
            out_ref[at] = (total * scale_rows * gain).astype(out_ref.dtype)


def normalize(mine, got, norm_gain):
    out = jax.ShapeDtypeStruct(mine[0].shape, jnp.bfloat16)
    states = pl.pallas_call(
        norm_kernel,
        out_shape=(out, out),
        in_specs=[VMEM_SPEC] * 5,
        out_specs=(VMEM_SPEC,) * 2,
        compiler_params=params(4),
        cost_estimate=pl.CostEstimate(
            flops=8 * mine[0].size, bytes_accessed=16 * mine[0].size, transcendentals=0
        ),
        name="normalize",
    )(mine[0], got[0], mine[1], got[1], norm_gain)
    return [part.reshape(-1, part.shape[2]) for part in states]


def join_kernel(mine0, got0, mine1, got1, out0, out1):
    for mine, got, out_ref in ((mine0, got0, out0), (mine1, got1, out1)):
        rows = mine.shape[0]
        if rows % 16:
            both = [mine[...].astype(jnp.float32), got[...].astype(jnp.float32)]
            out_ref[...] = jnp.concatenate(both, 0).astype(out_ref.dtype)
        else:
            out_ref[:rows, :] = mine[...]
            out_ref[rows:, :] = got[...]


def join(mine, got):
    rows, width = mine[0].shape
    out = jax.ShapeDtypeStruct((2 * rows, width), mine[0].dtype)
    return pl.pallas_call(
        join_kernel,
        out_shape=(out, out),
        in_specs=[VMEM_SPEC] * 4,
        out_specs=(VMEM_SPEC,) * 2,
        compiler_params=params(4),
        cost_estimate=pl.CostEstimate(
            flops=0, bytes_accessed=16 * rows * width, transcendentals=0
        ),
        name="join",
    )(mine[0], got[0], mine[1], got[1])


def local(
    enc_act,
    down_weight,
    norm_gain,
    text_in_weight,
    modulation_weight,
    key_value_weight,
    timesteps,
    lengths,
    image_queries,
    image_key_values,
):
    devices = lax.axis_size("seq")
    chips = devices // 2
    copies = devices // HEADS
    text_len = enc_act.shape[1]
    img_dev = image_queries.shape[1]
    part_rows = img_dev // copies
    factor = math.log2(math.e) / math.sqrt(HEAD_DIM)
    lanes = orders(chips)
    index = lax.axis_index("seq")
    chip, core = index // 2, index % 2
    place = jnp.stack([position(chip, lanes[0]), position(chip, lanes[1]), core, chip, lengths[0]])
    place = place.astype(jnp.int32)

    win0, kv0 = text_in_weight.T, key_value_weight
    mod0 = modulation_weight.transpose(1, 2, 0)
    time = time_embedding(timesteps)

    rounds = len(lanes[0])
    tie = lax.optimization_barrier

    def exchange(rows):
        return lax.all_to_all(rows, "seq", split_axis=0, concat_axis=0, tiled=True)

    image_key_values, image_queries = tie((image_key_values, image_queries))
    act, keys = tie((enc_act[0].T, pack(copies, image_key_values[0, :, 0], img_dev)))
    keys = exchange(keys)
    pieces = {}

    def beside(chain, masks):
        chain, held = tie((chain, [pieces[mask] for mask in masks]))
        pieces.update((mask, swap(piece, 2 * mask)) for mask, piece in zip(masks, held))
        return chain

    def arrived(chain, masks):
        chain, held = tie((chain, [pieces[mask] for mask in masks]))
        pieces.update(zip(masks, held))
        return chain

    encoded = list(encoder(lanes, place, act, down_weight))
    encoded[1::2], keys = tie((encoded[1::2], keys))
    keep, got = encoded[::2], [swap(other, 1) for other in encoded[1::2]]
    crossing = list(range(chips // 2, chips))
    for step in range(rounds - 1):
        sent, keep = add_halves(keep, got)
        if step == 0:
            sent, image_queries, image_key_values = tie((sent, image_queries, image_key_values))
            held = split(chips, copies, place, image_queries[0], image_key_values[0, :, 1])
            pieces.update(enumerate(held))
        masks = crossing[step : step + 1]
        sent = beside(sent, masks)
        got = [swap(part, 2 * order[step]) for part, order in zip(sent, lanes)]
        got = arrived(got, masks)
        if step == 0:
            sent, held = tie((sent, win0))
            win1 = swap(held, 1)
            got, win1 = tie((got, win1))
        if step == 1:
            sent, held, mod1 = tie((sent, kv0, mod0))
            kv1, mod1 = swap(held, 1), swap(mod1, 1)
            got, kv1, mod1 = tie((got, kv1, mod1))
    summed = add_all(keep, got)
    masks = list(range(1, chips // 2))
    summed = beside(summed, masks)
    got = [swap(part, 2 * order[-1]) for part, order in zip(summed, lanes)]
    lines = modulation(time, mod0, mod1)
    got, lines = tie((arrived(got, masks), lines))

    states = normalize(summed, got, norm_gain[None, :])
    for step in reversed(range(rounds - 1)):
        masks = crossing[rounds:] if step == 0 else crossing[rounds - 1 : rounds] * (step == 1)
        states = beside(states, masks)
        got = [swap(state, 2 * order[step]) for state, order in zip(states, lanes)]
        got = arrived(got, masks)
        if step:
            states = join(states, got)
    states = [state for pair in zip(states, got) for state in pair]

    blocks = project(lanes, place, states, lines, win0, win1, kv0, kv1)
    keep, sent = [blocks[0], blocks[2]], [blocks[1], blocks[3]]
    images = []
    for step in range(rounds):
        got = [swap(part, 2 * order[step]) for part, order in zip(sent, lanes)]
        if step == 0:
            pieces = [pieces[mask] for mask in range(chips)]
            sent, pieces = tie((sent, pieces))
            passed = swap(gather_other(pieces), 1)
            got, passed = tie((got, passed))
            keys = keys.reshape(-1, HEAD_DIM)
        elif step <= 2:
            sent, passed = tie((sent, passed))
            image = image_attention(place, keys, pieces, passed, factor, step - 1, 2)
            got, image = tie((got, image))
            images += image
        if step < rounds - 1:
            sent, keep = add_halves(keep, got)
    parts = [part[0] for pair in zip(keep, got) for part in pair]
    model_width = text_in_weight.shape[1] * devices
    mine, sent = combine(place, parts, chips, text_len // 2, model_width)
    got = swap(sent, 1)

    back = exchange(finish(place, pieces, passed, images, mine, got, img_dev, factor))
    attended, text_kv = unpack(copies, part_rows, back)
    return (attended[None], text_kv)


def solution(mesh):
    in_specs = (
        P("dp", None, "seq"),
        P("seq", None),
        P(),
        P(None, "seq"),
        P(None, None, "seq"),
        P("seq", None),
        P("dp"),
        P("dp"),
        P("dp", "seq", None),
        P("dp", "seq", None, None),
    )
    out_specs = (P("dp", "seq", None), P(("dp", "seq"), None))
    return jax.shard_map(local, mesh=mesh, in_specs=in_specs, out_specs=out_specs, check_vma=False)
```

```python
import functools
import math

import jax
import jax.numpy as jnp
from jax import lax
from jax.experimental import pallas as pl
from jax.experimental.pallas import tpu as pltpu
from jax.sharding import PartitionSpec as P

HEAD_DIM = 128
HEADS = 16
TEMB = 256
MIB = 1024 * 1024

epsilon = 1e-06

SMEM_SPEC = pl.BlockSpec(memory_space=pltpu.SMEM)
VMEM_SPEC = pl.BlockSpec(memory_space=pltpu.VMEM)


def params(mib):
    return pltpu.CompilerParams(vmem_limit_bytes=mib * MIB)


def swap(value, mask):
    devices = lax.axis_size("seq")
    return lax.ppermute(value, "seq", [(i, i ^ mask) for i in range(devices)])


def orders(chips):
    bits = [1 << i for i in range(chips.bit_length() - 1)]
    return (bits, [bits[1], bits[0]] + bits[2:])


def position(chip, order):
    last = len(order) - 1
    return sum(((chip >> (bit.bit_length() - 1)) & 1) << (last - i) for i, bit in enumerate(order))


def member(at, order):
    last = len(order) - 1
    return sum(bit for i, bit in enumerate(order) if (at >> (last - i)) & 1)


def time_embedding(timesteps):
    half_width = TEMB // 2
    freqs = jnp.exp(-math.log(10000.0) * jnp.arange(half_width, dtype=jnp.float32) / half_width)
    angles = timesteps.astype(jnp.float32)[:, None] * freqs[None, :]
    embedding = jnp.concatenate([jnp.cos(angles), jnp.sin(angles)], 1)
    return jax.nn.silu(embedding).astype(jnp.bfloat16)


def encoder_kernel(lanes, place_ref, act_ref, weight_ref, *refs):
    outs, lhs_ref = refs[:-1], refs[-1]
    chips, share, width = outs[0].shape
    core = place_ref[2]
    half = chips * share
    first = core == 0
    tile = width // 2
    lhs_ref[...] = act_ref[...].T
    for lane, order in enumerate(lanes):
        own_ref, other_ref = outs[2 * lane], outs[2 * lane + 1]
        for column in range(0, width, tile):
            start = lane * width + column
            result = jnp.dot(
                lhs_ref[...], weight_ref[:, start : start + tile], preferred_element_type=jnp.float32
            )
            own = jnp.where(first, result[:half], result[half:]).astype(own_ref.dtype)
            other = jnp.where(first, result[half:], result[:half]).astype(own_ref.dtype)
            own = own.reshape(chips, share, tile)
            other = other.reshape(chips, share, tile)
            for block in range(chips):
                to = place_ref[lane] ^ position(block, order)
                own_ref[to, :, column : column + tile] = own[block]
                other_ref[to, :, column : column + tile] = other[block]


def encoder(lanes, place, act, weight):
    chips = 1 << len(lanes[0])
    depth, rows = act.shape
    width = weight.shape[1]
    out = jax.ShapeDtypeStruct((chips, rows // 2 // chips, width // 2), jnp.bfloat16)
    return pl.pallas_call(
        functools.partial(encoder_kernel, lanes),
        out_shape=(out,) * 4,
        in_specs=[SMEM_SPEC, VMEM_SPEC, VMEM_SPEC],
        out_specs=(VMEM_SPEC,) * 4,
        scratch_shapes=[pltpu.VMEM((rows, depth), jnp.bfloat16)],
        compiler_params=params(16),
        cost_estimate=pl.CostEstimate(
            flops=2 * rows * depth * width,
            bytes_accessed=2 * (depth * rows + depth * width + rows * width),
            transcendentals=0,
        ),
        name="encoder",
    )(place, act, weight)


def modulation_kernel(time_ref, mod0_ref, mod1_ref, out_ref):
    contract = (((1,), (1,)), ((), ()))
    embedding = jnp.broadcast_to(time_ref[...].astype(jnp.float32), (16, time_ref.shape[1]))
    embedding = embedding.astype(jnp.bfloat16)
    row = lax.broadcasted_iota(jnp.int32, (16, mod0_ref.shape[1]), 0)
    for side, mod in enumerate((mod0_ref, mod1_ref)):
        shift, scale = [
            lax.dot_general(embedding, mod[at], contract, preferred_element_type=jnp.float32)
            for at in range(2)
        ]
        lines = jnp.where(row < 2, 1.0 + scale, shift)
        high = lines.astype(jnp.bfloat16).astype(jnp.float32)
        low = jnp.where(row % 2 == 0, high, lines - high)
        out_ref[side] = jnp.where(row < 4, low, 1.0 + scale)


def modulation(time, mod0, mod1):
    return pl.pallas_call(
        modulation_kernel,
        out_shape=jax.ShapeDtypeStruct((2, 16, mod0.shape[1]), jnp.float32),
        in_specs=[VMEM_SPEC] * 3,
        out_specs=VMEM_SPEC,
        compiler_params=params(4),
        name="modulation",
    )(time, mod0, mod1)


def slot_rows(chips, width):
    per_slot = 2 * 128 // width
    return chips * per_slot, -(-(chips * per_slot + 2) // 16) * 16


def project_kernel(lanes, place_ref, *refs):
    pieces, refs = (refs[:2], refs[2:4]), refs[4:]
    lines_ref, win0, win1, kv0, kv1, *outs, states, proj0, proj1, sums = refs
    chip = place_ref[3]
    half_chips = outs[0].shape[0]
    chips = 2 * half_chips
    rows = proj0.shape[0]
    share = rows // chips
    depth = states.shape[1]
    contract = (((1,), (1,)), ((), ()))
    for lane, order in enumerate(lanes):
        top, low = pieces[lane]
        states[: rows // 2, :] = top[...]
        states[rows // 2 :, :] = low[...]
        span = slice(lane * depth, (lane + 1) * depth)
        for win, proj in ((win0, proj0), (win1, proj1)):
            part = lax.dot_general(
                states[...], win[:, span], contract, preferred_element_type=jnp.float32
            )
            for at in range(chips):
                start = pl.multiple_of((chip ^ member(at, order)) * share, share)
                block = part[at * share : (at + 1) * share]
                if lane == 0:
                    proj[pl.ds(start, share), :] = block
                else:
                    proj[pl.ds(start, share), :] += block
    value0, value1 = proj0[...], proj1[...]
    first = jnp.sum(value0, 1, keepdims=True) + jnp.sum(value1, 1, keepdims=True)
    second = jnp.sum(value0 * value0, 1, keepdims=True) + jnp.sum(value1 * value1, 1, keepdims=True)
    lane = lax.broadcasted_iota(jnp.int32, sums.shape, 1)
    sums[...] = jnp.where(lane == 0, first, second).T
    left = []
    for side, value in enumerate((value0, value1)):
        lines = lines_ref[side]
        row = lax.broadcasted_iota(jnp.int32, lines.shape, 0)
        lines, scale = jnp.where(row < 4, lines, 0.0), lines[4:5]
        left.append(jnp.concatenate([value * scale, lines], 0).astype(jnp.bfloat16))
    width = outs[0].shape[2]
    slots, extra = slot_rows(chips, width)
    per_slot = slots // chips
    row = lax.broadcasted_iota(jnp.int32, (extra, width), 0)
    column = lax.broadcasted_iota(jnp.int32, (extra, width), 1)
    half = kv0.shape[1] // 2
    for lane, order in enumerate(lanes):
        line = sums[lane : lane + 1, :]
        high = line.astype(jnp.bfloat16).astype(jnp.float32)
        low = line - high
        if per_slot == 1:
            line = jnp.concatenate([high, low], 1)
        else:
            line = jnp.where(row % 2 == 0, high, low)
        line = jnp.where(row // per_slot == chip, line, 0.0)
        for at in reversed(range(chips)):
            out_ref, to = outs[2 * lane + at // half_chips], at % half_chips
            start = lane * half + (chip ^ member(at, order)) * width
            columns = pl.ds(pl.multiple_of(start, width), width)
            value = jnp.dot(left[0], kv0[:, columns], preferred_element_type=jnp.float32)
            value += jnp.dot(left[1], kv1[:, columns], preferred_element_type=jnp.float32)
            out_ref[to, :rows, :] = value[:rows].astype(out_ref.dtype)
            below = jnp.where(row == slots, value[rows : rows + 1] + value[rows + 1 : rows + 2], line)
            below = jnp.where(
                row == slots + 1, value[rows + 2 : rows + 3] + value[rows + 3 : rows + 4], below
            )
            out_ref[to, rows:, :] = below.astype(out_ref.dtype)


def project(lanes, place, pieces, lines, win0, win1, kv0, kv1):
    chips = 1 << len(lanes[0])
    rows = 2 * pieces[0].shape[0]
    features, depth = win0.shape
    total = kv0.shape[1]
    width = total // 2 // chips
    extra = slot_rows(chips, width)[1]
    out = jax.ShapeDtypeStruct((chips // 2, rows + extra, width), jnp.bfloat16)
    return pl.pallas_call(
        functools.partial(project_kernel, lanes),
        out_shape=(out,) * 4,
        in_specs=[SMEM_SPEC] + [VMEM_SPEC] * 9,
        out_specs=(VMEM_SPEC,) * 4,
        scratch_shapes=[
            pltpu.VMEM((rows, depth // 2), jnp.bfloat16),
            pltpu.VMEM((rows, features), jnp.float32),
            pltpu.VMEM((rows, features), jnp.float32),
            pltpu.VMEM((rows, 128), jnp.float32),
        ],
        compiler_params=params(14),
        cost_estimate=pl.CostEstimate(
            flops=4 * rows * features * (depth + total),
            bytes_accessed=2 * (rows * depth + 2 * features * (depth + total) + rows * total),
            transcendentals=0,
        ),
        name="project",
    )(place, *pieces, lines, win0, win1, kv0, kv1)


def combine_kernel(chips, model_width, place_ref, *refs):
    keep0, keep1, came_ref, mine_ref, sent_ref = refs
    core = place_ref[2]
    rows = mine_ref.shape[0]
    width = keep0.shape[2]
    slots = slot_rows(chips, width)[0]
    totals = [keep[0] + came_ref[lane, 0].astype(jnp.float32) for lane, keep in enumerate((keep0, keep1))]
    sums = []
    for total in totals:
        line = jnp.sum(total[rows : rows + slots], 0, keepdims=True)
        if width > 128:
            line = line[:, :128] + line[:, 128:]
        sums.append(line)
    mean_val = sums[0] / model_width
    scale = lax.rsqrt(sums[1] / model_width - mean_val * mean_val + epsilon)
    mean_val = jnp.broadcast_to(mean_val, (rows, rows)).T[:, 0:1]
    scale = jnp.broadcast_to(scale, (rows, rows)).T[:, 0:1]
    texts = []
    for total in totals:
        text = (total[:rows] - mean_val * total[rows + slots : rows + slots + 1]) * scale
        texts.append(text + total[rows + slots + 1 : rows + slots + 2])
    for part, text in enumerate(texts):
        span = slice(part * HEAD_DIM, (part + 1) * HEAD_DIM)
        if width > HEAD_DIM:
            low, high = text[:, :HEAD_DIM], text[:, HEAD_DIM:]
            mine_ref[:, span] = jnp.where(core == 0, low, high).astype(mine_ref.dtype)
            sent_ref[:, span] = jnp.where(core == 0, high, low).astype(mine_ref.dtype)
        else:
            mine_ref[:, span] = text.astype(mine_ref.dtype)
            sent_ref[:, span] = text.astype(mine_ref.dtype)


def combine(place, parts, chips, rows, model_width):
    out = jax.ShapeDtypeStruct((rows, 2 * HEAD_DIM), jnp.bfloat16)
    return pl.pallas_call(
        functools.partial(combine_kernel, chips, model_width),
        out_shape=(out, out),
        in_specs=[SMEM_SPEC] + [VMEM_SPEC] * 3,
        out_specs=(VMEM_SPEC, VMEM_SPEC),
        compiler_params=params(4),
        cost_estimate=pl.CostEstimate(
            flops=8 * rows * 512, bytes_accessed=12 * rows * 512, transcendentals=0
        ),
        name="combine",
    )(place, *parts)


def pack_kernel(copies, queries_ref, keys_ref, values_ref, out_ref):
    img_dev = keys_ref.shape[0]
    part_rows = img_dev // copies
    for device in range(out_ref.shape[0]):
        head, copy = device // copies, device % copies
        span = slice(head * HEAD_DIM, (head + 1) * HEAD_DIM)
        out_ref[device, :img_dev, :] = keys_ref[:, span]
        out_ref[device, img_dev : 2 * img_dev, :] = values_ref[:, span]
        out_ref[device, 2 * img_dev :, :] = queries_ref[copy * part_rows : (copy + 1) * part_rows, span]


def pack(copies, queries, keys, values):
    img_dev = keys.shape[0]
    rows = 2 * img_dev + img_dev // copies
    return pl.pallas_call(
        functools.partial(pack_kernel, copies),
        out_shape=jax.ShapeDtypeStruct((HEADS * copies, rows, HEAD_DIM), jnp.bfloat16),
        in_specs=[VMEM_SPEC] * 3,
        out_specs=VMEM_SPEC,
        compiler_params=params(8),
        cost_estimate=pl.CostEstimate(
            flops=0, bytes_accessed=4 * HEADS * copies * rows * HEAD_DIM, transcendentals=0
        ),
        name="pack",
    )(queries, keys, values)


def unpack_kernel(copies, part_rows, blocks_ref, attended_ref, text_ref):
    share = text_ref.shape[0]
    half = text_ref.shape[1] // 2
    for device in range(blocks_ref.shape[0]):
        head, copy = device // copies, device % copies
        start = head * HEAD_DIM
        rows = slice(copy * part_rows, (copy + 1) * part_rows)
        attended_ref[rows, start : start + HEAD_DIM] = blocks_ref[device, :part_rows, :]
        if copy == 0:
            block = blocks_ref[device, part_rows:, :].astype(jnp.float32)
            text_ref[:, start : start + HEAD_DIM] = block[:share].astype(text_ref.dtype)
            start += half
            text_ref[:, start : start + HEAD_DIM] = block[share:].astype(text_ref.dtype)


def unpack(copies, part_rows, blocks):
    share = (blocks.shape[1] - part_rows) // 2
    return pl.pallas_call(
        functools.partial(unpack_kernel, copies, part_rows),
        out_shape=(
            jax.ShapeDtypeStruct((part_rows * copies, HEADS * HEAD_DIM), jnp.bfloat16),
            jax.ShapeDtypeStruct((share, 2 * HEADS * HEAD_DIM), jnp.bfloat16),
        ),
        in_specs=[VMEM_SPEC],
        out_specs=(VMEM_SPEC, VMEM_SPEC),
        compiler_params=params(4),
        name="unpack",
    )(blocks)


def image_kernel(factor, call, img_dev, packed_ref, sum_ref, top_ref, keys_ref, wide_ref):
    wide_ref[:, HEAD_DIM:] = jnp.ones((wide_ref.shape[0], HEAD_DIM), wide_ref.dtype)
    for device in range(packed_ref.shape[0]):
        rows = slice(device * img_dev, (device + 1) * img_dev)
        keys_ref[rows, :] = packed_ref[device, :img_dev, :]
        wide_ref[rows, :HEAD_DIM] = packed_ref[device, img_dev : 2 * img_dev, :]
    group = max(1, 256 // (packed_ref.shape[1] - 2 * img_dev))
    rows = 256
    contract = (((1,), (1,)), ((), ()))
    count = sum_ref.shape[0]
    for start in range(0, count, rows):
        span = slice(start, start + rows)
        at = (call * count + start) // rows * group
        queries = packed_ref[at : at + group, 2 * img_dev :, :].reshape(rows, HEAD_DIM)
        scores = lax.dot_general(queries, keys_ref[...], contract, preferred_element_type=jnp.float32)
        scores = scores * factor
        top = jnp.max(scores, 1, keepdims=True)
        weights = jnp.exp2(scores - top).astype(jnp.bfloat16)
        sum_ref[span, :] = jnp.dot(weights, wide_ref[...], preferred_element_type=jnp.float32)
        top_ref[span, :] = jnp.broadcast_to(top, (rows, HEAD_DIM))


def image_attention(packed, img_dev, factor, call, calls):
    count = packed.shape[0] * (packed.shape[1] - 2 * img_dev) // calls
    total = packed.shape[0] * img_dev
    return pl.pallas_call(
        functools.partial(image_kernel, factor, call, img_dev),
        out_shape=(
            jax.ShapeDtypeStruct((count, 2 * HEAD_DIM), jnp.float32),
            jax.ShapeDtypeStruct((count, HEAD_DIM), jnp.float32),
        ),
        in_specs=[VMEM_SPEC],
        out_specs=(VMEM_SPEC, VMEM_SPEC),
        scratch_shapes=[
            pltpu.VMEM((total, HEAD_DIM), jnp.bfloat16),
            pltpu.VMEM((total, 2 * HEAD_DIM), jnp.bfloat16),
        ],
        compiler_params=params(14),
        cost_estimate=pl.CostEstimate(
            flops=4 * count * total * HEAD_DIM,
            bytes_accessed=4 * total * HEAD_DIM + 10 * count * HEAD_DIM,
            transcendentals=count * total,
        ),
        name="image_attention",
    )(packed)


def finish_kernel(factor, calls, img_dev, place_ref, packed_ref, *refs):
    images, (mine_ref, got_ref, out_ref) = refs[: 2 * calls], refs[2 * calls :]
    core, valid = place_ref[2], place_ref[4]
    devices = out_ref.shape[0]
    part_rows = packed_ref.shape[1] - 2 * img_dev
    half = mine_ref.shape[0]
    contract = (((1,), (1,)), ((), ()))
    mine, got = mine_ref[...], got_ref[...]
    keys = jnp.concatenate([mine[:, :HEAD_DIM], got[:, :HEAD_DIM]], 0)
    values = jnp.concatenate([mine[:, HEAD_DIM:], got[:, HEAD_DIM:]], 0)
    values = jnp.concatenate([values, jnp.ones(values.shape, values.dtype)], 1)
    lane = lax.broadcasted_iota(jnp.int32, (1, 2 * half), 1)
    text_position = jnp.where((lane >= half) == (core == 0), half, 0) + lane % half
    bias = jnp.where(text_position < valid, 0.0, -jnp.inf)
    group = max(1, 512 // part_rows)
    rows = group * part_rows
    each = devices // group // calls
    for step in range(devices // group):
        sum_ref, top_ref = images[2 * (step // each)], images[2 * (step // each) + 1]
        span = slice(step % each * rows, (step % each + 1) * rows)
        queries = packed_ref[step * group : (step + 1) * group, 2 * img_dev :, :]
        queries = queries.reshape(rows, HEAD_DIM)
        scores = lax.dot_general(queries, keys, contract, preferred_element_type=jnp.float32)
        scores = scores * factor + bias
        before = top_ref[span, :]
        top = jnp.maximum(before, jnp.max(scores, 1, keepdims=True))
        rescale = jnp.exp2(before - top)
        weights = jnp.exp2(scores - jnp.concatenate([top] * (2 * half // HEAD_DIM), 1))
        total = jnp.dot(weights.astype(jnp.bfloat16), values, preferred_element_type=jnp.float32)
        mixed = sum_ref[span, :HEAD_DIM] * rescale + total[:, :HEAD_DIM]
        total = sum_ref[span, HEAD_DIM:] * rescale + total[:, HEAD_DIM:]
        mixed = (mixed / total).astype(out_ref.dtype)
        out_ref[step * group : (step + 1) * group, :part_rows, :] = mixed.reshape(group, part_rows, HEAD_DIM)
    low = jnp.where(core == 0, mine.astype(jnp.float32), got.astype(jnp.float32))
    high = jnp.where(core == 0, got.astype(jnp.float32), mine.astype(jnp.float32))
    share = 2 * half // devices
    for device in range(devices):
        source = low if device < devices // 2 else high
        start = device * share % half
        block = source[start : start + share]
        block = jnp.concatenate([block[:, :HEAD_DIM], block[:, HEAD_DIM:]], 0)
        out_ref[device, part_rows:, :] = block.astype(out_ref.dtype)


def finish(place, packed, images, mine, got, img_dev, factor):
    devices, part_rows = packed.shape[0], packed.shape[1] - 2 * img_dev
    count = devices * part_rows
    share = 2 * mine.shape[0] // devices
    return pl.pallas_call(
        functools.partial(finish_kernel, factor, len(images) // 2, img_dev),
        out_shape=jax.ShapeDtypeStruct((devices, part_rows + 2 * share, HEAD_DIM), jnp.bfloat16),
        in_specs=[SMEM_SPEC] + [VMEM_SPEC] * (len(images) + 3),
        out_specs=VMEM_SPEC,
        compiler_params=params(10),
        cost_estimate=pl.CostEstimate(
            flops=4 * count * 2 * mine.shape[0] * HEAD_DIM,
            bytes_accessed=12 * count * HEAD_DIM,
            transcendentals=count * 2 * mine.shape[0],
        ),
        name="finish",
    )(place, packed, *images, mine, got)


def add_kernel(joint, *refs):
    ins, outs = refs[:4], refs[4:]
    if joint:
        outs = (outs[0].at[0], outs[1], outs[0].at[1], outs[2])
    for lane in range(2):
        mine, got = ins[2 * lane], ins[2 * lane + 1]
        half = mine.shape[0] // 2
        outs[2 * lane][...] = (
            mine[half:].astype(jnp.float32) + got[half:].astype(jnp.float32)
        ).astype(jnp.bfloat16)
        outs[2 * lane + 1][...] = mine[:half].astype(jnp.float32) + got[:half].astype(jnp.float32)


def add_halves(mine, got, joint=False):
    shape = (mine[0].shape[0] // 2,) + mine[0].shape[1:]
    sent, keep = jax.ShapeDtypeStruct(shape, jnp.bfloat16), jax.ShapeDtypeStruct(shape, jnp.float32)
    outs = (sent, keep) * 2
    if joint:
        outs = (jax.ShapeDtypeStruct((2,) + shape, jnp.bfloat16), keep, keep)
    outs = pl.pallas_call(
        functools.partial(add_kernel, joint),
        out_shape=outs,
        in_specs=[VMEM_SPEC] * 4,
        out_specs=(VMEM_SPEC,) * len(outs),
        compiler_params=params(6),
        cost_estimate=pl.CostEstimate(
            flops=2 * mine[0].size, bytes_accessed=12 * mine[0].size, transcendentals=0
        ),
        name="add_halves",
    )(mine[0], got[0], mine[1], got[1])
    if joint:
        return outs[0], outs[1:]
    return [outs[0], outs[2]], [outs[1], outs[3]]


def total_kernel(mine0, got0, mine1, got1, out_ref):
    for lane, (mine, got) in enumerate(((mine0, got0), (mine1, got1))):
        out_ref[lane] = (mine[...] + got[...].astype(jnp.float32)).astype(out_ref.dtype)


def add_all(mine, got):
    return pl.pallas_call(
        total_kernel,
        out_shape=jax.ShapeDtypeStruct((2,) + mine[0].shape, jnp.bfloat16),
        in_specs=[VMEM_SPEC] * 4,
        out_specs=VMEM_SPEC,
        compiler_params=params(4),
        cost_estimate=pl.CostEstimate(
            flops=2 * mine[0].size, bytes_accessed=16 * mine[0].size, transcendentals=0
        ),
        name="add_all",
    )(mine[0], got[0], mine[1], got[1])


def norm_kernel(mine_ref, got_ref, gain_ref, out0, out1):
    width = mine_ref.shape[3]
    for at in range(2):
        totals = [
            mine_ref[lane, at].astype(jnp.float32) + got_ref[lane, 1 - at].astype(jnp.float32)
            for lane in range(2)
        ]
        square = sum(jnp.sum(total * total, 1, keepdims=True) for total in totals)
        scale_rows = lax.rsqrt(square / (2 * width) + epsilon)
        for lane, (total, out_ref) in enumerate(zip(totals, (out0, out1))):
            gain = gain_ref[:, lane * width : (lane + 1) * width].astype(jnp.float32)
            out_ref[at] = (total * scale_rows * gain).astype(out_ref.dtype)


def normalize(mine, got, norm_gain):
    out = jax.ShapeDtypeStruct(mine.shape[1:], jnp.bfloat16)
    states = pl.pallas_call(
        norm_kernel,
        out_shape=(out, out),
        in_specs=[VMEM_SPEC] * 3,
        out_specs=(VMEM_SPEC,) * 2,
        compiler_params=params(4),
        cost_estimate=pl.CostEstimate(
            flops=4 * mine.size, bytes_accessed=8 * mine.size, transcendentals=0
        ),
        name="normalize",
    )(mine, got, norm_gain)
    return [part.reshape(-1, part.shape[2]) for part in states]


def join_kernel(mine0, got0, mine1, got1, out0, out1):
    for mine, got, out_ref in ((mine0, got0, out0), (mine1, got1, out1)):
        rows = mine.shape[0]
        if rows % 16:
            both = [mine[...].astype(jnp.float32), got[...].astype(jnp.float32)]
            out_ref[...] = jnp.concatenate(both, 0).astype(out_ref.dtype)
        else:
            out_ref[:rows, :] = mine[...]
            out_ref[rows:, :] = got[...]


def join(mine, got):
    rows, width = mine[0].shape
    out = jax.ShapeDtypeStruct((2 * rows, width), mine[0].dtype)
    return pl.pallas_call(
        join_kernel,
        out_shape=(out, out),
        in_specs=[VMEM_SPEC] * 4,
        out_specs=(VMEM_SPEC,) * 2,
        compiler_params=params(4),
        cost_estimate=pl.CostEstimate(
            flops=0, bytes_accessed=16 * rows * width, transcendentals=0
        ),
        name="join",
    )(mine[0], got[0], mine[1], got[1])


def local(
    enc_act,
    down_weight,
    norm_gain,
    text_in_weight,
    modulation_weight,
    key_value_weight,
    timesteps,
    lengths,
    image_queries,
    image_key_values,
):
    devices = lax.axis_size("seq")
    chips = devices // 2
    copies = devices // HEADS
    text_len = enc_act.shape[1]
    img_dev = image_queries.shape[1]
    part_rows = img_dev // copies
    factor = math.log2(math.e) / math.sqrt(HEAD_DIM)
    lanes = orders(chips)
    index = lax.axis_index("seq")
    chip, core = index // 2, index % 2
    place = jnp.stack([position(chip, lanes[0]), position(chip, lanes[1]), core, chip, lengths[0]])
    place = place.astype(jnp.int32)

    win0, kv0 = text_in_weight.T, key_value_weight
    mod0 = modulation_weight.transpose(1, 2, 0)
    time = time_embedding(timesteps)

    rounds = len(lanes[0])
    tie = lax.optimization_barrier

    def exchange(rows):
        return lax.all_to_all(rows, "seq", split_axis=0, concat_axis=0, tiled=True)

    image_key_values, image_queries = tie((image_key_values, image_queries))
    packed = pack(copies, image_queries[0], image_key_values[0, :, 0], image_key_values[0, :, 1])
    act, packed = tie((enc_act[0].T, packed))
    packed = exchange(packed)
    encoded = encoder(lanes, place, act, down_weight)
    keep, got = encoded[::2], [swap(other, 1) for other in encoded[1::2]]
    last = 2 * lanes[0][-1]
    for step in range(rounds - 1):
        sent, keep = add_halves(keep, got)
        got = [swap(part, 2 * order[step]) for part, order in zip(sent, lanes)]
    summed = add_all(keep, got)
    summed, held, held_kv, held_mod = tie((summed, win0, kv0, mod0))
    win1, kv1, mod1 = swap(held, 1), swap(held_kv, 1), swap(held_mod, 1)
    got, packed = tie((swap(summed, last), packed))

    states = normalize(summed, got, norm_gain[None, :])
    images = []
    for step in reversed(range(rounds - 1)):
        if step == 0:
            states, packed = tie((states, packed))
            image = image_attention(packed, img_dev, factor, 0, 2)
        got = [swap(state, 2 * order[step]) for state, order in zip(states, lanes)]
        if step == rounds - 2:
            lines = modulation(time, mod0, mod1)
            got, win1, kv1, lines = tie((got, win1, kv1, lines))
        if step:
            states = join(states, got)
    got, image = tie((got, image))
    images += image
    states = [state for pair in zip(states, got) for state in pair]

    blocks = project(lanes, place, states, lines, win0, win1, kv0, kv1)
    keep, sent = [blocks[0], blocks[2]], [blocks[1], blocks[3]]
    for step in range(rounds - 1):
        if step == 0:
            sent, packed = tie((sent, packed))
            image = image_attention(packed, img_dev, factor, 1, 2)
        got = [swap(part, 2 * order[step]) for part, order in zip(sent, lanes)]
        if step == 0:
            got, image = tie((got, image))
            images += image
        sent, keep = add_halves(keep, got, step == rounds - 2)
    parts = (*keep, swap(sent, last))
    model_width = text_in_weight.shape[1] * devices
    mine, sent = combine(place, parts, chips, text_len // 2, model_width)
    got = swap(sent, 1)

    back = exchange(finish(place, packed, images, mine, got, img_dev, factor))
    attended, text_kv = unpack(copies, part_rows, back)
    return (attended[None], text_kv)


def solution(mesh):
    in_specs = (
        P("dp", None, "seq"),
        P("seq", None),
        P(),
        P(None, "seq"),
        P(None, None, "seq"),
        P("seq", None),
        P("dp"),
        P("dp"),
        P("dp", "seq", None),
        P("dp", "seq", None, None),
    )
    out_specs = (P("dp", "seq", None), P(("dp", "seq"), None))
    return jax.shard_map(local, mesh=mesh, in_specs=in_specs, out_specs=out_specs, check_vma=False)
```

```python
import functools
import math

import jax
import jax.numpy as jnp
from jax import lax
from jax.experimental import pallas as pl
from jax.experimental.pallas import tpu as pltpu
from jax.sharding import PartitionSpec as P

HEAD_DIM = 128
HEADS = 16
TEMB = 256
MIB = 1024 * 1024

epsilon = 1e-06

SMEM_SPEC = pl.BlockSpec(memory_space=pltpu.SMEM)
VMEM_SPEC = pl.BlockSpec(memory_space=pltpu.VMEM)


def params(mib):
    return pltpu.CompilerParams(vmem_limit_bytes=mib * MIB)


def swap(value, mask):
    devices = lax.axis_size("seq")
    return lax.ppermute(value, "seq", [(i, i ^ mask) for i in range(devices)])


def orders(chips):
    bits = [1 << i for i in range(chips.bit_length() - 1)]
    return (bits, [bits[1], bits[0]] + bits[2:])


def position(chip, order):
    last = len(order) - 1
    return sum(((chip >> (bit.bit_length() - 1)) & 1) << (last - i) for i, bit in enumerate(order))


def member(at, order):
    last = len(order) - 1
    return sum(bit for i, bit in enumerate(order) if (at >> (last - i)) & 1)


def time_embedding(timesteps):
    half_width = TEMB // 2
    freqs = jnp.exp(-math.log(10000.0) * jnp.arange(half_width, dtype=jnp.float32) / half_width)
    angles = timesteps.astype(jnp.float32)[:, None] * freqs[None, :]
    embedding = jnp.concatenate([jnp.cos(angles), jnp.sin(angles)], 1)
    return jax.nn.silu(embedding).astype(jnp.bfloat16)


def encoder_kernel(lanes, place_ref, act_ref, weight_ref, *refs):
    outs, lhs_ref = refs[:-1], refs[-1]
    chips, share, width = outs[0].shape
    core = place_ref[2]
    half = chips * share
    first = core == 0
    tile = width // 2
    lhs_ref[...] = act_ref[...].T
    for lane, order in enumerate(lanes):
        own_ref, other_ref = outs[2 * lane], outs[2 * lane + 1]
        for column in range(0, width, tile):
            start = lane * width + column
            result = jnp.dot(
                lhs_ref[...], weight_ref[:, start : start + tile], preferred_element_type=jnp.float32
            )
            own = jnp.where(first, result[:half], result[half:]).astype(own_ref.dtype)
            other = jnp.where(first, result[half:], result[:half]).astype(own_ref.dtype)
            own = own.reshape(chips, share, tile)
            other = other.reshape(chips, share, tile)
            for block in range(chips):
                to = place_ref[lane] ^ position(block, order)
                own_ref[to, :, column : column + tile] = own[block]
                other_ref[to, :, column : column + tile] = other[block]


def encoder(lanes, place, act, weight):
    chips = 1 << len(lanes[0])
    depth, rows = act.shape
    width = weight.shape[1]
    out = jax.ShapeDtypeStruct((chips, rows // 2 // chips, width // 2), jnp.bfloat16)
    return pl.pallas_call(
        functools.partial(encoder_kernel, lanes),
        out_shape=(out,) * 4,
        in_specs=[SMEM_SPEC, VMEM_SPEC, VMEM_SPEC],
        out_specs=(VMEM_SPEC,) * 4,
        scratch_shapes=[pltpu.VMEM((rows, depth), jnp.bfloat16)],
        compiler_params=params(16),
        cost_estimate=pl.CostEstimate(
            flops=2 * rows * depth * width,
            bytes_accessed=2 * (depth * rows + depth * width + rows * width),
            transcendentals=0,
        ),
        name="encoder",
    )(place, act, weight)


def modulation_kernel(time_ref, mod0_ref, mod1_ref, out_ref):
    contract = (((1,), (1,)), ((), ()))
    embedding = jnp.broadcast_to(time_ref[...].astype(jnp.float32), (16, time_ref.shape[1]))
    embedding = embedding.astype(jnp.bfloat16)
    row = lax.broadcasted_iota(jnp.int32, (16, mod0_ref.shape[1]), 0)
    for side, mod in enumerate((mod0_ref, mod1_ref)):
        shift, scale = [
            lax.dot_general(embedding, mod[at], contract, preferred_element_type=jnp.float32)
            for at in range(2)
        ]
        lines = jnp.where(row < 2, 1.0 + scale, shift)
        high = lines.astype(jnp.bfloat16).astype(jnp.float32)
        low = jnp.where(row % 2 == 0, high, lines - high)
        out_ref[side] = jnp.where(row < 4, low, 1.0 + scale)


def modulation(time, mod0, mod1):
    return pl.pallas_call(
        modulation_kernel,
        out_shape=jax.ShapeDtypeStruct((2, 16, mod0.shape[1]), jnp.float32),
        in_specs=[VMEM_SPEC] * 3,
        out_specs=VMEM_SPEC,
        compiler_params=params(4),
        name="modulation",
    )(time, mod0, mod1)


def slot_rows(chips, width):
    per_slot = 2 * 128 // width
    return chips * per_slot, -(-(chips * per_slot + 2) // 16) * 16


def project_kernel(lanes, place_ref, *refs):
    pieces, refs = (refs[:2], refs[2:4]), refs[4:]
    lines_ref, win0, win1, kv0, kv1, *outs, states, proj0, proj1, sums = refs
    chip = place_ref[3]
    half_chips = outs[0].shape[0]
    chips = 2 * half_chips
    rows = proj0.shape[0]
    share = rows // chips
    depth = states.shape[1]
    contract = (((1,), (1,)), ((), ()))
    for lane, order in enumerate(lanes):
        top, low = pieces[lane]
        states[: rows // 2, :] = top[...]
        states[rows // 2 :, :] = low[...]
        span = slice(lane * depth, (lane + 1) * depth)
        for win, proj in ((win0, proj0), (win1, proj1)):
            part = lax.dot_general(
                states[...], win[:, span], contract, preferred_element_type=jnp.float32
            )
            for at in range(chips):
                start = pl.multiple_of((chip ^ member(at, order)) * share, share)
                block = part[at * share : (at + 1) * share]
                if lane == 0:
                    proj[pl.ds(start, share), :] = block
                else:
                    proj[pl.ds(start, share), :] += block
    value0, value1 = proj0[...], proj1[...]
    first = jnp.sum(value0, 1, keepdims=True) + jnp.sum(value1, 1, keepdims=True)
    second = jnp.sum(value0 * value0, 1, keepdims=True) + jnp.sum(value1 * value1, 1, keepdims=True)
    lane = lax.broadcasted_iota(jnp.int32, sums.shape, 1)
    sums[...] = jnp.where(lane == 0, first, second).T
    left = []
    for side, value in enumerate((value0, value1)):
        lines = lines_ref[side]
        row = lax.broadcasted_iota(jnp.int32, lines.shape, 0)
        lines, scale = jnp.where(row < 4, lines, 0.0), lines[4:5]
        left.append(jnp.concatenate([value * scale, lines], 0).astype(jnp.bfloat16))
    width = outs[0].shape[2]
    slots, extra = slot_rows(chips, width)
    per_slot = slots // chips
    row = lax.broadcasted_iota(jnp.int32, (extra, width), 0)
    column = lax.broadcasted_iota(jnp.int32, (extra, width), 1)
    half = kv0.shape[1] // 2
    for lane, order in enumerate(lanes):
        line = sums[lane : lane + 1, :]
        high = line.astype(jnp.bfloat16).astype(jnp.float32)
        low = line - high
        if per_slot == 1:
            line = jnp.concatenate([high, low], 1)
        else:
            line = jnp.where(row % 2 == 0, high, low)
        line = jnp.where(row // per_slot == chip, line, 0.0)
        for at in reversed(range(chips)):
            out_ref, to = outs[2 * lane + at // half_chips], at % half_chips
            start = lane * half + (chip ^ member(at, order)) * width
            columns = pl.ds(pl.multiple_of(start, width), width)
            value = jnp.dot(left[0], kv0[:, columns], preferred_element_type=jnp.float32)
            value += jnp.dot(left[1], kv1[:, columns], preferred_element_type=jnp.float32)
            out_ref[to, :rows, :] = value[:rows].astype(out_ref.dtype)
            below = jnp.where(row == slots, value[rows : rows + 1] + value[rows + 1 : rows + 2], line)
            below = jnp.where(
                row == slots + 1, value[rows + 2 : rows + 3] + value[rows + 3 : rows + 4], below
            )
            out_ref[to, rows:, :] = below.astype(out_ref.dtype)


def project(lanes, place, pieces, lines, win0, win1, kv0, kv1):
    chips = 1 << len(lanes[0])
    rows = 2 * pieces[0].shape[0]
    features, depth = win0.shape
    total = kv0.shape[1]
    width = total // 2 // chips
    extra = slot_rows(chips, width)[1]
    out = jax.ShapeDtypeStruct((chips // 2, rows + extra, width), jnp.bfloat16)
    return pl.pallas_call(
        functools.partial(project_kernel, lanes),
        out_shape=(out,) * 4,
        in_specs=[SMEM_SPEC] + [VMEM_SPEC] * 9,
        out_specs=(VMEM_SPEC,) * 4,
        scratch_shapes=[
            pltpu.VMEM((rows, depth // 2), jnp.bfloat16),
            pltpu.VMEM((rows, features), jnp.float32),
            pltpu.VMEM((rows, features), jnp.float32),
            pltpu.VMEM((rows, 128), jnp.float32),
        ],
        compiler_params=params(14),
        cost_estimate=pl.CostEstimate(
            flops=4 * rows * features * (depth + total),
            bytes_accessed=2 * (rows * depth + 2 * features * (depth + total) + rows * total),
            transcendentals=0,
        ),
        name="project",
    )(place, *pieces, lines, win0, win1, kv0, kv1)


def combine_kernel(chips, model_width, place_ref, *refs):
    keep0, keep1, came_ref, mine_ref, sent_ref = refs
    core = place_ref[2]
    rows = mine_ref.shape[0]
    width = keep0.shape[2]
    slots = slot_rows(chips, width)[0]
    totals = [keep[0] + came_ref[lane, 0].astype(jnp.float32) for lane, keep in enumerate((keep0, keep1))]
    sums = []
    for total in totals:
        line = jnp.sum(total[rows : rows + slots], 0, keepdims=True)
        if width > 128:
            line = line[:, :128] + line[:, 128:]
        sums.append(line)
    mean_val = sums[0] / model_width
    scale = lax.rsqrt(sums[1] / model_width - mean_val * mean_val + epsilon)
    mean_val = jnp.broadcast_to(mean_val, (rows, rows)).T[:, 0:1]
    scale = jnp.broadcast_to(scale, (rows, rows)).T[:, 0:1]
    texts = []
    for total in totals:
        text = (total[:rows] - mean_val * total[rows + slots : rows + slots + 1]) * scale
        texts.append(text + total[rows + slots + 1 : rows + slots + 2])
    for part, text in enumerate(texts):
        span = slice(part * HEAD_DIM, (part + 1) * HEAD_DIM)
        if width > HEAD_DIM:
            low, high = text[:, :HEAD_DIM], text[:, HEAD_DIM:]
            mine_ref[:, span] = jnp.where(core == 0, low, high).astype(mine_ref.dtype)
            sent_ref[:, span] = jnp.where(core == 0, high, low).astype(mine_ref.dtype)
        else:
            mine_ref[:, span] = text.astype(mine_ref.dtype)
            sent_ref[:, span] = text.astype(mine_ref.dtype)


def combine(place, parts, chips, rows, model_width):
    out = jax.ShapeDtypeStruct((rows, 2 * HEAD_DIM), jnp.bfloat16)
    return pl.pallas_call(
        functools.partial(combine_kernel, chips, model_width),
        out_shape=(out, out),
        in_specs=[SMEM_SPEC] + [VMEM_SPEC] * 3,
        out_specs=(VMEM_SPEC, VMEM_SPEC),
        compiler_params=params(4),
        cost_estimate=pl.CostEstimate(
            flops=8 * rows * 512, bytes_accessed=12 * rows * 512, transcendentals=0
        ),
        name="combine",
    )(place, *parts)


def pack_kernel(copies, queries_ref, keys_ref, values_ref, out_ref):
    img_dev = keys_ref.shape[0]
    part_rows = img_dev // copies
    for device in range(out_ref.shape[0]):
        head, copy = device // copies, device % copies
        span = slice(head * HEAD_DIM, (head + 1) * HEAD_DIM)
        out_ref[device, :img_dev, :] = keys_ref[:, span]
        out_ref[device, img_dev : 2 * img_dev, :] = values_ref[:, span]
        out_ref[device, 2 * img_dev :, :] = queries_ref[copy * part_rows : (copy + 1) * part_rows, span]


def pack(copies, queries, keys, values):
    img_dev = keys.shape[0]
    rows = 2 * img_dev + img_dev // copies
    return pl.pallas_call(
        functools.partial(pack_kernel, copies),
        out_shape=jax.ShapeDtypeStruct((HEADS * copies, rows, HEAD_DIM), jnp.bfloat16),
        in_specs=[VMEM_SPEC] * 3,
        out_specs=VMEM_SPEC,
        compiler_params=params(8),
        cost_estimate=pl.CostEstimate(
            flops=0, bytes_accessed=4 * HEADS * copies * rows * HEAD_DIM, transcendentals=0
        ),
        name="pack",
    )(queries, keys, values)


def unpack_kernel(copies, part_rows, place_ref, *refs):
    *pieces, near_ref, far_ref, attended_ref, text_ref = refs
    me = 2 * place_ref[3] + place_ref[2]
    share = text_ref.shape[0]
    half = text_ref.shape[1] // 2
    count = len(pieces) // 2
    passed = [near_ref.at[at] for at in range(count)] + [far_ref.at[at] for at in range(count)]
    blocks = [block for piece, other in zip(pieces, passed) for block in (piece.at[0], other)]
    for at, block_ref in enumerate(blocks):
        head, copy = (me ^ at) // copies, (me ^ at) % copies
        start = pl.multiple_of(head * HEAD_DIM, HEAD_DIM)
        rows = pl.ds(pl.multiple_of(copy * part_rows, part_rows), part_rows)
        attended_ref[rows, pl.ds(start, HEAD_DIM)] = block_ref[:part_rows, :]
        block = block_ref[part_rows:, :].astype(jnp.float32)
        text_ref[:, pl.ds(start, HEAD_DIM)] = block[:share].astype(text_ref.dtype)
        start = pl.multiple_of(half + head * HEAD_DIM, HEAD_DIM)
        text_ref[:, pl.ds(start, HEAD_DIM)] = block[share:].astype(text_ref.dtype)


def unpack(copies, part_rows, place, pieces, near, far):
    share = (near.shape[1] - part_rows) // 2
    return pl.pallas_call(
        functools.partial(unpack_kernel, copies, part_rows),
        out_shape=(
            jax.ShapeDtypeStruct((part_rows * copies, HEADS * HEAD_DIM), jnp.bfloat16),
            jax.ShapeDtypeStruct((share, 2 * HEADS * HEAD_DIM), jnp.bfloat16),
        ),
        in_specs=[SMEM_SPEC] + [VMEM_SPEC] * (len(pieces) + 2),
        out_specs=(VMEM_SPEC, VMEM_SPEC),
        compiler_params=params(6),
        name="unpack",
    )(place, *pieces, near, far)


def image_kernel(factor, call, img_dev, place_ref, packed_ref, sum_ref, top_ref, keys_ref, wide_ref):
    me = 2 * place_ref[3] + place_ref[2]
    wide_ref[:, HEAD_DIM:] = jnp.ones((wide_ref.shape[0], HEAD_DIM), wide_ref.dtype)
    for device in range(packed_ref.shape[0]):
        rows = slice(device * img_dev, (device + 1) * img_dev)
        keys_ref[rows, :] = packed_ref[device, :img_dev, :]
        wide_ref[rows, :HEAD_DIM] = packed_ref[device, img_dev : 2 * img_dev, :]
    group = max(1, 256 // (packed_ref.shape[1] - 2 * img_dev))
    rows = 256
    contract = (((1,), (1,)), ((), ()))
    count = sum_ref.shape[0]
    for start in range(0, count, rows):
        span = slice(start, start + rows)
        at = (call * count + start) // rows * group
        queries = [packed_ref[me ^ (at + i), 2 * img_dev :, :] for i in range(group)]
        queries = jnp.concatenate(queries, 0)
        scores = lax.dot_general(queries, keys_ref[...], contract, preferred_element_type=jnp.float32)
        scores = scores * factor
        top = jnp.max(scores, 1, keepdims=True)
        weights = jnp.exp2(scores - top).astype(jnp.bfloat16)
        sum_ref[span, :] = jnp.dot(weights, wide_ref[...], preferred_element_type=jnp.float32)
        top_ref[span, :] = jnp.broadcast_to(top, (rows, HEAD_DIM))


def image_attention(place, packed, img_dev, factor, call, calls):
    count = packed.shape[0] * (packed.shape[1] - 2 * img_dev) // calls
    total = packed.shape[0] * img_dev
    return pl.pallas_call(
        functools.partial(image_kernel, factor, call, img_dev),
        out_shape=(
            jax.ShapeDtypeStruct((count, 2 * HEAD_DIM), jnp.float32),
            jax.ShapeDtypeStruct((count, HEAD_DIM), jnp.float32),
        ),
        in_specs=[SMEM_SPEC, VMEM_SPEC],
        out_specs=(VMEM_SPEC, VMEM_SPEC),
        scratch_shapes=[
            pltpu.VMEM((total, HEAD_DIM), jnp.bfloat16),
            pltpu.VMEM((total, 2 * HEAD_DIM), jnp.bfloat16),
        ],
        compiler_params=params(14),
        cost_estimate=pl.CostEstimate(
            flops=4 * count * total * HEAD_DIM,
            bytes_accessed=4 * total * HEAD_DIM + 10 * count * HEAD_DIM,
            transcendentals=count * total,
        ),
        name="image_attention",
    )(place, packed)


def finish_kernel(factor, first, img_dev, place_ref, packed_ref, sum_ref, top_ref, mine_ref, got_ref, *refs):
    *outs, text_ref = refs
    core, valid = place_ref[2], place_ref[4]
    me = 2 * place_ref[3] + core
    part_rows = packed_ref.shape[1] - 2 * img_dev
    half = mine_ref.shape[0]
    contract = (((1,), (1,)), ((), ()))
    mine, got = mine_ref[...], got_ref[...]
    keys = jnp.concatenate([mine[:, :HEAD_DIM], got[:, :HEAD_DIM]], 0)
    values = jnp.concatenate([mine[:, HEAD_DIM:], got[:, HEAD_DIM:]], 0)
    values = jnp.concatenate([values, jnp.ones(values.shape, values.dtype)], 1)
    lane = lax.broadcasted_iota(jnp.int32, (1, 2 * half), 1)
    text_position = jnp.where((lane >= half) == (core == 0), half, 0) + lane % half
    bias = jnp.where(text_position < valid, 0.0, -jnp.inf)
    group = max(1, 512 // part_rows)
    rows = group * part_rows
    for step in range(2 * len(outs) // group):
        span = slice(step * rows, (step + 1) * rows)
        queries = [
            packed_ref[me ^ (2 * first + step * group + at), 2 * img_dev :, :] for at in range(group)
        ]
        queries = jnp.concatenate(queries, 0)
        scores = lax.dot_general(queries, keys, contract, preferred_element_type=jnp.float32)
        scores = scores * factor + bias
        before = top_ref[span, :]
        top = jnp.maximum(before, jnp.max(scores, 1, keepdims=True))
        rescale = jnp.exp2(before - top)
        weights = jnp.exp2(scores - jnp.concatenate([top] * (2 * half // HEAD_DIM), 1))
        total = jnp.dot(weights.astype(jnp.bfloat16), values, preferred_element_type=jnp.float32)
        mixed = sum_ref[span, :HEAD_DIM] * rescale + total[:, :HEAD_DIM]
        total = sum_ref[span, HEAD_DIM:] * rescale + total[:, HEAD_DIM:]
        mixed = (mixed / total).astype(jnp.bfloat16)
        for at in range(group):
            to = step * group + at
            outs[to // 2][to % 2, :part_rows, :] = mixed[at * part_rows : (at + 1) * part_rows]
    low, high = mine.astype(jnp.float32), got.astype(jnp.float32)
    text_ref[:half, :] = jnp.where(core == 0, low, high)
    text_ref[half:, :] = jnp.where(core == 0, high, low)
    share = (outs[0].shape[1] - part_rows) // 2
    for to in range(2 * len(outs)):
        start = pl.multiple_of((me ^ (2 * first + to)) * share, share)
        block = text_ref[pl.ds(start, share), :]
        block = jnp.concatenate([block[:, :HEAD_DIM], block[:, HEAD_DIM:]], 0)
        outs[to // 2][to % 2, part_rows:, :] = block.astype(jnp.bfloat16)


def finish(place, first, packed, image, mine, got, img_dev, factor):
    devices, part_rows = packed.shape[0], packed.shape[1] - 2 * img_dev
    half = mine.shape[0]
    count = image[0].shape[0]
    outs = count // part_rows // 2
    out = jax.ShapeDtypeStruct((2, part_rows + 4 * half // devices, HEAD_DIM), jnp.bfloat16)
    return pl.pallas_call(
        functools.partial(finish_kernel, factor, first, img_dev),
        out_shape=(out,) * outs,
        in_specs=[SMEM_SPEC] + [VMEM_SPEC] * 5,
        out_specs=(VMEM_SPEC,) * outs,
        scratch_shapes=[pltpu.VMEM((2 * half, 2 * HEAD_DIM), jnp.float32)],
        compiler_params=params(10),
        cost_estimate=pl.CostEstimate(
            flops=8 * count * half * HEAD_DIM,
            bytes_accessed=12 * count * HEAD_DIM,
            transcendentals=2 * count * half,
        ),
        name="finish",
    )(place, packed, *image, mine, got)


def gather_kernel(*refs):
    for at, piece in enumerate(refs[:-1]):
        refs[-1][at] = piece[1]


def gather_other(pieces):
    shape = (len(pieces),) + pieces[0].shape[1:]
    return pl.pallas_call(
        gather_kernel,
        out_shape=jax.ShapeDtypeStruct(shape, pieces[0].dtype),
        in_specs=[VMEM_SPEC] * len(pieces),
        out_specs=VMEM_SPEC,
        compiler_params=params(4),
        cost_estimate=pl.CostEstimate(
            flops=0, bytes_accessed=2 * len(pieces) * pieces[0].size, transcendentals=0
        ),
        name="gather_other",
    )(*pieces)


def add_kernel(joint, *refs):
    ins, outs = refs[:4], refs[4:]
    if joint:
        outs = (outs[0].at[0], outs[1], outs[0].at[1], outs[2])
    for lane in range(2):
        mine, got = ins[2 * lane], ins[2 * lane + 1]
        half = mine.shape[0] // 2
        outs[2 * lane][...] = (
            mine[half:].astype(jnp.float32) + got[half:].astype(jnp.float32)
        ).astype(jnp.bfloat16)
        outs[2 * lane + 1][...] = mine[:half].astype(jnp.float32) + got[:half].astype(jnp.float32)


def add_halves(mine, got, joint=False):
    shape = (mine[0].shape[0] // 2,) + mine[0].shape[1:]
    sent, keep = jax.ShapeDtypeStruct(shape, jnp.bfloat16), jax.ShapeDtypeStruct(shape, jnp.float32)
    outs = (sent, keep) * 2
    if joint:
        outs = (jax.ShapeDtypeStruct((2,) + shape, jnp.bfloat16), keep, keep)
    outs = pl.pallas_call(
        functools.partial(add_kernel, joint),
        out_shape=outs,
        in_specs=[VMEM_SPEC] * 4,
        out_specs=(VMEM_SPEC,) * len(outs),
        compiler_params=params(6),
        cost_estimate=pl.CostEstimate(
            flops=2 * mine[0].size, bytes_accessed=12 * mine[0].size, transcendentals=0
        ),
        name="add_halves",
    )(mine[0], got[0], mine[1], got[1])
    if joint:
        return outs[0], outs[1:]
    return [outs[0], outs[2]], [outs[1], outs[3]]


def total_kernel(mine0, got0, mine1, got1, out_ref):
    for lane, (mine, got) in enumerate(((mine0, got0), (mine1, got1))):
        out_ref[lane] = (mine[...] + got[...].astype(jnp.float32)).astype(out_ref.dtype)


def add_all(mine, got):
    return pl.pallas_call(
        total_kernel,
        out_shape=jax.ShapeDtypeStruct((2,) + mine[0].shape, jnp.bfloat16),
        in_specs=[VMEM_SPEC] * 4,
        out_specs=VMEM_SPEC,
        compiler_params=params(4),
        cost_estimate=pl.CostEstimate(
            flops=2 * mine[0].size, bytes_accessed=16 * mine[0].size, transcendentals=0
        ),
        name="add_all",
    )(mine[0], got[0], mine[1], got[1])


def norm_kernel(mine_ref, got_ref, gain_ref, out0, out1):
    width = mine_ref.shape[3]
    for at in range(2):
        totals = [
            mine_ref[lane, at].astype(jnp.float32) + got_ref[lane, 1 - at].astype(jnp.float32)
            for lane in range(2)
        ]
        square = sum(jnp.sum(total * total, 1, keepdims=True) for total in totals)
        scale_rows = lax.rsqrt(square / (2 * width) + epsilon)
        for lane, (total, out_ref) in enumerate(zip(totals, (out0, out1))):
            gain = gain_ref[:, lane * width : (lane + 1) * width].astype(jnp.float32)
            out_ref[at] = (total * scale_rows * gain).astype(out_ref.dtype)


def normalize(mine, got, norm_gain):
    out = jax.ShapeDtypeStruct(mine.shape[1:], jnp.bfloat16)
    states = pl.pallas_call(
        norm_kernel,
        out_shape=(out, out),
        in_specs=[VMEM_SPEC] * 3,
        out_specs=(VMEM_SPEC,) * 2,
        compiler_params=params(4),
        cost_estimate=pl.CostEstimate(
            flops=4 * mine.size, bytes_accessed=8 * mine.size, transcendentals=0
        ),
        name="normalize",
    )(mine, got, norm_gain)
    return [part.reshape(-1, part.shape[2]) for part in states]


def join_kernel(mine0, got0, mine1, got1, out0, out1):
    for mine, got, out_ref in ((mine0, got0, out0), (mine1, got1, out1)):
        rows = mine.shape[0]
        if rows % 16:
            both = [mine[...].astype(jnp.float32), got[...].astype(jnp.float32)]
            out_ref[...] = jnp.concatenate(both, 0).astype(out_ref.dtype)
        else:
            out_ref[:rows, :] = mine[...]
            out_ref[rows:, :] = got[...]


def join(mine, got):
    rows, width = mine[0].shape
    out = jax.ShapeDtypeStruct((2 * rows, width), mine[0].dtype)
    return pl.pallas_call(
        join_kernel,
        out_shape=(out, out),
        in_specs=[VMEM_SPEC] * 4,
        out_specs=(VMEM_SPEC,) * 2,
        compiler_params=params(4),
        cost_estimate=pl.CostEstimate(
            flops=0, bytes_accessed=16 * rows * width, transcendentals=0
        ),
        name="join",
    )(mine[0], got[0], mine[1], got[1])


def local(
    enc_act,
    down_weight,
    norm_gain,
    text_in_weight,
    modulation_weight,
    key_value_weight,
    timesteps,
    lengths,
    image_queries,
    image_key_values,
):
    devices = lax.axis_size("seq")
    chips = devices // 2
    copies = devices // HEADS
    text_len = enc_act.shape[1]
    img_dev = image_queries.shape[1]
    part_rows = img_dev // copies
    factor = math.log2(math.e) / math.sqrt(HEAD_DIM)
    lanes = orders(chips)
    index = lax.axis_index("seq")
    chip, core = index // 2, index % 2
    place = jnp.stack([position(chip, lanes[0]), position(chip, lanes[1]), core, chip, lengths[0]])
    place = place.astype(jnp.int32)

    win0, kv0 = text_in_weight.T, key_value_weight
    mod0 = modulation_weight.transpose(1, 2, 0)
    time = time_embedding(timesteps)

    rounds = len(lanes[0])
    tie = lax.optimization_barrier

    def exchange(rows):
        return lax.all_to_all(rows, "seq", split_axis=0, concat_axis=0, tiled=True)

    image_key_values, image_queries = tie((image_key_values, image_queries))
    packed = pack(copies, image_queries[0], image_key_values[0, :, 0], image_key_values[0, :, 1])
    act, packed = tie((enc_act[0].T, packed))
    packed = exchange(packed)
    encoded = encoder(lanes, place, act, down_weight)
    keep, got = encoded[::2], [swap(other, 1) for other in encoded[1::2]]
    last = 2 * lanes[0][-1]
    for step in range(rounds - 1):
        sent, keep = add_halves(keep, got)
        got = [swap(part, 2 * order[step]) for part, order in zip(sent, lanes)]
    summed, packed = tie((add_all(keep, got), packed))
    summed, held, held_kv, held_mod = tie((summed, win0, kv0, mod0))
    win1, kv1, mod1 = swap(held, 1), swap(held_kv, 1), swap(held_mod, 1)
    got = swap(summed, last)

    states = normalize(summed, got, norm_gain[None, :])
    images = []
    for step in reversed(range(rounds - 1)):
        if step == 0:
            states, packed = tie((states, packed))
            image = image_attention(place, packed, img_dev, factor, 0, 2)
        got = [swap(state, 2 * order[step]) for state, order in zip(states, lanes)]
        if step == rounds - 2:
            lines = modulation(time, mod0, mod1)
            got, win1, kv1, lines = tie((got, win1, kv1, lines))
        if step:
            states = join(states, got)
    got, image = tie((got, image))
    images += image
    states = [state for pair in zip(states, got) for state in pair]

    blocks = project(lanes, place, states, lines, win0, win1, kv0, kv1)
    keep, sent = [blocks[0], blocks[2]], [blocks[1], blocks[3]]
    for step in range(rounds - 1):
        if step == 0:
            sent, packed = tie((sent, packed))
            image = image_attention(place, packed, img_dev, factor, 1, 2)
        got = [swap(part, 2 * order[step]) for part, order in zip(sent, lanes)]
        if step == 0:
            got, image = tie((got, image))
            images += image
        sent, keep = add_halves(keep, got, step == rounds - 2)
    parts = (*keep, swap(sent, last))
    model_width = text_in_weight.shape[1] * devices
    mine, sent = combine(place, parts, chips, text_len // 2, model_width)
    got = swap(sent, 1)

    pieces = [None] * chips
    passed = [None] * 2
    for call in (1, 0):
        first = call * chips // 2
        image = images[2 * call : 2 * call + 2]
        blocks = finish(place, first, packed, image, mine, got, img_dev, factor)
        for at, block in enumerate(blocks):
            mask = first + at
            pieces[mask] = swap(block, 2 * mask) if mask else block
    for call in range(2):
        passed[call] = swap(gather_other(pieces[call * chips // 2 : (call + 1) * chips // 2]), 1)
    attended, text_kv = unpack(copies, part_rows, place, pieces, *passed)
    return (attended[None], text_kv)


def solution(mesh):
    in_specs = (
        P("dp", None, "seq"),
        P("seq", None),
        P(),
        P(None, "seq"),
        P(None, None, "seq"),
        P("seq", None),
        P("dp"),
        P("dp"),
        P("dp", "seq", None),
        P("dp", "seq", None, None),
    )
    out_specs = (P("dp", "seq", None), P(("dp", "seq"), None))
    return jax.shard_map(local, mesh=mesh, in_specs=in_specs, out_specs=out_specs, check_vma=False)
```

```python
import functools
import math

import jax
import jax.numpy as jnp
from jax import lax
from jax.experimental import pallas as pl
from jax.experimental.pallas import tpu as pltpu
from jax.sharding import PartitionSpec as P

HEAD_DIM = 128
HEADS = 16
TEMB = 256
MIB = 1024 * 1024

epsilon = 1e-06

SMEM_SPEC = pl.BlockSpec(memory_space=pltpu.SMEM)
VMEM_SPEC = pl.BlockSpec(memory_space=pltpu.VMEM)


def params(mib):
    return pltpu.CompilerParams(vmem_limit_bytes=mib * MIB)


def swap(value, mask):
    devices = lax.axis_size("seq")
    return lax.ppermute(value, "seq", [(i, i ^ mask) for i in range(devices)])


def orders(chips):
    bits = [1 << i for i in range(chips.bit_length() - 1)]
    return (bits, [bits[1], bits[0]] + bits[2:])


def position(chip, order):
    last = len(order) - 1
    return sum(((chip >> (bit.bit_length() - 1)) & 1) << (last - i) for i, bit in enumerate(order))


def member(at, order):
    last = len(order) - 1
    return sum(bit for i, bit in enumerate(order) if (at >> (last - i)) & 1)


def time_embedding(timesteps):
    half_width = TEMB // 2
    freqs = jnp.exp(-math.log(10000.0) * jnp.arange(half_width, dtype=jnp.float32) / half_width)
    angles = timesteps.astype(jnp.float32)[:, None] * freqs[None, :]
    embedding = jnp.concatenate([jnp.cos(angles), jnp.sin(angles)], 1)
    return jax.nn.silu(embedding).astype(jnp.bfloat16)


def encoder_kernel(lanes, place_ref, act_ref, weight_ref, *refs):
    outs, lhs_ref = refs[:-1], refs[-1]
    chips, share, width = outs[0].shape
    core = place_ref[2]
    half = chips * share
    first = core == 0
    tile = width // 2
    lhs_ref[...] = act_ref[...].T
    for lane, order in enumerate(lanes):
        own_ref, other_ref = outs[2 * lane], outs[2 * lane + 1]
        for column in range(0, width, tile):
            start = lane * width + column
            result = jnp.dot(
                lhs_ref[...], weight_ref[:, start : start + tile], preferred_element_type=jnp.float32
            )
            own = jnp.where(first, result[:half], result[half:]).astype(own_ref.dtype)
            other = jnp.where(first, result[half:], result[:half]).astype(own_ref.dtype)
            own = own.reshape(chips, share, tile)
            other = other.reshape(chips, share, tile)
            for block in range(chips):
                to = place_ref[lane] ^ position(block, order)
                own_ref[to, :, column : column + tile] = own[block]
                other_ref[to, :, column : column + tile] = other[block]


def encoder(lanes, place, act, weight):
    chips = 1 << len(lanes[0])
    depth, rows = act.shape
    width = weight.shape[1]
    out = jax.ShapeDtypeStruct((chips, rows // 2 // chips, width // 2), jnp.bfloat16)
    return pl.pallas_call(
        functools.partial(encoder_kernel, lanes),
        out_shape=(out,) * 4,
        in_specs=[SMEM_SPEC, VMEM_SPEC, VMEM_SPEC],
        out_specs=(VMEM_SPEC,) * 4,
        scratch_shapes=[pltpu.VMEM((rows, depth), jnp.bfloat16)],
        compiler_params=params(16),
        cost_estimate=pl.CostEstimate(
            flops=2 * rows * depth * width,
            bytes_accessed=2 * (depth * rows + depth * width + rows * width),
            transcendentals=0,
        ),
        name="encoder",
    )(place, act, weight)


def modulation_kernel(time_ref, mod0_ref, mod1_ref, out_ref):
    contract = (((1,), (1,)), ((), ()))
    embedding = jnp.broadcast_to(time_ref[...].astype(jnp.float32), (16, time_ref.shape[1]))
    embedding = embedding.astype(jnp.bfloat16)
    row = lax.broadcasted_iota(jnp.int32, (16, mod0_ref.shape[1]), 0)
    for side, mod in enumerate((mod0_ref, mod1_ref)):
        shift, scale = [
            lax.dot_general(embedding, mod[at], contract, preferred_element_type=jnp.float32)
            for at in range(2)
        ]
        lines = jnp.where(row < 2, 1.0 + scale, shift)
        high = lines.astype(jnp.bfloat16).astype(jnp.float32)
        low = jnp.where(row % 2 == 0, high, lines - high)
        out_ref[side] = jnp.where(row < 4, low, 1.0 + scale)


def modulation(time, mod0, mod1):
    return pl.pallas_call(
        modulation_kernel,
        out_shape=jax.ShapeDtypeStruct((2, 16, mod0.shape[1]), jnp.float32),
        in_specs=[VMEM_SPEC] * 3,
        out_specs=VMEM_SPEC,
        compiler_params=params(4),
        name="modulation",
    )(time, mod0, mod1)


def slot_rows(chips, width):
    per_slot = 2 * 128 // width
    return chips * per_slot, -(-(chips * per_slot + 2) // 16) * 16


def project_kernel(lanes, place_ref, *refs):
    pieces, refs = (refs[:2], refs[2:4]), refs[4:]
    lines_ref, win0, win1, kv0, kv1, *outs, states, proj0, proj1, sums = refs
    chip = place_ref[3]
    half_chips = outs[0].shape[0]
    chips = 2 * half_chips
    rows = proj0.shape[0]
    share = rows // chips
    depth = states.shape[1]
    contract = (((1,), (1,)), ((), ()))
    for lane, order in enumerate(lanes):
        top, low = pieces[lane]
        states[: rows // 2, :] = top[...]
        states[rows // 2 :, :] = low[...]
        span = slice(lane * depth, (lane + 1) * depth)
        for win, proj in ((win0, proj0), (win1, proj1)):
            part = lax.dot_general(
                states[...], win[:, span], contract, preferred_element_type=jnp.float32
            )
            for at in range(chips):
                start = pl.multiple_of((chip ^ member(at, order)) * share, share)
                block = part[at * share : (at + 1) * share]
                if lane == 0:
                    proj[pl.ds(start, share), :] = block
                else:
                    proj[pl.ds(start, share), :] += block
    value0, value1 = proj0[...], proj1[...]
    first = jnp.sum(value0, 1, keepdims=True) + jnp.sum(value1, 1, keepdims=True)
    second = jnp.sum(value0 * value0, 1, keepdims=True) + jnp.sum(value1 * value1, 1, keepdims=True)
    lane = lax.broadcasted_iota(jnp.int32, sums.shape, 1)
    sums[...] = jnp.where(lane == 0, first, second).T
    left = []
    for side, value in enumerate((value0, value1)):
        lines = lines_ref[side]
        row = lax.broadcasted_iota(jnp.int32, lines.shape, 0)
        lines, scale = jnp.where(row < 4, lines, 0.0), lines[4:5]
        left.append(jnp.concatenate([value * scale, lines], 0).astype(jnp.bfloat16))
    width = outs[0].shape[2]
    slots, extra = slot_rows(chips, width)
    per_slot = slots // chips
    row = lax.broadcasted_iota(jnp.int32, (extra, width), 0)
    column = lax.broadcasted_iota(jnp.int32, (extra, width), 1)
    half = kv0.shape[1] // 2
    for lane, order in enumerate(lanes):
        line = sums[lane : lane + 1, :]
        high = line.astype(jnp.bfloat16).astype(jnp.float32)
        low = line - high
        if per_slot == 1:
            line = jnp.concatenate([high, low], 1)
        else:
            line = jnp.where(row % 2 == 0, high, low)
        line = jnp.where(row // per_slot == chip, line, 0.0)
        for at in reversed(range(chips)):
            out_ref, to = outs[2 * lane + at // half_chips], at % half_chips
            start = lane * half + (chip ^ member(at, order)) * width
            columns = pl.ds(pl.multiple_of(start, width), width)
            value = jnp.dot(left[0], kv0[:, columns], preferred_element_type=jnp.float32)
            value += jnp.dot(left[1], kv1[:, columns], preferred_element_type=jnp.float32)
            out_ref[to, :rows, :] = value[:rows].astype(out_ref.dtype)
            below = jnp.where(row == slots, value[rows : rows + 1] + value[rows + 1 : rows + 2], line)
            below = jnp.where(
                row == slots + 1, value[rows + 2 : rows + 3] + value[rows + 3 : rows + 4], below
            )
            out_ref[to, rows:, :] = below.astype(out_ref.dtype)


def project(lanes, place, pieces, lines, win0, win1, kv0, kv1):
    chips = 1 << len(lanes[0])
    rows = 2 * pieces[0].shape[0]
    features, depth = win0.shape
    total = kv0.shape[1]
    width = total // 2 // chips
    extra = slot_rows(chips, width)[1]
    out = jax.ShapeDtypeStruct((chips // 2, rows + extra, width), jnp.bfloat16)
    return pl.pallas_call(
        functools.partial(project_kernel, lanes),
        out_shape=(out,) * 4,
        in_specs=[SMEM_SPEC] + [VMEM_SPEC] * 9,
        out_specs=(VMEM_SPEC,) * 4,
        scratch_shapes=[
            pltpu.VMEM((rows, depth // 2), jnp.bfloat16),
            pltpu.VMEM((rows, features), jnp.float32),
            pltpu.VMEM((rows, features), jnp.float32),
            pltpu.VMEM((rows, 128), jnp.float32),
        ],
        compiler_params=params(14),
        cost_estimate=pl.CostEstimate(
            flops=4 * rows * features * (depth + total),
            bytes_accessed=2 * (rows * depth + 2 * features * (depth + total) + rows * total),
            transcendentals=0,
        ),
        name="project",
    )(place, *pieces, lines, win0, win1, kv0, kv1)


def combine_kernel(chips, model_width, place_ref, *refs):
    keep0, keep1, came_ref, mine_ref, sent_ref = refs
    core = place_ref[2]
    rows = mine_ref.shape[0]
    width = keep0.shape[2]
    slots = slot_rows(chips, width)[0]
    totals = [keep[0] + came_ref[lane, 0].astype(jnp.float32) for lane, keep in enumerate((keep0, keep1))]
    sums = []
    for total in totals:
        line = jnp.sum(total[rows : rows + slots], 0, keepdims=True)
        if width > 128:
            line = line[:, :128] + line[:, 128:]
        sums.append(line)
    mean_val = sums[0] / model_width
    scale = lax.rsqrt(sums[1] / model_width - mean_val * mean_val + epsilon)
    mean_val = jnp.broadcast_to(mean_val, (rows, rows)).T[:, 0:1]
    scale = jnp.broadcast_to(scale, (rows, rows)).T[:, 0:1]
    texts = []
    for total in totals:
        text = (total[:rows] - mean_val * total[rows + slots : rows + slots + 1]) * scale
        texts.append(text + total[rows + slots + 1 : rows + slots + 2])
    for part, text in enumerate(texts):
        span = slice(part * HEAD_DIM, (part + 1) * HEAD_DIM)
        if width > HEAD_DIM:
            low, high = text[:, :HEAD_DIM], text[:, HEAD_DIM:]
            mine_ref[:, span] = jnp.where(core == 0, low, high).astype(mine_ref.dtype)
            sent_ref[:, span] = jnp.where(core == 0, high, low).astype(mine_ref.dtype)
        else:
            mine_ref[:, span] = text.astype(mine_ref.dtype)
            sent_ref[:, span] = text.astype(mine_ref.dtype)


def combine(place, parts, chips, rows, model_width):
    out = jax.ShapeDtypeStruct((rows, 2 * HEAD_DIM), jnp.bfloat16)
    return pl.pallas_call(
        functools.partial(combine_kernel, chips, model_width),
        out_shape=(out, out),
        in_specs=[SMEM_SPEC] + [VMEM_SPEC] * 3,
        out_specs=(VMEM_SPEC, VMEM_SPEC),
        compiler_params=params(4),
        cost_estimate=pl.CostEstimate(
            flops=8 * rows * 512, bytes_accessed=12 * rows * 512, transcendentals=0
        ),
        name="combine",
    )(place, *parts)


def pack_kernel(copies, keys_ref, values_ref, out_ref):
    img_dev = keys_ref.shape[0]
    for device in range(out_ref.shape[0]):
        head = device // copies
        span = slice(head * HEAD_DIM, (head + 1) * HEAD_DIM)
        out_ref[device, :img_dev, :] = keys_ref[:, span]
        out_ref[device, img_dev:, :] = values_ref[:, span]


def pack(copies, keys, values):
    img_dev = keys.shape[0]
    return pl.pallas_call(
        functools.partial(pack_kernel, copies),
        out_shape=jax.ShapeDtypeStruct((HEADS * copies, 2 * img_dev, HEAD_DIM), jnp.bfloat16),
        in_specs=[VMEM_SPEC] * 2,
        out_specs=VMEM_SPEC,
        compiler_params=params(8),
        cost_estimate=pl.CostEstimate(flops=0, bytes_accessed=8 * keys.size, transcendentals=0),
        name="pack",
    )(keys, values)


def split_kernel(copies, place_ref, queries_ref, *outs):
    chip, core = place_ref[3], place_ref[2]
    part_rows = queries_ref.shape[0] // copies
    for mask, out_ref in enumerate(outs):
        for side in range(2):
            device = 2 * (chip ^ mask) + (core ^ side)
            head, copy = device // copies, device % copies
            span = pl.ds(pl.multiple_of(head * HEAD_DIM, HEAD_DIM), HEAD_DIM)
            rows = pl.ds(pl.multiple_of(copy * part_rows, part_rows), part_rows)
            out_ref[side] = queries_ref[rows, span]


def split(chips, copies, place, queries):
    out = jax.ShapeDtypeStruct((2, queries.shape[0] // copies, HEAD_DIM), jnp.bfloat16)
    return pl.pallas_call(
        functools.partial(split_kernel, copies),
        out_shape=(out,) * chips,
        in_specs=[SMEM_SPEC, VMEM_SPEC],
        out_specs=(VMEM_SPEC,) * chips,
        compiler_params=params(4),
        cost_estimate=pl.CostEstimate(flops=0, bytes_accessed=4 * queries.size, transcendentals=0),
        name="split",
    )(place, queries)


def by_distance(pieces, passed):
    return [view for piece, other in zip(pieces, passed) for view in (piece.at[0], other)]


def unpack_kernel(copies, part_rows, place_ref, *refs):
    *pieces, near_ref, far_ref, attended_ref, text_ref = refs
    me = 2 * place_ref[3] + place_ref[2]
    share = text_ref.shape[0]
    half = text_ref.shape[1] // 2
    count = len(pieces) // 2
    passed = [near_ref.at[at] for at in range(count)] + [far_ref.at[at] for at in range(count)]
    blocks = [block for piece, other in zip(pieces, passed) for block in (piece.at[0], other)]
    for at, block_ref in enumerate(blocks):
        head, copy = (me ^ at) // copies, (me ^ at) % copies
        start = pl.multiple_of(head * HEAD_DIM, HEAD_DIM)
        rows = pl.ds(pl.multiple_of(copy * part_rows, part_rows), part_rows)
        attended_ref[rows, pl.ds(start, HEAD_DIM)] = block_ref[:part_rows, :]
        block = block_ref[part_rows:, :].astype(jnp.float32)
        text_ref[:, pl.ds(start, HEAD_DIM)] = block[:share].astype(text_ref.dtype)
        start = pl.multiple_of(half + head * HEAD_DIM, HEAD_DIM)
        text_ref[:, pl.ds(start, HEAD_DIM)] = block[share:].astype(text_ref.dtype)


def unpack(copies, part_rows, place, pieces, near, far):
    share = (near.shape[1] - part_rows) // 2
    return pl.pallas_call(
        functools.partial(unpack_kernel, copies, part_rows),
        out_shape=(
            jax.ShapeDtypeStruct((part_rows * copies, HEADS * HEAD_DIM), jnp.bfloat16),
            jax.ShapeDtypeStruct((share, 2 * HEADS * HEAD_DIM), jnp.bfloat16),
        ),
        in_specs=[SMEM_SPEC] + [VMEM_SPEC] * (len(pieces) + 2),
        out_specs=(VMEM_SPEC, VMEM_SPEC),
        compiler_params=params(6),
        name="unpack",
    )(place, *pieces, near, far)


def image_kernel(factor, first, packed_ref, *refs):
    *pieces, passed_ref, sum_ref, top_ref, keys_ref, wide_ref = refs
    blocks = by_distance(pieces, [passed_ref.at[first + at] for at in range(len(pieces))])
    img_dev = packed_ref.shape[1] // 2
    wide_ref[:, HEAD_DIM:] = jnp.ones((wide_ref.shape[0], HEAD_DIM), wide_ref.dtype)
    for device in range(packed_ref.shape[0]):
        rows = slice(device * img_dev, (device + 1) * img_dev)
        keys_ref[rows, :] = packed_ref[device, :img_dev, :]
        wide_ref[rows, :HEAD_DIM] = packed_ref[device, img_dev:, :]
    group = max(1, 256 // passed_ref.shape[1])
    rows = 256
    contract = (((1,), (1,)), ((), ()))
    count = sum_ref.shape[0]
    for start in range(0, count, rows):
        span = slice(start, start + rows)
        at = start // rows * group
        queries = jnp.concatenate([block[...] for block in blocks[at : at + group]], 0)
        scores = lax.dot_general(queries, keys_ref[...], contract, preferred_element_type=jnp.float32)
        scores = scores * factor
        top = jnp.max(scores, 1, keepdims=True)
        weights = jnp.exp2(scores - top).astype(jnp.bfloat16)
        sum_ref[span, :] = jnp.dot(weights, wide_ref[...], preferred_element_type=jnp.float32)
        top_ref[span, :] = jnp.broadcast_to(top, (rows, HEAD_DIM))


def image_attention(packed, first, pieces, passed, factor):
    count = 2 * len(pieces) * passed.shape[1]
    total = packed.size // HEAD_DIM // 2
    return pl.pallas_call(
        functools.partial(image_kernel, factor, first),
        out_shape=(
            jax.ShapeDtypeStruct((count, 2 * HEAD_DIM), jnp.float32),
            jax.ShapeDtypeStruct((count, HEAD_DIM), jnp.float32),
        ),
        in_specs=[VMEM_SPEC] * (len(pieces) + 2),
        out_specs=(VMEM_SPEC, VMEM_SPEC),
        scratch_shapes=[
            pltpu.VMEM((total, HEAD_DIM), jnp.bfloat16),
            pltpu.VMEM((total, 2 * HEAD_DIM), jnp.bfloat16),
        ],
        compiler_params=params(14),
        cost_estimate=pl.CostEstimate(
            flops=4 * count * total * HEAD_DIM,
            bytes_accessed=4 * total * HEAD_DIM + 10 * count * HEAD_DIM,
            transcendentals=count * total,
        ),
        name="image_attention",
    )(packed, *pieces, passed)


def finish_kernel(factor, first, count, place_ref, sum_ref, top_ref, mine_ref, got_ref, *refs):
    pieces, passed_ref, outs, text_ref = refs[:count], refs[count], refs[count + 1 : -1], refs[-1]
    blocks = by_distance(pieces, [passed_ref.at[first + at] for at in range(count)])
    core, valid = place_ref[2], place_ref[4]
    me = 2 * place_ref[3] + core
    part_rows = passed_ref.shape[1]
    half = mine_ref.shape[0]
    contract = (((1,), (1,)), ((), ()))
    mine, got = mine_ref[...], got_ref[...]
    keys = jnp.concatenate([mine[:, :HEAD_DIM], got[:, :HEAD_DIM]], 0)
    values = jnp.concatenate([mine[:, HEAD_DIM:], got[:, HEAD_DIM:]], 0)
    values = jnp.concatenate([values, jnp.ones(values.shape, values.dtype)], 1)
    lane = lax.broadcasted_iota(jnp.int32, (1, 2 * half), 1)
    text_position = jnp.where((lane >= half) == (core == 0), half, 0) + lane % half
    bias = jnp.where(text_position < valid, 0.0, -jnp.inf)
    group = max(1, 512 // part_rows)
    rows = group * part_rows
    for step in range(2 * len(outs) // group):
        span = slice(step * rows, (step + 1) * rows)
        queries = [block[...] for block in blocks[step * group : (step + 1) * group]]
        queries = jnp.concatenate(queries, 0)
        scores = lax.dot_general(queries, keys, contract, preferred_element_type=jnp.float32)
        scores = scores * factor + bias
        before = top_ref[span, :]
        top = jnp.maximum(before, jnp.max(scores, 1, keepdims=True))
        rescale = jnp.exp2(before - top)
        weights = jnp.exp2(scores - jnp.concatenate([top] * (2 * half // HEAD_DIM), 1))
        total = jnp.dot(weights.astype(jnp.bfloat16), values, preferred_element_type=jnp.float32)
        mixed = sum_ref[span, :HEAD_DIM] * rescale + total[:, :HEAD_DIM]
        total = sum_ref[span, HEAD_DIM:] * rescale + total[:, HEAD_DIM:]
        mixed = (mixed / total).astype(jnp.bfloat16)
        for at in range(group):
            to = step * group + at
            outs[to // 2][to % 2, :part_rows, :] = mixed[at * part_rows : (at + 1) * part_rows]
    low, high = mine.astype(jnp.float32), got.astype(jnp.float32)
    text_ref[:half, :] = jnp.where(core == 0, low, high)
    text_ref[half:, :] = jnp.where(core == 0, high, low)
    share = (outs[0].shape[1] - part_rows) // 2
    for to in range(2 * len(outs)):
        start = pl.multiple_of((me ^ (2 * first + to)) * share, share)
        block = text_ref[pl.ds(start, share), :]
        block = jnp.concatenate([block[:, :HEAD_DIM], block[:, HEAD_DIM:]], 0)
        outs[to // 2][to % 2, part_rows:, :] = block.astype(jnp.bfloat16)


def finish(place, first, pieces, passed, image, mine, got):
    chips, part_rows = passed.shape[0], passed.shape[1]
    half = mine.shape[0]
    outs = len(pieces)
    count = image[0].shape[0]
    out = jax.ShapeDtypeStruct((2, part_rows + 2 * half // chips, HEAD_DIM), jnp.bfloat16)
    factor = math.log2(math.e) / math.sqrt(HEAD_DIM)
    return pl.pallas_call(
        functools.partial(finish_kernel, factor, first, outs),
        out_shape=(out,) * outs,
        in_specs=[SMEM_SPEC] + [VMEM_SPEC] * (outs + 5),
        out_specs=(VMEM_SPEC,) * outs,
        scratch_shapes=[pltpu.VMEM((2 * half, 2 * HEAD_DIM), jnp.float32)],
        compiler_params=params(10),
        cost_estimate=pl.CostEstimate(
            flops=8 * count * half * HEAD_DIM,
            bytes_accessed=12 * count * HEAD_DIM,
            transcendentals=2 * count * half,
        ),
        name="finish",
    )(place, *image, mine, got, *pieces, passed)


def gather_kernel(*refs):
    for at, piece in enumerate(refs[:-1]):
        refs[-1][at] = piece[1]


def gather_other(pieces):
    shape = (len(pieces),) + pieces[0].shape[1:]
    return pl.pallas_call(
        gather_kernel,
        out_shape=jax.ShapeDtypeStruct(shape, pieces[0].dtype),
        in_specs=[VMEM_SPEC] * len(pieces),
        out_specs=VMEM_SPEC,
        compiler_params=params(4),
        cost_estimate=pl.CostEstimate(
            flops=0, bytes_accessed=2 * len(pieces) * pieces[0].size, transcendentals=0
        ),
        name="gather_other",
    )(*pieces)


def add_kernel(joint, *refs):
    ins, outs = refs[:4], refs[4:]
    if joint:
        outs = (outs[0].at[0], outs[1], outs[0].at[1], outs[2])
    for lane in range(2):
        mine, got = ins[2 * lane], ins[2 * lane + 1]
        half = mine.shape[0] // 2
        outs[2 * lane][...] = (
            mine[half:].astype(jnp.float32) + got[half:].astype(jnp.float32)
        ).astype(jnp.bfloat16)
        outs[2 * lane + 1][...] = mine[:half].astype(jnp.float32) + got[:half].astype(jnp.float32)


def add_halves(mine, got, joint=False):
    shape = (mine[0].shape[0] // 2,) + mine[0].shape[1:]
    sent, keep = jax.ShapeDtypeStruct(shape, jnp.bfloat16), jax.ShapeDtypeStruct(shape, jnp.float32)
    outs = (sent, keep) * 2
    if joint:
        outs = (jax.ShapeDtypeStruct((2,) + shape, jnp.bfloat16), keep, keep)
    outs = pl.pallas_call(
        functools.partial(add_kernel, joint),
        out_shape=outs,
        in_specs=[VMEM_SPEC] * 4,
        out_specs=(VMEM_SPEC,) * len(outs),
        compiler_params=params(6),
        cost_estimate=pl.CostEstimate(
            flops=2 * mine[0].size, bytes_accessed=12 * mine[0].size, transcendentals=0
        ),
        name="add_halves",
    )(mine[0], got[0], mine[1], got[1])
    if joint:
        return outs[0], outs[1:]
    return [outs[0], outs[2]], [outs[1], outs[3]]


def total_kernel(mine0, got0, mine1, got1, out_ref):
    for lane, (mine, got) in enumerate(((mine0, got0), (mine1, got1))):
        out_ref[lane] = (mine[...] + got[...].astype(jnp.float32)).astype(out_ref.dtype)


def add_all(mine, got):
    return pl.pallas_call(
        total_kernel,
        out_shape=jax.ShapeDtypeStruct((2,) + mine[0].shape, jnp.bfloat16),
        in_specs=[VMEM_SPEC] * 4,
        out_specs=VMEM_SPEC,
        compiler_params=params(4),
        cost_estimate=pl.CostEstimate(
            flops=2 * mine[0].size, bytes_accessed=16 * mine[0].size, transcendentals=0
        ),
        name="add_all",
    )(mine[0], got[0], mine[1], got[1])


def norm_kernel(mine_ref, got_ref, gain_ref, out0, out1):
    width = mine_ref.shape[3]
    for at in range(2):
        totals = [
            mine_ref[lane, at].astype(jnp.float32) + got_ref[lane, 1 - at].astype(jnp.float32)
            for lane in range(2)
        ]
        square = sum(jnp.sum(total * total, 1, keepdims=True) for total in totals)
        scale_rows = lax.rsqrt(square / (2 * width) + epsilon)
        for lane, (total, out_ref) in enumerate(zip(totals, (out0, out1))):
            gain = gain_ref[:, lane * width : (lane + 1) * width].astype(jnp.float32)
            out_ref[at] = (total * scale_rows * gain).astype(out_ref.dtype)


def normalize(mine, got, norm_gain):
    out = jax.ShapeDtypeStruct(mine.shape[1:], jnp.bfloat16)
    states = pl.pallas_call(
        norm_kernel,
        out_shape=(out, out),
        in_specs=[VMEM_SPEC] * 3,
        out_specs=(VMEM_SPEC,) * 2,
        compiler_params=params(4),
        cost_estimate=pl.CostEstimate(
            flops=4 * mine.size, bytes_accessed=8 * mine.size, transcendentals=0
        ),
        name="normalize",
    )(mine, got, norm_gain)
    return [part.reshape(-1, part.shape[2]) for part in states]


def join_kernel(mine0, got0, mine1, got1, out0, out1):
    for mine, got, out_ref in ((mine0, got0, out0), (mine1, got1, out1)):
        rows = mine.shape[0]
        if rows % 16:
            both = [mine[...].astype(jnp.float32), got[...].astype(jnp.float32)]
            out_ref[...] = jnp.concatenate(both, 0).astype(out_ref.dtype)
        else:
            out_ref[:rows, :] = mine[...]
            out_ref[rows:, :] = got[...]


def join(mine, got):
    rows, width = mine[0].shape
    out = jax.ShapeDtypeStruct((2 * rows, width), mine[0].dtype)
    return pl.pallas_call(
        join_kernel,
        out_shape=(out, out),
        in_specs=[VMEM_SPEC] * 4,
        out_specs=(VMEM_SPEC,) * 2,
        compiler_params=params(4),
        cost_estimate=pl.CostEstimate(
            flops=0, bytes_accessed=16 * rows * width, transcendentals=0
        ),
        name="join",
    )(mine[0], got[0], mine[1], got[1])


def local(
    enc_act,
    down_weight,
    norm_gain,
    text_in_weight,
    modulation_weight,
    key_value_weight,
    timesteps,
    lengths,
    image_queries,
    image_key_values,
):
    devices = lax.axis_size("seq")
    chips = devices // 2
    copies = devices // HEADS
    text_len = enc_act.shape[1]
    img_dev = image_queries.shape[1]
    part_rows = img_dev // copies
    factor = math.log2(math.e) / math.sqrt(HEAD_DIM)
    lanes = orders(chips)
    index = lax.axis_index("seq")
    chip, core = index // 2, index % 2
    place = jnp.stack([position(chip, lanes[0]), position(chip, lanes[1]), core, chip, lengths[0]])
    place = place.astype(jnp.int32)

    win0, kv0 = text_in_weight.T, key_value_weight
    mod0 = modulation_weight.transpose(1, 2, 0)
    time = time_embedding(timesteps)

    rounds = len(lanes[0])
    tie = lax.optimization_barrier

    def exchange(rows):
        return lax.all_to_all(rows, "seq", split_axis=0, concat_axis=0, tiled=True)

    image_key_values, image_queries = tie((image_key_values, image_queries))
    packed = pack(copies, image_key_values[0, :, 0], image_key_values[0, :, 1])
    act, packed = tie((enc_act[0].T, packed))
    packed = exchange(packed)
    pieces = {}

    def beside(chain, masks):
        chain, held = tie((chain, [pieces[mask] for mask in masks]))
        pieces.update((mask, swap(piece, 2 * mask)) for mask, piece in zip(masks, held))
        return chain

    def arrived(chain, masks):
        chain, held = tie((chain, [pieces[mask] for mask in masks]))
        pieces.update(zip(masks, held))
        return chain

    near, far = list(range(1, chips // 2)), list(range(chips // 2, chips))
    encoded = encoder(lanes, place, act, down_weight)
    keep, got = encoded[::2], [swap(other, 1) for other in encoded[1::2]]
    last = 2 * lanes[0][-1]
    for step in range(rounds - 1):
        sent, keep = add_halves(keep, got)
        if step == 0:
            sent, image_queries = tie((sent, image_queries))
            pieces.update(enumerate(split(chips, copies, place, image_queries[0])))
        masks = far[:1] * (step == 1)
        sent = beside(sent, masks)
        got = [swap(part, 2 * order[step]) for part, order in zip(sent, lanes)]
        got = arrived(got, masks)
    summed, packed = tie((add_all(keep, got), packed))
    summed, held, held_kv, held_mod = tie((summed, win0, kv0, mod0))
    win1, kv1, mod1 = swap(held, 1), swap(held_kv, 1), swap(held_mod, 1)
    summed = beside(summed, near)
    got = arrived(swap(summed, last), near)

    states = normalize(summed, got, norm_gain[None, :])
    images = []
    for step in reversed(range(rounds - 1)):
        masks = far[1:2] * (step == 1) if step else far[2:]
        states = beside(states, masks)
        got = [swap(state, 2 * order[step]) for state, order in zip(states, lanes)]
        got = arrived(got, masks)
        if step == rounds - 2:
            lines = modulation(time, mod0, mod1)
            got, win1, kv1, lines = tie((got, win1, kv1, lines))
        if step:
            states = join(states, got)
    states = [state for pair in zip(states, got) for state in pair]

    blocks = project(lanes, place, states, lines, win0, win1, kv0, kv1)
    keep, sent = [blocks[0], blocks[2]], [blocks[1], blocks[3]]
    pieces = [pieces[mask] for mask in range(chips)]
    for step in range(rounds - 1):
        got = [swap(part, 2 * order[step]) for part, order in zip(sent, lanes)]
        if step == 0:
            passed = swap(gather_other(pieces), 1)
            got, passed = tie((got, passed))
        if step == 1:
            sent, passed = tie((sent, passed))
            image = image_attention(packed, 0, pieces[: chips // 2], passed, factor)
            got, image = tie((got, image))
            images += image
        sent, keep = add_halves(keep, got, step == rounds - 2)
    sent, passed = tie((sent, passed))
    image = image_attention(packed, chips // 2, pieces[chips // 2 :], passed, factor)
    got, image = tie((swap(sent, last), image))
    images += image
    parts = (*keep, got)
    model_width = text_in_weight.shape[1] * devices
    mine, sent = combine(place, parts, chips, text_len // 2, model_width)
    got = swap(sent, 1)

    back = [None] * chips
    for call in (1, 0):
        span = slice(call * chips // 2, (call + 1) * chips // 2)
        image = images[2 * call : 2 * call + 2]
        blocks = finish(place, span.start, pieces[span], passed, image, mine, got)
        for mask, block in zip(range(chips)[span], blocks):
            back[mask] = swap(block, 2 * mask) if mask else block
    passed = [swap(gather_other(back[at : at + chips // 2]), 1) for at in (0, chips // 2)]
    attended, text_kv = unpack(copies, part_rows, place, back, *passed)
    return (attended[None], text_kv)


def solution(mesh):
    in_specs = (
        P("dp", None, "seq"),
        P("seq", None),
        P(),
        P(None, "seq"),
        P(None, None, "seq"),
        P("seq", None),
        P("dp"),
        P("dp"),
        P("dp", "seq", None),
        P("dp", "seq", None, None),
    )
    out_specs = (P("dp", "seq", None), P(("dp", "seq"), None))
    return jax.shard_map(local, mesh=mesh, in_specs=in_specs, out_specs=out_specs, check_vma=False)
```

```python
import functools
import math

import jax
import jax.numpy as jnp
from jax import lax
from jax.experimental import pallas as pl
from jax.experimental.pallas import tpu as pltpu
from jax.sharding import PartitionSpec as P

HEAD_DIM = 128
HEADS = 16
TEMB = 256
MIB = 1024 * 1024

epsilon = 1e-06

SMEM_SPEC = pl.BlockSpec(memory_space=pltpu.SMEM)
VMEM_SPEC = pl.BlockSpec(memory_space=pltpu.VMEM)


def params(mib):
    return pltpu.CompilerParams(vmem_limit_bytes=mib * MIB)


def swap(value, mask):
    devices = lax.axis_size("seq")
    return lax.ppermute(value, "seq", [(i, i ^ mask) for i in range(devices)])


def orders(chips):
    bits = [1 << i for i in range(chips.bit_length() - 1)]
    return (bits, [bits[1], bits[0]] + bits[2:])


def position(chip, order):
    last = len(order) - 1
    return sum(((chip >> (bit.bit_length() - 1)) & 1) << (last - i) for i, bit in enumerate(order))


def member(at, order):
    last = len(order) - 1
    return sum(bit for i, bit in enumerate(order) if (at >> (last - i)) & 1)


def time_embedding(timesteps):
    half_width = TEMB // 2
    freqs = jnp.exp(-math.log(10000.0) * jnp.arange(half_width, dtype=jnp.float32) / half_width)
    angles = timesteps.astype(jnp.float32)[:, None] * freqs[None, :]
    embedding = jnp.concatenate([jnp.cos(angles), jnp.sin(angles)], 1)
    return jax.nn.silu(embedding).astype(jnp.bfloat16)


def encoder_kernel(lanes, place_ref, act_ref, weight_ref, *refs):
    outs, lhs_ref = refs[:-1], refs[-1]
    chips, share, width = outs[0].shape
    core = place_ref[2]
    half = chips * share
    first = core == 0
    tile = width // 2
    lhs_ref[...] = act_ref[...].T
    for lane, order in enumerate(lanes):
        own_ref, other_ref = outs[2 * lane], outs[2 * lane + 1]
        for column in range(0, width, tile):
            start = lane * width + column
            result = jnp.dot(
                lhs_ref[...], weight_ref[:, start : start + tile], preferred_element_type=jnp.float32
            )
            own = jnp.where(first, result[:half], result[half:]).astype(own_ref.dtype)
            other = jnp.where(first, result[half:], result[:half]).astype(own_ref.dtype)
            own = own.reshape(chips, share, tile)
            other = other.reshape(chips, share, tile)
            for block in range(chips):
                to = place_ref[lane] ^ position(block, order)
                own_ref[to, :, column : column + tile] = own[block]
                other_ref[to, :, column : column + tile] = other[block]


def encoder(lanes, place, act, weight):
    chips = 1 << len(lanes[0])
    depth, rows = act.shape
    width = weight.shape[1]
    out = jax.ShapeDtypeStruct((chips, rows // 2 // chips, width // 2), jnp.bfloat16)
    return pl.pallas_call(
        functools.partial(encoder_kernel, lanes),
        out_shape=(out,) * 4,
        in_specs=[SMEM_SPEC, VMEM_SPEC, VMEM_SPEC],
        out_specs=(VMEM_SPEC,) * 4,
        scratch_shapes=[pltpu.VMEM((rows, depth), jnp.bfloat16)],
        compiler_params=params(16),
        cost_estimate=pl.CostEstimate(
            flops=2 * rows * depth * width,
            bytes_accessed=2 * (depth * rows + depth * width + rows * width),
            transcendentals=0,
        ),
        name="encoder",
    )(place, act, weight)


def modulation_kernel(time_ref, mod0_ref, mod1_ref, out_ref):
    contract = (((1,), (1,)), ((), ()))
    embedding = jnp.broadcast_to(time_ref[...].astype(jnp.float32), (16, time_ref.shape[1]))
    embedding = embedding.astype(jnp.bfloat16)
    row = lax.broadcasted_iota(jnp.int32, (16, mod0_ref.shape[1]), 0)
    for side, mod in enumerate((mod0_ref, mod1_ref)):
        shift, scale = [
            lax.dot_general(embedding, mod[at], contract, preferred_element_type=jnp.float32)
            for at in range(2)
        ]
        lines = jnp.where(row < 2, 1.0 + scale, shift)
        high = lines.astype(jnp.bfloat16).astype(jnp.float32)
        low = jnp.where(row % 2 == 0, high, lines - high)
        out_ref[side] = jnp.where(row < 4, low, 1.0 + scale)


def modulation(time, mod0, mod1):
    return pl.pallas_call(
        modulation_kernel,
        out_shape=jax.ShapeDtypeStruct((2, 16, mod0.shape[1]), jnp.float32),
        in_specs=[VMEM_SPEC] * 3,
        out_specs=VMEM_SPEC,
        compiler_params=params(4),
        name="modulation",
    )(time, mod0, mod1)


def slot_rows(chips, width):
    per_slot = 2 * 128 // width
    return chips * per_slot, -(-(chips * per_slot + 2) // 16) * 16


def project_kernel(lanes, place_ref, *refs):
    pieces, refs = (refs[:2], refs[2:4]), refs[4:]
    lines_ref, win0, win1, kv0, kv1, *outs, states, proj0, proj1, sums = refs
    chip = place_ref[3]
    half_chips = outs[0].shape[0]
    chips = 2 * half_chips
    rows = proj0.shape[0]
    share = rows // chips
    depth = states.shape[1]
    contract = (((1,), (1,)), ((), ()))
    for lane, order in enumerate(lanes):
        top, low = pieces[lane]
        states[: rows // 2, :] = top[...]
        states[rows // 2 :, :] = low[...]
        span = slice(lane * depth, (lane + 1) * depth)
        for win, proj in ((win0, proj0), (win1, proj1)):
            part = lax.dot_general(
                states[...], win[:, span], contract, preferred_element_type=jnp.float32
            )
            for at in range(chips):
                start = pl.multiple_of((chip ^ member(at, order)) * share, share)
                block = part[at * share : (at + 1) * share]
                if lane == 0:
                    proj[pl.ds(start, share), :] = block
                else:
                    proj[pl.ds(start, share), :] += block
    value0, value1 = proj0[...], proj1[...]
    first = jnp.sum(value0, 1, keepdims=True) + jnp.sum(value1, 1, keepdims=True)
    second = jnp.sum(value0 * value0, 1, keepdims=True) + jnp.sum(value1 * value1, 1, keepdims=True)
    lane = lax.broadcasted_iota(jnp.int32, sums.shape, 1)
    sums[...] = jnp.where(lane == 0, first, second).T
    left = []
    for side, value in enumerate((value0, value1)):
        lines = lines_ref[side]
        row = lax.broadcasted_iota(jnp.int32, lines.shape, 0)
        lines, scale = jnp.where(row < 4, lines, 0.0), lines[4:5]
        left.append(jnp.concatenate([value * scale, lines], 0).astype(jnp.bfloat16))
    width = outs[0].shape[2]
    slots, extra = slot_rows(chips, width)
    per_slot = slots // chips
    row = lax.broadcasted_iota(jnp.int32, (extra, width), 0)
    column = lax.broadcasted_iota(jnp.int32, (extra, width), 1)
    half = kv0.shape[1] // 2
    for lane, order in enumerate(lanes):
        line = sums[lane : lane + 1, :]
        high = line.astype(jnp.bfloat16).astype(jnp.float32)
        low = line - high
        if per_slot == 1:
            line = jnp.concatenate([high, low], 1)
        else:
            line = jnp.where(row % 2 == 0, high, low)
        line = jnp.where(row // per_slot == chip, line, 0.0)
        for at in reversed(range(chips)):
            out_ref, to = outs[2 * lane + at // half_chips], at % half_chips
            start = lane * half + (chip ^ member(at, order)) * width
            columns = pl.ds(pl.multiple_of(start, width), width)
            value = jnp.dot(left[0], kv0[:, columns], preferred_element_type=jnp.float32)
            value += jnp.dot(left[1], kv1[:, columns], preferred_element_type=jnp.float32)
            out_ref[to, :rows, :] = value[:rows].astype(out_ref.dtype)
            below = jnp.where(row == slots, value[rows : rows + 1] + value[rows + 1 : rows + 2], line)
            below = jnp.where(
                row == slots + 1, value[rows + 2 : rows + 3] + value[rows + 3 : rows + 4], below
            )
            out_ref[to, rows:, :] = below.astype(out_ref.dtype)


def project(lanes, place, pieces, lines, win0, win1, kv0, kv1):
    chips = 1 << len(lanes[0])
    rows = 2 * pieces[0].shape[0]
    features, depth = win0.shape
    total = kv0.shape[1]
    width = total // 2 // chips
    extra = slot_rows(chips, width)[1]
    out = jax.ShapeDtypeStruct((chips // 2, rows + extra, width), jnp.bfloat16)
    return pl.pallas_call(
        functools.partial(project_kernel, lanes),
        out_shape=(out,) * 4,
        in_specs=[SMEM_SPEC] + [VMEM_SPEC] * 9,
        out_specs=(VMEM_SPEC,) * 4,
        scratch_shapes=[
            pltpu.VMEM((rows, depth // 2), jnp.bfloat16),
            pltpu.VMEM((rows, features), jnp.float32),
            pltpu.VMEM((rows, features), jnp.float32),
            pltpu.VMEM((rows, 128), jnp.float32),
        ],
        compiler_params=params(14),
        cost_estimate=pl.CostEstimate(
            flops=4 * rows * features * (depth + total),
            bytes_accessed=2 * (rows * depth + 2 * features * (depth + total) + rows * total),
            transcendentals=0,
        ),
        name="project",
    )(place, *pieces, lines, win0, win1, kv0, kv1)


def combine_kernel(chips, model_width, place_ref, *refs):
    keep0, keep1, came_ref, mine_ref, sent_ref = refs
    core = place_ref[2]
    rows = mine_ref.shape[0]
    width = keep0.shape[2]
    slots = slot_rows(chips, width)[0]
    totals = [keep[0] + came_ref[lane, 0].astype(jnp.float32) for lane, keep in enumerate((keep0, keep1))]
    sums = []
    for total in totals:
        line = jnp.sum(total[rows : rows + slots], 0, keepdims=True)
        if width > 128:
            line = line[:, :128] + line[:, 128:]
        sums.append(line)
    mean_val = sums[0] / model_width
    scale = lax.rsqrt(sums[1] / model_width - mean_val * mean_val + epsilon)
    mean_val = jnp.broadcast_to(mean_val, (rows, rows)).T[:, 0:1]
    scale = jnp.broadcast_to(scale, (rows, rows)).T[:, 0:1]
    texts = []
    for total in totals:
        text = (total[:rows] - mean_val * total[rows + slots : rows + slots + 1]) * scale
        texts.append(text + total[rows + slots + 1 : rows + slots + 2])
    for part, text in enumerate(texts):
        span = slice(part * HEAD_DIM, (part + 1) * HEAD_DIM)
        if width > HEAD_DIM:
            low, high = text[:, :HEAD_DIM], text[:, HEAD_DIM:]
            mine_ref[:, span] = jnp.where(core == 0, low, high).astype(mine_ref.dtype)
            sent_ref[:, span] = jnp.where(core == 0, high, low).astype(mine_ref.dtype)
        else:
            mine_ref[:, span] = text.astype(mine_ref.dtype)
            sent_ref[:, span] = text.astype(mine_ref.dtype)


def combine(place, parts, chips, rows, model_width):
    out = jax.ShapeDtypeStruct((rows, 2 * HEAD_DIM), jnp.bfloat16)
    return pl.pallas_call(
        functools.partial(combine_kernel, chips, model_width),
        out_shape=(out, out),
        in_specs=[SMEM_SPEC] + [VMEM_SPEC] * 3,
        out_specs=(VMEM_SPEC, VMEM_SPEC),
        compiler_params=params(4),
        cost_estimate=pl.CostEstimate(
            flops=8 * rows * 512, bytes_accessed=12 * rows * 512, transcendentals=0
        ),
        name="combine",
    )(place, *parts)


def pack_kernel(copies, queries_ref, keys_ref, values_ref, out_ref):
    img_dev = keys_ref.shape[0]
    part_rows = img_dev // copies
    for device in range(out_ref.shape[0]):
        head, copy = device // copies, device % copies
        span = slice(head * HEAD_DIM, (head + 1) * HEAD_DIM)
        out_ref[device, :img_dev, :] = keys_ref[:, span]
        out_ref[device, img_dev : 2 * img_dev, :] = values_ref[:, span]
        out_ref[device, 2 * img_dev :, :] = queries_ref[copy * part_rows : (copy + 1) * part_rows, span]


def pack(copies, queries, keys, values):
    img_dev = keys.shape[0]
    rows = 2 * img_dev + img_dev // copies
    return pl.pallas_call(
        functools.partial(pack_kernel, copies),
        out_shape=jax.ShapeDtypeStruct((HEADS * copies, rows, HEAD_DIM), jnp.bfloat16),
        in_specs=[VMEM_SPEC] * 3,
        out_specs=VMEM_SPEC,
        compiler_params=params(8),
        cost_estimate=pl.CostEstimate(
            flops=0, bytes_accessed=4 * HEADS * copies * rows * HEAD_DIM, transcendentals=0
        ),
        name="pack",
    )(queries, keys, values)


def unpack_kernel(copies, part_rows, masks, place_ref, *refs):
    *pieces, near_ref, far_ref, attended_ref, text_ref = refs
    me = 2 * place_ref[3] + place_ref[2]
    share = text_ref.shape[0]
    half = text_ref.shape[1] // 2
    count = len(pieces) // 2
    passed = [near_ref.at[at] for at in range(count)] + [far_ref.at[at] for at in range(count)]
    blocks = [block for piece, other in zip(pieces, passed) for block in (piece.at[0], other)]
    for at, block_ref in enumerate(blocks):
        device = me ^ (2 * masks[at // 2] + at % 2)
        head, copy = device // copies, device % copies
        start = pl.multiple_of(head * HEAD_DIM, HEAD_DIM)
        rows = pl.ds(pl.multiple_of(copy * part_rows, part_rows), part_rows)
        attended_ref[rows, pl.ds(start, HEAD_DIM)] = block_ref[:part_rows, :]
        block = block_ref[part_rows:, :].astype(jnp.float32)
        text_ref[:, pl.ds(start, HEAD_DIM)] = block[:share].astype(text_ref.dtype)
        start = pl.multiple_of(half + head * HEAD_DIM, HEAD_DIM)
        text_ref[:, pl.ds(start, HEAD_DIM)] = block[share:].astype(text_ref.dtype)


def unpack(copies, part_rows, masks, place, pieces, near, far):
    share = (near.shape[1] - part_rows) // 2
    return pl.pallas_call(
        functools.partial(unpack_kernel, copies, part_rows, masks),
        out_shape=(
            jax.ShapeDtypeStruct((part_rows * copies, HEADS * HEAD_DIM), jnp.bfloat16),
            jax.ShapeDtypeStruct((share, 2 * HEADS * HEAD_DIM), jnp.bfloat16),
        ),
        in_specs=[SMEM_SPEC] + [VMEM_SPEC] * (len(pieces) + 2),
        out_specs=(VMEM_SPEC, VMEM_SPEC),
        compiler_params=params(6),
        name="unpack",
    )(place, *pieces, near, far)


def image_kernel(factor, masks, img_dev, place_ref, packed_ref, sum_ref, top_ref, keys_ref, wide_ref):
    me = 2 * place_ref[3] + place_ref[2]
    wide_ref[:, HEAD_DIM:] = jnp.ones((wide_ref.shape[0], HEAD_DIM), wide_ref.dtype)
    for device in range(packed_ref.shape[0]):
        rows = slice(device * img_dev, (device + 1) * img_dev)
        keys_ref[rows, :] = packed_ref[device, :img_dev, :]
        wide_ref[rows, :HEAD_DIM] = packed_ref[device, img_dev : 2 * img_dev, :]
    group = max(1, 256 // (packed_ref.shape[1] - 2 * img_dev))
    rows = 256
    contract = (((1,), (1,)), ((), ()))
    count = sum_ref.shape[0]
    for start in range(0, count, rows):
        span = slice(start, start + rows)
        at = start // rows * group
        queries = [
            packed_ref[me ^ (2 * masks[i // 2] + i % 2), 2 * img_dev :, :] for i in range(at, at + group)
        ]
        queries = jnp.concatenate(queries, 0)
        scores = lax.dot_general(queries, keys_ref[...], contract, preferred_element_type=jnp.float32)
        scores = scores * factor
        top = jnp.max(scores, 1, keepdims=True)
        weights = jnp.exp2(scores - top).astype(jnp.bfloat16)
        sum_ref[span, :] = jnp.dot(weights, wide_ref[...], preferred_element_type=jnp.float32)
        top_ref[span, :] = jnp.broadcast_to(top, (rows, HEAD_DIM))


def image_attention(place, packed, img_dev, factor, masks):
    count = 2 * len(masks) * (packed.shape[1] - 2 * img_dev)
    total = packed.shape[0] * img_dev
    return pl.pallas_call(
        functools.partial(image_kernel, factor, masks, img_dev),
        out_shape=(
            jax.ShapeDtypeStruct((count, 2 * HEAD_DIM), jnp.float32),
            jax.ShapeDtypeStruct((count, HEAD_DIM), jnp.float32),
        ),
        in_specs=[SMEM_SPEC, VMEM_SPEC],
        out_specs=(VMEM_SPEC, VMEM_SPEC),
        scratch_shapes=[
            pltpu.VMEM((total, HEAD_DIM), jnp.bfloat16),
            pltpu.VMEM((total, 2 * HEAD_DIM), jnp.bfloat16),
        ],
        compiler_params=params(14),
        cost_estimate=pl.CostEstimate(
            flops=4 * count * total * HEAD_DIM,
            bytes_accessed=4 * total * HEAD_DIM + 10 * count * HEAD_DIM,
            transcendentals=count * total,
        ),
        name="image_attention",
    )(place, packed)


def send_order(chips):
    half = chips // 2
    turns = [mask for at in range(half) for mask in (half + at, half - 1 - at)]
    return turns[:half], turns[half:]


def finish_kernel(factor, masks, img_dev, place_ref, packed_ref, sum_ref, top_ref, mine_ref, got_ref, *refs):
    *outs, text_ref = refs
    core, valid = place_ref[2], place_ref[4]
    me = 2 * place_ref[3] + core
    part_rows = packed_ref.shape[1] - 2 * img_dev
    half = mine_ref.shape[0]
    contract = (((1,), (1,)), ((), ()))
    mine, got = mine_ref[...], got_ref[...]
    keys = jnp.concatenate([mine[:, :HEAD_DIM], got[:, :HEAD_DIM]], 0)
    values = jnp.concatenate([mine[:, HEAD_DIM:], got[:, HEAD_DIM:]], 0)
    values = jnp.concatenate([values, jnp.ones(values.shape, values.dtype)], 1)
    lane = lax.broadcasted_iota(jnp.int32, (1, 2 * half), 1)
    text_position = jnp.where((lane >= half) == (core == 0), half, 0) + lane % half
    bias = jnp.where(text_position < valid, 0.0, -jnp.inf)
    group = max(1, 512 // part_rows)
    rows = group * part_rows
    for step in range(2 * len(outs) // group):
        span = slice(step * rows, (step + 1) * rows)
        queries = [
            packed_ref[me ^ (2 * masks[at // 2] + at % 2), 2 * img_dev :, :]
            for at in range(step * group, (step + 1) * group)
        ]
        queries = jnp.concatenate(queries, 0)
        scores = lax.dot_general(queries, keys, contract, preferred_element_type=jnp.float32)
        scores = scores * factor + bias
        before = top_ref[span, :]
        top = jnp.maximum(before, jnp.max(scores, 1, keepdims=True))
        rescale = jnp.exp2(before - top)
        weights = jnp.exp2(scores - jnp.concatenate([top] * (2 * half // HEAD_DIM), 1))
        total = jnp.dot(weights.astype(jnp.bfloat16), values, preferred_element_type=jnp.float32)
        mixed = sum_ref[span, :HEAD_DIM] * rescale + total[:, :HEAD_DIM]
        total = sum_ref[span, HEAD_DIM:] * rescale + total[:, HEAD_DIM:]
        mixed = (mixed / total).astype(jnp.bfloat16)
        for at in range(group):
            to = step * group + at
            outs[to // 2][to % 2, :part_rows, :] = mixed[at * part_rows : (at + 1) * part_rows]
    low, high = mine.astype(jnp.float32), got.astype(jnp.float32)
    text_ref[:half, :] = jnp.where(core == 0, low, high)
    text_ref[half:, :] = jnp.where(core == 0, high, low)
    share = (outs[0].shape[1] - part_rows) // 2
    for to in range(2 * len(outs)):
        start = pl.multiple_of((me ^ (2 * masks[to // 2] + to % 2)) * share, share)
        block = text_ref[pl.ds(start, share), :]
        block = jnp.concatenate([block[:, :HEAD_DIM], block[:, HEAD_DIM:]], 0)
        outs[to // 2][to % 2, part_rows:, :] = block.astype(jnp.bfloat16)


def finish(place, masks, packed, image, mine, got, img_dev, factor):
    devices, part_rows = packed.shape[0], packed.shape[1] - 2 * img_dev
    half = mine.shape[0]
    count = image[0].shape[0]
    outs = count // part_rows // 2
    out = jax.ShapeDtypeStruct((2, part_rows + 4 * half // devices, HEAD_DIM), jnp.bfloat16)
    return pl.pallas_call(
        functools.partial(finish_kernel, factor, masks, img_dev),
        out_shape=(out,) * outs,
        in_specs=[SMEM_SPEC] + [VMEM_SPEC] * 5,
        out_specs=(VMEM_SPEC,) * outs,
        scratch_shapes=[pltpu.VMEM((2 * half, 2 * HEAD_DIM), jnp.float32)],
        compiler_params=params(10),
        cost_estimate=pl.CostEstimate(
            flops=8 * count * half * HEAD_DIM,
            bytes_accessed=12 * count * HEAD_DIM,
            transcendentals=2 * count * half,
        ),
        name="finish",
    )(place, packed, *image, mine, got)


def gather_kernel(*refs):
    for at, piece in enumerate(refs[:-1]):
        refs[-1][at] = piece[1]


def gather_other(pieces):
    shape = (len(pieces),) + pieces[0].shape[1:]
    return pl.pallas_call(
        gather_kernel,
        out_shape=jax.ShapeDtypeStruct(shape, pieces[0].dtype),
        in_specs=[VMEM_SPEC] * len(pieces),
        out_specs=VMEM_SPEC,
        compiler_params=params(4),
        cost_estimate=pl.CostEstimate(
            flops=0, bytes_accessed=2 * len(pieces) * pieces[0].size, transcendentals=0
        ),
        name="gather_other",
    )(*pieces)


def add_kernel(joint, *refs):
    ins, outs = refs[:4], refs[4:]
    if joint:
        outs = (outs[0].at[0], outs[1], outs[0].at[1], outs[2])
    for lane in range(2):
        mine, got = ins[2 * lane], ins[2 * lane + 1]
        half = mine.shape[0] // 2
        outs[2 * lane][...] = (
            mine[half:].astype(jnp.float32) + got[half:].astype(jnp.float32)
        ).astype(jnp.bfloat16)
        outs[2 * lane + 1][...] = mine[:half].astype(jnp.float32) + got[:half].astype(jnp.float32)


def add_halves(mine, got, joint=False):
    shape = (mine[0].shape[0] // 2,) + mine[0].shape[1:]
    sent, keep = jax.ShapeDtypeStruct(shape, jnp.bfloat16), jax.ShapeDtypeStruct(shape, jnp.float32)
    outs = (sent, keep) * 2
    if joint:
        outs = (jax.ShapeDtypeStruct((2,) + shape, jnp.bfloat16), keep, keep)
    outs = pl.pallas_call(
        functools.partial(add_kernel, joint),
        out_shape=outs,
        in_specs=[VMEM_SPEC] * 4,
        out_specs=(VMEM_SPEC,) * len(outs),
        compiler_params=params(6),
        cost_estimate=pl.CostEstimate(
            flops=2 * mine[0].size, bytes_accessed=12 * mine[0].size, transcendentals=0
        ),
        name="add_halves",
    )(mine[0], got[0], mine[1], got[1])
    if joint:
        return outs[0], outs[1:]
    return [outs[0], outs[2]], [outs[1], outs[3]]


def total_kernel(mine0, got0, mine1, got1, out_ref):
    for lane, (mine, got) in enumerate(((mine0, got0), (mine1, got1))):
        out_ref[lane] = (mine[...] + got[...].astype(jnp.float32)).astype(out_ref.dtype)


def add_all(mine, got):
    return pl.pallas_call(
        total_kernel,
        out_shape=jax.ShapeDtypeStruct((2,) + mine[0].shape, jnp.bfloat16),
        in_specs=[VMEM_SPEC] * 4,
        out_specs=VMEM_SPEC,
        compiler_params=params(4),
        cost_estimate=pl.CostEstimate(
            flops=2 * mine[0].size, bytes_accessed=16 * mine[0].size, transcendentals=0
        ),
        name="add_all",
    )(mine[0], got[0], mine[1], got[1])


def norm_kernel(mine_ref, got_ref, gain_ref, out0, out1):
    width = mine_ref.shape[3]
    for at in range(2):
        totals = [
            mine_ref[lane, at].astype(jnp.float32) + got_ref[lane, 1 - at].astype(jnp.float32)
            for lane in range(2)
        ]
        square = sum(jnp.sum(total * total, 1, keepdims=True) for total in totals)
        scale_rows = lax.rsqrt(square / (2 * width) + epsilon)
        for lane, (total, out_ref) in enumerate(zip(totals, (out0, out1))):
            gain = gain_ref[:, lane * width : (lane + 1) * width].astype(jnp.float32)
            out_ref[at] = (total * scale_rows * gain).astype(out_ref.dtype)


def normalize(mine, got, norm_gain):
    out = jax.ShapeDtypeStruct(mine.shape[1:], jnp.bfloat16)
    states = pl.pallas_call(
        norm_kernel,
        out_shape=(out, out),
        in_specs=[VMEM_SPEC] * 3,
        out_specs=(VMEM_SPEC,) * 2,
        compiler_params=params(4),
        cost_estimate=pl.CostEstimate(
            flops=4 * mine.size, bytes_accessed=8 * mine.size, transcendentals=0
        ),
        name="normalize",
    )(mine, got, norm_gain)
    return [part.reshape(-1, part.shape[2]) for part in states]


def join_kernel(mine0, got0, mine1, got1, out0, out1):
    for mine, got, out_ref in ((mine0, got0, out0), (mine1, got1, out1)):
        rows = mine.shape[0]
        if rows % 16:
            both = [mine[...].astype(jnp.float32), got[...].astype(jnp.float32)]
            out_ref[...] = jnp.concatenate(both, 0).astype(out_ref.dtype)
        else:
            out_ref[:rows, :] = mine[...]
            out_ref[rows:, :] = got[...]


def join(mine, got):
    rows, width = mine[0].shape
    out = jax.ShapeDtypeStruct((2 * rows, width), mine[0].dtype)
    return pl.pallas_call(
        join_kernel,
        out_shape=(out, out),
        in_specs=[VMEM_SPEC] * 4,
        out_specs=(VMEM_SPEC,) * 2,
        compiler_params=params(4),
        cost_estimate=pl.CostEstimate(
            flops=0, bytes_accessed=16 * rows * width, transcendentals=0
        ),
        name="join",
    )(mine[0], got[0], mine[1], got[1])


def local(
    enc_act,
    down_weight,
    norm_gain,
    text_in_weight,
    modulation_weight,
    key_value_weight,
    timesteps,
    lengths,
    image_queries,
    image_key_values,
):
    devices = lax.axis_size("seq")
    chips = devices // 2
    copies = devices // HEADS
    text_len = enc_act.shape[1]
    img_dev = image_queries.shape[1]
    part_rows = img_dev // copies
    factor = math.log2(math.e) / math.sqrt(HEAD_DIM)
    lanes = orders(chips)
    index = lax.axis_index("seq")
    chip, core = index // 2, index % 2
    place = jnp.stack([position(chip, lanes[0]), position(chip, lanes[1]), core, chip, lengths[0]])
    place = place.astype(jnp.int32)

    win0, kv0 = text_in_weight.T, key_value_weight
    mod0 = modulation_weight.transpose(1, 2, 0)
    time = time_embedding(timesteps)

    rounds = len(lanes[0])
    turns = send_order(chips)
    tie = lax.optimization_barrier

    def exchange(rows):
        return lax.all_to_all(rows, "seq", split_axis=0, concat_axis=0, tiled=True)

    image_key_values, image_queries = tie((image_key_values, image_queries))
    packed = pack(copies, image_queries[0], image_key_values[0, :, 0], image_key_values[0, :, 1])
    act, packed = tie((enc_act[0].T, packed))
    packed = exchange(packed)
    encoded = encoder(lanes, place, act, down_weight)
    keep, got = encoded[::2], [swap(other, 1) for other in encoded[1::2]]
    last = 2 * lanes[0][-1]
    for step in range(rounds - 1):
        sent, keep = add_halves(keep, got)
        got = [swap(part, 2 * order[step]) for part, order in zip(sent, lanes)]
    summed, packed = tie((add_all(keep, got), packed))
    summed, held, held_kv, held_mod = tie((summed, win0, kv0, mod0))
    win1, kv1, mod1 = swap(held, 1), swap(held_kv, 1), swap(held_mod, 1)
    got = swap(summed, last)

    states = normalize(summed, got, norm_gain[None, :])
    images = []
    for step in reversed(range(rounds - 1)):
        if step == 0:
            states, packed = tie((states, packed))
            image = image_attention(place, packed, img_dev, factor, turns[0])
        got = [swap(state, 2 * order[step]) for state, order in zip(states, lanes)]
        if step == rounds - 2:
            lines = modulation(time, mod0, mod1)
            got, win1, kv1, lines = tie((got, win1, kv1, lines))
        if step:
            states = join(states, got)
    got, image = tie((got, image))
    images += image
    states = [state for pair in zip(states, got) for state in pair]

    blocks = project(lanes, place, states, lines, win0, win1, kv0, kv1)
    keep, sent = [blocks[0], blocks[2]], [blocks[1], blocks[3]]
    for step in range(rounds - 1):
        if step == 0:
            sent, packed = tie((sent, packed))
            image = image_attention(place, packed, img_dev, factor, turns[1])
        got = [swap(part, 2 * order[step]) for part, order in zip(sent, lanes)]
        if step == 0:
            got, image = tie((got, image))
            images += image
        sent, keep = add_halves(keep, got, step == rounds - 2)
    parts = (*keep, swap(sent, last))
    model_width = text_in_weight.shape[1] * devices
    mine, sent = combine(place, parts, chips, text_len // 2, model_width)
    got = swap(sent, 1)

    pieces, passed = [], []
    for call, masks in enumerate(turns):
        image = images[2 * call : 2 * call + 2]
        blocks = finish(place, masks, packed, image, mine, got, img_dev, factor)
        pieces += [swap(block, 2 * mask) if mask else block for mask, block in zip(masks, blocks)]
    for call in range(2):
        passed.append(swap(gather_other(pieces[call * chips // 2 : (call + 1) * chips // 2]), 1))
    attended, text_kv = unpack(copies, part_rows, turns[0] + turns[1], place, pieces, *passed)
    return (attended[None], text_kv)


def solution(mesh):
    in_specs = (
        P("dp", None, "seq"),
        P("seq", None),
        P(),
        P(None, "seq"),
        P(None, None, "seq"),
        P("seq", None),
        P("dp"),
        P("dp"),
        P("dp", "seq", None),
        P("dp", "seq", None, None),
    )
    out_specs = (P("dp", "seq", None), P(("dp", "seq"), None))
    return jax.shard_map(local, mesh=mesh, in_specs=in_specs, out_specs=out_specs, check_vma=False)
```

```python
import functools
import math

import jax
import jax.numpy as jnp
from jax import lax
from jax.experimental import pallas as pl
from jax.experimental.pallas import tpu as pltpu
from jax.sharding import PartitionSpec as P

HEAD_DIM = 128
HEADS = 16
TEMB = 256
MIB = 1024 * 1024

epsilon = 1e-06

SMEM_SPEC = pl.BlockSpec(memory_space=pltpu.SMEM)
VMEM_SPEC = pl.BlockSpec(memory_space=pltpu.VMEM)


def params(mib):
    return pltpu.CompilerParams(vmem_limit_bytes=mib * MIB)


def swap(value, mask):
    devices = lax.axis_size("seq")
    return lax.ppermute(value, "seq", [(i, i ^ mask) for i in range(devices)])


def orders(chips):
    bits = [1 << i for i in range(chips.bit_length() - 1)]
    return (bits, [bits[1], bits[0]] + bits[2:])


def member(at, order):
    last = len(order) - 1
    return sum(bit for i, bit in enumerate(order) if (at >> (last - i)) & 1)


def time_embedding(timesteps):
    half_width = TEMB // 2
    freqs = jnp.exp(-math.log(10000.0) * jnp.arange(half_width, dtype=jnp.float32) / half_width)
    angles = timesteps.astype(jnp.float32)[:, None] * freqs[None, :]
    embedding = jnp.concatenate([jnp.cos(angles), jnp.sin(angles)], 1)
    return jax.nn.silu(embedding).astype(jnp.bfloat16)


def encoder_kernel(chips, place_ref, act_ref, weight_ref, own_ref, other_ref, lhs_ref):
    chip, core = place_ref[1], place_ref[0]
    half = lhs_ref.shape[0] // 2
    half_chips = chips // 2
    width = weight_ref.shape[1]
    first = core == 0
    tile = width // 4
    lhs_ref[...] = act_ref[...].T
    for column in range(0, width, tile):
        columns = slice(column, column + tile)
        result = jnp.dot(lhs_ref[...], weight_ref[:, columns], preferred_element_type=jnp.float32)
        own = jnp.where(first, result[:half], result[half:]).astype(own_ref.dtype)
        other = jnp.where(first, result[half:], result[:half]).astype(own_ref.dtype)
        own = own.reshape(chips, half // chips, tile)
        other = other.reshape(chips, half // chips, tile)
        for block in range(chips):
            away = chip ^ block
            to = away % half_chips * 2 + away // half_chips
            own_ref[to, :, columns] = own[block]
            other_ref[to, :, columns] = other[block]


def encoder(chips, place, act, weight):
    depth, rows = act.shape
    width = weight.shape[1]
    out = jax.ShapeDtypeStruct((chips, rows // 2 // chips, width), jnp.bfloat16)
    return pl.pallas_call(
        functools.partial(encoder_kernel, chips),
        out_shape=(out, out),
        in_specs=[SMEM_SPEC, VMEM_SPEC, VMEM_SPEC],
        out_specs=(VMEM_SPEC,) * 2,
        scratch_shapes=[pltpu.VMEM((rows, depth), jnp.bfloat16)],
        compiler_params=params(16),
        cost_estimate=pl.CostEstimate(
            flops=2 * rows * depth * width,
            bytes_accessed=2 * (depth * rows + depth * width + rows * width),
            transcendentals=0,
        ),
        name="encoder",
    )(place, act, weight)


def fold_kernel(own_ref, got_ref, keep_ref, *sent):
    keep_ref[...] = own_ref[:2].astype(jnp.float32) + got_ref[:2].astype(jnp.float32)
    for at, out_ref in enumerate(sent):
        span = slice(2 * at + 2, 2 * at + 4)
        total = own_ref[span].astype(jnp.float32) + got_ref[span].astype(jnp.float32)
        out_ref[...] = total.astype(out_ref.dtype)


def fold(own, got):
    shape = (2,) + own.shape[1:]
    count = own.shape[0] // 2 - 1
    keep, *sent = pl.pallas_call(
        fold_kernel,
        out_shape=(jax.ShapeDtypeStruct(shape, jnp.float32),)
        + (jax.ShapeDtypeStruct(shape, jnp.bfloat16),) * count,
        in_specs=[VMEM_SPEC] * 2,
        out_specs=(VMEM_SPEC,) * (1 + count),
        compiler_params=params(8),
        cost_estimate=pl.CostEstimate(flops=own.size, bytes_accessed=8 * own.size, transcendentals=0),
        name="fold",
    )(own, got)
    return keep, sent


def modulation_kernel(time_ref, mod0_ref, mod1_ref, out_ref):
    contract = (((1,), (1,)), ((), ()))
    embedding = jnp.broadcast_to(time_ref[...].astype(jnp.float32), (16, time_ref.shape[1]))
    embedding = embedding.astype(jnp.bfloat16)
    row = lax.broadcasted_iota(jnp.int32, (16, mod0_ref.shape[1]), 0)
    for side, mod in enumerate((mod0_ref, mod1_ref)):
        shift, scale = [
            lax.dot_general(embedding, mod[at], contract, preferred_element_type=jnp.float32)
            for at in range(2)
        ]
        lines = jnp.where(row < 2, 1.0 + scale, shift)
        high = lines.astype(jnp.bfloat16).astype(jnp.float32)
        low = jnp.where(row % 2 == 0, high, lines - high)
        out_ref[side] = jnp.where(row < 4, low, 1.0 + scale)


def modulation(time, mod0, mod1):
    return pl.pallas_call(
        modulation_kernel,
        out_shape=jax.ShapeDtypeStruct((2, 16, mod0.shape[1]), jnp.float32),
        in_specs=[VMEM_SPEC] * 3,
        out_specs=VMEM_SPEC,
        compiler_params=params(4),
        name="modulation",
    )(time, mod0, mod1)


def slot_rows(chips, width):
    per_slot = 2 * 128 // width
    return chips * per_slot, -(-(chips * per_slot + 2) // 16) * 16


def project_kernel(lanes, place_ref, *refs):
    pieces, refs = (refs[:2], refs[2:4]), refs[4:]
    lines_ref, win0, win1, kv0, kv1, *outs, states, proj0, proj1, sums = refs
    chip = place_ref[1]
    half_chips = outs[0].shape[0]
    chips = 2 * half_chips
    rows = proj0.shape[0]
    share = rows // chips
    depth = states.shape[1]
    contract = (((1,), (1,)), ((), ()))
    for lane, order in enumerate(lanes):
        top, low = pieces[lane]
        states[: rows // 2, :] = top[...]
        states[rows // 2 :, :] = low[...]
        span = slice(lane * depth, (lane + 1) * depth)
        for win, proj in ((win0, proj0), (win1, proj1)):
            part = lax.dot_general(
                states[...], win[:, span], contract, preferred_element_type=jnp.float32
            )
            for at in range(chips):
                start = pl.multiple_of((chip ^ member(at, order)) * share, share)
                block = part[at * share : (at + 1) * share]
                if lane == 0:
                    proj[pl.ds(start, share), :] = block
                else:
                    proj[pl.ds(start, share), :] += block
    value0, value1 = proj0[...], proj1[...]
    first = jnp.sum(value0, 1, keepdims=True) + jnp.sum(value1, 1, keepdims=True)
    second = jnp.sum(value0 * value0, 1, keepdims=True) + jnp.sum(value1 * value1, 1, keepdims=True)
    lane = lax.broadcasted_iota(jnp.int32, sums.shape, 1)
    sums[...] = jnp.where(lane == 0, first, second).T
    left = []
    for side, value in enumerate((value0, value1)):
        lines = lines_ref[side]
        row = lax.broadcasted_iota(jnp.int32, lines.shape, 0)
        lines, scale = jnp.where(row < 4, lines, 0.0), lines[4:5]
        left.append(jnp.concatenate([value * scale, lines], 0).astype(jnp.bfloat16))
    width = outs[0].shape[2]
    slots, extra = slot_rows(chips, width)
    per_slot = slots // chips
    row = lax.broadcasted_iota(jnp.int32, (extra, width), 0)
    column = lax.broadcasted_iota(jnp.int32, (extra, width), 1)
    half = kv0.shape[1] // 2
    for lane, order in enumerate(lanes):
        line = sums[lane : lane + 1, :]
        high = line.astype(jnp.bfloat16).astype(jnp.float32)
        low = line - high
        if per_slot == 1:
            line = jnp.concatenate([high, low], 1)
        else:
            line = jnp.where(row % 2 == 0, high, low)
        line = jnp.where(row // per_slot == chip, line, 0.0)
        for at in reversed(range(chips)):
            out_ref, to = outs[2 * lane + at // half_chips], at % half_chips
            start = lane * half + (chip ^ member(at, order)) * width
            columns = pl.ds(pl.multiple_of(start, width), width)
            value = jnp.dot(left[0], kv0[:, columns], preferred_element_type=jnp.float32)
            value += jnp.dot(left[1], kv1[:, columns], preferred_element_type=jnp.float32)
            out_ref[to, :rows, :] = value[:rows].astype(out_ref.dtype)
            below = jnp.where(row == slots, value[rows : rows + 1] + value[rows + 1 : rows + 2], line)
            below = jnp.where(
                row == slots + 1, value[rows + 2 : rows + 3] + value[rows + 3 : rows + 4], below
            )
            out_ref[to, rows:, :] = below.astype(out_ref.dtype)


def project(lanes, place, pieces, lines, win0, win1, kv0, kv1):
    chips = 1 << len(lanes[0])
    rows = 2 * pieces[0].shape[0]
    features, depth = win0.shape
    total = kv0.shape[1]
    width = total // 2 // chips
    extra = slot_rows(chips, width)[1]
    out = jax.ShapeDtypeStruct((chips // 2, rows + extra, width), jnp.bfloat16)
    return pl.pallas_call(
        functools.partial(project_kernel, lanes),
        out_shape=(out,) * 4,
        in_specs=[SMEM_SPEC] + [VMEM_SPEC] * 9,
        out_specs=(VMEM_SPEC,) * 4,
        scratch_shapes=[
            pltpu.VMEM((rows, depth // 2), jnp.bfloat16),
            pltpu.VMEM((rows, features), jnp.float32),
            pltpu.VMEM((rows, features), jnp.float32),
            pltpu.VMEM((rows, 128), jnp.float32),
        ],
        compiler_params=params(14),
        cost_estimate=pl.CostEstimate(
            flops=4 * rows * features * (depth + total),
            bytes_accessed=2 * (rows * depth + 2 * features * (depth + total) + rows * total),
            transcendentals=0,
        ),
        name="project",
    )(place, *pieces, lines, win0, win1, kv0, kv1)


def combine_kernel(chips, model_width, place_ref, *refs):
    keep0, keep1, came_ref, mine_ref, sent_ref = refs
    core = place_ref[0]
    rows = mine_ref.shape[0]
    width = keep0.shape[2]
    slots = slot_rows(chips, width)[0]
    totals = [keep[0] + came_ref[lane, 0].astype(jnp.float32) for lane, keep in enumerate((keep0, keep1))]
    sums = []
    for total in totals:
        line = jnp.sum(total[rows : rows + slots], 0, keepdims=True)
        if width > 128:
            line = line[:, :128] + line[:, 128:]
        sums.append(line)
    mean_val = sums[0] / model_width
    scale = lax.rsqrt(sums[1] / model_width - mean_val * mean_val + epsilon)
    mean_val = jnp.broadcast_to(mean_val, (rows, rows)).T[:, 0:1]
    scale = jnp.broadcast_to(scale, (rows, rows)).T[:, 0:1]
    texts = []
    for total in totals:
        text = (total[:rows] - mean_val * total[rows + slots : rows + slots + 1]) * scale
        texts.append(text + total[rows + slots + 1 : rows + slots + 2])
    for part, text in enumerate(texts):
        span = slice(part * HEAD_DIM, (part + 1) * HEAD_DIM)
        if width > HEAD_DIM:
            low, high = text[:, :HEAD_DIM], text[:, HEAD_DIM:]
            mine_ref[:, span] = jnp.where(core == 0, low, high).astype(mine_ref.dtype)
            sent_ref[:, span] = jnp.where(core == 0, high, low).astype(mine_ref.dtype)
        else:
            mine_ref[:, span] = text.astype(mine_ref.dtype)
            sent_ref[:, span] = text.astype(mine_ref.dtype)


def combine(place, parts, chips, rows, model_width):
    out = jax.ShapeDtypeStruct((rows, 2 * HEAD_DIM), jnp.bfloat16)
    return pl.pallas_call(
        functools.partial(combine_kernel, chips, model_width),
        out_shape=(out, out),
        in_specs=[SMEM_SPEC] + [VMEM_SPEC] * 3,
        out_specs=(VMEM_SPEC, VMEM_SPEC),
        compiler_params=params(4),
        cost_estimate=pl.CostEstimate(
            flops=8 * rows * 512, bytes_accessed=12 * rows * 512, transcendentals=0
        ),
        name="combine",
    )(place, *parts)


def pack_kernel(copies, queries_ref, keys_ref, values_ref, out_ref):
    img_dev = keys_ref.shape[0]
    part_rows = img_dev // copies
    for device in range(out_ref.shape[0]):
        head, copy = device // copies, device % copies
        span = slice(head * HEAD_DIM, (head + 1) * HEAD_DIM)
        out_ref[device, :img_dev, :] = keys_ref[:, span]
        out_ref[device, img_dev : 2 * img_dev, :] = values_ref[:, span]
        out_ref[device, 2 * img_dev :, :] = queries_ref[copy * part_rows : (copy + 1) * part_rows, span]


def pack(copies, queries, keys, values):
    img_dev = keys.shape[0]
    rows = 2 * img_dev + img_dev // copies
    return pl.pallas_call(
        functools.partial(pack_kernel, copies),
        out_shape=jax.ShapeDtypeStruct((HEADS * copies, rows, HEAD_DIM), jnp.bfloat16),
        in_specs=[VMEM_SPEC] * 3,
        out_specs=VMEM_SPEC,
        compiler_params=params(8),
        cost_estimate=pl.CostEstimate(
            flops=0, bytes_accessed=4 * HEADS * copies * rows * HEAD_DIM, transcendentals=0
        ),
        name="pack",
    )(queries, keys, values)


def unpack_kernel(copies, part_rows, masks, place_ref, *refs):
    *pieces, near_ref, far_ref, attended_ref, text_ref = refs
    me = 2 * place_ref[1] + place_ref[0]
    share = text_ref.shape[0]
    half = text_ref.shape[1] // 2
    count = len(pieces) // 2
    passed = [near_ref.at[at] for at in range(count)] + [far_ref.at[at] for at in range(count)]
    blocks = [block for piece, other in zip(pieces, passed) for block in (piece.at[0], other)]
    for at, block_ref in enumerate(blocks):
        device = me ^ (2 * masks[at // 2] + at % 2)
        head, copy = device // copies, device % copies
        start = pl.multiple_of(head * HEAD_DIM, HEAD_DIM)
        rows = pl.ds(pl.multiple_of(copy * part_rows, part_rows), part_rows)
        attended_ref[rows, pl.ds(start, HEAD_DIM)] = block_ref[:part_rows, :]
        block = block_ref[part_rows:, :].astype(jnp.float32)
        text_ref[:, pl.ds(start, HEAD_DIM)] = block[:share].astype(text_ref.dtype)
        start = pl.multiple_of(half + head * HEAD_DIM, HEAD_DIM)
        text_ref[:, pl.ds(start, HEAD_DIM)] = block[share:].astype(text_ref.dtype)


def unpack(copies, part_rows, masks, place, pieces, near, far):
    share = (near.shape[1] - part_rows) // 2
    return pl.pallas_call(
        functools.partial(unpack_kernel, copies, part_rows, masks),
        out_shape=(
            jax.ShapeDtypeStruct((part_rows * copies, HEADS * HEAD_DIM), jnp.bfloat16),
            jax.ShapeDtypeStruct((share, 2 * HEADS * HEAD_DIM), jnp.bfloat16),
        ),
        in_specs=[SMEM_SPEC] + [VMEM_SPEC] * (len(pieces) + 2),
        out_specs=(VMEM_SPEC, VMEM_SPEC),
        compiler_params=params(6),
        name="unpack",
    )(place, *pieces, near, far)


def image_kernel(factor, masks, img_dev, place_ref, packed_ref, sum_ref, top_ref, keys_ref, wide_ref):
    me = 2 * place_ref[1] + place_ref[0]
    wide_ref[:, HEAD_DIM:] = jnp.ones((wide_ref.shape[0], HEAD_DIM), wide_ref.dtype)
    for device in range(packed_ref.shape[0]):
        rows = slice(device * img_dev, (device + 1) * img_dev)
        keys_ref[rows, :] = packed_ref[device, :img_dev, :]
        wide_ref[rows, :HEAD_DIM] = packed_ref[device, img_dev : 2 * img_dev, :]
    group = max(1, 256 // (packed_ref.shape[1] - 2 * img_dev))
    rows = 256
    contract = (((1,), (1,)), ((), ()))
    count = sum_ref.shape[0]
    for start in range(0, count, rows):
        span = slice(start, start + rows)
        at = start // rows * group
        queries = [
            packed_ref[me ^ (2 * masks[i // 2] + i % 2), 2 * img_dev :, :] for i in range(at, at + group)
        ]
        queries = jnp.concatenate(queries, 0)
        scores = lax.dot_general(queries, keys_ref[...], contract, preferred_element_type=jnp.float32)
        scores = scores * factor
        top = jnp.max(scores, 1, keepdims=True)
        weights = jnp.exp2(scores - top).astype(jnp.bfloat16)
        sum_ref[span, :] = jnp.dot(weights, wide_ref[...], preferred_element_type=jnp.float32)
        top_ref[span, :] = jnp.broadcast_to(top, (rows, HEAD_DIM))


def image_attention(place, packed, img_dev, factor, masks):
    count = 2 * len(masks) * (packed.shape[1] - 2 * img_dev)
    total = packed.shape[0] * img_dev
    return pl.pallas_call(
        functools.partial(image_kernel, factor, masks, img_dev),
        out_shape=(
            jax.ShapeDtypeStruct((count, 2 * HEAD_DIM), jnp.float32),
            jax.ShapeDtypeStruct((count, HEAD_DIM), jnp.float32),
        ),
        in_specs=[SMEM_SPEC, VMEM_SPEC],
        out_specs=(VMEM_SPEC, VMEM_SPEC),
        scratch_shapes=[
            pltpu.VMEM((total, HEAD_DIM), jnp.bfloat16),
            pltpu.VMEM((total, 2 * HEAD_DIM), jnp.bfloat16),
        ],
        compiler_params=params(14),
        cost_estimate=pl.CostEstimate(
            flops=4 * count * total * HEAD_DIM,
            bytes_accessed=4 * total * HEAD_DIM + 10 * count * HEAD_DIM,
            transcendentals=count * total,
        ),
        name="image_attention",
    )(place, packed)


def send_order(chips):
    half = chips // 2
    turns = [mask for at in range(half) for mask in (half + at, half - 1 - at)]
    return turns[:half], turns[half:]


def finish_kernel(factor, masks, img_dev, place_ref, packed_ref, sum_ref, top_ref, mine_ref, got_ref, *refs):
    *outs, text_ref = refs
    core, valid = place_ref[0], place_ref[2]
    me = 2 * place_ref[1] + core
    part_rows = packed_ref.shape[1] - 2 * img_dev
    half = mine_ref.shape[0]
    contract = (((1,), (1,)), ((), ()))
    mine, got = mine_ref[...], got_ref[...]
    keys = jnp.concatenate([mine[:, :HEAD_DIM], got[:, :HEAD_DIM]], 0)
    values = jnp.concatenate([mine[:, HEAD_DIM:], got[:, HEAD_DIM:]], 0)
    values = jnp.concatenate([values, jnp.ones(values.shape, values.dtype)], 1)
    lane = lax.broadcasted_iota(jnp.int32, (1, 2 * half), 1)
    text_position = jnp.where((lane >= half) == (core == 0), half, 0) + lane % half
    bias = jnp.where(text_position < valid, 0.0, -jnp.inf)
    group = max(1, 512 // part_rows)
    rows = group * part_rows
    for step in range(2 * len(outs) // group):
        span = slice(step * rows, (step + 1) * rows)
        queries = [
            packed_ref[me ^ (2 * masks[at // 2] + at % 2), 2 * img_dev :, :]
            for at in range(step * group, (step + 1) * group)
        ]
        queries = jnp.concatenate(queries, 0)
        scores = lax.dot_general(queries, keys, contract, preferred_element_type=jnp.float32)
        scores = scores * factor + bias
        before = top_ref[span, :]
        top = jnp.maximum(before, jnp.max(scores, 1, keepdims=True))
        rescale = jnp.exp2(before - top)
        weights = jnp.exp2(scores - jnp.concatenate([top] * (2 * half // HEAD_DIM), 1))
        total = jnp.dot(weights.astype(jnp.bfloat16), values, preferred_element_type=jnp.float32)
        mixed = sum_ref[span, :HEAD_DIM] * rescale + total[:, :HEAD_DIM]
        total = sum_ref[span, HEAD_DIM:] * rescale + total[:, HEAD_DIM:]
        mixed = (mixed / total).astype(jnp.bfloat16)
        for at in range(group):
            to = step * group + at
            outs[to // 2][to % 2, :part_rows, :] = mixed[at * part_rows : (at + 1) * part_rows]
    low, high = mine.astype(jnp.float32), got.astype(jnp.float32)
    text_ref[:half, :] = jnp.where(core == 0, low, high)
    text_ref[half:, :] = jnp.where(core == 0, high, low)
    share = (outs[0].shape[1] - part_rows) // 2
    for to in range(2 * len(outs)):
        start = pl.multiple_of((me ^ (2 * masks[to // 2] + to % 2)) * share, share)
        block = text_ref[pl.ds(start, share), :]
        block = jnp.concatenate([block[:, :HEAD_DIM], block[:, HEAD_DIM:]], 0)
        outs[to // 2][to % 2, part_rows:, :] = block.astype(jnp.bfloat16)


def finish(place, masks, packed, image, mine, got, img_dev, factor):
    devices, part_rows = packed.shape[0], packed.shape[1] - 2 * img_dev
    half = mine.shape[0]
    count = image[0].shape[0]
    outs = count // part_rows // 2
    out = jax.ShapeDtypeStruct((2, part_rows + 4 * half // devices, HEAD_DIM), jnp.bfloat16)
    return pl.pallas_call(
        functools.partial(finish_kernel, factor, masks, img_dev),
        out_shape=(out,) * outs,
        in_specs=[SMEM_SPEC] + [VMEM_SPEC] * 5,
        out_specs=(VMEM_SPEC,) * outs,
        scratch_shapes=[pltpu.VMEM((2 * half, 2 * HEAD_DIM), jnp.float32)],
        compiler_params=params(10),
        cost_estimate=pl.CostEstimate(
            flops=8 * count * half * HEAD_DIM,
            bytes_accessed=12 * count * HEAD_DIM,
            transcendentals=2 * count * half,
        ),
        name="finish",
    )(place, packed, *image, mine, got)


def gather_kernel(*refs):
    for at, piece in enumerate(refs[:-1]):
        refs[-1][at] = piece[1]


def gather_other(pieces):
    shape = (len(pieces),) + pieces[0].shape[1:]
    return pl.pallas_call(
        gather_kernel,
        out_shape=jax.ShapeDtypeStruct(shape, pieces[0].dtype),
        in_specs=[VMEM_SPEC] * len(pieces),
        out_specs=VMEM_SPEC,
        compiler_params=params(4),
        cost_estimate=pl.CostEstimate(
            flops=0, bytes_accessed=2 * len(pieces) * pieces[0].size, transcendentals=0
        ),
        name="gather_other",
    )(*pieces)


def add_kernel(joint, *refs):
    ins, outs = refs[:4], refs[4:]
    if joint:
        outs = (outs[0].at[0], outs[1], outs[0].at[1], outs[2])
    for lane in range(2):
        mine, got = ins[2 * lane], ins[2 * lane + 1]
        half = mine.shape[0] // 2
        outs[2 * lane][...] = (
            mine[half:].astype(jnp.float32) + got[half:].astype(jnp.float32)
        ).astype(jnp.bfloat16)
        outs[2 * lane + 1][...] = mine[:half].astype(jnp.float32) + got[:half].astype(jnp.float32)


def add_halves(mine, got, joint=False):
    shape = (mine[0].shape[0] // 2,) + mine[0].shape[1:]
    sent, keep = jax.ShapeDtypeStruct(shape, jnp.bfloat16), jax.ShapeDtypeStruct(shape, jnp.float32)
    outs = (sent, keep) * 2
    if joint:
        outs = (jax.ShapeDtypeStruct((2,) + shape, jnp.bfloat16), keep, keep)
    outs = pl.pallas_call(
        functools.partial(add_kernel, joint),
        out_shape=outs,
        in_specs=[VMEM_SPEC] * 4,
        out_specs=(VMEM_SPEC,) * len(outs),
        compiler_params=params(6),
        cost_estimate=pl.CostEstimate(
            flops=2 * mine[0].size, bytes_accessed=12 * mine[0].size, transcendentals=0
        ),
        name="add_halves",
    )(mine[0], got[0], mine[1], got[1])
    if joint:
        return outs[0], outs[1:]
    return [outs[0], outs[2]], [outs[1], outs[3]]


def total_kernel(keep_ref, *refs):
    total = keep_ref[...]
    for got_ref in refs[:-1]:
        total += got_ref[...].astype(jnp.float32)
    refs[-1][...] = total.astype(refs[-1].dtype)


def add_all(keep, got):
    return pl.pallas_call(
        total_kernel,
        out_shape=jax.ShapeDtypeStruct(keep.shape, jnp.bfloat16),
        in_specs=[VMEM_SPEC] * (1 + len(got)),
        out_specs=VMEM_SPEC,
        compiler_params=params(4),
        cost_estimate=pl.CostEstimate(
            flops=4 * keep.size, bytes_accessed=12 * keep.size, transcendentals=0
        ),
        name="add_all",
    )(keep, *got)


def norm_kernel(mine_ref, got_ref, gain_ref, *outs):
    width = mine_ref.shape[2] // 2
    for at in range(2):
        total = mine_ref[at].astype(jnp.float32) + got_ref[1 - at].astype(jnp.float32)
        scale_rows = lax.rsqrt(jnp.mean(total * total, 1, keepdims=True) + epsilon)
        total = total * scale_rows * gain_ref[...].astype(jnp.float32)
        for lane, out_ref in enumerate(outs):
            out_ref[at] = total[:, lane * width : (lane + 1) * width].astype(out_ref.dtype)


def normalize(mine, got, norm_gain):
    out = jax.ShapeDtypeStruct(mine.shape[:2] + (mine.shape[2] // 2,), jnp.bfloat16)
    states = pl.pallas_call(
        norm_kernel,
        out_shape=(out, out),
        in_specs=[VMEM_SPEC] * 3,
        out_specs=(VMEM_SPEC,) * 2,
        compiler_params=params(4),
        cost_estimate=pl.CostEstimate(
            flops=4 * mine.size, bytes_accessed=8 * mine.size, transcendentals=0
        ),
        name="normalize",
    )(mine, got, norm_gain)
    return [part.reshape(-1, part.shape[2]) for part in states]


def join_kernel(mine0, got0, mine1, got1, out0, out1):
    for mine, got, out_ref in ((mine0, got0, out0), (mine1, got1, out1)):
        rows = mine.shape[0]
        if rows % 16:
            both = [mine[...].astype(jnp.float32), got[...].astype(jnp.float32)]
            out_ref[...] = jnp.concatenate(both, 0).astype(out_ref.dtype)
        else:
            out_ref[:rows, :] = mine[...]
            out_ref[rows:, :] = got[...]


def join(mine, got):
    rows, width = mine[0].shape
    out = jax.ShapeDtypeStruct((2 * rows, width), mine[0].dtype)
    return pl.pallas_call(
        join_kernel,
        out_shape=(out, out),
        in_specs=[VMEM_SPEC] * 4,
        out_specs=(VMEM_SPEC,) * 2,
        compiler_params=params(4),
        cost_estimate=pl.CostEstimate(
            flops=0, bytes_accessed=16 * rows * width, transcendentals=0
        ),
        name="join",
    )(mine[0], got[0], mine[1], got[1])


def local(
    enc_act,
    down_weight,
    norm_gain,
    text_in_weight,
    modulation_weight,
    key_value_weight,
    timesteps,
    lengths,
    image_queries,
    image_key_values,
):
    devices = lax.axis_size("seq")
    chips = devices // 2
    copies = devices // HEADS
    text_len = enc_act.shape[1]
    img_dev = image_queries.shape[1]
    part_rows = img_dev // copies
    factor = math.log2(math.e) / math.sqrt(HEAD_DIM)
    lanes = orders(chips)
    index = lax.axis_index("seq")
    chip, core = index // 2, index % 2
    place = jnp.stack([core, chip, lengths[0]])
    place = place.astype(jnp.int32)

    win0, kv0 = text_in_weight.T, key_value_weight
    mod0 = modulation_weight.transpose(1, 2, 0)
    time = time_embedding(timesteps)

    rounds = len(lanes[0])
    turns = send_order(chips)
    tie = lax.optimization_barrier

    def exchange(rows):
        return lax.all_to_all(rows, "seq", split_axis=0, concat_axis=0, tiled=True)

    image_key_values, image_queries = tie((image_key_values, image_queries))
    packed = pack(copies, image_queries[0], image_key_values[0, :, 0], image_key_values[0, :, 1])
    act, packed = tie((enc_act[0].T, packed))
    packed = exchange(packed)
    own, other = encoder(chips, place, act, down_weight)
    last = 2 * lanes[0][-1]
    keep, sent = fold(own, swap(other, 1))
    got = [swap(part, 2 * mask) for mask, part in enumerate(sent, 1)]
    summed, packed = tie((add_all(keep, got), packed))
    summed, held, held_kv, held_mod = tie((summed, win0, kv0, mod0))
    win1, kv1, mod1 = swap(held, 1), swap(held_kv, 1), swap(held_mod, 1)
    got = swap(summed, last)

    states = normalize(summed, got, norm_gain[None, :])
    images = []
    for step in reversed(range(rounds - 1)):
        if step == 0:
            states, packed = tie((states, packed))
            image = image_attention(place, packed, img_dev, factor, turns[0])
        got = [swap(state, 2 * order[step]) for state, order in zip(states, lanes)]
        if step == rounds - 2:
            lines = modulation(time, mod0, mod1)
            got, win1, kv1, lines = tie((got, win1, kv1, lines))
        if step:
            states = join(states, got)
    got, image = tie((got, image))
    images += image
    states = [state for pair in zip(states, got) for state in pair]

    blocks = project(lanes, place, states, lines, win0, win1, kv0, kv1)
    keep, sent = [blocks[0], blocks[2]], [blocks[1], blocks[3]]
    for step in range(rounds - 1):
        if step == 0:
            sent, packed = tie((sent, packed))
            image = image_attention(place, packed, img_dev, factor, turns[1])
        got = [swap(part, 2 * order[step]) for part, order in zip(sent, lanes)]
        if step == 0:
            got, image = tie((got, image))
            images += image
        sent, keep = add_halves(keep, got, step == rounds - 2)
    parts = (*keep, swap(sent, last))
    model_width = text_in_weight.shape[1] * devices
    mine, sent = combine(place, parts, chips, text_len // 2, model_width)
    got = swap(sent, 1)

    pieces, passed = [], []
    for call, masks in enumerate(turns):
        image = images[2 * call : 2 * call + 2]
        blocks = finish(place, masks, packed, image, mine, got, img_dev, factor)
        pieces += [swap(block, 2 * mask) if mask else block for mask, block in zip(masks, blocks)]
    for call in range(2):
        passed.append(swap(gather_other(pieces[call * chips // 2 : (call + 1) * chips // 2]), 1))
    attended, text_kv = unpack(copies, part_rows, turns[0] + turns[1], place, pieces, *passed)
    return (attended[None], text_kv)


def solution(mesh):
    in_specs = (
        P("dp", None, "seq"),
        P("seq", None),
        P(),
        P(None, "seq"),
        P(None, None, "seq"),
        P("seq", None),
        P("dp"),
        P("dp"),
        P("dp", "seq", None),
        P("dp", "seq", None, None),
    )
    out_specs = (P("dp", "seq", None), P(("dp", "seq"), None))
    return jax.shard_map(local, mesh=mesh, in_specs=in_specs, out_specs=out_specs, check_vma=False)
```

```python
import functools
import math

import jax
import jax.numpy as jnp
from jax import lax
from jax.experimental import pallas as pl
from jax.experimental.pallas import tpu as pltpu
from jax.sharding import PartitionSpec as P

HEAD_DIM = 128
HEADS = 16
TEMB = 256
MIB = 1024 * 1024

epsilon = 1e-06

SMEM_SPEC = pl.BlockSpec(memory_space=pltpu.SMEM)
VMEM_SPEC = pl.BlockSpec(memory_space=pltpu.VMEM)


def params(mib):
    return pltpu.CompilerParams(vmem_limit_bytes=mib * MIB)


def swap(value, mask):
    devices = lax.axis_size("seq")
    return lax.ppermute(value, "seq", [(i, i ^ mask) for i in range(devices)])


def orders(chips):
    bits = [1 << i for i in range(chips.bit_length() - 1)]
    return (bits, [bits[1], bits[0]] + bits[2:])


def position(chip, order):
    last = len(order) - 1
    return sum(((chip >> (bit.bit_length() - 1)) & 1) << (last - i) for i, bit in enumerate(order))


def member(at, order):
    last = len(order) - 1
    return sum(bit for i, bit in enumerate(order) if (at >> (last - i)) & 1)


def time_embedding(timesteps):
    half_width = TEMB // 2
    freqs = jnp.exp(-math.log(10000.0) * jnp.arange(half_width, dtype=jnp.float32) / half_width)
    angles = timesteps.astype(jnp.float32)[:, None] * freqs[None, :]
    embedding = jnp.concatenate([jnp.cos(angles), jnp.sin(angles)], 1)
    return jax.nn.silu(embedding).astype(jnp.bfloat16)


def encoder_kernel(lanes, place_ref, act_ref, weight_ref, *refs):
    outs, lhs_ref = refs[:-1], refs[-1]
    chips, share, width = outs[0].shape
    core = place_ref[2]
    half = chips * share
    first = core == 0
    tile = width // 2
    lhs_ref[...] = act_ref[...].T
    for lane, order in enumerate(lanes):
        own_ref, other_ref = outs[2 * lane], outs[2 * lane + 1]
        for column in range(0, width, tile):
            start = lane * width + column
            result = jnp.dot(
                lhs_ref[...], weight_ref[:, start : start + tile], preferred_element_type=jnp.float32
            )
            own = jnp.where(first, result[:half], result[half:]).astype(own_ref.dtype)
            other = jnp.where(first, result[half:], result[:half]).astype(own_ref.dtype)
            own = own.reshape(chips, share, tile)
            other = other.reshape(chips, share, tile)
            for block in range(chips):
                to = place_ref[lane] ^ position(block, order)
                own_ref[to, :, column : column + tile] = own[block]
                other_ref[to, :, column : column + tile] = other[block]


def encoder(lanes, place, act, weight):
    chips = 1 << len(lanes[0])
    depth, rows = act.shape
    width = weight.shape[1]
    out = jax.ShapeDtypeStruct((chips, rows // 2 // chips, width // 2), jnp.bfloat16)
    return pl.pallas_call(
        functools.partial(encoder_kernel, lanes),
        out_shape=(out,) * 4,
        in_specs=[SMEM_SPEC, VMEM_SPEC, VMEM_SPEC],
        out_specs=(VMEM_SPEC,) * 4,
        scratch_shapes=[pltpu.VMEM((rows, depth), jnp.bfloat16)],
        compiler_params=params(16),
        cost_estimate=pl.CostEstimate(
            flops=2 * rows * depth * width,
            bytes_accessed=2 * (depth * rows + depth * width + rows * width),
            transcendentals=0,
        ),
        name="encoder",
    )(place, act, weight)


def modulation_kernel(time_ref, mod0_ref, mod1_ref, out_ref):
    contract = (((1,), (1,)), ((), ()))
    embedding = jnp.broadcast_to(time_ref[...].astype(jnp.float32), (16, time_ref.shape[1]))
    embedding = embedding.astype(jnp.bfloat16)
    row = lax.broadcasted_iota(jnp.int32, (16, mod0_ref.shape[1]), 0)
    for side, mod in enumerate((mod0_ref, mod1_ref)):
        shift, scale = [
            lax.dot_general(embedding, mod[at], contract, preferred_element_type=jnp.float32)
            for at in range(2)
        ]
        lines = jnp.where(row < 2, 1.0 + scale, shift)
        high = lines.astype(jnp.bfloat16).astype(jnp.float32)
        low = jnp.where(row % 2 == 0, high, lines - high)
        out_ref[side] = jnp.where(row < 4, low, 1.0 + scale)


def modulation(time, mod0, mod1):
    return pl.pallas_call(
        modulation_kernel,
        out_shape=jax.ShapeDtypeStruct((2, 16, mod0.shape[1]), jnp.float32),
        in_specs=[VMEM_SPEC] * 3,
        out_specs=VMEM_SPEC,
        compiler_params=params(4),
        name="modulation",
    )(time, mod0, mod1)


def slot_rows(chips, width):
    means, squares = chips * 2 * 128 // width, chips * 128 // width
    return means, squares, -(-max(means + chips, squares + chips + 2) // 16) * 16


def project_kernel(lanes, place_ref, *refs):
    pieces, refs = (refs[:2], refs[2:4]), refs[4:]
    lines_ref, win0, win1, kv0, kv1, *outs, states, proj0, proj1, sums, keys_shift = refs
    chip = place_ref[3]
    half_chips = outs[0].shape[0]
    chips = 2 * half_chips
    rows = proj0.shape[0]
    share = rows // chips
    depth = states.shape[1]
    contract = (((1,), (1,)), ((), ()))
    for lane, order in enumerate(lanes):
        top, low = pieces[lane]
        states[: rows // 2, :] = top[...]
        states[rows // 2 :, :] = low[...]
        span = slice(lane * depth, (lane + 1) * depth)
        for win, proj in ((win0, proj0), (win1, proj1)):
            part = lax.dot_general(
                states[...], win[:, span], contract, preferred_element_type=jnp.float32
            )
            for at in range(chips):
                start = pl.multiple_of((chip ^ member(at, order)) * share, share)
                block = part[at * share : (at + 1) * share]
                if lane == 0:
                    proj[pl.ds(start, share), :] = block
                else:
                    proj[pl.ds(start, share), :] += block
    mean = jnp.sum(proj0[...], 1, keepdims=True) + jnp.sum(proj1[...], 1, keepdims=True)
    mean = mean / (2 * proj0.shape[1])
    value0, value1 = proj0[...] - mean, proj1[...] - mean
    square = jnp.sum(value0 * value0, 1, keepdims=True) + jnp.sum(value1 * value1, 1, keepdims=True)
    lane = lax.broadcasted_iota(jnp.int32, sums.shape, 1)
    sums[...] = jnp.where(lane == 0, mean, square).T
    left = []
    for side, value in enumerate((value0, value1)):
        lines = lines_ref[side]
        row = lax.broadcasted_iota(jnp.int32, lines.shape, 0)
        lines, scale = jnp.where(row < 4, lines, 0.0), lines[4:5]
        left.append(jnp.concatenate([value * scale, lines], 0).astype(jnp.bfloat16))
    width = outs[0].shape[2]
    means, squares, extra = slot_rows(chips, width)
    row = lax.broadcasted_iota(jnp.int32, (extra, width), 0)
    column = lax.broadcasted_iota(jnp.int32, (extra, width), 1)
    half = kv0.shape[1] // 2
    for lane, order in enumerate(lanes):
        line = sums[lane : lane + 1, :]
        if lane == 0:
            high = line.astype(jnp.bfloat16).astype(jnp.float32)
            low = line - high
            if width > 128:
                line = jnp.concatenate([high, low], 1)
            else:
                line = jnp.where(row % 2 == 0, high, low)
            line = jnp.where(row // (means // chips) == chip, line, 0.0)
        else:
            place = row * (width // 128) + column // 128
            line = jnp.concatenate([line] * (width // 128), 1)
            line = jnp.where(place == chip, line, 0.0)
        base = (means, squares)[lane]
        for at in reversed(range(chips)):
            out_ref, to = outs[2 * lane + at // half_chips], at % half_chips
            target = chip ^ member(at, order)
            columns = pl.ds(pl.multiple_of(lane * half + target * width, width), width)
            value = jnp.dot(left[0], kv0[:, columns], preferred_element_type=jnp.float32)
            value += jnp.dot(left[1], kv1[:, columns], preferred_element_type=jnp.float32)
            out_ref[to, :rows, :] = value[:rows].astype(out_ref.dtype)
            scale = value[rows : rows + 1] + value[rows + 1 : rows + 2]
            shift = value[rows + 2 : rows + 3] + value[rows + 3 : rows + 4]
            below = jnp.where(row == base + chip, scale, line)
            if lane == 0:
                keys_shift[target] = jnp.broadcast_to(shift, keys_shift.shape[1:])
            else:
                below = jnp.where(row == base + chips, shift, below)
                below = jnp.where(row == base + chips + 1, keys_shift[target][:1], below)
            out_ref[to, rows:, :] = below.astype(out_ref.dtype)


def project(lanes, place, pieces, lines, win0, win1, kv0, kv1):
    chips = 1 << len(lanes[0])
    rows = 2 * pieces[0].shape[0]
    features, depth = win0.shape
    total = kv0.shape[1]
    width = total // 2 // chips
    extra = slot_rows(chips, width)[2]
    out = jax.ShapeDtypeStruct((chips // 2, rows + extra, width), jnp.bfloat16)
    return pl.pallas_call(
        functools.partial(project_kernel, lanes),
        out_shape=(out,) * 4,
        in_specs=[SMEM_SPEC] + [VMEM_SPEC] * 9,
        out_specs=(VMEM_SPEC,) * 4,
        scratch_shapes=[
            pltpu.VMEM((rows, depth // 2), jnp.bfloat16),
            pltpu.VMEM((rows, features), jnp.float32),
            pltpu.VMEM((rows, features), jnp.float32),
            pltpu.VMEM((rows, 128), jnp.float32),
            pltpu.VMEM((chips, 8, width), jnp.float32),
        ],
        compiler_params=params(14),
        cost_estimate=pl.CostEstimate(
            flops=4 * rows * features * (depth + total),
            bytes_accessed=2 * (rows * depth + 2 * features * (depth + total) + rows * total),
            transcendentals=0,
        ),
        name="project",
    )(place, *pieces, lines, win0, win1, kv0, kv1)


def combine_kernel(chips, model_width, place_ref, *refs):
    keep0, keep1, came_ref, mine_ref, sent_ref = refs
    core = place_ref[2]
    rows = mine_ref.shape[0]
    width = keep0.shape[2]
    means, squares, _ = slot_rows(chips, width)
    totals = [keep[0] + came_ref[lane, 0].astype(jnp.float32) for lane, keep in enumerate((keep0, keep1))]
    below = [total[rows:] for total in totals]
    if width > 128:
        mean = below[0][:chips, :128] + below[0][:chips, 128:]
    else:
        lines = [below[0][2 * at : 2 * at + 1] + below[0][2 * at + 1 : 2 * at + 2] for at in range(chips)]
        mean = jnp.concatenate(lines, 0)
    away = mean - jnp.mean(mean, 0, keepdims=True)
    square = jnp.sum(below[1][:squares], 0, keepdims=True)
    square = sum(square[:, at : at + 128] for at in range(0, width, 128))
    square += jnp.sum(away * away, 0, keepdims=True) * (model_width / chips)
    scale = lax.rsqrt(square / model_width + epsilon)
    turned = jnp.concatenate([away, scale, jnp.zeros((rows - chips - 1, rows), jnp.float32)], 0).T
    scale = turned[:, chips : chips + 1]
    texts = []
    for lane, total in enumerate(totals):
        base = (means, squares)[lane]
        text = total[:rows]
        for at in range(chips):
            text += turned[:, at : at + 1] * below[lane][base + at : base + at + 1]
        shift = below[1][squares + chips + 1 - lane : squares + chips + 2 - lane]
        texts.append(text * scale + shift)
    for part, text in enumerate(texts):
        span = slice(part * HEAD_DIM, (part + 1) * HEAD_DIM)
        if width > HEAD_DIM:
            low, high = text[:, :HEAD_DIM], text[:, HEAD_DIM:]
            mine_ref[:, span] = jnp.where(core == 0, low, high).astype(mine_ref.dtype)
            sent_ref[:, span] = jnp.where(core == 0, high, low).astype(mine_ref.dtype)
        else:
            mine_ref[:, span] = text.astype(mine_ref.dtype)
            sent_ref[:, span] = text.astype(mine_ref.dtype)


def combine(place, parts, chips, rows, model_width):
    out = jax.ShapeDtypeStruct((rows, 2 * HEAD_DIM), jnp.bfloat16)
    return pl.pallas_call(
        functools.partial(combine_kernel, chips, model_width),
        out_shape=(out, out),
        in_specs=[SMEM_SPEC] + [VMEM_SPEC] * 3,
        out_specs=(VMEM_SPEC, VMEM_SPEC),
        compiler_params=params(4),
        cost_estimate=pl.CostEstimate(
            flops=8 * rows * 512, bytes_accessed=12 * rows * 512, transcendentals=0
        ),
        name="combine",
    )(place, *parts)


def pack_kernel(copies, queries_ref, keys_ref, values_ref, out_ref):
    img_dev = keys_ref.shape[0]
    part_rows = img_dev // copies
    for device in range(out_ref.shape[0]):
        head, copy = device // copies, device % copies
        span = slice(head * HEAD_DIM, (head + 1) * HEAD_DIM)
        out_ref[device, :img_dev, :] = keys_ref[:, span]
        out_ref[device, img_dev : 2 * img_dev, :] = values_ref[:, span]
        out_ref[device, 2 * img_dev :, :] = queries_ref[copy * part_rows : (copy + 1) * part_rows, span]


def pack(copies, queries, keys, values):
    img_dev = keys.shape[0]
    rows = 2 * img_dev + img_dev // copies
    return pl.pallas_call(
        functools.partial(pack_kernel, copies),
        out_shape=jax.ShapeDtypeStruct((HEADS * copies, rows, HEAD_DIM), jnp.bfloat16),
        in_specs=[VMEM_SPEC] * 3,
        out_specs=VMEM_SPEC,
        compiler_params=params(8),
        cost_estimate=pl.CostEstimate(
            flops=0, bytes_accessed=4 * HEADS * copies * rows * HEAD_DIM, transcendentals=0
        ),
        name="pack",
    )(queries, keys, values)


def unpack_kernel(copies, part_rows, masks, place_ref, *refs):
    *pieces, near_ref, far_ref, attended_ref, text_ref = refs
    me = 2 * place_ref[3] + place_ref[2]
    share = text_ref.shape[0]
    half = text_ref.shape[1] // 2
    count = len(pieces) // 2
    passed = [near_ref.at[at] for at in range(count)] + [far_ref.at[at] for at in range(count)]
    blocks = [block for piece, other in zip(pieces, passed) for block in (piece.at[0], other)]
    for at, block_ref in enumerate(blocks):
        device = me ^ (2 * masks[at // 2] + at % 2)
        head, copy = device // copies, device % copies
        start = pl.multiple_of(head * HEAD_DIM, HEAD_DIM)
        rows = pl.ds(pl.multiple_of(copy * part_rows, part_rows), part_rows)
        attended_ref[rows, pl.ds(start, HEAD_DIM)] = block_ref[:part_rows, :]
        block = block_ref[part_rows:, :].astype(jnp.float32)
        text_ref[:, pl.ds(start, HEAD_DIM)] = block[:share].astype(text_ref.dtype)
        start = pl.multiple_of(half + head * HEAD_DIM, HEAD_DIM)
        text_ref[:, pl.ds(start, HEAD_DIM)] = block[share:].astype(text_ref.dtype)


def unpack(copies, part_rows, masks, place, pieces, near, far):
    share = (near.shape[1] - part_rows) // 2
    return pl.pallas_call(
        functools.partial(unpack_kernel, copies, part_rows, masks),
        out_shape=(
            jax.ShapeDtypeStruct((part_rows * copies, HEADS * HEAD_DIM), jnp.bfloat16),
            jax.ShapeDtypeStruct((share, 2 * HEADS * HEAD_DIM), jnp.bfloat16),
        ),
        in_specs=[SMEM_SPEC] + [VMEM_SPEC] * (len(pieces) + 2),
        out_specs=(VMEM_SPEC, VMEM_SPEC),
        compiler_params=params(6),
        name="unpack",
    )(place, *pieces, near, far)


def image_kernel(factor, masks, img_dev, place_ref, packed_ref, sum_ref, top_ref, keys_ref, wide_ref):
    me = 2 * place_ref[3] + place_ref[2]
    wide_ref[:, HEAD_DIM:] = jnp.ones((wide_ref.shape[0], HEAD_DIM), wide_ref.dtype)
    for device in range(packed_ref.shape[0]):
        rows = slice(device * img_dev, (device + 1) * img_dev)
        keys_ref[rows, :] = packed_ref[device, :img_dev, :]
        wide_ref[rows, :HEAD_DIM] = packed_ref[device, img_dev : 2 * img_dev, :]
    group = max(1, 256 // (packed_ref.shape[1] - 2 * img_dev))
    rows = 256
    contract = (((1,), (1,)), ((), ()))
    count = sum_ref.shape[0]
    for start in range(0, count, rows):
        span = slice(start, start + rows)
        at = start // rows * group
        queries = [
            packed_ref[me ^ (2 * masks[i // 2] + i % 2), 2 * img_dev :, :] for i in range(at, at + group)
        ]
        queries = jnp.concatenate(queries, 0)
        scores = lax.dot_general(queries, keys_ref[...], contract, preferred_element_type=jnp.float32)
        scores = scores * factor
        top = jnp.max(scores, 1, keepdims=True)
        weights = jnp.exp2(scores - top).astype(jnp.bfloat16)
        sum_ref[span, :] = jnp.dot(weights, wide_ref[...], preferred_element_type=jnp.float32)
        top_ref[span, :] = jnp.broadcast_to(top, (rows, HEAD_DIM))


def image_attention(place, packed, img_dev, factor, masks):
    count = 2 * len(masks) * (packed.shape[1] - 2 * img_dev)
    total = packed.shape[0] * img_dev
    return pl.pallas_call(
        functools.partial(image_kernel, factor, masks, img_dev),
        out_shape=(
            jax.ShapeDtypeStruct((count, 2 * HEAD_DIM), jnp.float32),
            jax.ShapeDtypeStruct((count, HEAD_DIM), jnp.float32),
        ),
        in_specs=[SMEM_SPEC, VMEM_SPEC],
        out_specs=(VMEM_SPEC, VMEM_SPEC),
        scratch_shapes=[
            pltpu.VMEM((total, HEAD_DIM), jnp.bfloat16),
            pltpu.VMEM((total, 2 * HEAD_DIM), jnp.bfloat16),
        ],
        compiler_params=params(14),
        cost_estimate=pl.CostEstimate(
            flops=4 * count * total * HEAD_DIM,
            bytes_accessed=4 * total * HEAD_DIM + 10 * count * HEAD_DIM,
            transcendentals=count * total,
        ),
        name="image_attention",
    )(place, packed)


def send_order(chips):
    half = chips // 2
    turns = [mask for at in range(half) for mask in (half + at, half - 1 - at)]
    return turns[:half], turns[half:]


def finish_kernel(factor, masks, img_dev, place_ref, packed_ref, sum_ref, top_ref, mine_ref, got_ref, *refs):
    *outs, text_ref = refs
    core, valid = place_ref[2], place_ref[4]
    me = 2 * place_ref[3] + core
    part_rows = packed_ref.shape[1] - 2 * img_dev
    half = mine_ref.shape[0]
    contract = (((1,), (1,)), ((), ()))
    mine, got = mine_ref[...], got_ref[...]
    keys = jnp.concatenate([mine[:, :HEAD_DIM], got[:, :HEAD_DIM]], 0)
    values = jnp.concatenate([mine[:, HEAD_DIM:], got[:, HEAD_DIM:]], 0)
    values = jnp.concatenate([values, jnp.ones(values.shape, values.dtype)], 1)
    lane = lax.broadcasted_iota(jnp.int32, (1, 2 * half), 1)
    text_position = jnp.where((lane >= half) == (core == 0), half, 0) + lane % half
    bias = jnp.where(text_position < valid, 0.0, -jnp.inf)
    group = max(1, 512 // part_rows)
    rows = group * part_rows
    for step in range(2 * len(outs) // group):
        span = slice(step * rows, (step + 1) * rows)
        queries = [
            packed_ref[me ^ (2 * masks[at // 2] + at % 2), 2 * img_dev :, :]
            for at in range(step * group, (step + 1) * group)
        ]
        queries = jnp.concatenate(queries, 0)
        scores = lax.dot_general(queries, keys, contract, preferred_element_type=jnp.float32)
        scores = scores * factor + bias
        before = top_ref[span, :]
        top = jnp.maximum(before, jnp.max(scores, 1, keepdims=True))
        rescale = jnp.exp2(before - top)
        weights = jnp.exp2(scores - jnp.concatenate([top] * (2 * half // HEAD_DIM), 1))
        total = jnp.dot(weights.astype(jnp.bfloat16), values, preferred_element_type=jnp.float32)
        mixed = sum_ref[span, :HEAD_DIM] * rescale + total[:, :HEAD_DIM]
        total = sum_ref[span, HEAD_DIM:] * rescale + total[:, HEAD_DIM:]
        mixed = (mixed / total).astype(jnp.bfloat16)
        for at in range(group):
            to = step * group + at
            outs[to // 2][to % 2, :part_rows, :] = mixed[at * part_rows : (at + 1) * part_rows]
    low, high = mine.astype(jnp.float32), got.astype(jnp.float32)
    text_ref[:half, :] = jnp.where(core == 0, low, high)
    text_ref[half:, :] = jnp.where(core == 0, high, low)
    share = (outs[0].shape[1] - part_rows) // 2
    for to in range(2 * len(outs)):
        start = pl.multiple_of((me ^ (2 * masks[to // 2] + to % 2)) * share, share)
        block = text_ref[pl.ds(start, share), :]
        block = jnp.concatenate([block[:, :HEAD_DIM], block[:, HEAD_DIM:]], 0)
        outs[to // 2][to % 2, part_rows:, :] = block.astype(jnp.bfloat16)


def finish(place, masks, packed, image, mine, got, img_dev, factor):
    devices, part_rows = packed.shape[0], packed.shape[1] - 2 * img_dev
    half = mine.shape[0]
    count = image[0].shape[0]
    outs = count // part_rows // 2
    out = jax.ShapeDtypeStruct((2, part_rows + 4 * half // devices, HEAD_DIM), jnp.bfloat16)
    return pl.pallas_call(
        functools.partial(finish_kernel, factor, masks, img_dev),
        out_shape=(out,) * outs,
        in_specs=[SMEM_SPEC] + [VMEM_SPEC] * 5,
        out_specs=(VMEM_SPEC,) * outs,
        scratch_shapes=[pltpu.VMEM((2 * half, 2 * HEAD_DIM), jnp.float32)],
        compiler_params=params(10),
        cost_estimate=pl.CostEstimate(
            flops=8 * count * half * HEAD_DIM,
            bytes_accessed=12 * count * HEAD_DIM,
            transcendentals=2 * count * half,
        ),
        name="finish",
    )(place, packed, *image, mine, got)


def gather_kernel(*refs):
    for at, piece in enumerate(refs[:-1]):
        refs[-1][at] = piece[1]


def gather_other(pieces):
    shape = (len(pieces),) + pieces[0].shape[1:]
    return pl.pallas_call(
        gather_kernel,
        out_shape=jax.ShapeDtypeStruct(shape, pieces[0].dtype),
        in_specs=[VMEM_SPEC] * len(pieces),
        out_specs=VMEM_SPEC,
        compiler_params=params(4),
        cost_estimate=pl.CostEstimate(
            flops=0, bytes_accessed=2 * len(pieces) * pieces[0].size, transcendentals=0
        ),
        name="gather_other",
    )(*pieces)


def add_kernel(joint, *refs):
    ins, outs = refs[:4], refs[4:]
    if joint:
        outs = (outs[0].at[0], outs[1], outs[0].at[1], outs[2])
    for lane in range(2):
        mine, got = ins[2 * lane], ins[2 * lane + 1]
        half = mine.shape[0] // 2
        outs[2 * lane][...] = (
            mine[half:].astype(jnp.float32) + got[half:].astype(jnp.float32)
        ).astype(jnp.bfloat16)
        outs[2 * lane + 1][...] = mine[:half].astype(jnp.float32) + got[:half].astype(jnp.float32)


def add_halves(mine, got, joint=False):
    shape = (mine[0].shape[0] // 2,) + mine[0].shape[1:]
    sent, keep = jax.ShapeDtypeStruct(shape, jnp.bfloat16), jax.ShapeDtypeStruct(shape, jnp.float32)
    outs = (sent, keep) * 2
    if joint:
        outs = (jax.ShapeDtypeStruct((2,) + shape, jnp.bfloat16), keep, keep)
    outs = pl.pallas_call(
        functools.partial(add_kernel, joint),
        out_shape=outs,
        in_specs=[VMEM_SPEC] * 4,
        out_specs=(VMEM_SPEC,) * len(outs),
        compiler_params=params(6),
        cost_estimate=pl.CostEstimate(
            flops=2 * mine[0].size, bytes_accessed=12 * mine[0].size, transcendentals=0
        ),
        name="add_halves",
    )(mine[0], got[0], mine[1], got[1])
    if joint:
        return outs[0], outs[1:]
    return [outs[0], outs[2]], [outs[1], outs[3]]


def total_kernel(mine0, got0, mine1, got1, out_ref):
    for lane, (mine, got) in enumerate(((mine0, got0), (mine1, got1))):
        out_ref[lane] = (mine[...] + got[...].astype(jnp.float32)).astype(out_ref.dtype)


def add_all(mine, got):
    return pl.pallas_call(
        total_kernel,
        out_shape=jax.ShapeDtypeStruct((2,) + mine[0].shape, jnp.bfloat16),
        in_specs=[VMEM_SPEC] * 4,
        out_specs=VMEM_SPEC,
        compiler_params=params(4),
        cost_estimate=pl.CostEstimate(
            flops=2 * mine[0].size, bytes_accessed=16 * mine[0].size, transcendentals=0
        ),
        name="add_all",
    )(mine[0], got[0], mine[1], got[1])


def norm_kernel(mine_ref, got_ref, gain_ref, out0, out1):
    width = mine_ref.shape[3]
    for at in range(2):
        totals = [
            mine_ref[lane, at].astype(jnp.float32) + got_ref[lane, 1 - at].astype(jnp.float32)
            for lane in range(2)
        ]
        square = sum(jnp.sum(total * total, 1, keepdims=True) for total in totals)
        scale_rows = lax.rsqrt(square / (2 * width) + epsilon)
        for lane, (total, out_ref) in enumerate(zip(totals, (out0, out1))):
            gain = gain_ref[:, lane * width : (lane + 1) * width].astype(jnp.float32)
            out_ref[at] = (total * scale_rows * gain).astype(out_ref.dtype)


def normalize(mine, got, norm_gain):
    out = jax.ShapeDtypeStruct(mine.shape[1:], jnp.bfloat16)
    states = pl.pallas_call(
        norm_kernel,
        out_shape=(out, out),
        in_specs=[VMEM_SPEC] * 3,
        out_specs=(VMEM_SPEC,) * 2,
        compiler_params=params(4),
        cost_estimate=pl.CostEstimate(
            flops=4 * mine.size, bytes_accessed=8 * mine.size, transcendentals=0
        ),
        name="normalize",
    )(mine, got, norm_gain)
    return [part.reshape(-1, part.shape[2]) for part in states]


def join_kernel(mine0, got0, mine1, got1, out0, out1):
    for mine, got, out_ref in ((mine0, got0, out0), (mine1, got1, out1)):
        rows = mine.shape[0]
        if rows % 16:
            both = [mine[...].astype(jnp.float32), got[...].astype(jnp.float32)]
            out_ref[...] = jnp.concatenate(both, 0).astype(out_ref.dtype)
        else:
            out_ref[:rows, :] = mine[...]
            out_ref[rows:, :] = got[...]


def join(mine, got):
    rows, width = mine[0].shape
    out = jax.ShapeDtypeStruct((2 * rows, width), mine[0].dtype)
    return pl.pallas_call(
        join_kernel,
        out_shape=(out, out),
        in_specs=[VMEM_SPEC] * 4,
        out_specs=(VMEM_SPEC,) * 2,
        compiler_params=params(4),
        cost_estimate=pl.CostEstimate(
            flops=0, bytes_accessed=16 * rows * width, transcendentals=0
        ),
        name="join",
    )(mine[0], got[0], mine[1], got[1])


def local(
    enc_act,
    down_weight,
    norm_gain,
    text_in_weight,
    modulation_weight,
    key_value_weight,
    timesteps,
    lengths,
    image_queries,
    image_key_values,
):
    devices = lax.axis_size("seq")
    chips = devices // 2
    copies = devices // HEADS
    text_len = enc_act.shape[1]
    img_dev = image_queries.shape[1]
    part_rows = img_dev // copies
    factor = math.log2(math.e) / math.sqrt(HEAD_DIM)
    lanes = orders(chips)
    index = lax.axis_index("seq")
    chip, core = index // 2, index % 2
    place = jnp.stack([position(chip, lanes[0]), position(chip, lanes[1]), core, chip, lengths[0]])
    place = place.astype(jnp.int32)

    win0, kv0 = text_in_weight.T, key_value_weight
    mod0 = modulation_weight.transpose(1, 2, 0)
    time = time_embedding(timesteps)

    rounds = len(lanes[0])
    turns = send_order(chips)
    tie = lax.optimization_barrier

    def exchange(rows):
        return lax.all_to_all(rows, "seq", split_axis=0, concat_axis=0, tiled=True)

    image_key_values, image_queries = tie((image_key_values, image_queries))
    packed = pack(copies, image_queries[0], image_key_values[0, :, 0], image_key_values[0, :, 1])
    act, packed = tie((enc_act[0].T, packed))
    packed = exchange(packed)
    encoded = encoder(lanes, place, act, down_weight)
    keep, got = encoded[::2], [swap(other, 1) for other in encoded[1::2]]
    last = 2 * lanes[0][-1]
    for step in range(rounds - 1):
        sent, keep = add_halves(keep, got)
        got = [swap(part, 2 * order[step]) for part, order in zip(sent, lanes)]
    summed, packed = tie((add_all(keep, got), packed))
    summed, held, held_kv, held_mod = tie((summed, win0, kv0, mod0))
    win1, kv1, mod1 = swap(held, 1), swap(held_kv, 1), swap(held_mod, 1)
    got = swap(summed, last)

    states = normalize(summed, got, norm_gain[None, :])
    images = []
    for step in reversed(range(rounds - 1)):
        if step == 0:
            states, packed = tie((states, packed))
            image = image_attention(place, packed, img_dev, factor, turns[0])
        got = [swap(state, 2 * order[step]) for state, order in zip(states, lanes)]
        if step == rounds - 2:
            lines = modulation(time, mod0, mod1)
            got, win1, kv1, lines = tie((got, win1, kv1, lines))
        if step:
            states = join(states, got)
    got, image = tie((got, image))
    images += image
    states = [state for pair in zip(states, got) for state in pair]

    blocks = project(lanes, place, states, lines, win0, win1, kv0, kv1)
    keep, sent = [blocks[0], blocks[2]], [blocks[1], blocks[3]]
    for step in range(rounds - 1):
        if step == 0:
            sent, packed = tie((sent, packed))
            image = image_attention(place, packed, img_dev, factor, turns[1])
        got = [swap(part, 2 * order[step]) for part, order in zip(sent, lanes)]
        if step == 0:
            got, image = tie((got, image))
            images += image
        sent, keep = add_halves(keep, got, step == rounds - 2)
    parts = (*keep, swap(sent, last))
    model_width = text_in_weight.shape[1] * devices
    mine, sent = combine(place, parts, chips, text_len // 2, model_width)
    got = swap(sent, 1)

    pieces, passed = [], []
    for call, masks in enumerate(turns):
        image = images[2 * call : 2 * call + 2]
        blocks = finish(place, masks, packed, image, mine, got, img_dev, factor)
        pieces += [swap(block, 2 * mask) if mask else block for mask, block in zip(masks, blocks)]
    for call in range(2):
        passed.append(swap(gather_other(pieces[call * chips // 2 : (call + 1) * chips // 2]), 1))
    attended, text_kv = unpack(copies, part_rows, turns[0] + turns[1], place, pieces, *passed)
    return (attended[None], text_kv)


def solution(mesh):
    in_specs = (
        P("dp", None, "seq"),
        P("seq", None),
        P(),
        P(None, "seq"),
        P(None, None, "seq"),
        P("seq", None),
        P("dp"),
        P("dp"),
        P("dp", "seq", None),
        P("dp", "seq", None, None),
    )
    out_specs = (P("dp", "seq", None), P(("dp", "seq"), None))
    return jax.shard_map(local, mesh=mesh, in_specs=in_specs, out_specs=out_specs, check_vma=False)
```

```python
import functools
import math

import jax
import jax.numpy as jnp
from jax import lax
from jax.experimental import pallas as pl
from jax.experimental.pallas import tpu as pltpu
from jax.sharding import PartitionSpec as P

HEAD_DIM = 128
HEADS = 16
TEMB = 256
MIB = 1024 * 1024

epsilon = 1e-06

SMEM_SPEC = pl.BlockSpec(memory_space=pltpu.SMEM)
VMEM_SPEC = pl.BlockSpec(memory_space=pltpu.VMEM)


def params(mib):
    return pltpu.CompilerParams(vmem_limit_bytes=mib * MIB)


def swap(value, mask):
    devices = lax.axis_size("seq")
    return lax.ppermute(value, "seq", [(i, i ^ mask) for i in range(devices)])


def orders(chips):
    bits = [1 << i for i in range(chips.bit_length() - 1)]
    return (bits, [bits[1], bits[0]] + bits[2:])


def position(chip, order):
    last = len(order) - 1
    return sum(((chip >> (bit.bit_length() - 1)) & 1) << (last - i) for i, bit in enumerate(order))


def member(at, order):
    last = len(order) - 1
    return sum(bit for i, bit in enumerate(order) if (at >> (last - i)) & 1)


def time_embedding(timesteps):
    half_width = TEMB // 2
    freqs = jnp.exp(-math.log(10000.0) * jnp.arange(half_width, dtype=jnp.float32) / half_width)
    angles = timesteps.astype(jnp.float32)[:, None] * freqs[None, :]
    embedding = jnp.concatenate([jnp.cos(angles), jnp.sin(angles)], 1)
    return jax.nn.silu(embedding).astype(jnp.bfloat16)


def encoder_kernel(order, place_ref, act_ref, weight_ref, own_ref, other_ref, lhs_ref):
    at, core = place_ref[0], place_ref[2]
    chips = 1 << len(order)
    half = lhs_ref.shape[0] // 2
    width = weight_ref.shape[1]
    first = core == 0
    tile = width // 4
    lhs_ref[...] = act_ref[...].T
    for column in range(0, width, tile):
        columns = slice(column, column + tile)
        result = jnp.dot(lhs_ref[...], weight_ref[:, columns], preferred_element_type=jnp.float32)
        own = jnp.where(first, result[:half], result[half:]).astype(own_ref.dtype)
        other = jnp.where(first, result[half:], result[:half]).astype(own_ref.dtype)
        own = own.reshape(chips, half // chips, tile)
        other = other.reshape(chips, half // chips, tile)
        for block in range(chips):
            to = at ^ position(block, order)
            own_ref[to, :, columns] = own[block]
            other_ref[to, :, columns] = other[block]


def encoder(order, place, act, weight):
    chips = 1 << len(order)
    depth, rows = act.shape
    width = weight.shape[1]
    out = jax.ShapeDtypeStruct((chips, rows // 2 // chips, width), jnp.bfloat16)
    return pl.pallas_call(
        functools.partial(encoder_kernel, order),
        out_shape=(out, out),
        in_specs=[SMEM_SPEC, VMEM_SPEC, VMEM_SPEC],
        out_specs=(VMEM_SPEC,) * 2,
        scratch_shapes=[pltpu.VMEM((rows, depth), jnp.bfloat16)],
        compiler_params=params(16),
        cost_estimate=pl.CostEstimate(
            flops=2 * rows * depth * width,
            bytes_accessed=2 * (depth * rows + depth * width + rows * width),
            transcendentals=0,
        ),
        name="encoder",
    )(place, act, weight)


def modulation_kernel(time_ref, mod0_ref, mod1_ref, out_ref):
    contract = (((1,), (1,)), ((), ()))
    embedding = jnp.broadcast_to(time_ref[...].astype(jnp.float32), (16, time_ref.shape[1]))
    embedding = embedding.astype(jnp.bfloat16)
    row = lax.broadcasted_iota(jnp.int32, (16, mod0_ref.shape[1]), 0)
    for side, mod in enumerate((mod0_ref, mod1_ref)):
        shift, scale = [
            lax.dot_general(embedding, mod[at], contract, preferred_element_type=jnp.float32)
            for at in range(2)
        ]
        lines = jnp.where(row < 2, 1.0 + scale, shift)
        high = lines.astype(jnp.bfloat16).astype(jnp.float32)
        low = jnp.where(row % 2 == 0, high, lines - high)
        out_ref[side] = jnp.where(row < 4, low, 1.0 + scale)


def modulation(time, mod0, mod1):
    return pl.pallas_call(
        modulation_kernel,
        out_shape=jax.ShapeDtypeStruct((2, 16, mod0.shape[1]), jnp.float32),
        in_specs=[VMEM_SPEC] * 3,
        out_specs=VMEM_SPEC,
        compiler_params=params(4),
        name="modulation",
    )(time, mod0, mod1)


def slot_rows(chips, width):
    means, squares = chips * 2 * 128 // width, chips * 128 // width
    return means, squares, -(-max(means + chips, squares + chips + 2) // 16) * 16


def project_kernel(lanes, place_ref, *refs):
    pieces, refs = (refs[:2], refs[2:4]), refs[4:]
    lines_ref, win0, win1, kv0, kv1, *outs, states, proj0, proj1, sums, keys_shift = refs
    chip = place_ref[3]
    half_chips = outs[0].shape[0]
    chips = 2 * half_chips
    rows = proj0.shape[0]
    share = rows // chips
    depth = states.shape[1]
    contract = (((1,), (1,)), ((), ()))
    for lane, order in enumerate(lanes):
        top, low = pieces[lane]
        states[: rows // 2, :] = top[...]
        states[rows // 2 :, :] = low[...]
        span = slice(lane * depth, (lane + 1) * depth)
        for win, proj in ((win0, proj0), (win1, proj1)):
            part = lax.dot_general(
                states[...], win[:, span], contract, preferred_element_type=jnp.float32
            )
            for at in range(chips):
                start = pl.multiple_of((chip ^ member(at, order)) * share, share)
                block = part[at * share : (at + 1) * share]
                if lane == 0:
                    proj[pl.ds(start, share), :] = block
                else:
                    proj[pl.ds(start, share), :] += block
    mean = jnp.sum(proj0[...], 1, keepdims=True) + jnp.sum(proj1[...], 1, keepdims=True)
    mean = mean / (2 * proj0.shape[1])
    value0, value1 = proj0[...] - mean, proj1[...] - mean
    square = jnp.sum(value0 * value0, 1, keepdims=True) + jnp.sum(value1 * value1, 1, keepdims=True)
    lane = lax.broadcasted_iota(jnp.int32, sums.shape, 1)
    sums[...] = jnp.where(lane == 0, mean, square).T
    left = []
    for side, value in enumerate((value0, value1)):
        lines = lines_ref[side]
        row = lax.broadcasted_iota(jnp.int32, lines.shape, 0)
        lines, scale = jnp.where(row < 4, lines, 0.0), lines[4:5]
        left.append(jnp.concatenate([value * scale, lines], 0).astype(jnp.bfloat16))
    width = outs[0].shape[2]
    means, squares, extra = slot_rows(chips, width)
    row = lax.broadcasted_iota(jnp.int32, (extra, width), 0)
    column = lax.broadcasted_iota(jnp.int32, (extra, width), 1)
    half = kv0.shape[1] // 2
    for lane, order in enumerate(lanes):
        line = sums[lane : lane + 1, :]
        if lane == 0:
            high = line.astype(jnp.bfloat16).astype(jnp.float32)
            low = line - high
            if width > 128:
                line = jnp.concatenate([high, low], 1)
            else:
                line = jnp.where(row % 2 == 0, high, low)
            line = jnp.where(row // (means // chips) == chip, line, 0.0)
        else:
            place = row * (width // 128) + column // 128
            line = jnp.concatenate([line] * (width // 128), 1)
            line = jnp.where(place == chip, line, 0.0)
        base = (means, squares)[lane]
        for at in reversed(range(chips)):
            out_ref, to = outs[2 * lane + at // half_chips], at % half_chips
            target = chip ^ member(at, order)
            columns = pl.ds(pl.multiple_of(lane * half + target * width, width), width)
            value = jnp.dot(left[0], kv0[:, columns], preferred_element_type=jnp.float32)
            value += jnp.dot(left[1], kv1[:, columns], preferred_element_type=jnp.float32)
            out_ref[to, :rows, :] = value[:rows].astype(out_ref.dtype)
            scale = value[rows : rows + 1] + value[rows + 1 : rows + 2]
            shift = value[rows + 2 : rows + 3] + value[rows + 3 : rows + 4]
            below = jnp.where(row == base + chip, scale, line)
            if lane == 0:
                keys_shift[target] = jnp.broadcast_to(shift, keys_shift.shape[1:])
            else:
                below = jnp.where(row == base + chips, shift, below)
                below = jnp.where(row == base + chips + 1, keys_shift[target][:1], below)
            out_ref[to, rows:, :] = below.astype(out_ref.dtype)


def project(lanes, place, pieces, lines, win0, win1, kv0, kv1):
    chips = 1 << len(lanes[0])
    rows = 2 * pieces[0].shape[0]
    features, depth = win0.shape
    total = kv0.shape[1]
    width = total // 2 // chips
    extra = slot_rows(chips, width)[2]
    out = jax.ShapeDtypeStruct((chips // 2, rows + extra, width), jnp.bfloat16)
    return pl.pallas_call(
        functools.partial(project_kernel, lanes),
        out_shape=(out,) * 4,
        in_specs=[SMEM_SPEC] + [VMEM_SPEC] * 9,
        out_specs=(VMEM_SPEC,) * 4,
        scratch_shapes=[
            pltpu.VMEM((rows, depth // 2), jnp.bfloat16),
            pltpu.VMEM((rows, features), jnp.float32),
            pltpu.VMEM((rows, features), jnp.float32),
            pltpu.VMEM((rows, 128), jnp.float32),
            pltpu.VMEM((chips, 8, width), jnp.float32),
        ],
        compiler_params=params(14),
        cost_estimate=pl.CostEstimate(
            flops=4 * rows * features * (depth + total),
            bytes_accessed=2 * (rows * depth + 2 * features * (depth + total) + rows * total),
            transcendentals=0,
        ),
        name="project",
    )(place, *pieces, lines, win0, win1, kv0, kv1)


def combine_kernel(chips, model_width, place_ref, *refs):
    keep0, keep1, came_ref, mine_ref, sent_ref = refs
    core = place_ref[2]
    rows = mine_ref.shape[0]
    width = keep0.shape[2]
    means, squares, _ = slot_rows(chips, width)
    totals = [keep[0] + came_ref[lane, 0].astype(jnp.float32) for lane, keep in enumerate((keep0, keep1))]
    below = [total[rows:] for total in totals]
    if width > 128:
        mean = below[0][:chips, :128] + below[0][:chips, 128:]
    else:
        lines = [below[0][2 * at : 2 * at + 1] + below[0][2 * at + 1 : 2 * at + 2] for at in range(chips)]
        mean = jnp.concatenate(lines, 0)
    away = mean - jnp.mean(mean, 0, keepdims=True)
    square = jnp.sum(below[1][:squares], 0, keepdims=True)
    square = sum(square[:, at : at + 128] for at in range(0, width, 128))
    square += jnp.sum(away * away, 0, keepdims=True) * (model_width / chips)
    scale = lax.rsqrt(square / model_width + epsilon)
    turned = jnp.concatenate([away, scale, jnp.zeros((rows - chips - 1, rows), jnp.float32)], 0).T
    scale = turned[:, chips : chips + 1]
    texts = []
    for lane, total in enumerate(totals):
        base = (means, squares)[lane]
        text = total[:rows]
        for at in range(chips):
            text += turned[:, at : at + 1] * below[lane][base + at : base + at + 1]
        shift = below[1][squares + chips + 1 - lane : squares + chips + 2 - lane]
        texts.append(text * scale + shift)
    for part, text in enumerate(texts):
        span = slice(part * HEAD_DIM, (part + 1) * HEAD_DIM)
        if width > HEAD_DIM:
            low, high = text[:, :HEAD_DIM], text[:, HEAD_DIM:]
            mine_ref[:, span] = jnp.where(core == 0, low, high).astype(mine_ref.dtype)
            sent_ref[:, span] = jnp.where(core == 0, high, low).astype(mine_ref.dtype)
        else:
            mine_ref[:, span] = text.astype(mine_ref.dtype)
            sent_ref[:, span] = text.astype(mine_ref.dtype)


def combine(place, parts, chips, rows, model_width):
    out = jax.ShapeDtypeStruct((rows, 2 * HEAD_DIM), jnp.bfloat16)
    return pl.pallas_call(
        functools.partial(combine_kernel, chips, model_width),
        out_shape=(out, out),
        in_specs=[SMEM_SPEC] + [VMEM_SPEC] * 3,
        out_specs=(VMEM_SPEC, VMEM_SPEC),
        compiler_params=params(4),
        cost_estimate=pl.CostEstimate(
            flops=8 * rows * 512, bytes_accessed=12 * rows * 512, transcendentals=0
        ),
        name="combine",
    )(place, *parts)


def pack_kernel(copies, queries_ref, keys_ref, values_ref, out_ref):
    img_dev = keys_ref.shape[0]
    part_rows = img_dev // copies
    for device in range(out_ref.shape[0]):
        head, copy = device // copies, device % copies
        span = slice(head * HEAD_DIM, (head + 1) * HEAD_DIM)
        out_ref[device, :img_dev, :] = keys_ref[:, span]
        out_ref[device, img_dev : 2 * img_dev, :] = values_ref[:, span]
        out_ref[device, 2 * img_dev :, :] = queries_ref[copy * part_rows : (copy + 1) * part_rows, span]


def pack(copies, queries, keys, values):
    img_dev = keys.shape[0]
    rows = 2 * img_dev + img_dev // copies
    return pl.pallas_call(
        functools.partial(pack_kernel, copies),
        out_shape=jax.ShapeDtypeStruct((HEADS * copies, rows, HEAD_DIM), jnp.bfloat16),
        in_specs=[VMEM_SPEC] * 3,
        out_specs=VMEM_SPEC,
        compiler_params=params(8),
        cost_estimate=pl.CostEstimate(
            flops=0, bytes_accessed=4 * HEADS * copies * rows * HEAD_DIM, transcendentals=0
        ),
        name="pack",
    )(queries, keys, values)


def unpack_kernel(copies, part_rows, masks, place_ref, *refs):
    *pieces, near_ref, far_ref, attended_ref, text_ref = refs
    me = 2 * place_ref[3] + place_ref[2]
    share = text_ref.shape[0]
    half = text_ref.shape[1] // 2
    count = len(pieces) // 2
    passed = [near_ref.at[at] for at in range(count)] + [far_ref.at[at] for at in range(count)]
    blocks = [block for piece, other in zip(pieces, passed) for block in (piece.at[0], other)]
    for at, block_ref in enumerate(blocks):
        device = me ^ (2 * masks[at // 2] + at % 2)
        head, copy = device // copies, device % copies
        start = pl.multiple_of(head * HEAD_DIM, HEAD_DIM)
        rows = pl.ds(pl.multiple_of(copy * part_rows, part_rows), part_rows)
        attended_ref[rows, pl.ds(start, HEAD_DIM)] = block_ref[:part_rows, :]
        block = block_ref[part_rows:, :].astype(jnp.float32)
        text_ref[:, pl.ds(start, HEAD_DIM)] = block[:share].astype(text_ref.dtype)
        start = pl.multiple_of(half + head * HEAD_DIM, HEAD_DIM)
        text_ref[:, pl.ds(start, HEAD_DIM)] = block[share:].astype(text_ref.dtype)


def unpack(copies, part_rows, masks, place, pieces, near, far):
    share = (near.shape[1] - part_rows) // 2
    return pl.pallas_call(
        functools.partial(unpack_kernel, copies, part_rows, masks),
        out_shape=(
            jax.ShapeDtypeStruct((part_rows * copies, HEADS * HEAD_DIM), jnp.bfloat16),
            jax.ShapeDtypeStruct((share, 2 * HEADS * HEAD_DIM), jnp.bfloat16),
        ),
        in_specs=[SMEM_SPEC] + [VMEM_SPEC] * (len(pieces) + 2),
        out_specs=(VMEM_SPEC, VMEM_SPEC),
        compiler_params=params(6),
        name="unpack",
    )(place, *pieces, near, far)


def image_kernel(factor, masks, img_dev, place_ref, packed_ref, sum_ref, top_ref, keys_ref, wide_ref):
    me = 2 * place_ref[3] + place_ref[2]
    wide_ref[:, HEAD_DIM:] = jnp.ones((wide_ref.shape[0], HEAD_DIM), wide_ref.dtype)
    for device in range(packed_ref.shape[0]):
        rows = slice(device * img_dev, (device + 1) * img_dev)
        keys_ref[rows, :] = packed_ref[device, :img_dev, :]
        wide_ref[rows, :HEAD_DIM] = packed_ref[device, img_dev : 2 * img_dev, :]
    group = max(1, 256 // (packed_ref.shape[1] - 2 * img_dev))
    rows = 256
    contract = (((1,), (1,)), ((), ()))
    count = sum_ref.shape[0]
    for start in range(0, count, rows):
        span = slice(start, start + rows)
        at = start // rows * group
        queries = [
            packed_ref[me ^ (2 * masks[i // 2] + i % 2), 2 * img_dev :, :] for i in range(at, at + group)
        ]
        queries = jnp.concatenate(queries, 0)
        scores = lax.dot_general(queries, keys_ref[...], contract, preferred_element_type=jnp.float32)
        scores = scores * factor
        top = jnp.max(scores, 1, keepdims=True)
        weights = jnp.exp2(scores - top).astype(jnp.bfloat16)
        sum_ref[span, :] = jnp.dot(weights, wide_ref[...], preferred_element_type=jnp.float32)
        top_ref[span, :] = jnp.broadcast_to(top, (rows, HEAD_DIM))


def image_attention(place, packed, img_dev, factor, masks):
    count = 2 * len(masks) * (packed.shape[1] - 2 * img_dev)
    total = packed.shape[0] * img_dev
    return pl.pallas_call(
        functools.partial(image_kernel, factor, masks, img_dev),
        out_shape=(
            jax.ShapeDtypeStruct((count, 2 * HEAD_DIM), jnp.float32),
            jax.ShapeDtypeStruct((count, HEAD_DIM), jnp.float32),
        ),
        in_specs=[SMEM_SPEC, VMEM_SPEC],
        out_specs=(VMEM_SPEC, VMEM_SPEC),
        scratch_shapes=[
            pltpu.VMEM((total, HEAD_DIM), jnp.bfloat16),
            pltpu.VMEM((total, 2 * HEAD_DIM), jnp.bfloat16),
        ],
        compiler_params=params(14),
        cost_estimate=pl.CostEstimate(
            flops=4 * count * total * HEAD_DIM,
            bytes_accessed=4 * total * HEAD_DIM + 10 * count * HEAD_DIM,
            transcendentals=count * total,
        ),
        name="image_attention",
    )(place, packed)


def send_order(chips):
    half = chips // 2
    turns = [mask for at in range(half) for mask in (half + at, half - 1 - at)]
    return turns[:half], turns[half:]


def finish_kernel(factor, masks, img_dev, place_ref, packed_ref, sum_ref, top_ref, mine_ref, got_ref, *refs):
    *outs, text_ref = refs
    core, valid = place_ref[2], place_ref[4]
    me = 2 * place_ref[3] + core
    part_rows = packed_ref.shape[1] - 2 * img_dev
    half = mine_ref.shape[0]
    contract = (((1,), (1,)), ((), ()))
    mine, got = mine_ref[...], got_ref[...]
    keys = jnp.concatenate([mine[:, :HEAD_DIM], got[:, :HEAD_DIM]], 0)
    values = jnp.concatenate([mine[:, HEAD_DIM:], got[:, HEAD_DIM:]], 0)
    values = jnp.concatenate([values, jnp.ones(values.shape, values.dtype)], 1)
    lane = lax.broadcasted_iota(jnp.int32, (1, 2 * half), 1)
    text_position = jnp.where((lane >= half) == (core == 0), half, 0) + lane % half
    bias = jnp.where(text_position < valid, 0.0, -jnp.inf)
    group = max(1, 512 // part_rows)
    rows = group * part_rows
    for step in range(2 * len(outs) // group):
        span = slice(step * rows, (step + 1) * rows)
        queries = [
            packed_ref[me ^ (2 * masks[at // 2] + at % 2), 2 * img_dev :, :]
            for at in range(step * group, (step + 1) * group)
        ]
        queries = jnp.concatenate(queries, 0)
        scores = lax.dot_general(queries, keys, contract, preferred_element_type=jnp.float32)
        scores = scores * factor + bias
        before = top_ref[span, :]
        top = jnp.maximum(before, jnp.max(scores, 1, keepdims=True))
        rescale = jnp.exp2(before - top)
        weights = jnp.exp2(scores - jnp.concatenate([top] * (2 * half // HEAD_DIM), 1))
        total = jnp.dot(weights.astype(jnp.bfloat16), values, preferred_element_type=jnp.float32)
        mixed = sum_ref[span, :HEAD_DIM] * rescale + total[:, :HEAD_DIM]
        total = sum_ref[span, HEAD_DIM:] * rescale + total[:, HEAD_DIM:]
        mixed = (mixed / total).astype(jnp.bfloat16)
        for at in range(group):
            to = step * group + at
            outs[to // 2][to % 2, :part_rows, :] = mixed[at * part_rows : (at + 1) * part_rows]
    low, high = mine.astype(jnp.float32), got.astype(jnp.float32)
    text_ref[:half, :] = jnp.where(core == 0, low, high)
    text_ref[half:, :] = jnp.where(core == 0, high, low)
    share = (outs[0].shape[1] - part_rows) // 2
    for to in range(2 * len(outs)):
        start = pl.multiple_of((me ^ (2 * masks[to // 2] + to % 2)) * share, share)
        block = text_ref[pl.ds(start, share), :]
        block = jnp.concatenate([block[:, :HEAD_DIM], block[:, HEAD_DIM:]], 0)
        outs[to // 2][to % 2, part_rows:, :] = block.astype(jnp.bfloat16)


def finish(place, masks, packed, image, mine, got, img_dev, factor):
    devices, part_rows = packed.shape[0], packed.shape[1] - 2 * img_dev
    half = mine.shape[0]
    count = image[0].shape[0]
    outs = count // part_rows // 2
    out = jax.ShapeDtypeStruct((2, part_rows + 4 * half // devices, HEAD_DIM), jnp.bfloat16)
    return pl.pallas_call(
        functools.partial(finish_kernel, factor, masks, img_dev),
        out_shape=(out,) * outs,
        in_specs=[SMEM_SPEC] + [VMEM_SPEC] * 5,
        out_specs=(VMEM_SPEC,) * outs,
        scratch_shapes=[pltpu.VMEM((2 * half, 2 * HEAD_DIM), jnp.float32)],
        compiler_params=params(10),
        cost_estimate=pl.CostEstimate(
            flops=8 * count * half * HEAD_DIM,
            bytes_accessed=12 * count * HEAD_DIM,
            transcendentals=2 * count * half,
        ),
        name="finish",
    )(place, packed, *image, mine, got)


def gather_kernel(*refs):
    for at, piece in enumerate(refs[:-1]):
        refs[-1][at] = piece[1]


def gather_other(pieces):
    shape = (len(pieces),) + pieces[0].shape[1:]
    return pl.pallas_call(
        gather_kernel,
        out_shape=jax.ShapeDtypeStruct(shape, pieces[0].dtype),
        in_specs=[VMEM_SPEC] * len(pieces),
        out_specs=VMEM_SPEC,
        compiler_params=params(4),
        cost_estimate=pl.CostEstimate(
            flops=0, bytes_accessed=2 * len(pieces) * pieces[0].size, transcendentals=0
        ),
        name="gather_other",
    )(*pieces)


def add_kernel(joint, *refs):
    ins, outs = refs[:4], refs[4:]
    if joint:
        outs = (outs[0].at[0], outs[1], outs[0].at[1], outs[2])
    for lane in range(2):
        mine, got = ins[2 * lane], ins[2 * lane + 1]
        half = mine.shape[0] // 2
        outs[2 * lane][...] = (
            mine[half:].astype(jnp.float32) + got[half:].astype(jnp.float32)
        ).astype(jnp.bfloat16)
        outs[2 * lane + 1][...] = mine[:half].astype(jnp.float32) + got[:half].astype(jnp.float32)


def add_halves(mine, got, joint=False):
    shape = (mine[0].shape[0] // 2,) + mine[0].shape[1:]
    sent, keep = jax.ShapeDtypeStruct(shape, jnp.bfloat16), jax.ShapeDtypeStruct(shape, jnp.float32)
    outs = (sent, keep) * 2
    if joint:
        outs = (jax.ShapeDtypeStruct((2,) + shape, jnp.bfloat16), keep, keep)
    outs = pl.pallas_call(
        functools.partial(add_kernel, joint),
        out_shape=outs,
        in_specs=[VMEM_SPEC] * 4,
        out_specs=(VMEM_SPEC,) * len(outs),
        compiler_params=params(6),
        cost_estimate=pl.CostEstimate(
            flops=2 * mine[0].size, bytes_accessed=12 * mine[0].size, transcendentals=0
        ),
        name="add_halves",
    )(mine[0], got[0], mine[1], got[1])
    if joint:
        return outs[0], outs[1:]
    return [outs[0], outs[2]], [outs[1], outs[3]]


def fold_kernel(mine_ref, got_ref, sent_ref, keep_ref):
    half = mine_ref.shape[0] // 2
    total = mine_ref[half:].astype(jnp.float32) + got_ref[half:].astype(jnp.float32)
    sent_ref[...] = total.astype(sent_ref.dtype)
    keep_ref[...] = mine_ref[:half].astype(jnp.float32) + got_ref[:half].astype(jnp.float32)


def fold(mine, got):
    shape = (mine.shape[0] // 2,) + mine.shape[1:]
    return pl.pallas_call(
        fold_kernel,
        out_shape=(jax.ShapeDtypeStruct(shape, jnp.bfloat16), jax.ShapeDtypeStruct(shape, jnp.float32)),
        in_specs=[VMEM_SPEC] * 2,
        out_specs=(VMEM_SPEC,) * 2,
        compiler_params=params(8),
        cost_estimate=pl.CostEstimate(flops=mine.size, bytes_accessed=8 * mine.size, transcendentals=0),
        name="fold",
    )(mine, got)


def total_kernel(keep_ref, *refs):
    total = keep_ref[...]
    for got_ref in refs[:-1]:
        total += got_ref[...].astype(jnp.float32)
    refs[-1][...] = total.astype(refs[-1].dtype)


def add_all(keep, got):
    return pl.pallas_call(
        total_kernel,
        out_shape=jax.ShapeDtypeStruct(keep.shape, jnp.bfloat16),
        in_specs=[VMEM_SPEC] * (1 + len(got)),
        out_specs=VMEM_SPEC,
        compiler_params=params(4),
        cost_estimate=pl.CostEstimate(
            flops=4 * keep.size, bytes_accessed=12 * keep.size, transcendentals=0
        ),
        name="add_all",
    )(keep, *got)


def norm_kernel(mine_ref, got_ref, gain_ref, *outs):
    width = mine_ref.shape[2] // 2
    for at in range(2):
        total = mine_ref[at].astype(jnp.float32) + got_ref[1 - at].astype(jnp.float32)
        scale_rows = lax.rsqrt(jnp.mean(total * total, 1, keepdims=True) + epsilon)
        total = total * scale_rows * gain_ref[...].astype(jnp.float32)
        for lane, out_ref in enumerate(outs):
            out_ref[at] = total[:, lane * width : (lane + 1) * width].astype(out_ref.dtype)


def normalize(mine, got, norm_gain):
    out = jax.ShapeDtypeStruct(mine.shape[:2] + (mine.shape[2] // 2,), jnp.bfloat16)
    states = pl.pallas_call(
        norm_kernel,
        out_shape=(out, out),
        in_specs=[VMEM_SPEC] * 3,
        out_specs=(VMEM_SPEC,) * 2,
        compiler_params=params(4),
        cost_estimate=pl.CostEstimate(
            flops=4 * mine.size, bytes_accessed=8 * mine.size, transcendentals=0
        ),
        name="normalize",
    )(mine, got, norm_gain)
    return [part.reshape(-1, part.shape[2]) for part in states]


def join_kernel(mine0, got0, mine1, got1, out0, out1):
    for mine, got, out_ref in ((mine0, got0, out0), (mine1, got1, out1)):
        rows = mine.shape[0]
        if rows % 16:
            both = [mine[...].astype(jnp.float32), got[...].astype(jnp.float32)]
            out_ref[...] = jnp.concatenate(both, 0).astype(out_ref.dtype)
        else:
            out_ref[:rows, :] = mine[...]
            out_ref[rows:, :] = got[...]


def join(mine, got):
    rows, width = mine[0].shape
    out = jax.ShapeDtypeStruct((2 * rows, width), mine[0].dtype)
    return pl.pallas_call(
        join_kernel,
        out_shape=(out, out),
        in_specs=[VMEM_SPEC] * 4,
        out_specs=(VMEM_SPEC,) * 2,
        compiler_params=params(4),
        cost_estimate=pl.CostEstimate(
            flops=0, bytes_accessed=16 * rows * width, transcendentals=0
        ),
        name="join",
    )(mine[0], got[0], mine[1], got[1])


def local(
    enc_act,
    down_weight,
    norm_gain,
    text_in_weight,
    modulation_weight,
    key_value_weight,
    timesteps,
    lengths,
    image_queries,
    image_key_values,
):
    devices = lax.axis_size("seq")
    chips = devices // 2
    copies = devices // HEADS
    text_len = enc_act.shape[1]
    img_dev = image_queries.shape[1]
    part_rows = img_dev // copies
    factor = math.log2(math.e) / math.sqrt(HEAD_DIM)
    lanes = orders(chips)
    index = lax.axis_index("seq")
    chip, core = index // 2, index % 2
    place = jnp.stack([position(chip, lanes[0]), position(chip, lanes[1]), core, chip, lengths[0]])
    place = place.astype(jnp.int32)

    win0, kv0 = text_in_weight.T, key_value_weight
    mod0 = modulation_weight.transpose(1, 2, 0)
    time = time_embedding(timesteps)

    rounds = len(lanes[0])
    turns = send_order(chips)
    tie = lax.optimization_barrier

    def exchange(rows):
        return lax.all_to_all(rows, "seq", split_axis=0, concat_axis=0, tiled=True)

    image_key_values, image_queries = tie((image_key_values, image_queries))
    packed = pack(copies, image_queries[0], image_key_values[0, :, 0], image_key_values[0, :, 1])
    act, packed = tie((enc_act[0].T, packed))
    packed = exchange(packed)
    keep, other = encoder(lanes[0], place, act, down_weight)
    got = swap(other, 1)
    last = 2 * lanes[0][-1]
    for bit in lanes[0][:-1]:
        sent, keep = fold(keep, got)
        got = swap(sent, 2 * bit)
    summed, packed = tie((add_all(keep, [got]), packed))
    summed, held, held_kv, held_mod = tie((summed, win0, kv0, mod0))
    win1, kv1, mod1 = swap(held, 1), swap(held_kv, 1), swap(held_mod, 1)
    got = swap(summed, last)

    states = normalize(summed, got, norm_gain[None, :])
    images = []
    for step in reversed(range(rounds - 1)):
        if step == 0:
            states, packed = tie((states, packed))
            image = image_attention(place, packed, img_dev, factor, turns[0])
        got = [swap(state, 2 * order[step]) for state, order in zip(states, lanes)]
        if step == rounds - 2:
            lines = modulation(time, mod0, mod1)
            got, win1, kv1, lines = tie((got, win1, kv1, lines))
        if step:
            states = join(states, got)
    got, image = tie((got, image))
    images += image
    states = [state for pair in zip(states, got) for state in pair]

    blocks = project(lanes, place, states, lines, win0, win1, kv0, kv1)
    keep, sent = [blocks[0], blocks[2]], [blocks[1], blocks[3]]
    for step in range(rounds - 1):
        if step == 0:
            sent, packed = tie((sent, packed))
            image = image_attention(place, packed, img_dev, factor, turns[1])
        got = [swap(part, 2 * order[step]) for part, order in zip(sent, lanes)]
        if step == 0:
            got, image = tie((got, image))
            images += image
        sent, keep = add_halves(keep, got, step == rounds - 2)
    parts = (*keep, swap(sent, last))
    model_width = text_in_weight.shape[1] * devices
    mine, sent = combine(place, parts, chips, text_len // 2, model_width)
    got = swap(sent, 1)

    pieces, passed = [], []
    for call, masks in enumerate(turns):
        image = images[2 * call : 2 * call + 2]
        blocks = finish(place, masks, packed, image, mine, got, img_dev, factor)
        pieces += [swap(block, 2 * mask) if mask else block for mask, block in zip(masks, blocks)]
    for call in range(2):
        passed.append(swap(gather_other(pieces[call * chips // 2 : (call + 1) * chips // 2]), 1))
    attended, text_kv = unpack(copies, part_rows, turns[0] + turns[1], place, pieces, *passed)
    return (attended[None], text_kv)


def solution(mesh):
    in_specs = (
        P("dp", None, "seq"),
        P("seq", None),
        P(),
        P(None, "seq"),
        P(None, None, "seq"),
        P("seq", None),
        P("dp"),
        P("dp"),
        P("dp", "seq", None),
        P("dp", "seq", None, None),
    )
    out_specs = (P("dp", "seq", None), P(("dp", "seq"), None))
    return jax.shard_map(local, mesh=mesh, in_specs=in_specs, out_specs=out_specs, check_vma=False)
```

```python
import functools
import math

import jax
import jax.numpy as jnp
from jax import lax
from jax.experimental import pallas as pl
from jax.experimental.pallas import tpu as pltpu
from jax.sharding import PartitionSpec as P

HEAD_DIM = 128
HEADS = 16
TEMB = 256
MIB = 1024 * 1024

epsilon = 1e-06

SMEM_SPEC = pl.BlockSpec(memory_space=pltpu.SMEM)
VMEM_SPEC = pl.BlockSpec(memory_space=pltpu.VMEM)


def params(mib):
    return pltpu.CompilerParams(vmem_limit_bytes=mib * MIB)


def swap(value, mask):
    devices = lax.axis_size("seq")
    return lax.ppermute(value, "seq", [(i, i ^ mask) for i in range(devices)])


def orders(chips):
    bits = [1 << i for i in range(chips.bit_length() - 1)]
    return (bits, [bits[1], bits[0]] + bits[2:])


def position(chip, order):
    last = len(order) - 1
    return sum(((chip >> (bit.bit_length() - 1)) & 1) << (last - i) for i, bit in enumerate(order))


def member(at, order):
    last = len(order) - 1
    return sum(bit for i, bit in enumerate(order) if (at >> (last - i)) & 1)


def time_embedding(timesteps):
    half_width = TEMB // 2
    freqs = jnp.exp(-math.log(10000.0) * jnp.arange(half_width, dtype=jnp.float32) / half_width)
    angles = timesteps.astype(jnp.float32)[:, None] * freqs[None, :]
    embedding = jnp.concatenate([jnp.cos(angles), jnp.sin(angles)], 1)
    return jax.nn.silu(embedding).astype(jnp.bfloat16)


def encoder_kernel(lanes, place_ref, act_ref, weight_ref, *refs):
    outs, lhs_ref = refs[:-1], refs[-1]
    chips, share, width = outs[0].shape
    core = place_ref[2]
    half = chips * share
    first = core == 0
    tile = width // 2
    lhs_ref[...] = act_ref[...].T
    for lane, order in enumerate(lanes):
        own_ref, other_ref = outs[2 * lane], outs[2 * lane + 1]
        for column in range(0, width, tile):
            start = lane * width + column
            result = jnp.dot(
                lhs_ref[...], weight_ref[:, start : start + tile], preferred_element_type=jnp.float32
            )
            own = jnp.where(first, result[:half], result[half:]).astype(own_ref.dtype)
            other = jnp.where(first, result[half:], result[:half]).astype(own_ref.dtype)
            own = own.reshape(chips, share, tile)
            other = other.reshape(chips, share, tile)
            for block in range(chips):
                to = place_ref[lane] ^ position(block, order)
                own_ref[to, :, column : column + tile] = own[block]
                other_ref[to, :, column : column + tile] = other[block]


def encoder(lanes, place, act, weight):
    chips = 1 << len(lanes[0])
    depth, rows = act.shape
    width = weight.shape[1]
    out = jax.ShapeDtypeStruct((chips, rows // 2 // chips, width // 2), jnp.bfloat16)
    return pl.pallas_call(
        functools.partial(encoder_kernel, lanes),
        out_shape=(out,) * 4,
        in_specs=[SMEM_SPEC, VMEM_SPEC, VMEM_SPEC],
        out_specs=(VMEM_SPEC,) * 4,
        scratch_shapes=[pltpu.VMEM((rows, depth), jnp.bfloat16)],
        compiler_params=params(16),
        cost_estimate=pl.CostEstimate(
            flops=2 * rows * depth * width,
            bytes_accessed=2 * (depth * rows + depth * width + rows * width),
            transcendentals=0,
        ),
        name="encoder",
    )(place, act, weight)


def modulation_kernel(time_ref, mod0_ref, mod1_ref, out_ref):
    contract = (((1,), (1,)), ((), ()))
    embedding = jnp.broadcast_to(time_ref[...].astype(jnp.float32), (16, time_ref.shape[1]))
    embedding = embedding.astype(jnp.bfloat16)
    row = lax.broadcasted_iota(jnp.int32, (16, mod0_ref.shape[1]), 0)
    for side, mod in enumerate((mod0_ref, mod1_ref)):
        shift, scale = [
            lax.dot_general(embedding, mod[at], contract, preferred_element_type=jnp.float32)
            for at in range(2)
        ]
        lines = jnp.where(row < 2, 1.0 + scale, shift)
        high = lines.astype(jnp.bfloat16).astype(jnp.float32)
        low = jnp.where(row % 2 == 0, high, lines - high)
        out_ref[side] = jnp.where(row < 4, low, 1.0 + scale)


def modulation(time, mod0, mod1):
    return pl.pallas_call(
        modulation_kernel,
        out_shape=jax.ShapeDtypeStruct((2, 16, mod0.shape[1]), jnp.float32),
        in_specs=[VMEM_SPEC] * 3,
        out_specs=VMEM_SPEC,
        compiler_params=params(4),
        name="modulation",
    )(time, mod0, mod1)


def slot_rows(chips, width):
    means, squares = chips * 2 * 128 // width, chips * 128 // width
    return means, squares, -(-max(means + chips, squares + chips + 2) // 16) * 16


def project_kernel(lanes, place_ref, *refs):
    pieces, refs = (refs[:2], refs[2:4]), refs[4:]
    lines_ref, win0, win1, kv0, kv1, *outs, states, proj0, proj1, sums, keys_shift = refs
    chip = place_ref[3]
    half_chips = outs[0].shape[0]
    chips = 2 * half_chips
    rows = proj0.shape[0]
    share = rows // chips
    depth = states.shape[1]
    contract = (((1,), (1,)), ((), ()))
    for lane, order in enumerate(lanes):
        top, low = pieces[lane]
        states[: rows // 2, :] = top[...]
        states[rows // 2 :, :] = low[...]
        span = slice(lane * depth, (lane + 1) * depth)
        for win, proj in ((win0, proj0), (win1, proj1)):
            part = lax.dot_general(
                states[...], win[:, span], contract, preferred_element_type=jnp.float32
            )
            for at in range(chips):
                start = pl.multiple_of((chip ^ member(at, order)) * share, share)
                block = part[at * share : (at + 1) * share]
                if lane == 0:
                    proj[pl.ds(start, share), :] = block
                else:
                    proj[pl.ds(start, share), :] += block
    mean = jnp.sum(proj0[...], 1, keepdims=True) + jnp.sum(proj1[...], 1, keepdims=True)
    mean = mean / (2 * proj0.shape[1])
    value0, value1 = proj0[...] - mean, proj1[...] - mean
    square = jnp.sum(value0 * value0, 1, keepdims=True) + jnp.sum(value1 * value1, 1, keepdims=True)
    lane = lax.broadcasted_iota(jnp.int32, sums.shape, 1)
    sums[...] = jnp.where(lane == 0, mean, square).T
    left = []
    for side, value in enumerate((value0, value1)):
        lines = lines_ref[side]
        row = lax.broadcasted_iota(jnp.int32, lines.shape, 0)
        lines, scale = jnp.where(row < 4, lines, 0.0), lines[4:5]
        left.append(jnp.concatenate([value * scale, lines], 0).astype(jnp.bfloat16))
    width = outs[0].shape[2]
    means, squares, extra = slot_rows(chips, width)
    row = lax.broadcasted_iota(jnp.int32, (extra, width), 0)
    column = lax.broadcasted_iota(jnp.int32, (extra, width), 1)
    half = kv0.shape[1] // 2
    for lane, order in enumerate(lanes):
        line = sums[lane : lane + 1, :]
        if lane == 0:
            high = line.astype(jnp.bfloat16).astype(jnp.float32)
            low = line - high
            if width > 128:
                line = jnp.concatenate([high, low], 1)
            else:
                line = jnp.where(row % 2 == 0, high, low)
            line = jnp.where(row // (means // chips) == chip, line, 0.0)
        else:
            place = row * (width // 128) + column // 128
            line = jnp.concatenate([line] * (width // 128), 1)
            line = jnp.where(place == chip, line, 0.0)
        base = (means, squares)[lane]
        for at in reversed(range(chips)):
            out_ref, to = outs[2 * lane + at // half_chips], at % half_chips
            target = chip ^ member(at, order)
            columns = pl.ds(pl.multiple_of(lane * half + target * width, width), width)
            value = jnp.dot(left[0], kv0[:, columns], preferred_element_type=jnp.float32)
            value += jnp.dot(left[1], kv1[:, columns], preferred_element_type=jnp.float32)
            out_ref[to, :rows, :] = value[:rows].astype(out_ref.dtype)
            scale = value[rows : rows + 1] + value[rows + 1 : rows + 2]
            shift = value[rows + 2 : rows + 3] + value[rows + 3 : rows + 4]
            below = jnp.where(row == base + chip, scale, line)
            if lane == 0:
                keys_shift[target] = jnp.broadcast_to(shift, keys_shift.shape[1:])
            else:
                below = jnp.where(row == base + chips, shift, below)
                below = jnp.where(row == base + chips + 1, keys_shift[target][:1], below)
            out_ref[to, rows:, :] = below.astype(out_ref.dtype)


def project(lanes, place, pieces, lines, win0, win1, kv0, kv1):
    chips = 1 << len(lanes[0])
    rows = 2 * pieces[0].shape[0]
    features, depth = win0.shape
    total = kv0.shape[1]
    width = total // 2 // chips
    extra = slot_rows(chips, width)[2]
    out = jax.ShapeDtypeStruct((chips // 2, rows + extra, width), jnp.bfloat16)
    return pl.pallas_call(
        functools.partial(project_kernel, lanes),
        out_shape=(out,) * 4,
        in_specs=[SMEM_SPEC] + [VMEM_SPEC] * 9,
        out_specs=(VMEM_SPEC,) * 4,
        scratch_shapes=[
            pltpu.VMEM((rows, depth // 2), jnp.bfloat16),
            pltpu.VMEM((rows, features), jnp.float32),
            pltpu.VMEM((rows, features), jnp.float32),
            pltpu.VMEM((rows, 128), jnp.float32),
            pltpu.VMEM((chips, 8, width), jnp.float32),
        ],
        compiler_params=params(14),
        cost_estimate=pl.CostEstimate(
            flops=4 * rows * features * (depth + total),
            bytes_accessed=2 * (rows * depth + 2 * features * (depth + total) + rows * total),
            transcendentals=0,
        ),
        name="project",
    )(place, *pieces, lines, win0, win1, kv0, kv1)


def combine_kernel(chips, model_width, place_ref, *refs):
    keep0, keep1, came_ref, mine_ref, sent_ref = refs
    core = place_ref[2]
    rows = mine_ref.shape[0]
    width = keep0.shape[2]
    means, squares, _ = slot_rows(chips, width)
    totals = [keep[0] + came_ref[lane, 0].astype(jnp.float32) for lane, keep in enumerate((keep0, keep1))]
    below = [total[rows:] for total in totals]
    if width > 128:
        mean = below[0][:chips, :128] + below[0][:chips, 128:]
    else:
        lines = [below[0][2 * at : 2 * at + 1] + below[0][2 * at + 1 : 2 * at + 2] for at in range(chips)]
        mean = jnp.concatenate(lines, 0)
    away = mean - jnp.mean(mean, 0, keepdims=True)
    square = jnp.sum(below[1][:squares], 0, keepdims=True)
    square = sum(square[:, at : at + 128] for at in range(0, width, 128))
    square += jnp.sum(away * away, 0, keepdims=True) * (model_width / chips)
    scale = lax.rsqrt(square / model_width + epsilon)
    turned = jnp.concatenate([away, scale, jnp.zeros((rows - chips - 1, rows), jnp.float32)], 0).T
    scale = turned[:, chips : chips + 1]
    texts = []
    for lane, total in enumerate(totals):
        base = (means, squares)[lane]
        text = total[:rows]
        for at in range(chips):
            text += turned[:, at : at + 1] * below[lane][base + at : base + at + 1]
        shift = below[1][squares + chips + 1 - lane : squares + chips + 2 - lane]
        texts.append(text * scale + shift)
    for part, text in enumerate(texts):
        span = slice(part * HEAD_DIM, (part + 1) * HEAD_DIM)
        if width > HEAD_DIM:
            low, high = text[:, :HEAD_DIM], text[:, HEAD_DIM:]
            mine_ref[:, span] = jnp.where(core == 0, low, high).astype(mine_ref.dtype)
            sent_ref[:, span] = jnp.where(core == 0, high, low).astype(mine_ref.dtype)
        else:
            mine_ref[:, span] = text.astype(mine_ref.dtype)
            sent_ref[:, span] = text.astype(mine_ref.dtype)


def combine(place, parts, chips, rows, model_width):
    out = jax.ShapeDtypeStruct((rows, 2 * HEAD_DIM), jnp.bfloat16)
    return pl.pallas_call(
        functools.partial(combine_kernel, chips, model_width),
        out_shape=(out, out),
        in_specs=[SMEM_SPEC] + [VMEM_SPEC] * 3,
        out_specs=(VMEM_SPEC, VMEM_SPEC),
        compiler_params=params(4),
        cost_estimate=pl.CostEstimate(
            flops=8 * rows * 512, bytes_accessed=12 * rows * 512, transcendentals=0
        ),
        name="combine",
    )(place, *parts)


def pack_kernel(copies, queries_ref, keys_ref, values_ref, out_ref):
    img_dev = keys_ref.shape[0]
    part_rows = img_dev // copies
    for device in range(out_ref.shape[0]):
        head, copy = device // copies, device % copies
        span = slice(head * HEAD_DIM, (head + 1) * HEAD_DIM)
        out_ref[device, :img_dev, :] = keys_ref[:, span]
        out_ref[device, img_dev : 2 * img_dev, :] = values_ref[:, span]
        out_ref[device, 2 * img_dev :, :] = queries_ref[copy * part_rows : (copy + 1) * part_rows, span]


def pack(copies, queries, keys, values):
    img_dev = keys.shape[0]
    rows = 2 * img_dev + img_dev // copies
    return pl.pallas_call(
        functools.partial(pack_kernel, copies),
        out_shape=jax.ShapeDtypeStruct((HEADS * copies, rows, HEAD_DIM), jnp.bfloat16),
        in_specs=[VMEM_SPEC] * 3,
        out_specs=VMEM_SPEC,
        compiler_params=params(8),
        cost_estimate=pl.CostEstimate(
            flops=0, bytes_accessed=4 * HEADS * copies * rows * HEAD_DIM, transcendentals=0
        ),
        name="pack",
    )(queries, keys, values)


def unpack_kernel(copies, part_rows, masks, place_ref, *refs):
    *pieces, near_ref, far_ref, attended_ref, text_ref = refs
    me = 2 * place_ref[3] + place_ref[2]
    share = text_ref.shape[0]
    half = text_ref.shape[1] // 2
    count = len(pieces) // 2
    passed = [near_ref.at[at] for at in range(count)] + [far_ref.at[at] for at in range(count)]
    blocks = [block for piece, other in zip(pieces, passed) for block in (piece.at[0], other)]
    for at, block_ref in enumerate(blocks):
        device = me ^ (2 * masks[at // 2] + at % 2)
        head, copy = device // copies, device % copies
        start = pl.multiple_of(head * HEAD_DIM, HEAD_DIM)
        rows = pl.ds(pl.multiple_of(copy * part_rows, part_rows), part_rows)
        attended_ref[rows, pl.ds(start, HEAD_DIM)] = block_ref[:part_rows, :]
        block = block_ref[part_rows:, :].astype(jnp.float32)
        text_ref[:, pl.ds(start, HEAD_DIM)] = block[:share].astype(text_ref.dtype)
        start = pl.multiple_of(half + head * HEAD_DIM, HEAD_DIM)
        text_ref[:, pl.ds(start, HEAD_DIM)] = block[share:].astype(text_ref.dtype)


def unpack(copies, part_rows, masks, place, pieces, near, far):
    share = (near.shape[1] - part_rows) // 2
    return pl.pallas_call(
        functools.partial(unpack_kernel, copies, part_rows, masks),
        out_shape=(
            jax.ShapeDtypeStruct((part_rows * copies, HEADS * HEAD_DIM), jnp.bfloat16),
            jax.ShapeDtypeStruct((share, 2 * HEADS * HEAD_DIM), jnp.bfloat16),
        ),
        in_specs=[SMEM_SPEC] + [VMEM_SPEC] * (len(pieces) + 2),
        out_specs=(VMEM_SPEC, VMEM_SPEC),
        compiler_params=params(6),
        name="unpack",
    )(place, *pieces, near, far)


def image_kernel(factor, masks, img_dev, place_ref, packed_ref, sum_ref, top_ref, keys_ref, wide_ref):
    me = 2 * place_ref[3] + place_ref[2]
    wide_ref[:, HEAD_DIM:] = jnp.ones((wide_ref.shape[0], HEAD_DIM), wide_ref.dtype)
    for device in range(packed_ref.shape[0]):
        rows = slice(device * img_dev, (device + 1) * img_dev)
        keys_ref[rows, :] = packed_ref[device, :img_dev, :]
        wide_ref[rows, :HEAD_DIM] = packed_ref[device, img_dev : 2 * img_dev, :]
    group = max(1, 256 // (packed_ref.shape[1] - 2 * img_dev))
    rows = 256
    contract = (((1,), (1,)), ((), ()))
    count = sum_ref.shape[0]
    for start in range(0, count, rows):
        span = slice(start, start + rows)
        at = start // rows * group
        queries = [
            packed_ref[me ^ (2 * masks[i // 2] + i % 2), 2 * img_dev :, :] for i in range(at, at + group)
        ]
        queries = jnp.concatenate(queries, 0)
        scores = lax.dot_general(queries, keys_ref[...], contract, preferred_element_type=jnp.float32)
        scores = scores * factor
        top = jnp.max(scores, 1, keepdims=True)
        weights = jnp.exp2(scores - top).astype(jnp.bfloat16)
        sum_ref[span, :] = jnp.dot(weights, wide_ref[...], preferred_element_type=jnp.float32)
        top_ref[span, :] = jnp.broadcast_to(top, (rows, HEAD_DIM))


def image_attention(place, packed, img_dev, factor, masks):
    count = 2 * len(masks) * (packed.shape[1] - 2 * img_dev)
    total = packed.shape[0] * img_dev
    return pl.pallas_call(
        functools.partial(image_kernel, factor, masks, img_dev),
        out_shape=(
            jax.ShapeDtypeStruct((count, 2 * HEAD_DIM), jnp.float32),
            jax.ShapeDtypeStruct((count, HEAD_DIM), jnp.float32),
        ),
        in_specs=[SMEM_SPEC, VMEM_SPEC],
        out_specs=(VMEM_SPEC, VMEM_SPEC),
        scratch_shapes=[
            pltpu.VMEM((total, HEAD_DIM), jnp.bfloat16),
            pltpu.VMEM((total, 2 * HEAD_DIM), jnp.bfloat16),
        ],
        compiler_params=params(14),
        cost_estimate=pl.CostEstimate(
            flops=4 * count * total * HEAD_DIM,
            bytes_accessed=4 * total * HEAD_DIM + 10 * count * HEAD_DIM,
            transcendentals=count * total,
        ),
        name="image_attention",
    )(place, packed)


def send_order(chips):
    half = chips // 2
    turns = [mask for at in range(half) for mask in (half + at, (at + 1) % half)]
    return turns[:half], turns[half:]


def finish_kernel(factor, masks, img_dev, place_ref, packed_ref, sum_ref, top_ref, mine_ref, got_ref, *refs):
    *outs, text_ref = refs
    core, valid = place_ref[2], place_ref[4]
    me = 2 * place_ref[3] + core
    part_rows = packed_ref.shape[1] - 2 * img_dev
    half = mine_ref.shape[0]
    contract = (((1,), (1,)), ((), ()))
    mine, got = mine_ref[...], got_ref[...]
    keys = jnp.concatenate([mine[:, :HEAD_DIM], got[:, :HEAD_DIM]], 0)
    values = jnp.concatenate([mine[:, HEAD_DIM:], got[:, HEAD_DIM:]], 0)
    values = jnp.concatenate([values, jnp.ones(values.shape, values.dtype)], 1)
    lane = lax.broadcasted_iota(jnp.int32, (1, 2 * half), 1)
    text_position = jnp.where((lane >= half) == (core == 0), half, 0) + lane % half
    bias = jnp.where(text_position < valid, 0.0, -jnp.inf)
    group = max(1, 512 // part_rows)
    rows = group * part_rows
    for step in range(2 * len(outs) // group):
        span = slice(step * rows, (step + 1) * rows)
        queries = [
            packed_ref[me ^ (2 * masks[at // 2] + at % 2), 2 * img_dev :, :]
            for at in range(step * group, (step + 1) * group)
        ]
        queries = jnp.concatenate(queries, 0)
        scores = lax.dot_general(queries, keys, contract, preferred_element_type=jnp.float32)
        scores = scores * factor + bias
        before = top_ref[span, :]
        top = jnp.maximum(before, jnp.max(scores, 1, keepdims=True))
        rescale = jnp.exp2(before - top)
        weights = jnp.exp2(scores - jnp.concatenate([top] * (2 * half // HEAD_DIM), 1))
        total = jnp.dot(weights.astype(jnp.bfloat16), values, preferred_element_type=jnp.float32)
        mixed = sum_ref[span, :HEAD_DIM] * rescale + total[:, :HEAD_DIM]
        total = sum_ref[span, HEAD_DIM:] * rescale + total[:, HEAD_DIM:]
        mixed = (mixed / total).astype(jnp.bfloat16)
        for at in range(group):
            to = step * group + at
            outs[to // 2][to % 2, :part_rows, :] = mixed[at * part_rows : (at + 1) * part_rows]
    low, high = mine.astype(jnp.float32), got.astype(jnp.float32)
    text_ref[:half, :] = jnp.where(core == 0, low, high)
    text_ref[half:, :] = jnp.where(core == 0, high, low)
    share = (outs[0].shape[1] - part_rows) // 2
    for to in range(2 * len(outs)):
        start = pl.multiple_of((me ^ (2 * masks[to // 2] + to % 2)) * share, share)
        block = text_ref[pl.ds(start, share), :]
        block = jnp.concatenate([block[:, :HEAD_DIM], block[:, HEAD_DIM:]], 0)
        outs[to // 2][to % 2, part_rows:, :] = block.astype(jnp.bfloat16)


def finish(place, masks, packed, image, mine, got, img_dev, factor):
    devices, part_rows = packed.shape[0], packed.shape[1] - 2 * img_dev
    half = mine.shape[0]
    count = image[0].shape[0]
    outs = count // part_rows // 2
    out = jax.ShapeDtypeStruct((2, part_rows + 4 * half // devices, HEAD_DIM), jnp.bfloat16)
    return pl.pallas_call(
        functools.partial(finish_kernel, factor, masks, img_dev),
        out_shape=(out,) * outs,
        in_specs=[SMEM_SPEC] + [VMEM_SPEC] * 5,
        out_specs=(VMEM_SPEC,) * outs,
        scratch_shapes=[pltpu.VMEM((2 * half, 2 * HEAD_DIM), jnp.float32)],
        compiler_params=params(10),
        cost_estimate=pl.CostEstimate(
            flops=8 * count * half * HEAD_DIM,
            bytes_accessed=12 * count * HEAD_DIM,
            transcendentals=2 * count * half,
        ),
        name="finish",
    )(place, packed, *image, mine, got)


def gather_kernel(*refs):
    for at, piece in enumerate(refs[:-1]):
        refs[-1][at] = piece[1]


def gather_other(pieces):
    shape = (len(pieces),) + pieces[0].shape[1:]
    return pl.pallas_call(
        gather_kernel,
        out_shape=jax.ShapeDtypeStruct(shape, pieces[0].dtype),
        in_specs=[VMEM_SPEC] * len(pieces),
        out_specs=VMEM_SPEC,
        compiler_params=params(4),
        cost_estimate=pl.CostEstimate(
            flops=0, bytes_accessed=2 * len(pieces) * pieces[0].size, transcendentals=0
        ),
        name="gather_other",
    )(*pieces)


def add_kernel(joint, *refs):
    ins, outs = refs[:4], refs[4:]
    if joint:
        outs = (outs[0].at[0], outs[1], outs[0].at[1], outs[2])
    for lane in range(2):
        mine, got = ins[2 * lane], ins[2 * lane + 1]
        half = mine.shape[0] // 2
        outs[2 * lane][...] = (
            mine[half:].astype(jnp.float32) + got[half:].astype(jnp.float32)
        ).astype(jnp.bfloat16)
        outs[2 * lane + 1][...] = mine[:half].astype(jnp.float32) + got[:half].astype(jnp.float32)


def add_halves(mine, got, joint=False):
    shape = (mine[0].shape[0] // 2,) + mine[0].shape[1:]
    sent, keep = jax.ShapeDtypeStruct(shape, jnp.bfloat16), jax.ShapeDtypeStruct(shape, jnp.float32)
    outs = (sent, keep) * 2
    if joint:
        outs = (jax.ShapeDtypeStruct((2,) + shape, jnp.bfloat16), keep, keep)
    outs = pl.pallas_call(
        functools.partial(add_kernel, joint),
        out_shape=outs,
        in_specs=[VMEM_SPEC] * 4,
        out_specs=(VMEM_SPEC,) * len(outs),
        compiler_params=params(6),
        cost_estimate=pl.CostEstimate(
            flops=2 * mine[0].size, bytes_accessed=12 * mine[0].size, transcendentals=0
        ),
        name="add_halves",
    )(mine[0], got[0], mine[1], got[1])
    if joint:
        return outs[0], outs[1:]
    return [outs[0], outs[2]], [outs[1], outs[3]]


def total_kernel(mine0, got0, mine1, got1, out_ref):
    for lane, (mine, got) in enumerate(((mine0, got0), (mine1, got1))):
        out_ref[lane] = (mine[...] + got[...].astype(jnp.float32)).astype(out_ref.dtype)


def add_all(mine, got):
    return pl.pallas_call(
        total_kernel,
        out_shape=jax.ShapeDtypeStruct((2,) + mine[0].shape, jnp.bfloat16),
        in_specs=[VMEM_SPEC] * 4,
        out_specs=VMEM_SPEC,
        compiler_params=params(4),
        cost_estimate=pl.CostEstimate(
            flops=2 * mine[0].size, bytes_accessed=16 * mine[0].size, transcendentals=0
        ),
        name="add_all",
    )(mine[0], got[0], mine[1], got[1])


def norm_kernel(mine_ref, got_ref, gain_ref, out0, out1):
    width = mine_ref.shape[3]
    for at in range(2):
        totals = [
            mine_ref[lane, at].astype(jnp.float32) + got_ref[lane, 1 - at].astype(jnp.float32)
            for lane in range(2)
        ]
        square = sum(jnp.sum(total * total, 1, keepdims=True) for total in totals)
        scale_rows = lax.rsqrt(square / (2 * width) + epsilon)
        for lane, (total, out_ref) in enumerate(zip(totals, (out0, out1))):
            gain = gain_ref[:, lane * width : (lane + 1) * width].astype(jnp.float32)
            out_ref[at] = (total * scale_rows * gain).astype(out_ref.dtype)


def normalize(mine, got, norm_gain):
    out = jax.ShapeDtypeStruct(mine.shape[1:], jnp.bfloat16)
    states = pl.pallas_call(
        norm_kernel,
        out_shape=(out, out),
        in_specs=[VMEM_SPEC] * 3,
        out_specs=(VMEM_SPEC,) * 2,
        compiler_params=params(4),
        cost_estimate=pl.CostEstimate(
            flops=4 * mine.size, bytes_accessed=8 * mine.size, transcendentals=0
        ),
        name="normalize",
    )(mine, got, norm_gain)
    return [part.reshape(-1, part.shape[2]) for part in states]


def join_kernel(mine0, got0, mine1, got1, out0, out1):
    for mine, got, out_ref in ((mine0, got0, out0), (mine1, got1, out1)):
        rows = mine.shape[0]
        if rows % 16:
            both = [mine[...].astype(jnp.float32), got[...].astype(jnp.float32)]
            out_ref[...] = jnp.concatenate(both, 0).astype(out_ref.dtype)
        else:
            out_ref[:rows, :] = mine[...]
            out_ref[rows:, :] = got[...]


def join(mine, got):
    rows, width = mine[0].shape
    out = jax.ShapeDtypeStruct((2 * rows, width), mine[0].dtype)
    return pl.pallas_call(
        join_kernel,
        out_shape=(out, out),
        in_specs=[VMEM_SPEC] * 4,
        out_specs=(VMEM_SPEC,) * 2,
        compiler_params=params(4),
        cost_estimate=pl.CostEstimate(
            flops=0, bytes_accessed=16 * rows * width, transcendentals=0
        ),
        name="join",
    )(mine[0], got[0], mine[1], got[1])


def local(
    enc_act,
    down_weight,
    norm_gain,
    text_in_weight,
    modulation_weight,
    key_value_weight,
    timesteps,
    lengths,
    image_queries,
    image_key_values,
):
    devices = lax.axis_size("seq")
    chips = devices // 2
    copies = devices // HEADS
    text_len = enc_act.shape[1]
    img_dev = image_queries.shape[1]
    part_rows = img_dev // copies
    factor = math.log2(math.e) / math.sqrt(HEAD_DIM)
    lanes = orders(chips)
    index = lax.axis_index("seq")
    chip, core = index // 2, index % 2
    place = jnp.stack([position(chip, lanes[0]), position(chip, lanes[1]), core, chip, lengths[0]])
    place = place.astype(jnp.int32)

    win0, kv0 = text_in_weight.T, key_value_weight
    mod0 = modulation_weight.transpose(1, 2, 0)
    time = time_embedding(timesteps)

    rounds = len(lanes[0])
    turns = send_order(chips)
    tie = lax.optimization_barrier

    def exchange(rows):
        return lax.all_to_all(rows, "seq", split_axis=0, concat_axis=0, tiled=True)

    image_key_values, image_queries = tie((image_key_values, image_queries))
    packed = pack(copies, image_queries[0], image_key_values[0, :, 0], image_key_values[0, :, 1])
    act, packed = tie((enc_act[0].T, packed))
    packed = exchange(packed)
    encoded = encoder(lanes, place, act, down_weight)
    keep, got = encoded[::2], [swap(other, 1) for other in encoded[1::2]]
    last = 2 * lanes[0][-1]
    for step in range(rounds - 1):
        sent, keep = add_halves(keep, got)
        got = [swap(part, 2 * order[step]) for part, order in zip(sent, lanes)]
    summed, packed = tie((add_all(keep, got), packed))
    summed, held, held_kv, held_mod = tie((summed, win0, kv0, mod0))
    win1, kv1, mod1 = swap(held, 1), swap(held_kv, 1), swap(held_mod, 1)
    got = swap(summed, last)

    states = normalize(summed, got, norm_gain[None, :])
    images = []
    for step in reversed(range(rounds - 1)):
        if step == 0:
            states, packed = tie((states, packed))
            image = image_attention(place, packed, img_dev, factor, turns[0])
        got = [swap(state, 2 * order[step]) for state, order in zip(states, lanes)]
        if step == rounds - 2:
            lines = modulation(time, mod0, mod1)
            got, win1, kv1, lines = tie((got, win1, kv1, lines))
        if step:
            states = join(states, got)
    got, image = tie((got, image))
    images += image
    states = [state for pair in zip(states, got) for state in pair]

    blocks = project(lanes, place, states, lines, win0, win1, kv0, kv1)
    keep, sent = [blocks[0], blocks[2]], [blocks[1], blocks[3]]
    for step in range(rounds - 1):
        if step == 0:
            sent, packed = tie((sent, packed))
            image = image_attention(place, packed, img_dev, factor, turns[1])
        got = [swap(part, 2 * order[step]) for part, order in zip(sent, lanes)]
        if step == 0:
            got, image = tie((got, image))
            images += image
        sent, keep = add_halves(keep, got, step == rounds - 2)
    parts = (*keep, swap(sent, last))
    model_width = text_in_weight.shape[1] * devices
    mine, sent = combine(place, parts, chips, text_len // 2, model_width)
    got = swap(sent, 1)

    pieces, passed = [], []
    for call, masks in enumerate(turns):
        image = images[2 * call : 2 * call + 2]
        blocks = finish(place, masks, packed, image, mine, got, img_dev, factor)
        pieces += [swap(block, 2 * mask) if mask else block for mask, block in zip(masks, blocks)]
    for call in range(2):
        passed.append(swap(gather_other(pieces[call * chips // 2 : (call + 1) * chips // 2]), 1))
    attended, text_kv = unpack(copies, part_rows, turns[0] + turns[1], place, pieces, *passed)
    return (attended[None], text_kv)


def solution(mesh):
    in_specs = (
        P("dp", None, "seq"),
        P("seq", None),
        P(),
        P(None, "seq"),
        P(None, None, "seq"),
        P("seq", None),
        P("dp"),
        P("dp"),
        P("dp", "seq", None),
        P("dp", "seq", None, None),
    )
    out_specs = (P("dp", "seq", None), P(("dp", "seq"), None))
    return jax.shard_map(local, mesh=mesh, in_specs=in_specs, out_specs=out_specs, check_vma=False)
```

```python
import functools
import math

import jax
import jax.numpy as jnp
from jax import lax
from jax.experimental import pallas as pl
from jax.experimental.pallas import tpu as pltpu
from jax.sharding import PartitionSpec as P

HEAD_DIM = 128
HEADS = 16
TEMB = 256
MIB = 1024 * 1024

epsilon = 1e-06

SMEM_SPEC = pl.BlockSpec(memory_space=pltpu.SMEM)
VMEM_SPEC = pl.BlockSpec(memory_space=pltpu.VMEM)


def params(mib):
    return pltpu.CompilerParams(vmem_limit_bytes=mib * MIB)


def swap(value, mask):
    devices = lax.axis_size("seq")
    return lax.ppermute(value, "seq", [(i, i ^ mask) for i in range(devices)])


def orders(chips):
    bits = [1 << i for i in range(chips.bit_length() - 1)]
    return (bits, [bits[1], bits[0]] + bits[2:])


def position(chip, order):
    last = len(order) - 1
    return sum(((chip >> (bit.bit_length() - 1)) & 1) << (last - i) for i, bit in enumerate(order))


def member(at, order):
    last = len(order) - 1
    return sum(bit for i, bit in enumerate(order) if (at >> (last - i)) & 1)


def time_embedding(timesteps):
    half_width = TEMB // 2
    freqs = jnp.exp(-math.log(10000.0) * jnp.arange(half_width, dtype=jnp.float32) / half_width)
    angles = timesteps.astype(jnp.float32)[:, None] * freqs[None, :]
    embedding = jnp.concatenate([jnp.cos(angles), jnp.sin(angles)], 1)
    return jax.nn.silu(embedding).astype(jnp.bfloat16)


def encoder_kernel(lanes, place_ref, act_ref, weight_ref, *refs):
    outs, lhs_ref = refs[:-1], refs[-1]
    chips, share, width = outs[0].shape
    core = place_ref[2]
    half = chips * share
    first = core == 0
    tile = width // 2
    lhs_ref[...] = act_ref[...].T
    for lane, order in enumerate(lanes):
        own_ref, other_ref = outs[2 * lane], outs[2 * lane + 1]
        for column in range(0, width, tile):
            start = lane * width + column
            result = jnp.dot(
                lhs_ref[...], weight_ref[:, start : start + tile], preferred_element_type=jnp.float32
            )
            own = jnp.where(first, result[:half], result[half:]).astype(own_ref.dtype)
            other = jnp.where(first, result[half:], result[:half]).astype(own_ref.dtype)
            own = own.reshape(chips, share, tile)
            other = other.reshape(chips, share, tile)
            for block in range(chips):
                to = place_ref[lane] ^ position(block, order)
                own_ref[to, :, column : column + tile] = own[block]
                other_ref[to, :, column : column + tile] = other[block]


def encoder(lanes, place, act, weight):
    chips = 1 << len(lanes[0])
    depth, rows = act.shape
    width = weight.shape[1]
    out = jax.ShapeDtypeStruct((chips, rows // 2 // chips, width // 2), jnp.bfloat16)
    return pl.pallas_call(
        functools.partial(encoder_kernel, lanes),
        out_shape=(out,) * 4,
        in_specs=[SMEM_SPEC, VMEM_SPEC, VMEM_SPEC],
        out_specs=(VMEM_SPEC,) * 4,
        scratch_shapes=[pltpu.VMEM((rows, depth), jnp.bfloat16)],
        compiler_params=params(16),
        cost_estimate=pl.CostEstimate(
            flops=2 * rows * depth * width,
            bytes_accessed=2 * (depth * rows + depth * width + rows * width),
            transcendentals=0,
        ),
        name="encoder",
    )(place, act, weight)


def modulation_kernel(time_ref, mod0_ref, mod1_ref, out_ref):
    contract = (((1,), (1,)), ((), ()))
    embedding = jnp.broadcast_to(time_ref[...].astype(jnp.float32), (16, time_ref.shape[1]))
    embedding = embedding.astype(jnp.bfloat16)
    row = lax.broadcasted_iota(jnp.int32, (16, mod0_ref.shape[1]), 0)
    for side, mod in enumerate((mod0_ref, mod1_ref)):
        shift, scale = [
            lax.dot_general(embedding, mod[at], contract, preferred_element_type=jnp.float32)
            for at in range(2)
        ]
        lines = jnp.where(row < 2, 1.0 + scale, shift)
        high = lines.astype(jnp.bfloat16).astype(jnp.float32)
        low = jnp.where(row % 2 == 0, high, lines - high)
        out_ref[side] = jnp.where(row < 4, low, 1.0 + scale)


def modulation(time, mod0, mod1):
    return pl.pallas_call(
        modulation_kernel,
        out_shape=jax.ShapeDtypeStruct((2, 16, mod0.shape[1]), jnp.float32),
        in_specs=[VMEM_SPEC] * 3,
        out_specs=VMEM_SPEC,
        compiler_params=params(4),
        name="modulation",
    )(time, mod0, mod1)


def slot_rows(chips, width):
    means, squares = chips * 2 * 128 // width, chips * 128 // width
    return means, squares, -(-max(means + chips, squares + chips + 2) // 16) * 16


def project_kernel(lanes, place_ref, *refs):
    pieces, refs = (refs[:2], refs[2:4]), refs[4:]
    lines_ref, win0, win1, kv0, kv1, *outs, states, proj0, proj1, sums, keys_shift = refs
    chip = place_ref[3]
    half_chips = outs[0].shape[0]
    chips = 2 * half_chips
    rows = proj0.shape[0]
    share = rows // chips
    depth = states.shape[1]
    contract = (((1,), (1,)), ((), ()))
    for lane, order in enumerate(lanes):
        top, low = pieces[lane]
        states[: rows // 2, :] = top[...]
        states[rows // 2 :, :] = low[...]
        span = slice(lane * depth, (lane + 1) * depth)
        for win, proj in ((win0, proj0), (win1, proj1)):
            part = lax.dot_general(
                states[...], win[:, span], contract, preferred_element_type=jnp.float32
            )
            for at in range(chips):
                start = pl.multiple_of((chip ^ member(at, order)) * share, share)
                block = part[at * share : (at + 1) * share]
                if lane == 0:
                    proj[pl.ds(start, share), :] = block
                else:
                    proj[pl.ds(start, share), :] += block
    mean = jnp.sum(proj0[...], 1, keepdims=True) + jnp.sum(proj1[...], 1, keepdims=True)
    mean = mean / (2 * proj0.shape[1])
    value0, value1 = proj0[...] - mean, proj1[...] - mean
    square = jnp.sum(value0 * value0, 1, keepdims=True) + jnp.sum(value1 * value1, 1, keepdims=True)
    lane = lax.broadcasted_iota(jnp.int32, sums.shape, 1)
    sums[...] = jnp.where(lane == 0, mean, square).T
    left = []
    for side, value in enumerate((value0, value1)):
        lines = lines_ref[side]
        row = lax.broadcasted_iota(jnp.int32, lines.shape, 0)
        lines, scale = jnp.where(row < 4, lines, 0.0), lines[4:5]
        left.append(jnp.concatenate([value * scale, lines], 0).astype(jnp.bfloat16))
    width = outs[0].shape[2]
    means, squares, extra = slot_rows(chips, width)
    row = lax.broadcasted_iota(jnp.int32, (extra, width), 0)
    column = lax.broadcasted_iota(jnp.int32, (extra, width), 1)
    half = kv0.shape[1] // 2
    for lane, order in enumerate(lanes):
        line = sums[lane : lane + 1, :]
        if lane == 0:
            high = line.astype(jnp.bfloat16).astype(jnp.float32)
            low = line - high
            if width > 128:
                line = jnp.concatenate([high, low], 1)
            else:
                line = jnp.where(row % 2 == 0, high, low)
            line = jnp.where(row // (means // chips) == chip, line, 0.0)
        else:
            place = row * (width // 128) + column // 128
            line = jnp.concatenate([line] * (width // 128), 1)
            line = jnp.where(place == chip, line, 0.0)
        base = (means, squares)[lane]
        for at in reversed(range(chips)):
            out_ref, to = outs[2 * lane + at // half_chips], at % half_chips
            target = chip ^ member(at, order)
            columns = pl.ds(pl.multiple_of(lane * half + target * width, width), width)
            value = jnp.dot(left[0], kv0[:, columns], preferred_element_type=jnp.float32)
            value += jnp.dot(left[1], kv1[:, columns], preferred_element_type=jnp.float32)
            out_ref[to, :rows, :] = value[:rows].astype(out_ref.dtype)
            scale = value[rows : rows + 1] + value[rows + 1 : rows + 2]
            shift = value[rows + 2 : rows + 3] + value[rows + 3 : rows + 4]
            below = jnp.where(row == base + chip, scale, line)
            if lane == 0:
                keys_shift[target] = jnp.broadcast_to(shift, keys_shift.shape[1:])
            else:
                below = jnp.where(row == base + chips, shift, below)
                below = jnp.where(row == base + chips + 1, keys_shift[target][:1], below)
            out_ref[to, rows:, :] = below.astype(out_ref.dtype)


def project(lanes, place, pieces, lines, win0, win1, kv0, kv1):
    chips = 1 << len(lanes[0])
    rows = 2 * pieces[0].shape[0]
    features, depth = win0.shape
    total = kv0.shape[1]
    width = total // 2 // chips
    extra = slot_rows(chips, width)[2]
    out = jax.ShapeDtypeStruct((chips // 2, rows + extra, width), jnp.bfloat16)
    return pl.pallas_call(
        functools.partial(project_kernel, lanes),
        out_shape=(out,) * 4,
        in_specs=[SMEM_SPEC] + [VMEM_SPEC] * 9,
        out_specs=(VMEM_SPEC,) * 4,
        scratch_shapes=[
            pltpu.VMEM((rows, depth // 2), jnp.bfloat16),
            pltpu.VMEM((rows, features), jnp.float32),
            pltpu.VMEM((rows, features), jnp.float32),
            pltpu.VMEM((rows, 128), jnp.float32),
            pltpu.VMEM((chips, 8, width), jnp.float32),
        ],
        compiler_params=params(14),
        cost_estimate=pl.CostEstimate(
            flops=4 * rows * features * (depth + total),
            bytes_accessed=2 * (rows * depth + 2 * features * (depth + total) + rows * total),
            transcendentals=0,
        ),
        name="project",
    )(place, *pieces, lines, win0, win1, kv0, kv1)


def combine_kernel(chips, model_width, place_ref, *refs):
    keep0, keep1, came_ref, mine_ref, sent_ref = refs
    core = place_ref[2]
    rows = mine_ref.shape[0]
    width = keep0.shape[2]
    means, squares, _ = slot_rows(chips, width)
    totals = [keep[0] + came_ref[lane, 0].astype(jnp.float32) for lane, keep in enumerate((keep0, keep1))]
    below = [total[rows:] for total in totals]
    if width > 128:
        mean = below[0][:chips, :128] + below[0][:chips, 128:]
    else:
        lines = [below[0][2 * at : 2 * at + 1] + below[0][2 * at + 1 : 2 * at + 2] for at in range(chips)]
        mean = jnp.concatenate(lines, 0)
    away = mean - jnp.mean(mean, 0, keepdims=True)
    square = jnp.sum(below[1][:squares], 0, keepdims=True)
    square = sum(square[:, at : at + 128] for at in range(0, width, 128))
    square += jnp.sum(away * away, 0, keepdims=True) * (model_width / chips)
    scale = lax.rsqrt(square / model_width + epsilon)
    turned = jnp.concatenate([away, scale, jnp.zeros((rows - chips - 1, rows), jnp.float32)], 0).T
    scale = turned[:, chips : chips + 1]
    texts = []
    for lane, total in enumerate(totals):
        base = (means, squares)[lane]
        text = total[:rows]
        for at in range(chips):
            text += turned[:, at : at + 1] * below[lane][base + at : base + at + 1]
        shift = below[1][squares + chips + 1 - lane : squares + chips + 2 - lane]
        texts.append(text * scale + shift)
    for part, text in enumerate(texts):
        span = slice(part * HEAD_DIM, (part + 1) * HEAD_DIM)
        if width > HEAD_DIM:
            low, high = text[:, :HEAD_DIM], text[:, HEAD_DIM:]
            mine_ref[:, span] = jnp.where(core == 0, low, high).astype(mine_ref.dtype)
            sent_ref[:, span] = jnp.where(core == 0, high, low).astype(mine_ref.dtype)
        else:
            mine_ref[:, span] = text.astype(mine_ref.dtype)
            sent_ref[:, span] = text.astype(mine_ref.dtype)


def combine(place, parts, chips, rows, model_width):
    out = jax.ShapeDtypeStruct((rows, 2 * HEAD_DIM), jnp.bfloat16)
    return pl.pallas_call(
        functools.partial(combine_kernel, chips, model_width),
        out_shape=(out, out),
        in_specs=[SMEM_SPEC] + [VMEM_SPEC] * 3,
        out_specs=(VMEM_SPEC, VMEM_SPEC),
        compiler_params=params(4),
        cost_estimate=pl.CostEstimate(
            flops=8 * rows * 512, bytes_accessed=12 * rows * 512, transcendentals=0
        ),
        name="combine",
    )(place, *parts)


def pack_kernel(copies, queries_ref, keys_ref, values_ref, out_ref):
    img_dev = keys_ref.shape[0]
    part_rows = img_dev // copies
    for device in range(out_ref.shape[0]):
        head, copy = device // copies, device % copies
        span = slice(head * HEAD_DIM, (head + 1) * HEAD_DIM)
        out_ref[device, :img_dev, :] = keys_ref[:, span]
        out_ref[device, img_dev : 2 * img_dev, :] = values_ref[:, span]
        out_ref[device, 2 * img_dev :, :] = queries_ref[copy * part_rows : (copy + 1) * part_rows, span]


def pack(copies, queries, keys, values):
    img_dev = keys.shape[0]
    rows = 2 * img_dev + img_dev // copies
    return pl.pallas_call(
        functools.partial(pack_kernel, copies),
        out_shape=jax.ShapeDtypeStruct((HEADS * copies, rows, HEAD_DIM), jnp.bfloat16),
        in_specs=[VMEM_SPEC] * 3,
        out_specs=VMEM_SPEC,
        compiler_params=params(8),
        cost_estimate=pl.CostEstimate(
            flops=0, bytes_accessed=4 * HEADS * copies * rows * HEAD_DIM, transcendentals=0
        ),
        name="pack",
    )(queries, keys, values)


def unpack_kernel(copies, part_rows, masks, place_ref, *refs):
    *pieces, near_ref, far_ref, attended_ref, text_ref = refs
    me = 2 * place_ref[3] + place_ref[2]
    share = text_ref.shape[0]
    half = text_ref.shape[1] // 2
    count = len(pieces) // 2
    passed = [near_ref.at[at] for at in range(count)] + [far_ref.at[at] for at in range(count)]
    blocks = [block for piece, other in zip(pieces, passed) for block in (piece.at[0], other)]
    for at, block_ref in enumerate(blocks):
        device = me ^ (2 * masks[at // 2] + at % 2)
        head, copy = device // copies, device % copies
        start = pl.multiple_of(head * HEAD_DIM, HEAD_DIM)
        rows = pl.ds(pl.multiple_of(copy * part_rows, part_rows), part_rows)
        attended_ref[rows, pl.ds(start, HEAD_DIM)] = block_ref[:part_rows, :]
        block = block_ref[part_rows:, :].astype(jnp.float32)
        text_ref[:, pl.ds(start, HEAD_DIM)] = block[:share].astype(text_ref.dtype)
        start = pl.multiple_of(half + head * HEAD_DIM, HEAD_DIM)
        text_ref[:, pl.ds(start, HEAD_DIM)] = block[share:].astype(text_ref.dtype)


def unpack(copies, part_rows, masks, place, pieces, near, far):
    share = (near.shape[1] - part_rows) // 2
    return pl.pallas_call(
        functools.partial(unpack_kernel, copies, part_rows, masks),
        out_shape=(
            jax.ShapeDtypeStruct((part_rows * copies, HEADS * HEAD_DIM), jnp.bfloat16),
            jax.ShapeDtypeStruct((share, 2 * HEADS * HEAD_DIM), jnp.bfloat16),
        ),
        in_specs=[SMEM_SPEC] + [VMEM_SPEC] * (len(pieces) + 2),
        out_specs=(VMEM_SPEC, VMEM_SPEC),
        compiler_params=params(6),
        name="unpack",
    )(place, *pieces, near, far)


def image_kernel(factor, masks, img_dev, place_ref, packed_ref, sum_ref, top_ref, keys_ref, wide_ref):
    me = 2 * place_ref[3] + place_ref[2]
    wide_ref[:, HEAD_DIM:] = jnp.ones((wide_ref.shape[0], HEAD_DIM), wide_ref.dtype)
    for device in range(packed_ref.shape[0]):
        rows = slice(device * img_dev, (device + 1) * img_dev)
        keys_ref[rows, :] = packed_ref[device, :img_dev, :]
        wide_ref[rows, :HEAD_DIM] = packed_ref[device, img_dev : 2 * img_dev, :]
    group = max(1, 256 // (packed_ref.shape[1] - 2 * img_dev))
    rows = 256
    contract = (((1,), (1,)), ((), ()))
    count = sum_ref.shape[0]
    for start in range(0, count, rows):
        span = slice(start, start + rows)
        at = start // rows * group
        queries = [
            packed_ref[me ^ (2 * masks[i // 2] + i % 2), 2 * img_dev :, :] for i in range(at, at + group)
        ]
        queries = jnp.concatenate(queries, 0)
        scores = lax.dot_general(queries, keys_ref[...], contract, preferred_element_type=jnp.float32)
        scores = scores * factor
        top = jnp.max(scores, 1, keepdims=True)
        weights = jnp.exp2(scores - top).astype(jnp.bfloat16)
        sum_ref[span, :] = jnp.dot(weights, wide_ref[...], preferred_element_type=jnp.float32)
        top_ref[span, :] = jnp.broadcast_to(top, (rows, HEAD_DIM))


def image_attention(place, packed, img_dev, factor, masks):
    count = 2 * len(masks) * (packed.shape[1] - 2 * img_dev)
    total = packed.shape[0] * img_dev
    return pl.pallas_call(
        functools.partial(image_kernel, factor, masks, img_dev),
        out_shape=(
            jax.ShapeDtypeStruct((count, 2 * HEAD_DIM), jnp.float32),
            jax.ShapeDtypeStruct((count, HEAD_DIM), jnp.float32),
        ),
        in_specs=[SMEM_SPEC, VMEM_SPEC],
        out_specs=(VMEM_SPEC, VMEM_SPEC),
        scratch_shapes=[
            pltpu.VMEM((total, HEAD_DIM), jnp.bfloat16),
            pltpu.VMEM((total, 2 * HEAD_DIM), jnp.bfloat16),
        ],
        compiler_params=params(14),
        cost_estimate=pl.CostEstimate(
            flops=4 * count * total * HEAD_DIM,
            bytes_accessed=4 * total * HEAD_DIM + 10 * count * HEAD_DIM,
            transcendentals=count * total,
        ),
        name="image_attention",
    )(place, packed)


def send_order(chips):
    half = chips // 2
    turns = [mask for at in range(half) for mask in (half + at, half - 1 - at)]
    return turns[:half], turns[half:]


def finish_kernel(factor, masks, img_dev, place_ref, packed_ref, *refs):
    images, mine_ref, got_ref, *outs, text_ref = refs[:4], *refs[4:]
    core, valid = place_ref[2], place_ref[4]
    me = 2 * place_ref[3] + core
    part_rows = packed_ref.shape[1] - 2 * img_dev
    half = mine_ref.shape[0]
    contract = (((1,), (1,)), ((), ()))
    mine, got = mine_ref[...], got_ref[...]
    keys = jnp.concatenate([mine[:, :HEAD_DIM], got[:, :HEAD_DIM]], 0)
    values = jnp.concatenate([mine[:, HEAD_DIM:], got[:, HEAD_DIM:]], 0)
    values = jnp.concatenate([values, jnp.ones(values.shape, values.dtype)], 1)
    lane = lax.broadcasted_iota(jnp.int32, (1, 2 * half), 1)
    text_position = jnp.where((lane >= half) == (core == 0), half, 0) + lane % half
    bias = jnp.where(text_position < valid, 0.0, -jnp.inf)
    group = max(1, 512 // part_rows)
    rows = group * part_rows
    each = len(outs) // group
    for step in range(2 * each):
        sum_ref, top_ref = images[step // each * 2 : step // each * 2 + 2]
        span = slice(step % each * rows, (step % each + 1) * rows)
        queries = [
            packed_ref[me ^ (2 * masks[at // 2] + at % 2), 2 * img_dev :, :]
            for at in range(step * group, (step + 1) * group)
        ]
        queries = jnp.concatenate(queries, 0)
        scores = lax.dot_general(queries, keys, contract, preferred_element_type=jnp.float32)
        scores = scores * factor + bias
        before = top_ref[span, :]
        top = jnp.maximum(before, jnp.max(scores, 1, keepdims=True))
        rescale = jnp.exp2(before - top)
        weights = jnp.exp2(scores - jnp.concatenate([top] * (2 * half // HEAD_DIM), 1))
        total = jnp.dot(weights.astype(jnp.bfloat16), values, preferred_element_type=jnp.float32)
        mixed = sum_ref[span, :HEAD_DIM] * rescale + total[:, :HEAD_DIM]
        total = sum_ref[span, HEAD_DIM:] * rescale + total[:, HEAD_DIM:]
        mixed = (mixed / total).astype(jnp.bfloat16)
        for at in range(group):
            to = step * group + at
            outs[to // 2][to % 2, :part_rows, :] = mixed[at * part_rows : (at + 1) * part_rows]
    low, high = mine.astype(jnp.float32), got.astype(jnp.float32)
    text_ref[:half, :] = jnp.where(core == 0, low, high)
    text_ref[half:, :] = jnp.where(core == 0, high, low)
    share = (outs[0].shape[1] - part_rows) // 2
    for to in range(2 * len(outs)):
        start = pl.multiple_of((me ^ (2 * masks[to // 2] + to % 2)) * share, share)
        block = text_ref[pl.ds(start, share), :]
        block = jnp.concatenate([block[:, :HEAD_DIM], block[:, HEAD_DIM:]], 0)
        outs[to // 2][to % 2, part_rows:, :] = block.astype(jnp.bfloat16)


def finish(place, masks, packed, images, mine, got, img_dev, factor):
    devices, part_rows = packed.shape[0], packed.shape[1] - 2 * img_dev
    half = mine.shape[0]
    count = 2 * images[0].shape[0]
    outs = count // part_rows // 2
    out = jax.ShapeDtypeStruct((2, part_rows + 4 * half // devices, HEAD_DIM), jnp.bfloat16)
    return pl.pallas_call(
        functools.partial(finish_kernel, factor, masks, img_dev),
        out_shape=(out,) * outs,
        in_specs=[SMEM_SPEC] + [VMEM_SPEC] * 7,
        out_specs=(VMEM_SPEC,) * outs,
        scratch_shapes=[pltpu.VMEM((2 * half, 2 * HEAD_DIM), jnp.float32)],
        compiler_params=params(10),
        cost_estimate=pl.CostEstimate(
            flops=8 * count * half * HEAD_DIM,
            bytes_accessed=12 * count * HEAD_DIM,
            transcendentals=2 * count * half,
        ),
        name="finish",
    )(place, packed, *images, mine, got)


def gather_kernel(*refs):
    for at, piece in enumerate(refs[:-1]):
        refs[-1][at] = piece[1]


def gather_other(pieces):
    shape = (len(pieces),) + pieces[0].shape[1:]
    return pl.pallas_call(
        gather_kernel,
        out_shape=jax.ShapeDtypeStruct(shape, pieces[0].dtype),
        in_specs=[VMEM_SPEC] * len(pieces),
        out_specs=VMEM_SPEC,
        compiler_params=params(4),
        cost_estimate=pl.CostEstimate(
            flops=0, bytes_accessed=2 * len(pieces) * pieces[0].size, transcendentals=0
        ),
        name="gather_other",
    )(*pieces)


def add_kernel(joint, *refs):
    ins, outs = refs[:4], refs[4:]
    if joint:
        outs = (outs[0].at[0], outs[1], outs[0].at[1], outs[2])
    for lane in range(2):
        mine, got = ins[2 * lane], ins[2 * lane + 1]
        half = mine.shape[0] // 2
        outs[2 * lane][...] = (
            mine[half:].astype(jnp.float32) + got[half:].astype(jnp.float32)
        ).astype(jnp.bfloat16)
        outs[2 * lane + 1][...] = mine[:half].astype(jnp.float32) + got[:half].astype(jnp.float32)


def add_halves(mine, got, joint=False):
    shape = (mine[0].shape[0] // 2,) + mine[0].shape[1:]
    sent, keep = jax.ShapeDtypeStruct(shape, jnp.bfloat16), jax.ShapeDtypeStruct(shape, jnp.float32)
    outs = (sent, keep) * 2
    if joint:
        outs = (jax.ShapeDtypeStruct((2,) + shape, jnp.bfloat16), keep, keep)
    outs = pl.pallas_call(
        functools.partial(add_kernel, joint),
        out_shape=outs,
        in_specs=[VMEM_SPEC] * 4,
        out_specs=(VMEM_SPEC,) * len(outs),
        compiler_params=params(6),
        cost_estimate=pl.CostEstimate(
            flops=2 * mine[0].size, bytes_accessed=12 * mine[0].size, transcendentals=0
        ),
        name="add_halves",
    )(mine[0], got[0], mine[1], got[1])
    if joint:
        return outs[0], outs[1:]
    return [outs[0], outs[2]], [outs[1], outs[3]]


def total_kernel(mine0, got0, mine1, got1, out_ref):
    for lane, (mine, got) in enumerate(((mine0, got0), (mine1, got1))):
        out_ref[lane] = (mine[...] + got[...].astype(jnp.float32)).astype(out_ref.dtype)


def add_all(mine, got):
    return pl.pallas_call(
        total_kernel,
        out_shape=jax.ShapeDtypeStruct((2,) + mine[0].shape, jnp.bfloat16),
        in_specs=[VMEM_SPEC] * 4,
        out_specs=VMEM_SPEC,
        compiler_params=params(4),
        cost_estimate=pl.CostEstimate(
            flops=2 * mine[0].size, bytes_accessed=16 * mine[0].size, transcendentals=0
        ),
        name="add_all",
    )(mine[0], got[0], mine[1], got[1])


def norm_kernel(mine_ref, got_ref, gain_ref, out0, out1):
    width = mine_ref.shape[3]
    for at in range(2):
        totals = [
            mine_ref[lane, at].astype(jnp.float32) + got_ref[lane, 1 - at].astype(jnp.float32)
            for lane in range(2)
        ]
        square = sum(jnp.sum(total * total, 1, keepdims=True) for total in totals)
        scale_rows = lax.rsqrt(square / (2 * width) + epsilon)
        for lane, (total, out_ref) in enumerate(zip(totals, (out0, out1))):
            gain = gain_ref[:, lane * width : (lane + 1) * width].astype(jnp.float32)
            out_ref[at] = (total * scale_rows * gain).astype(out_ref.dtype)


def normalize(mine, got, norm_gain):
    out = jax.ShapeDtypeStruct(mine.shape[1:], jnp.bfloat16)
    states = pl.pallas_call(
        norm_kernel,
        out_shape=(out, out),
        in_specs=[VMEM_SPEC] * 3,
        out_specs=(VMEM_SPEC,) * 2,
        compiler_params=params(4),
        cost_estimate=pl.CostEstimate(
            flops=4 * mine.size, bytes_accessed=8 * mine.size, transcendentals=0
        ),
        name="normalize",
    )(mine, got, norm_gain)
    return [part.reshape(-1, part.shape[2]) for part in states]


def join_kernel(mine0, got0, mine1, got1, out0, out1):
    for mine, got, out_ref in ((mine0, got0, out0), (mine1, got1, out1)):
        rows = mine.shape[0]
        if rows % 16:
            both = [mine[...].astype(jnp.float32), got[...].astype(jnp.float32)]
            out_ref[...] = jnp.concatenate(both, 0).astype(out_ref.dtype)
        else:
            out_ref[:rows, :] = mine[...]
            out_ref[rows:, :] = got[...]


def join(mine, got):
    rows, width = mine[0].shape
    out = jax.ShapeDtypeStruct((2 * rows, width), mine[0].dtype)
    return pl.pallas_call(
        join_kernel,
        out_shape=(out, out),
        in_specs=[VMEM_SPEC] * 4,
        out_specs=(VMEM_SPEC,) * 2,
        compiler_params=params(4),
        cost_estimate=pl.CostEstimate(
            flops=0, bytes_accessed=16 * rows * width, transcendentals=0
        ),
        name="join",
    )(mine[0], got[0], mine[1], got[1])


def local(
    enc_act,
    down_weight,
    norm_gain,
    text_in_weight,
    modulation_weight,
    key_value_weight,
    timesteps,
    lengths,
    image_queries,
    image_key_values,
):
    devices = lax.axis_size("seq")
    chips = devices // 2
    copies = devices // HEADS
    text_len = enc_act.shape[1]
    img_dev = image_queries.shape[1]
    part_rows = img_dev // copies
    factor = math.log2(math.e) / math.sqrt(HEAD_DIM)
    lanes = orders(chips)
    index = lax.axis_index("seq")
    chip, core = index // 2, index % 2
    place = jnp.stack([position(chip, lanes[0]), position(chip, lanes[1]), core, chip, lengths[0]])
    place = place.astype(jnp.int32)

    win0, kv0 = text_in_weight.T, key_value_weight
    mod0 = modulation_weight.transpose(1, 2, 0)
    time = time_embedding(timesteps)

    rounds = len(lanes[0])
    turns = send_order(chips)
    tie = lax.optimization_barrier

    def exchange(rows):
        return lax.all_to_all(rows, "seq", split_axis=0, concat_axis=0, tiled=True)

    image_key_values, image_queries = tie((image_key_values, image_queries))
    packed = pack(copies, image_queries[0], image_key_values[0, :, 0], image_key_values[0, :, 1])
    act, packed = tie((enc_act[0].T, packed))
    packed = exchange(packed)
    encoded = encoder(lanes, place, act, down_weight)
    keep, got = encoded[::2], [swap(other, 1) for other in encoded[1::2]]
    last = 2 * lanes[0][-1]
    for step in range(rounds - 1):
        sent, keep = add_halves(keep, got)
        got = [swap(part, 2 * order[step]) for part, order in zip(sent, lanes)]
    summed, packed = tie((add_all(keep, got), packed))
    summed, held, held_kv, held_mod = tie((summed, win0, kv0, mod0))
    win1, kv1, mod1 = swap(held, 1), swap(held_kv, 1), swap(held_mod, 1)
    got = swap(summed, last)

    states = normalize(summed, got, norm_gain[None, :])
    images = []
    for step in reversed(range(rounds - 1)):
        if step == 0:
            states, packed = tie((states, packed))
            image = image_attention(place, packed, img_dev, factor, turns[0])
        got = [swap(state, 2 * order[step]) for state, order in zip(states, lanes)]
        if step == rounds - 2:
            lines = modulation(time, mod0, mod1)
            got, win1, kv1, lines = tie((got, win1, kv1, lines))
        if step:
            states = join(states, got)
    got, image = tie((got, image))
    images += image
    states = [state for pair in zip(states, got) for state in pair]

    blocks = project(lanes, place, states, lines, win0, win1, kv0, kv1)
    keep, sent = [blocks[0], blocks[2]], [blocks[1], blocks[3]]
    for step in range(rounds - 1):
        if step == 0:
            sent, packed = tie((sent, packed))
            image = image_attention(place, packed, img_dev, factor, turns[1])
        got = [swap(part, 2 * order[step]) for part, order in zip(sent, lanes)]
        if step == 0:
            got, image = tie((got, image))
            images += image
        sent, keep = add_halves(keep, got, step == rounds - 2)
    parts = (*keep, swap(sent, last))
    model_width = text_in_weight.shape[1] * devices
    mine, sent = combine(place, parts, chips, text_len // 2, model_width)
    got = swap(sent, 1)

    masks, passed = turns[0] + turns[1], []
    blocks = finish(place, masks, packed, images, mine, got, img_dev, factor)
    pieces = [swap(block, 2 * mask) if mask else block for mask, block in zip(masks, blocks)]
    for call in range(2):
        passed.append(swap(gather_other(pieces[call * chips // 2 : (call + 1) * chips // 2]), 1))
    attended, text_kv = unpack(copies, part_rows, masks, place, pieces, *passed)
    return (attended[None], text_kv)


def solution(mesh):
    in_specs = (
        P("dp", None, "seq"),
        P("seq", None),
        P(),
        P(None, "seq"),
        P(None, None, "seq"),
        P("seq", None),
        P("dp"),
        P("dp"),
        P("dp", "seq", None),
        P("dp", "seq", None, None),
    )
    out_specs = (P("dp", "seq", None), P(("dp", "seq"), None))
    return jax.shard_map(local, mesh=mesh, in_specs=in_specs, out_specs=out_specs, check_vma=False)
```

```python
import functools
import math

import jax
import jax.numpy as jnp
from jax import lax
from jax.experimental import pallas as pl
from jax.experimental.pallas import tpu as pltpu
from jax.sharding import PartitionSpec as P

HEAD_DIM = 128
HEADS = 16
TEMB = 256
MIB = 1024 * 1024

epsilon = 1e-06

SMEM_SPEC = pl.BlockSpec(memory_space=pltpu.SMEM)
VMEM_SPEC = pl.BlockSpec(memory_space=pltpu.VMEM)


def params(mib):
    return pltpu.CompilerParams(vmem_limit_bytes=mib * MIB)


def swap(value, mask):
    devices = lax.axis_size("seq")
    return lax.ppermute(value, "seq", [(i, i ^ mask) for i in range(devices)])


def orders(chips):
    bits = [1 << i for i in range(chips.bit_length() - 1)]
    return (bits, [bits[1], bits[0]] + bits[2:])


def position(chip, order):
    last = len(order) - 1
    return sum(((chip >> (bit.bit_length() - 1)) & 1) << (last - i) for i, bit in enumerate(order))


def member(at, order):
    last = len(order) - 1
    return sum(bit for i, bit in enumerate(order) if (at >> (last - i)) & 1)


def time_embedding(timesteps):
    half_width = TEMB // 2
    freqs = jnp.exp(-math.log(10000.0) * jnp.arange(half_width, dtype=jnp.float32) / half_width)
    angles = timesteps.astype(jnp.float32)[:, None] * freqs[None, :]
    embedding = jnp.concatenate([jnp.cos(angles), jnp.sin(angles)], 1)
    return jax.nn.silu(embedding).astype(jnp.bfloat16)


def encoder_kernel(lanes, place_ref, act_ref, weight_ref, *refs):
    outs, lhs_ref = refs[:-1], refs[-1]
    chips, share, width = outs[0].shape
    core = place_ref[2]
    half = chips * share
    first = core == 0
    tile = width // 2
    lhs_ref[...] = act_ref[...].T
    for lane, order in enumerate(lanes):
        own_ref, other_ref = outs[2 * lane], outs[2 * lane + 1]
        for column in range(0, width, tile):
            start = lane * width + column
            result = jnp.dot(
                lhs_ref[...], weight_ref[:, start : start + tile], preferred_element_type=jnp.float32
            )
            own = jnp.where(first, result[:half], result[half:]).astype(own_ref.dtype)
            other = jnp.where(first, result[half:], result[:half]).astype(own_ref.dtype)
            own = own.reshape(chips, share, tile)
            other = other.reshape(chips, share, tile)
            for block in range(chips):
                to = place_ref[lane] ^ position(block, order)
                own_ref[to, :, column : column + tile] = own[block]
                other_ref[to, :, column : column + tile] = other[block]


def encoder(lanes, place, act, weight):
    chips = 1 << len(lanes[0])
    depth, rows = act.shape
    width = weight.shape[1]
    out = jax.ShapeDtypeStruct((chips, rows // 2 // chips, width // 2), jnp.bfloat16)
    return pl.pallas_call(
        functools.partial(encoder_kernel, lanes),
        out_shape=(out,) * 4,
        in_specs=[SMEM_SPEC, VMEM_SPEC, VMEM_SPEC],
        out_specs=(VMEM_SPEC,) * 4,
        scratch_shapes=[pltpu.VMEM((rows, depth), jnp.bfloat16)],
        compiler_params=params(16),
        cost_estimate=pl.CostEstimate(
            flops=2 * rows * depth * width,
            bytes_accessed=2 * (depth * rows + depth * width + rows * width),
            transcendentals=0,
        ),
        name="encoder",
    )(place, act, weight)


def modulation_kernel(time_ref, mod0_ref, mod1_ref, out_ref):
    contract = (((1,), (1,)), ((), ()))
    embedding = jnp.broadcast_to(time_ref[...].astype(jnp.float32), (16, time_ref.shape[1]))
    embedding = embedding.astype(jnp.bfloat16)
    row = lax.broadcasted_iota(jnp.int32, (16, mod0_ref.shape[1]), 0)
    for side, mod in enumerate((mod0_ref, mod1_ref)):
        shift, scale = [
            lax.dot_general(embedding, mod[at], contract, preferred_element_type=jnp.float32)
            for at in range(2)
        ]
        lines = jnp.where(row < 2, 1.0 + scale, shift)
        high = lines.astype(jnp.bfloat16).astype(jnp.float32)
        low = jnp.where(row % 2 == 0, high, lines - high)
        out_ref[side] = jnp.where(row < 4, low, 1.0 + scale)


def modulation(time, mod0, mod1):
    return pl.pallas_call(
        modulation_kernel,
        out_shape=jax.ShapeDtypeStruct((2, 16, mod0.shape[1]), jnp.float32),
        in_specs=[VMEM_SPEC] * 3,
        out_specs=VMEM_SPEC,
        compiler_params=params(4),
        name="modulation",
    )(time, mod0, mod1)


def slot_rows(chips, width):
    means, squares = chips * 2 * 128 // width, chips * 128 // width
    return means, squares, -(-max(means + chips, squares + chips + 2) // 16) * 16


def project_kernel(lanes, place_ref, *refs):
    pieces, refs = (refs[:2], refs[2:4]), refs[4:]
    lines_ref, win0, win1, kv0, kv1, *outs, states, proj0, proj1, sums, keys_shift = refs
    chip = place_ref[3]
    half_chips = outs[0].shape[0]
    chips = 2 * half_chips
    rows = proj0.shape[0]
    share = rows // chips
    depth = states.shape[1]
    contract = (((1,), (1,)), ((), ()))
    for lane, order in enumerate(lanes):
        top, low = pieces[lane]
        states[: rows // 2, :] = top[...]
        states[rows // 2 :, :] = low[...]
        span = slice(lane * depth, (lane + 1) * depth)
        for win, proj in ((win0, proj0), (win1, proj1)):
            part = lax.dot_general(
                states[...], win[:, span], contract, preferred_element_type=jnp.float32
            )
            for at in range(chips):
                start = pl.multiple_of((chip ^ member(at, order)) * share, share)
                block = part[at * share : (at + 1) * share]
                if lane == 0:
                    proj[pl.ds(start, share), :] = block
                else:
                    proj[pl.ds(start, share), :] += block
    mean = jnp.sum(proj0[...], 1, keepdims=True) + jnp.sum(proj1[...], 1, keepdims=True)
    mean = mean / (2 * proj0.shape[1])
    value0, value1 = proj0[...] - mean, proj1[...] - mean
    square = jnp.sum(value0 * value0, 1, keepdims=True) + jnp.sum(value1 * value1, 1, keepdims=True)
    lane = lax.broadcasted_iota(jnp.int32, sums.shape, 1)
    sums[...] = jnp.where(lane == 0, mean, square).T
    left = []
    for side, value in enumerate((value0, value1)):
        lines = lines_ref[side]
        row = lax.broadcasted_iota(jnp.int32, lines.shape, 0)
        lines, scale = jnp.where(row < 4, lines, 0.0), lines[4:5]
        left.append(jnp.concatenate([value * scale, lines], 0).astype(jnp.bfloat16))
    width = outs[0].shape[2]
    means, squares, extra = slot_rows(chips, width)
    row = lax.broadcasted_iota(jnp.int32, (extra, width), 0)
    column = lax.broadcasted_iota(jnp.int32, (extra, width), 1)
    half = kv0.shape[1] // 2
    for lane, order in enumerate(lanes):
        line = sums[lane : lane + 1, :]
        if lane == 0:
            high = line.astype(jnp.bfloat16).astype(jnp.float32)
            low = line - high
            if width > 128:
                line = jnp.concatenate([high, low], 1)
            else:
                line = jnp.where(row % 2 == 0, high, low)
            line = jnp.where(row // (means // chips) == chip, line, 0.0)
        else:
            place = row * (width // 128) + column // 128
            line = jnp.concatenate([line] * (width // 128), 1)
            line = jnp.where(place == chip, line, 0.0)
        base = (means, squares)[lane]
        for at in reversed(range(chips)):
            out_ref, to = outs[2 * lane + at // half_chips], at % half_chips
            target = chip ^ member(at, order)
            columns = pl.ds(pl.multiple_of(lane * half + target * width, width), width)
            value = jnp.dot(left[0], kv0[:, columns], preferred_element_type=jnp.float32)
            value += jnp.dot(left[1], kv1[:, columns], preferred_element_type=jnp.float32)
            out_ref[to, :rows, :] = value[:rows].astype(out_ref.dtype)
            scale = value[rows : rows + 1] + value[rows + 1 : rows + 2]
            shift = value[rows + 2 : rows + 3] + value[rows + 3 : rows + 4]
            below = jnp.where(row == base + chip, scale, line)
            if lane == 0:
                keys_shift[target] = jnp.broadcast_to(shift, keys_shift.shape[1:])
            else:
                below = jnp.where(row == base + chips, shift, below)
                below = jnp.where(row == base + chips + 1, keys_shift[target][:1], below)
            out_ref[to, rows:, :] = below.astype(out_ref.dtype)


def project(lanes, place, pieces, lines, win0, win1, kv0, kv1):
    chips = 1 << len(lanes[0])
    rows = 2 * pieces[0].shape[0]
    features, depth = win0.shape
    total = kv0.shape[1]
    width = total // 2 // chips
    extra = slot_rows(chips, width)[2]
    out = jax.ShapeDtypeStruct((chips // 2, rows + extra, width), jnp.bfloat16)
    return pl.pallas_call(
        functools.partial(project_kernel, lanes),
        out_shape=(out,) * 4,
        in_specs=[SMEM_SPEC] + [VMEM_SPEC] * 9,
        out_specs=(VMEM_SPEC,) * 4,
        scratch_shapes=[
            pltpu.VMEM((rows, depth // 2), jnp.bfloat16),
            pltpu.VMEM((rows, features), jnp.float32),
            pltpu.VMEM((rows, features), jnp.float32),
            pltpu.VMEM((rows, 128), jnp.float32),
            pltpu.VMEM((chips, 8, width), jnp.float32),
        ],
        compiler_params=params(14),
        cost_estimate=pl.CostEstimate(
            flops=4 * rows * features * (depth + total),
            bytes_accessed=2 * (rows * depth + 2 * features * (depth + total) + rows * total),
            transcendentals=0,
        ),
        name="project",
    )(place, *pieces, lines, win0, win1, kv0, kv1)


def combine_kernel(chips, model_width, place_ref, *refs):
    keep0, keep1, came_ref, mine_ref, sent_ref = refs
    core = place_ref[2]
    rows = mine_ref.shape[0]
    width = keep0.shape[2]
    means, squares, _ = slot_rows(chips, width)
    totals = [keep[0] + came_ref[lane, 0].astype(jnp.float32) for lane, keep in enumerate((keep0, keep1))]
    below = [total[rows:] for total in totals]
    if width > 128:
        mean = below[0][:chips, :128] + below[0][:chips, 128:]
    else:
        lines = [below[0][2 * at : 2 * at + 1] + below[0][2 * at + 1 : 2 * at + 2] for at in range(chips)]
        mean = jnp.concatenate(lines, 0)
    away = mean - jnp.mean(mean, 0, keepdims=True)
    square = jnp.sum(below[1][:squares], 0, keepdims=True)
    square = sum(square[:, at : at + 128] for at in range(0, width, 128))
    square += jnp.sum(away * away, 0, keepdims=True) * (model_width / chips)
    scale = lax.rsqrt(square / model_width + epsilon)
    turned = jnp.concatenate([away, scale, jnp.zeros((rows - chips - 1, rows), jnp.float32)], 0).T
    scale = turned[:, chips : chips + 1]
    texts = []
    for lane, total in enumerate(totals):
        base = (means, squares)[lane]
        text = total[:rows]
        for at in range(chips):
            text += turned[:, at : at + 1] * below[lane][base + at : base + at + 1]
        shift = below[1][squares + chips + 1 - lane : squares + chips + 2 - lane]
        texts.append(text * scale + shift)
    for part, text in enumerate(texts):
        span = slice(part * HEAD_DIM, (part + 1) * HEAD_DIM)
        if width > HEAD_DIM:
            low, high = text[:, :HEAD_DIM], text[:, HEAD_DIM:]
            mine_ref[:, span] = jnp.where(core == 0, low, high).astype(mine_ref.dtype)
            sent_ref[:, span] = jnp.where(core == 0, high, low).astype(mine_ref.dtype)
        else:
            mine_ref[:, span] = text.astype(mine_ref.dtype)
            sent_ref[:, span] = text.astype(mine_ref.dtype)


def combine(place, parts, chips, rows, model_width):
    out = jax.ShapeDtypeStruct((rows, 2 * HEAD_DIM), jnp.bfloat16)
    return pl.pallas_call(
        functools.partial(combine_kernel, chips, model_width),
        out_shape=(out, out),
        in_specs=[SMEM_SPEC] + [VMEM_SPEC] * 3,
        out_specs=(VMEM_SPEC, VMEM_SPEC),
        compiler_params=params(4),
        cost_estimate=pl.CostEstimate(
            flops=8 * rows * 512, bytes_accessed=12 * rows * 512, transcendentals=0
        ),
        name="combine",
    )(place, *parts)


def pack_kernel(copies, queries_ref, keys_ref, values_ref, out_ref):
    img_dev = keys_ref.shape[0]
    part_rows = img_dev // copies
    for device in range(out_ref.shape[0]):
        head, copy = device // copies, device % copies
        span = slice(head * HEAD_DIM, (head + 1) * HEAD_DIM)
        out_ref[device, :img_dev, :] = keys_ref[:, span]
        out_ref[device, img_dev : 2 * img_dev, :] = values_ref[:, span]
        out_ref[device, 2 * img_dev :, :] = queries_ref[copy * part_rows : (copy + 1) * part_rows, span]


def pack(copies, queries, keys, values):
    img_dev = keys.shape[0]
    rows = 2 * img_dev + img_dev // copies
    return pl.pallas_call(
        functools.partial(pack_kernel, copies),
        out_shape=jax.ShapeDtypeStruct((HEADS * copies, rows, HEAD_DIM), jnp.bfloat16),
        in_specs=[VMEM_SPEC] * 3,
        out_specs=VMEM_SPEC,
        compiler_params=params(8),
        cost_estimate=pl.CostEstimate(
            flops=0, bytes_accessed=4 * HEADS * copies * rows * HEAD_DIM, transcendentals=0
        ),
        name="pack",
    )(queries, keys, values)


def unpack_kernel(copies, part_rows, masks, place_ref, *refs):
    *pieces, near_ref, far_ref, attended_ref, text_ref = refs
    me = 2 * place_ref[3] + place_ref[2]
    share = text_ref.shape[0]
    half = text_ref.shape[1] // 2
    count = len(pieces) // 2
    passed = [near_ref.at[at] for at in range(count)] + [far_ref.at[at] for at in range(count)]
    blocks = [block for piece, other in zip(pieces, passed) for block in (piece.at[0], other)]
    for at, block_ref in enumerate(blocks):
        device = me ^ (2 * masks[at // 2] + at % 2)
        head, copy = device // copies, device % copies
        start = pl.multiple_of(head * HEAD_DIM, HEAD_DIM)
        rows = pl.ds(pl.multiple_of(copy * part_rows, part_rows), part_rows)
        attended_ref[rows, pl.ds(start, HEAD_DIM)] = block_ref[:part_rows, :]
        block = block_ref[part_rows:, :].astype(jnp.float32)
        text_ref[:, pl.ds(start, HEAD_DIM)] = block[:share].astype(text_ref.dtype)
        start = pl.multiple_of(half + head * HEAD_DIM, HEAD_DIM)
        text_ref[:, pl.ds(start, HEAD_DIM)] = block[share:].astype(text_ref.dtype)


def unpack(copies, part_rows, masks, place, pieces, near, far):
    share = (near.shape[1] - part_rows) // 2
    return pl.pallas_call(
        functools.partial(unpack_kernel, copies, part_rows, masks),
        out_shape=(
            jax.ShapeDtypeStruct((part_rows * copies, HEADS * HEAD_DIM), jnp.bfloat16),
            jax.ShapeDtypeStruct((share, 2 * HEADS * HEAD_DIM), jnp.bfloat16),
        ),
        in_specs=[SMEM_SPEC] + [VMEM_SPEC] * (len(pieces) + 2),
        out_specs=(VMEM_SPEC, VMEM_SPEC),
        compiler_params=params(6),
        name="unpack",
    )(place, *pieces, near, far)


def image_kernel(factor, masks, img_dev, place_ref, packed_ref, sum_ref, top_ref, keys_ref, wide_ref):
    me = 2 * place_ref[3] + place_ref[2]
    wide_ref[:, HEAD_DIM:] = jnp.ones((wide_ref.shape[0], HEAD_DIM), wide_ref.dtype)
    for device in range(packed_ref.shape[0]):
        rows = slice(device * img_dev, (device + 1) * img_dev)
        keys_ref[rows, :] = packed_ref[device, :img_dev, :]
        wide_ref[rows, :HEAD_DIM] = packed_ref[device, img_dev : 2 * img_dev, :]
    group = max(1, 256 // (packed_ref.shape[1] - 2 * img_dev))
    rows = 256
    contract = (((1,), (1,)), ((), ()))
    count = sum_ref.shape[0]
    for start in range(0, count, rows):
        span = slice(start, start + rows)
        at = start // rows * group
        queries = [
            packed_ref[me ^ (2 * masks[i // 2] + i % 2), 2 * img_dev :, :] for i in range(at, at + group)
        ]
        queries = jnp.concatenate(queries, 0)
        scores = lax.dot_general(queries, keys_ref[...], contract, preferred_element_type=jnp.float32)
        scores = scores * factor
        top = jnp.max(scores, 1, keepdims=True)
        weights = jnp.exp2(scores - top).astype(jnp.bfloat16)
        sum_ref[span, :] = jnp.dot(weights, wide_ref[...], preferred_element_type=jnp.float32)
        top_ref[span, :] = jnp.broadcast_to(top, (rows, HEAD_DIM))


def image_attention(place, packed, img_dev, factor, masks):
    count = 2 * len(masks) * (packed.shape[1] - 2 * img_dev)
    total = packed.shape[0] * img_dev
    return pl.pallas_call(
        functools.partial(image_kernel, factor, masks, img_dev),
        out_shape=(
            jax.ShapeDtypeStruct((count, 2 * HEAD_DIM), jnp.float32),
            jax.ShapeDtypeStruct((count, HEAD_DIM), jnp.float32),
        ),
        in_specs=[SMEM_SPEC, VMEM_SPEC],
        out_specs=(VMEM_SPEC, VMEM_SPEC),
        scratch_shapes=[
            pltpu.VMEM((total, HEAD_DIM), jnp.bfloat16),
            pltpu.VMEM((total, 2 * HEAD_DIM), jnp.bfloat16),
        ],
        compiler_params=params(14),
        cost_estimate=pl.CostEstimate(
            flops=4 * count * total * HEAD_DIM,
            bytes_accessed=4 * total * HEAD_DIM + 10 * count * HEAD_DIM,
            transcendentals=count * total,
        ),
        name="image_attention",
    )(place, packed)


def send_order(chips):
    half = chips // 2
    cut = half // 2
    far, near = list(range(half, chips)), list(range(half))[::-1]
    return far[:cut] + near[:cut], far[cut:] + near[cut:]


def finish_kernel(factor, masks, img_dev, place_ref, packed_ref, sum_ref, top_ref, mine_ref, got_ref, *refs):
    *outs, text_ref = refs
    core, valid = place_ref[2], place_ref[4]
    me = 2 * place_ref[3] + core
    part_rows = packed_ref.shape[1] - 2 * img_dev
    half = mine_ref.shape[0]
    contract = (((1,), (1,)), ((), ()))
    mine, got = mine_ref[...], got_ref[...]
    keys = jnp.concatenate([mine[:, :HEAD_DIM], got[:, :HEAD_DIM]], 0)
    values = jnp.concatenate([mine[:, HEAD_DIM:], got[:, HEAD_DIM:]], 0)
    values = jnp.concatenate([values, jnp.ones(values.shape, values.dtype)], 1)
    lane = lax.broadcasted_iota(jnp.int32, (1, 2 * half), 1)
    text_position = jnp.where((lane >= half) == (core == 0), half, 0) + lane % half
    bias = jnp.where(text_position < valid, 0.0, -jnp.inf)
    group = max(1, 512 // part_rows)
    rows = group * part_rows
    for step in range(2 * len(outs) // group):
        span = slice(step * rows, (step + 1) * rows)
        queries = [
            packed_ref[me ^ (2 * masks[at // 2] + at % 2), 2 * img_dev :, :]
            for at in range(step * group, (step + 1) * group)
        ]
        queries = jnp.concatenate(queries, 0)
        scores = lax.dot_general(queries, keys, contract, preferred_element_type=jnp.float32)
        scores = scores * factor + bias
        before = top_ref[span, :]
        top = jnp.maximum(before, jnp.max(scores, 1, keepdims=True))
        rescale = jnp.exp2(before - top)
        weights = jnp.exp2(scores - jnp.concatenate([top] * (2 * half // HEAD_DIM), 1))
        total = jnp.dot(weights.astype(jnp.bfloat16), values, preferred_element_type=jnp.float32)
        mixed = sum_ref[span, :HEAD_DIM] * rescale + total[:, :HEAD_DIM]
        total = sum_ref[span, HEAD_DIM:] * rescale + total[:, HEAD_DIM:]
        mixed = (mixed / total).astype(jnp.bfloat16)
        for at in range(group):
            to = step * group + at
            outs[to // 2][to % 2, :part_rows, :] = mixed[at * part_rows : (at + 1) * part_rows]
    low, high = mine.astype(jnp.float32), got.astype(jnp.float32)
    text_ref[:half, :] = jnp.where(core == 0, low, high)
    text_ref[half:, :] = jnp.where(core == 0, high, low)
    share = (outs[0].shape[1] - part_rows) // 2
    for to in range(2 * len(outs)):
        start = pl.multiple_of((me ^ (2 * masks[to // 2] + to % 2)) * share, share)
        block = text_ref[pl.ds(start, share), :]
        block = jnp.concatenate([block[:, :HEAD_DIM], block[:, HEAD_DIM:]], 0)
        outs[to // 2][to % 2, part_rows:, :] = block.astype(jnp.bfloat16)


def finish(place, masks, packed, image, mine, got, img_dev, factor):
    devices, part_rows = packed.shape[0], packed.shape[1] - 2 * img_dev
    half = mine.shape[0]
    count = image[0].shape[0]
    outs = count // part_rows // 2
    out = jax.ShapeDtypeStruct((2, part_rows + 4 * half // devices, HEAD_DIM), jnp.bfloat16)
    return pl.pallas_call(
        functools.partial(finish_kernel, factor, masks, img_dev),
        out_shape=(out,) * outs,
        in_specs=[SMEM_SPEC] + [VMEM_SPEC] * 5,
        out_specs=(VMEM_SPEC,) * outs,
        scratch_shapes=[pltpu.VMEM((2 * half, 2 * HEAD_DIM), jnp.float32)],
        compiler_params=params(10),
        cost_estimate=pl.CostEstimate(
            flops=8 * count * half * HEAD_DIM,
            bytes_accessed=12 * count * HEAD_DIM,
            transcendentals=2 * count * half,
        ),
        name="finish",
    )(place, packed, *image, mine, got)


def gather_kernel(*refs):
    for at, piece in enumerate(refs[:-1]):
        refs[-1][at] = piece[1]


def gather_other(pieces):
    shape = (len(pieces),) + pieces[0].shape[1:]
    return pl.pallas_call(
        gather_kernel,
        out_shape=jax.ShapeDtypeStruct(shape, pieces[0].dtype),
        in_specs=[VMEM_SPEC] * len(pieces),
        out_specs=VMEM_SPEC,
        compiler_params=params(4),
        cost_estimate=pl.CostEstimate(
            flops=0, bytes_accessed=2 * len(pieces) * pieces[0].size, transcendentals=0
        ),
        name="gather_other",
    )(*pieces)


def add_kernel(joint, *refs):
    ins, outs = refs[:4], refs[4:]
    if joint:
        outs = (outs[0].at[0], outs[1], outs[0].at[1], outs[2])
    for lane in range(2):
        mine, got = ins[2 * lane], ins[2 * lane + 1]
        half = mine.shape[0] // 2
        outs[2 * lane][...] = (
            mine[half:].astype(jnp.float32) + got[half:].astype(jnp.float32)
        ).astype(jnp.bfloat16)
        outs[2 * lane + 1][...] = mine[:half].astype(jnp.float32) + got[:half].astype(jnp.float32)


def add_halves(mine, got, joint=False):
    shape = (mine[0].shape[0] // 2,) + mine[0].shape[1:]
    sent, keep = jax.ShapeDtypeStruct(shape, jnp.bfloat16), jax.ShapeDtypeStruct(shape, jnp.float32)
    outs = (sent, keep) * 2
    if joint:
        outs = (jax.ShapeDtypeStruct((2,) + shape, jnp.bfloat16), keep, keep)
    outs = pl.pallas_call(
        functools.partial(add_kernel, joint),
        out_shape=outs,
        in_specs=[VMEM_SPEC] * 4,
        out_specs=(VMEM_SPEC,) * len(outs),
        compiler_params=params(6),
        cost_estimate=pl.CostEstimate(
            flops=2 * mine[0].size, bytes_accessed=12 * mine[0].size, transcendentals=0
        ),
        name="add_halves",
    )(mine[0], got[0], mine[1], got[1])
    if joint:
        return outs[0], outs[1:]
    return [outs[0], outs[2]], [outs[1], outs[3]]


def total_kernel(mine0, got0, mine1, got1, out_ref):
    for lane, (mine, got) in enumerate(((mine0, got0), (mine1, got1))):
        out_ref[lane] = (mine[...] + got[...].astype(jnp.float32)).astype(out_ref.dtype)


def add_all(mine, got):
    return pl.pallas_call(
        total_kernel,
        out_shape=jax.ShapeDtypeStruct((2,) + mine[0].shape, jnp.bfloat16),
        in_specs=[VMEM_SPEC] * 4,
        out_specs=VMEM_SPEC,
        compiler_params=params(4),
        cost_estimate=pl.CostEstimate(
            flops=2 * mine[0].size, bytes_accessed=16 * mine[0].size, transcendentals=0
        ),
        name="add_all",
    )(mine[0], got[0], mine[1], got[1])


def norm_kernel(mine_ref, got_ref, gain_ref, out0, out1):
    width = mine_ref.shape[3]
    for at in range(2):
        totals = [
            mine_ref[lane, at].astype(jnp.float32) + got_ref[lane, 1 - at].astype(jnp.float32)
            for lane in range(2)
        ]
        square = sum(jnp.sum(total * total, 1, keepdims=True) for total in totals)
        scale_rows = lax.rsqrt(square / (2 * width) + epsilon)
        for lane, (total, out_ref) in enumerate(zip(totals, (out0, out1))):
            gain = gain_ref[:, lane * width : (lane + 1) * width].astype(jnp.float32)
            out_ref[at] = (total * scale_rows * gain).astype(out_ref.dtype)


def normalize(mine, got, norm_gain):
    out = jax.ShapeDtypeStruct(mine.shape[1:], jnp.bfloat16)
    states = pl.pallas_call(
        norm_kernel,
        out_shape=(out, out),
        in_specs=[VMEM_SPEC] * 3,
        out_specs=(VMEM_SPEC,) * 2,
        compiler_params=params(4),
        cost_estimate=pl.CostEstimate(
            flops=4 * mine.size, bytes_accessed=8 * mine.size, transcendentals=0
        ),
        name="normalize",
    )(mine, got, norm_gain)
    return [part.reshape(-1, part.shape[2]) for part in states]


def join_kernel(mine0, got0, mine1, got1, out0, out1):
    for mine, got, out_ref in ((mine0, got0, out0), (mine1, got1, out1)):
        rows = mine.shape[0]
        if rows % 16:
            both = [mine[...].astype(jnp.float32), got[...].astype(jnp.float32)]
            out_ref[...] = jnp.concatenate(both, 0).astype(out_ref.dtype)
        else:
            out_ref[:rows, :] = mine[...]
            out_ref[rows:, :] = got[...]


def join(mine, got):
    rows, width = mine[0].shape
    out = jax.ShapeDtypeStruct((2 * rows, width), mine[0].dtype)
    return pl.pallas_call(
        join_kernel,
        out_shape=(out, out),
        in_specs=[VMEM_SPEC] * 4,
        out_specs=(VMEM_SPEC,) * 2,
        compiler_params=params(4),
        cost_estimate=pl.CostEstimate(
            flops=0, bytes_accessed=16 * rows * width, transcendentals=0
        ),
        name="join",
    )(mine[0], got[0], mine[1], got[1])


def local(
    enc_act,
    down_weight,
    norm_gain,
    text_in_weight,
    modulation_weight,
    key_value_weight,
    timesteps,
    lengths,
    image_queries,
    image_key_values,
):
    devices = lax.axis_size("seq")
    chips = devices // 2
    copies = devices // HEADS
    text_len = enc_act.shape[1]
    img_dev = image_queries.shape[1]
    part_rows = img_dev // copies
    factor = math.log2(math.e) / math.sqrt(HEAD_DIM)
    lanes = orders(chips)
    index = lax.axis_index("seq")
    chip, core = index // 2, index % 2
    place = jnp.stack([position(chip, lanes[0]), position(chip, lanes[1]), core, chip, lengths[0]])
    place = place.astype(jnp.int32)

    win0, kv0 = text_in_weight.T, key_value_weight
    mod0 = modulation_weight.transpose(1, 2, 0)
    time = time_embedding(timesteps)

    rounds = len(lanes[0])
    turns = send_order(chips)
    tie = lax.optimization_barrier

    def exchange(rows):
        return lax.all_to_all(rows, "seq", split_axis=0, concat_axis=0, tiled=True)

    image_key_values, image_queries = tie((image_key_values, image_queries))
    packed = pack(copies, image_queries[0], image_key_values[0, :, 0], image_key_values[0, :, 1])
    act, packed = tie((enc_act[0].T, packed))
    packed = exchange(packed)
    encoded = encoder(lanes, place, act, down_weight)
    keep, got = encoded[::2], [swap(other, 1) for other in encoded[1::2]]
    last = 2 * lanes[0][-1]
    for step in range(rounds - 1):
        sent, keep = add_halves(keep, got)
        got = [swap(part, 2 * order[step]) for part, order in zip(sent, lanes)]
    summed, packed = tie((add_all(keep, got), packed))
    summed, held, held_kv, held_mod = tie((summed, win0, kv0, mod0))
    win1, kv1, mod1 = swap(held, 1), swap(held_kv, 1), swap(held_mod, 1)
    got = swap(summed, last)

    states = normalize(summed, got, norm_gain[None, :])
    images = []
    for step in reversed(range(rounds - 1)):
        if step == 0:
            states, packed = tie((states, packed))
            image = image_attention(place, packed, img_dev, factor, turns[0])
        got = [swap(state, 2 * order[step]) for state, order in zip(states, lanes)]
        if step == rounds - 2:
            lines = modulation(time, mod0, mod1)
            got, win1, kv1, lines = tie((got, win1, kv1, lines))
        if step:
            states = join(states, got)
    got, image = tie((got, image))
    images += image
    states = [state for pair in zip(states, got) for state in pair]

    blocks = project(lanes, place, states, lines, win0, win1, kv0, kv1)
    keep, sent = [blocks[0], blocks[2]], [blocks[1], blocks[3]]
    for step in range(rounds - 1):
        if step == 0:
            sent, packed = tie((sent, packed))
            image = image_attention(place, packed, img_dev, factor, turns[1])
        got = [swap(part, 2 * order[step]) for part, order in zip(sent, lanes)]
        if step == 0:
            got, image = tie((got, image))
            images += image
        sent, keep = add_halves(keep, got, step == rounds - 2)
    parts = (*keep, swap(sent, last))
    model_width = text_in_weight.shape[1] * devices
    mine, sent = combine(place, parts, chips, text_len // 2, model_width)
    got = swap(sent, 1)

    pieces, passed = [], []
    for call, masks in enumerate(turns):
        image = images[2 * call : 2 * call + 2]
        blocks = finish(place, masks, packed, image, mine, got, img_dev, factor)
        pieces += [swap(block, 2 * mask) if mask else block for mask, block in zip(masks, blocks)]
    for call in range(2):
        passed.append(swap(gather_other(pieces[call * chips // 2 : (call + 1) * chips // 2]), 1))
    attended, text_kv = unpack(copies, part_rows, turns[0] + turns[1], place, pieces, *passed)
    return (attended[None], text_kv)


def solution(mesh):
    in_specs = (
        P("dp", None, "seq"),
        P("seq", None),
        P(),
        P(None, "seq"),
        P(None, None, "seq"),
        P("seq", None),
        P("dp"),
        P("dp"),
        P("dp", "seq", None),
        P("dp", "seq", None, None),
    )
    out_specs = (P("dp", "seq", None), P(("dp", "seq"), None))
    return jax.shard_map(local, mesh=mesh, in_specs=in_specs, out_specs=out_specs, check_vma=False)
```
